32 devices in a mesh: batch: 8 (over z, core), ctx: 4 (over y, x).
Axes of the slice: x: 2, y: 2, z: 4, core: 2. Of those that a mesh axis runs over, the one named last changes fastest.
Arguments:
- tokens: bfloat16 [8, 512, 2048], P('batch', 'ctx'), may hold values from -6 to 6
- out_grad: bfloat16 [8, 512, 2048], P('batch', 'ctx'), may hold values from -6 to 6
- ln1_gain: bfloat16 [2048], P(('batch', 'ctx')), may hold values from 0.5 to 1.5
- ln1_shift: bfloat16 [2048], P(('batch', 'ctx')), may hold values from -3 to 3
- qkv_weight: bfloat16 [2048, 6144], P(('batch', 'ctx')), may hold values from -0.125 to 0.125
- qkv_bias: bfloat16 [6144], P(('batch', 'ctx')), may hold values from -3 to 3
- out_weight: bfloat16 [2048, 2048], P(('batch', 'ctx')), may hold values from -1 to 1
- ln2_gain: bfloat16 [2048], P(('batch', 'ctx')), may hold values from 0.5 to 1.5
- ln2_shift: bfloat16 [2048], P(('batch', 'ctx')), may hold values from -3 to 3
- gate_weight: bfloat16 [2048, 5632], P(('batch', 'ctx')), may hold values from -0.125 to 0.125
- up_weight: bfloat16 [2048, 5632], P(('batch', 'ctx')), may hold values from -0.125 to 0.125
- down_weight: bfloat16 [2048, 5632], P(('batch', 'ctx')), may hold values from -0.078125 to 0.078125
Outputs:
- mixed: bfloat16 [8, 512, 2048], P('batch', 'ctx')
- tokens_grad: float32 [8, 512, 2048], P('batch', 'ctx')
- ln1_gain_grad: float32 [2048], P(('batch', 'ctx'))
- ln1_shift_grad: float32 [2048], P(('batch', 'ctx'))
- qkv_weight_grad: float32 [2048, 6144], P(('batch', 'ctx'))
- qkv_bias_grad: float32 [6144], P(('batch', 'ctx'))
- out_weight_grad: float32 [2048, 2048], P(('batch', 'ctx'))
- ln2_gain_grad: float32 [2048], P(('batch', 'ctx'))
- ln2_shift_grad: float32 [2048], P(('batch', 'ctx'))
- gate_weight_grad: float32 [2048, 5632], P(('batch', 'ctx'))
- up_weight_grad: float32 [2048, 5632], P(('batch', 'ctx'))
- down_weight_grad: float32 [2048, 5632], P(('batch', 'ctx'))
The draws below stay inside these ranges and needn't reach their ends.
All inputs are finite; a program needn't handle non-finite values.
Results may differ from the reference program's by a relative error of at most 0.03.
Values may be sent and summed in bfloat16 or wider, within the bound.
A program may use at most 576 MiB of HBM per device.

```python
import jax
import jax.numpy as jnp
from jax import lax

D = 2048
FF = 5632
H = 32
HD = 64
ROT = 16
LENGTH = 512
NSEQ = 8


def shard_levels(own_key, extent, split, smallest, high):
    def one(dim, shards_of):
        heights = jax.random.uniform(jax.random.fold_in(jax.random.fold_in(own_key, 6), dim), (shards_of,), jnp.float32, smallest / len(split), high / len(split))
        return jnp.repeat(jnp.exp(heights), extent[dim] // shards_of).reshape((-1,) + (1,) * (len(extent) - dim - 1))

    level = one(*split[0])
    for cut in split[1:]:
        level = level * one(*cut)
    return level


def scatter_about(stream_key, extent, scale, reach, pieces=(), held_as=jnp.bfloat16):
    level = shard_levels(stream_key, extent, pieces, -0.22, 0.18) if pieces else 1.0
    values = jax.random.normal(stream_key, extent, jnp.float32) * scale * level
    return jnp.minimum(jnp.maximum(values, -reach), reach).astype(held_as)


def setup_inputs(seed: int = 0) -> dict:
    seeds = jax.random.split(jax.random.key(seed), 13)
    tokens = scatter_about(seeds[0], (NSEQ, LENGTH, D), 1.0, 6.0, ((0, 8), (1, 4)))
    out_grad = scatter_about(seeds[1], (NSEQ, LENGTH, D), 1.0, 6.0, ((0, 8), (1, 4)))
    ln1_gain = jnp.clip(1.0 + 0.1 * jax.random.normal(seeds[2], (D,), jnp.float32), 0.5, 1.5).astype(jnp.bfloat16)
    ln1_shift = scatter_about(seeds[3], (D,), 0.5, 3.0, ((0, 32),))
    qkv_weight = scatter_about(seeds[4], (D, 3 * D), D ** -0.5, 0.125, ((0, 32),))
    qkv_bias = scatter_about(seeds[5], (3 * D,), 0.5, 3.0, ((0, 32),))
    out_weight = scatter_about(seeds[6], (D, D), (D // 64) ** -0.5, 1.0, ((0, 32),))
    ln2_gain = jnp.clip(1.0 + 0.1 * jax.random.normal(seeds[7], (D,), jnp.float32), 0.5, 1.5).astype(jnp.bfloat16)
    ln2_shift = scatter_about(seeds[8], (D,), 0.5, 3.0, ((0, 32),))
    gate_weight = scatter_about(seeds[9], (D, FF), D ** -0.5, 0.125, ((0, 32),))
    up_weight = scatter_about(seeds[10], (D, FF), D ** -0.5, 0.125, ((0, 32),))
    down_weight = scatter_about(seeds[11], (D, FF), FF ** -0.5, 0.078125, ((0, 32),))
    return dict(tokens=tokens, out_grad=out_grad, ln1_gain=ln1_gain, ln1_shift=ln1_shift, qkv_weight=qkv_weight, qkv_bias=qkv_bias, out_weight=out_weight, ln2_gain=ln2_gain, ln2_shift=ln2_shift, gate_weight=gate_weight, up_weight=up_weight, down_weight=down_weight)


@jax.custom_vjp
def low(v):
    return lax.optimization_barrier(v.astype(jnp.bfloat16)).astype(jnp.float32)

@jax.custom_vjp
def low_back(v):
    return v

def low_keep(v):
    return (low(v), None)

def low_pass(kept, grad):
    return (grad,)

def back_keep(v):
    return (v, None)

def back_low(kept, grad):
    return (low(grad),)
low.defvjp(low_keep, low_pass)
low_back.defvjp(back_keep, back_low)

def matmul(left, right):
    return jnp.dot(left, right, preferred_element_type=jnp.float32, precision=lax.Precision.HIGHEST)

def layer_norm(values, gain, shift):
    centre = lax.optimization_barrier(jnp.mean(values, axis=-1, keepdims=True))
    centred = values - centre
    spread = lax.optimization_barrier(jnp.mean(centred * centred, axis=-1, keepdims=True))
    return centred * lax.rsqrt(spread + 1e-05) * gain + shift

def rotary(values, positions):
    half_dims = ROT // 2
    frequency = 10000.0 ** (-jnp.arange(half_dims, dtype=jnp.float32) * 2.0 / ROT)
    angles = positions.astype(jnp.float32)[:, None] * frequency[None, :]
    cosine_term = jnp.cos(angles)[:, None, :]
    sine_term = jnp.sin(angles)[:, None, :]
    first_half = values[..., :half_dims]
    second_half = values[..., half_dims:ROT]
    return jnp.concatenate([first_half * cosine_term - second_half * sine_term, second_half * cosine_term + first_half * sine_term, values[..., ROT:]], axis=-1)

def attention(queries, keys, values):
    block_rows = 512 if LENGTH % 512 == 0 else LENGTH
    key_places = jnp.arange(LENGTH, dtype=jnp.int32)

    def one_block(query_pair):
        query_block, first_row = query_pair
        raw_scores = jnp.einsum('qhd,khd->hqk', query_block, keys, precision=lax.Precision.HIGHEST)
        scores = low_back(raw_scores * 0.125)
        query_places = first_row + jnp.arange(block_rows, dtype=jnp.int32)
        allowed = (key_places[None, :] <= query_places[:, None])[None]
        scores = jnp.where(allowed, scores, -1e+30)
        largest = lax.optimization_barrier(jnp.max(scores, axis=-1, keepdims=True))
        weights = jnp.where(allowed, jnp.exp(scores - largest), 0.0)
        weights = weights / lax.optimization_barrier(jnp.sum(weights, axis=-1, keepdims=True))
        return jnp.einsum('hqk,khd->qhd', low(weights), values, precision=lax.Precision.HIGHEST)
    starts = jnp.arange(LENGTH // block_rows, dtype=jnp.int32) * block_rows
    outputs = lax.map(jax.checkpoint(one_block), (queries.reshape(LENGTH // block_rows, block_rows, H, HD), starts))
    return outputs.reshape(LENGTH, H * HD)

def residual_block(inputs, ln1_gain, ln1_shift, qkv_weight, qkv_bias, out_weight, ln2_gain, ln2_shift, gate_weight, up_weight, down_weight):
    places = jnp.arange(LENGTH, dtype=jnp.int32)
    normed = low(layer_norm(inputs, ln1_gain, ln1_shift))
    projected = low_back(matmul(normed, qkv_weight) + qkv_bias)
    turned = rotary(projected[:, :2 * D].reshape(LENGTH, 2 * H, HD), places)
    queries = low(turned[:, :H])
    keys = low(turned[:, H:])
    values = low(projected[:, 2 * D:].reshape(LENGTH, H, HD))
    attended = low_back(low(attention(queries, keys, values)))
    middle = inputs + low_back(matmul(attended, out_weight))
    normed_two = low(layer_norm(middle, ln2_gain, ln2_shift))
    gate_value = low_back(matmul(normed_two, gate_weight))
    up_value = low_back(matmul(normed_two, up_weight))
    hidden = low(gate_value / (1.0 + jnp.exp(-gate_value)) * up_value)
    branch_out = lax.dot_general(hidden, down_weight, (((1,), (1,)), ((), ())), precision=lax.Precision.HIGHEST, preferred_element_type=jnp.float32)
    return middle + low_back(branch_out)

def reference(tokens, out_grad, ln1_gain, ln1_shift, qkv_weight, qkv_bias, out_weight, ln2_gain, ln2_shift, gate_weight, up_weight, down_weight):
    params = tuple((member.astype(jnp.float32) for member in (ln1_gain, ln1_shift, qkv_weight, qkv_bias, out_weight, ln2_gain, ln2_shift, gate_weight, up_weight, down_weight)))

    def per_sequence(running, seq_pair):
        inputs, cotangent = seq_pair
        result, pullback = jax.vjp(residual_block, inputs.astype(jnp.float32), *params)
        gradients = pullback(cotangent.astype(jnp.float32))
        running = tuple((earlier + one_grad for earlier, one_grad in zip(running, gradients[1:])))
        return (running, (result.astype(jnp.bfloat16), gradients[0]))
    zeros_start = tuple((jnp.zeros(member.shape, jnp.float32) for member in params))
    totals, (outputs, input_grads) = lax.scan(per_sequence, zeros_start, (tokens, out_grad))
    return (outputs, input_grads, totals[0], totals[1], totals[2], totals[3], totals[4], totals[5], totals[6], totals[7], totals[8], totals[9])
```

```python
import functools

import jax
import jax.numpy as jnp
import numpy as np
from jax import lax
from jax.experimental import pallas as pl
from jax.experimental.pallas import tpu as pltpu
from jax.sharding import PartitionSpec as P

D = 2048
FF = 5632
H = 32
HD = 64
ROT = 16


def layer_norm(values, gain, shift):
    centre = jnp.mean(values, axis=-1, keepdims=True)
    centred = values - centre
    spread = jnp.mean(centred * centred, axis=-1, keepdims=True)
    return centred * lax.rsqrt(spread + 1e-05) * gain + shift


def rotary(values, positions):
    half_dims = ROT // 2
    frequency = 10000.0 ** (-jnp.arange(half_dims, dtype=jnp.float32) * 2.0 / ROT)
    angles = positions.astype(jnp.float32)[:, None] * frequency[None, :]
    cosine_term = jnp.cos(angles)[:, None, :]
    sine_term = jnp.sin(angles)[:, None, :]
    first_half = values[..., :half_dims]
    second_half = values[..., half_dims:ROT]
    return jnp.concatenate(
        [
            first_half * cosine_term - second_half * sine_term,
            second_half * cosine_term + first_half * sine_term,
            values[..., ROT:],
        ],
        axis=-1,
    )


def swish_product(gate_value, up_value):
    return gate_value / (1.0 + jnp.exp(-gate_value)) * up_value


def project_back(left, right):
    return lax.dot_general(
        left, right, (((1,), (1,)), ((), ())), preferred_element_type=jnp.float32
    )


def outer_rows(left, right):
    return lax.dot_general(
        left, right, (((0,), (0,)), ((), ())), preferred_element_type=jnp.float32
    )


def local(
    tokens,
    out_grad,
    ln1_gain,
    ln1_shift,
    qkv_weight,
    qkv_bias,
    out_weight,
    ln2_gain,
    ln2_shift,
    gate_weight,
    up_weight,
    down_weight,
):
    local_rows = tokens.shape[1]
    seq_length = local_rows * lax.axis_size("ctx")
    inputs = tokens.reshape(local_rows, D).astype(jnp.float32)
    cotangent = out_grad.reshape(local_rows, D).astype(jnp.float32)
    places = lax.axis_index("ctx") * local_rows + jnp.arange(local_rows, dtype=jnp.int32)
    attn_set = (
        lax.all_gather(qkv_weight, ("batch", "ctx"), axis=0, tiled=True),
        lax.all_gather(out_weight, ("batch", "ctx"), axis=0, tiled=True),
        lax.all_gather(qkv_bias, ("batch", "ctx"), axis=0, tiled=True),
        lax.all_gather(ln1_gain, ("batch", "ctx"), axis=0, tiled=True),
        lax.all_gather(ln1_shift, ("batch", "ctx"), axis=0, tiled=True),
    )
    gain_one = attn_set[3].astype(jnp.float32)
    shift_one = attn_set[4].astype(jnp.float32)
    normed = layer_norm(inputs, gain_one, shift_one)
    normed_low = normed.astype(jnp.bfloat16)
    projected = jnp.dot(normed_low, attn_set[0], preferred_element_type=jnp.float32) + attn_set[
        2
    ].astype(jnp.float32)
    pair_heads = projected[:, : 2 * D].reshape(local_rows, 2 * H, HD)
    turned = rotary(pair_heads, places)
    queries = turned[:, :H].astype(jnp.bfloat16)
    key_rows = turned[:, H:].reshape(local_rows, D).astype(jnp.bfloat16)
    value_rows = projected[:, 2 * D :].astype(jnp.bfloat16)
    start_state = (
        jnp.full((H, local_rows), -1e30, jnp.float32),
        jnp.zeros((H, local_rows), jnp.float32),
        jnp.zeros((H, local_rows, HD), jnp.float32),
    )
    carry = start_state
    key_piece = lax.all_gather(key_rows, "ctx", axis=0, tiled=True)
    value_piece = lax.all_gather(value_rows, "ctx", axis=0, tiled=True)
    piece_rows = key_piece.shape[0]
    block_rows = 512
    block_count = piece_rows // block_rows

    def inner(state, block):
        largest, totals, accum = state
        key_block, value_block, offset = block
        raw_scores = (
            jnp.einsum("qhd,khd->hqk", queries, key_block, preferred_element_type=jnp.float32)
            * 0.125
        )
        key_places = offset + jnp.arange(block_rows, dtype=jnp.int32)
        allowed = (key_places[None, :] <= places[:, None])[None]
        raw_scores = jnp.where(allowed, raw_scores, -1e30)
        new_largest = jnp.maximum(largest, jnp.max(raw_scores, axis=-1))
        weights = jnp.where(allowed, jnp.exp(raw_scores - new_largest[..., None]), 0.0)
        factor = jnp.exp(largest - new_largest)
        totals = totals * factor + jnp.sum(weights, axis=-1)
        accum = accum * factor[..., None] + jnp.einsum(
            "hqk,khd->hqd",
            weights.astype(jnp.bfloat16),
            value_block,
            preferred_element_type=jnp.float32,
        )
        return ((new_largest, totals, accum), None)

    offsets = jnp.arange(block_count, dtype=jnp.int32) * block_rows
    blocks = (
        key_piece.reshape(block_count, block_rows, H, HD),
        value_piece.reshape(block_count, block_rows, H, HD),
        offsets,
    )
    carry, unused = lax.scan(inner, carry, blocks)
    largest, totals, accum = carry
    attended = jnp.transpose(accum / totals[..., None], (1, 0, 2)).reshape(local_rows, D)
    log_total = largest + jnp.log(totals)
    attended_low = attended.astype(jnp.bfloat16)
    middle = inputs + jnp.dot(attended_low, attn_set[1], preferred_element_type=jnp.float32)
    mlp_set = (
        lax.all_gather(gate_weight, ("batch", "ctx"), axis=0, tiled=True),
        lax.all_gather(up_weight, ("batch", "ctx"), axis=0, tiled=True),
        lax.all_gather(down_weight, ("batch", "ctx"), axis=0, tiled=True),
        lax.all_gather(ln2_gain, ("batch", "ctx"), axis=0, tiled=True),
        lax.all_gather(ln2_shift, ("batch", "ctx"), axis=0, tiled=True),
    )
    gain_two = mlp_set[3].astype(jnp.float32)
    shift_two = mlp_set[4].astype(jnp.float32)
    normed_two_low = layer_norm(middle, gain_two, shift_two).astype(jnp.bfloat16)
    gate_value = jnp.dot(normed_two_low, mlp_set[0], preferred_element_type=jnp.float32)
    up_value = jnp.dot(normed_two_low, mlp_set[1], preferred_element_type=jnp.float32)
    hidden_low = swish_product(gate_value, up_value).astype(jnp.bfloat16)
    mixed = (middle + project_back(hidden_low, mlp_set[2])).astype(jnp.bfloat16)
    mlp_back = (
        lax.all_gather(gate_weight, ("batch", "ctx"), axis=0, tiled=True),
        lax.all_gather(up_weight, ("batch", "ctx"), axis=0, tiled=True),
        lax.all_gather(down_weight, ("batch", "ctx"), axis=0, tiled=True),
        lax.all_gather(ln2_gain, ("batch", "ctx"), axis=0, tiled=True),
        lax.all_gather(ln2_shift, ("batch", "ctx"), axis=0, tiled=True),
    )
    attn_back = (
        lax.all_gather(qkv_weight, ("batch", "ctx"), axis=0, tiled=True),
        lax.all_gather(out_weight, ("batch", "ctx"), axis=0, tiled=True),
        lax.all_gather(qkv_bias, ("batch", "ctx"), axis=0, tiled=True),
        lax.all_gather(ln1_gain, ("batch", "ctx"), axis=0, tiled=True),
        lax.all_gather(ln1_shift, ("batch", "ctx"), axis=0, tiled=True),
    )
    branch_two = cotangent.astype(jnp.bfloat16)
    hidden_grad = jnp.dot(branch_two, mlp_back[2], preferred_element_type=jnp.float32)
    unused_value, act_pull = jax.vjp(swish_product, gate_value, up_value)
    gate_grad, up_grad = act_pull(hidden_grad)
    gate_low = gate_grad.astype(jnp.bfloat16)
    up_low = up_grad.astype(jnp.bfloat16)
    normed_two_grad = project_back(gate_low, mlp_back[0]) + project_back(up_low, mlp_back[1])
    unused_two, norm_pull_two = jax.vjp(layer_norm, middle, gain_two, shift_two)
    middle_part, gain_two_grad, shift_two_grad = norm_pull_two(normed_two_grad)
    middle_grad = cotangent + middle_part
    gate_weight_grad, up_weight_grad, down_weight_grad = (
        lax.psum_scatter(
            outer_rows(left, right).astype(jnp.bfloat16), ("batch", "ctx"), scatter_dimension=0, tiled=True
        ).astype(jnp.float32)
        for left, right in ((normed_two_low, gate_low), (normed_two_low, up_low), (branch_two, hidden_low))
    )
    branch_one = middle_grad.astype(jnp.bfloat16)
    out_term = outer_rows(attended_low, branch_one)
    attended_grad = project_back(branch_one, attn_back[1]).astype(jnp.bfloat16)
    grad_heads = attended_grad.reshape(local_rows, H, HD)
    delta = jnp.transpose(
        jnp.sum((attended_grad.astype(jnp.float32) * attended).reshape(local_rows, H, HD), axis=-1)
    )
    key_all, value_all = (
        lax.all_gather(key_rows, "ctx", axis=0, tiled=True),
        lax.all_gather(value_rows, "ctx", axis=0, tiled=True),
    )
    back_rows = 512
    back_count = seq_length // back_rows

    def back_block(query_grad, block):
        key_block, value_block, offset = block
        raw_scores = (
            jnp.einsum("qhd,khd->hqk", queries, key_block, preferred_element_type=jnp.float32)
            * 0.125
        )
        key_places = offset + jnp.arange(back_rows, dtype=jnp.int32)
        allowed = (key_places[None, :] <= places[:, None])[None]
        probs = jnp.where(allowed, jnp.exp(raw_scores - log_total[..., None]), 0.0)
        prob_grad = jnp.einsum(
            "qhd,khd->hqk", grad_heads, value_block, preferred_element_type=jnp.float32
        )
        score_grad = (probs * (prob_grad - delta[..., None])).astype(jnp.bfloat16)
        query_grad = (
            query_grad
            + jnp.einsum("hqk,khd->qhd", score_grad, key_block, preferred_element_type=jnp.float32)
            * 0.125
        )
        key_grad = (
            jnp.einsum("hqk,qhd->khd", score_grad, queries, preferred_element_type=jnp.float32)
            * 0.125
        )
        value_grad = jnp.einsum(
            "hqk,qhd->khd",
            probs.astype(jnp.bfloat16),
            grad_heads,
            preferred_element_type=jnp.float32,
        )
        return (
            query_grad,
            jnp.concatenate(
                [key_grad.reshape(back_rows, D), value_grad.reshape(back_rows, D)], axis=1
            ),
        )

    back_offsets = jnp.arange(back_count, dtype=jnp.int32) * back_rows
    back_blocks = (
        key_all.reshape(back_count, back_rows, H, HD),
        value_all.reshape(back_count, back_rows, H, HD),
        back_offsets,
    )
    query_grad, kv_terms = lax.scan(
        back_block, jnp.zeros((local_rows, H, HD), jnp.float32), back_blocks
    )
    kv_local = lax.psum_scatter(
        kv_terms.reshape(seq_length, 2 * D).astype(jnp.bfloat16),
        "ctx",
        scatter_dimension=0,
        tiled=True,
    ).astype(jnp.float32)

    def turn_heads(heads_in):
        return rotary(heads_in, places)

    unused_three, turn_pull = jax.vjp(turn_heads, pair_heads)
    pair_grad = turn_pull(
        jnp.concatenate([query_grad, kv_local[:, :D].reshape(local_rows, H, HD)], axis=1)
    )[0]
    projected_grad = jnp.concatenate(
        [pair_grad.reshape(local_rows, 2 * D), kv_local[:, D:]], axis=1
    ).astype(jnp.bfloat16)
    qkv_term = outer_rows(normed_low, projected_grad)
    bias_term = jnp.sum(projected_grad.astype(jnp.float32), axis=0)
    normed_grad = project_back(projected_grad, attn_back[0])
    unused_four, norm_pull = jax.vjp(layer_norm, inputs, gain_one, shift_one)
    input_part, gain_one_grad, shift_one_grad = norm_pull(normed_grad)
    tokens_grad = (middle_grad + input_part).reshape(1, local_rows, D)
    summed = (
        lax.psum_scatter(qkv_term, ("batch", "ctx"), scatter_dimension=0, tiled=True),
        lax.psum_scatter(out_term, ("batch", "ctx"), scatter_dimension=0, tiled=True),
        lax.psum_scatter(bias_term, ("batch", "ctx"), scatter_dimension=0, tiled=True),
        lax.psum_scatter(gain_one_grad, ("batch", "ctx"), scatter_dimension=0, tiled=True),
        lax.psum_scatter(shift_one_grad, ("batch", "ctx"), scatter_dimension=0, tiled=True),
        lax.psum_scatter(gain_two_grad, ("batch", "ctx"), scatter_dimension=0, tiled=True),
        lax.psum_scatter(shift_two_grad, ("batch", "ctx"), scatter_dimension=0, tiled=True),
    )
    return (
        mixed.reshape(1, local_rows, D),
        tokens_grad,
        summed[3],
        summed[4],
        summed[0],
        summed[2],
        summed[1],
        summed[5],
        summed[6],
        gate_weight_grad,
        up_weight_grad,
        down_weight_grad,
    )


BF = jnp.bfloat16
F32 = jnp.float32
MESH = pl.DeviceIdType.MESH
ANY = pl.ANY
VM = pltpu.VMEM
REMOTE_SEMS = 200
LOCAL_SEMS = 64


def nt(left, right):
    return lax.dot_general(left, right, (((1,), (1,)), ((), ())), preferred_element_type=F32)


def tn(left, right):
    return lax.dot_general(left, right, (((0,), (0,)), ((), ())), preferred_element_type=F32)


def nn(left, right):
    return jnp.dot(left, right, preferred_element_type=F32)


def norm_stats(values):
    centre = jnp.mean(values, axis=-1, keepdims=True)
    centred = values - centre
    spread = jnp.mean(centred * centred, axis=-1, keepdims=True)
    scale = lax.rsqrt(spread + 1e-05)
    return centred * scale, scale


def norm_back(grad, unit, scale, gain):
    weighted = grad * gain
    lead = jnp.mean(weighted, axis=-1, keepdims=True)
    tilt = jnp.mean(weighted * unit, axis=-1, keepdims=True)
    return scale * (weighted - lead - unit * tilt)


def turn_tables(length):
    half = ROT // 2
    freq = (np.float32(10000.0) ** (-np.arange(half, dtype=np.float32) * np.float32(2.0) / np.float32(ROT))).astype(np.float32)
    angles = np.arange(length, dtype=np.float32)[:, None] * freq[None, :]
    cosine, sine = np.cos(angles), np.sin(angles)
    tables = np.zeros((3, length, 128), np.float32)
    tables[0] = 1.0
    for start in (0, HD):
        tables[0, :, start : start + half] = cosine
        tables[0, :, start + half : start + ROT] = cosine
        tables[1, :, start : start + half] = -sine
        tables[2, :, start + half : start + ROT] = sine
    return tables


class Names:
    pass


def layer_kernel(dims, names_in, names_out, names_scratch, *refs):
    R, C, PL, rows, S, shard, QW, FW = dims
    r = Names()
    for name, ref in zip(names_in + names_out + names_scratch, refs):
        setattr(r, name, ref)
    batch = lax.axis_index("batch")
    c = lax.axis_index("ctx")
    z = batch // 2
    core = lax.rem(batch, 2)
    q = core * C + c
    HS = PL // 2 * rows
    TOK = PL * rows
    KB = PL * shard
    GW = 2 * FW

    counter = [0]
    local_count = [0]

    def slots(count):
        first = counter[0]
        counter[0] += count
        return first

    def mate(i):
        other = lax.rem(q + i, PL)
        return (z * 2 + other // C, lax.rem(other, C))

    def row_mate(i):
        return (batch, lax.rem(c + i, C))

    sibling = (z * 2 + 1 - core, c)

    def plane_dev(t):
        return (t * 2 + core, c)

    def rcopy(src, dst, send, recv, dev):
        return pltpu.make_async_remote_copy(
            src_ref=src, dst_ref=dst, send_sem=r.ss.at[send], recv_sem=r.rs.at[recv], device_id=dev, device_id_type=MESH
        )

    drains = []

    def lcopy(src, dst):
        copy = pltpu.make_async_copy(src, dst, r.ls.at[local_count[0]])
        local_count[0] += 1
        copy.start()
        return copy

    barrier = pltpu.get_barrier_semaphore()
    for i in range(1, PL):
        pl.semaphore_signal(barrier, inc=1, device_id=mate(i), device_id_type=MESH)
    for i in range(1, R):
        pl.semaphore_signal(barrier, inc=1, device_id=plane_dev(lax.rem(z + i, R)), device_id_type=MESH)
    pl.semaphore_wait(barrier, PL - 1 + R - 1)

    OFFS = (2, -2, 1, -1)

    class ZGather:
        def __init__(self, whole, height):
            self.whole, self.height, self.base = whole, height, slots(5)

        def block(self, s):
            return self.whole.at[pl.ds(pl.multiple_of(s * self.height, 16), self.height)]

        def start(self, src):
            for k, off in enumerate(OFFS):
                t = z + off

                @pl.when((t >= 0) & (t < R))
                def _():
                    rcopy(src, self.block(z), self.base + k, self.base + z, plane_dev(t)).start()

                def drain(k=k, t=t):
                    @pl.when((t >= 0) & (t < R))
                    def _():
                        rcopy(src, self.block(z), self.base + k, self.base + z, plane_dev(t)).wait_send()

                drains.append(drain)

        def got(self, s):
            rcopy(self.block(s), self.block(s), self.base, self.base + s, sibling).wait_recv()

        def relay(self):
            for at, s, to in ((R - 2, 0, R - 1), (1, R - 1, 0)):

                @pl.when(z == at)
                def _():
                    self.got(s)
                    rcopy(self.block(s), self.block(s), self.base + 4, self.base + s, plane_dev(to)).start()

                def drain(at=at, s=s, to=to):
                    @pl.when(z == at)
                    def _():
                        rcopy(self.block(s), self.block(s), self.base + 4, self.base + s, plane_dev(to)).wait_send()

                drains.append(drain)

        def wait(self):
            for s in range(R):
                skip = z == s
                if s == 0:
                    skip = skip | (z == R - 2)
                if s == R - 1:
                    skip = skip | (z == 1)

                @pl.when(jnp.logical_not(skip))
                def _():
                    self.got(s)

    class Spread:
        def __init__(self, stage):
            self.stage, self.base = stage, slots(PL)

        def start(self, target):
            self.target = target
            for i in range(1, PL):
                other = lax.rem(q + i, PL)
                copy = rcopy(self.stage.at[other], target, self.base + i, self.base + i, mate(i))
                copy.start()

        def wait_send(self):
            for i in range(1, PL):
                other = lax.rem(q + i, PL)
                rcopy(self.stage.at[other], self.target, self.base + i, self.base + i, mate(i)).wait_send()

        def wait(self, block):
            for i in range(1, PL):
                rcopy(self.stage.at[0], block(lax.rem(q - i + PL, PL)), self.base + i, self.base + i, mate(i)).wait_recv()

    class Gather:
        def __init__(self, whole):
            self.whole, self.base = whole, slots(2 * C)

        def block(self, s):
            return self.whole.at[pl.ds(pl.multiple_of(s * rows, 16), rows)]

        def start(self, src):
            self.local = lcopy(src, self.block(q))
            sends = []
            for i in range(1, C):
                sends.append(rcopy(src, self.block(q), self.base + i, self.base + i, row_mate(i)))
            sends.append(rcopy(src, self.block(q), self.base, self.base, sibling))
            for copy in sends:
                copy.start()
                drains.append(copy.wait_send)

        def relay(self):
            for i in range(1, C):
                block = self.block(core * C + lax.rem(c - i + C, C))
                rcopy(block, block, self.base, self.base + i, sibling).wait_recv()
                copy = rcopy(block, block, self.base + C - 1 + i, self.base + C - 1 + i, sibling)
                copy.start()
                drains.append(copy.wait_send)

        def wait(self):
            for i in range(C):
                block = self.block((1 - core) * C + lax.rem(c - i + C, C))
                sem = self.base if i == 0 else self.base + C - 1 + i
                rcopy(block, block, self.base, sem, sibling).wait_recv()
            self.local.wait()

    class Reduce:
        def __init__(self, k):
            self.parts, self.from_sib = getattr(r, f"parts{k}"), getattr(r, f"fromsib{k}")
            self.out, self.got, self.own = getattr(r, f"redout{k}"), getattr(r, f"redin{k}"), getattr(r, f"redown{k}")
            self.base = slots(C)

        def send_sib(self):
            copy = rcopy(self.parts.at[0], self.from_sib, self.base, self.base, sibling)
            copy.start()
            drains.append(copy.wait_send)

        def middle(self):
            mine = lcopy(self.parts.at[1], r.mine)
            rcopy(self.parts.at[0], self.from_sib, self.base, self.base, sibling).wait_recv()
            theirs = lcopy(self.from_sib, r.theirs)
            mine.wait()
            theirs.wait()
            for i in (1, 2, 3, 0):
                span = pl.ds(pl.multiple_of(lax.rem(c + i, C) * rows, 16), rows)
                total = r.mine[span, :].astype(F32) + r.theirs[span, :].astype(F32)
                if i == 0:
                    self.own[...] = total
                else:
                    self.out[i - 1] = total.astype(BF)
                    copy = rcopy(self.out.at[i - 1], self.got.at[i - 1], self.base + i, self.base + i, row_mate(i))
                    copy.start()
                    drains.append(copy.wait_send)

        def finish(self):
            for i in range(1, C):
                rcopy(self.out.at[i - 1], self.got.at[i - 1], self.base + i, self.base + i, row_mate(i)).wait_recv()
            total = self.own[...]
            for i in range(1, C):
                total = total + self.got[i - 1].astype(F32)
            return total

    middle_plane = (z > 0) & (z < R - 1)

    class ZReduce:
        def __init__(self, grads, got, extra, relayed, height):
            self.grads, self.got, self.extra, self.relayed, self.height = grads, got, extra, relayed, height
            self.base = slots(6)

        def block(self, t):
            return self.grads.at[pl.ds(pl.multiple_of(t * self.height, 16), self.height)]

        def start(self):
            for k, off in enumerate(OFFS):
                t = z + off
                slot = 2 if abs(off) == 2 else (0 if off == 1 else 1)
                ok = (t >= 0) & (t < R)
                if off == 2:
                    ok = ok & (z != 1)
                if off == -2:
                    ok = ok & (z != R - 2)

                def copy(k=k, t=t, slot=slot):
                    return rcopy(self.block(t), self.got.at[slot], self.base + k, self.base + slot, plane_dev(t))

                @pl.when(ok)
                def _():
                    copy().start()

                def drain(ok=ok, copy=copy):
                    @pl.when(ok)
                    def _():
                        copy().wait_send()

                drains.append(drain)
            for at, owner, via in ((0, R - 1, 1), (R - 1, 0, R - 2)):

                def copy(owner=owner, via=via):
                    return rcopy(self.block(owner), self.extra, self.base + 4, self.base + 4, plane_dev(via))

                @pl.when(z == at)
                def _():
                    copy().start()

                def drain(at=at, copy=copy):
                    @pl.when(z == at)
                    def _():
                        copy().wait_send()

                drains.append(drain)

        def relay(self):
            @pl.when(middle_plane)
            def _():
                owner = jnp.where(z == 1, R - 1, 0)
                rcopy(self.extra, self.extra, self.base + 4, self.base + 4, sibling).wait_recv()

                def body(a, b, o):
                    o[...] = (a[...].astype(F32) + b[...].astype(F32)).astype(BF)

                width = self.grads.shape[1]
                spec = pl.BlockSpec((64, width), lambda i: (i, 0))
                pltpu.emit_pipeline(body, grid=(self.height // 64,), in_specs=[spec, spec], out_specs=[spec])(
                    self.block(owner), self.extra, self.relayed
                )
                rcopy(self.relayed, self.got.at[2], self.base + 5, self.base + 2, plane_dev(owner)).start()

            def drain():
                @pl.when(middle_plane)
                def _():
                    owner = jnp.where(z == 1, R - 1, 0)
                    rcopy(self.relayed, self.got.at[2], self.base + 5, self.base + 2, plane_dev(owner)).wait_send()

            drains.append(drain)

        def finish(self, put):
            @pl.when(z > 0)
            def _():
                rcopy(self.got.at[0], self.got.at[0], self.base, self.base, sibling).wait_recv()

            @pl.when(z < R - 1)
            def _():
                rcopy(self.got.at[1], self.got.at[1], self.base, self.base + 1, sibling).wait_recv()

            rcopy(self.got.at[2], self.got.at[2], self.base, self.base + 2, sibling).wait_recv()
            first = jnp.where(z == 0, 1, 0)
            second = jnp.where(middle_plane, 1, 2)

            def body(own, a, b, d, o):
                total = own[...].astype(F32) + a[...].astype(F32) + b[...].astype(F32)
                put(o, total + jnp.where(middle_plane, d[...].astype(F32), 0.0))

            return body, (self.block(z), self.got.at[first], self.got.at[2], self.got.at[second])

    zg_o, zg_qkv = ZGather(r.w_o, shard), ZGather(r.w_qkv, KB)
    zg_gu, zg_d = ZGather(r.w_gu, KB), ZGather(r.w_d, KB)
    sp_qkv, sp_gu, sp_d = Spread(r.st_qkv), Spread(r.st_gu), Spread(r.st_d)
    ag_normed, ag_cot, ag_two, ag_one = Gather(r.a_normed), Gather(r.a_cot), Gather(r.a_two), Gather(r.a_one)

    def mine_rows(whole, height):
        return whole.at[pl.ds(pl.multiple_of((z * PL + q) * height, 16), height)]

    zg_o.start(r.in_o)
    local_o = lcopy(r.in_o, zg_o.block(z))
    base_small = slots(PL)
    for i in range(1, PL):
        copy = rcopy(r.in_small, r.small.at[z * PL + q], base_small + i, base_small + i, mate(i))
        copy.start()
        drains.append(copy.wait_send)
    local_small = lcopy(r.in_small, r.small.at[z * PL + q])
    for other in range(PL):
        for j in range(3):
            for zh in range(R):
                at = j * D + zh * PL * HD + other * HD
                r.st_qkv[other, :, j * QW + zh * HD : j * QW + (zh + 1) * HD] = r.in_qkv[:, at : at + HD]
    sp_qkv.start(mine_rows(r.w_qkv, shard))
    local_qkv = lcopy(r.st_qkv.at[q], mine_rows(r.w_qkv, shard))

    local_small.wait()
    for i in range(1, PL):
        rcopy(r.in_small, r.small.at[z * PL + lax.rem(q - i + PL, PL)], base_small, base_small + i, mate(i)).wait_recv()
    base_smallz = slots(R)
    plane_small = r.small.at[pl.ds(z * PL, PL)]
    for i in range(1, R):
        copy = rcopy(plane_small, plane_small, base_smallz + i, base_smallz + i, plane_dev(lax.rem(z + i, R)))
        copy.start()
        drains.append(copy.wait_send)
    tokens = r.in_tokens[...].astype(F32)
    unit, _ = norm_stats(tokens)
    for i in range(1, R):
        block = r.small.at[pl.ds(lax.rem(z - i + R, R) * PL, PL)]
        rcopy(block, block, base_smallz, base_smallz + i, sibling).wait_recv()
    for d in range(R * PL):
        for k in range(4):
            r.vec[k : k + 1, shard * d : shard * (d + 1)] = r.small[d, k : k + 1, 0:shard]
        for k in range(3):
            r.biases[3 * d + k : 3 * d + k + 1, 0:HD] = r.small[d, 4 + k : 5 + k, 0:HD]
    for j in range(3):
        for zh in range(R):
            row = r.biases[pl.ds(j * H + zh * PL + q, 1), 0:HD]
            r.bias[0:1, j * QW + zh * HD : j * QW + (zh + 1) * HD] = row
    r.x_normed[...] = (unit * r.vec[0:1, :] + r.vec[1:2, :]).astype(BF)
    ag_normed.start(r.x_normed)

    for other in range(PL):
        at = other * FW
        r.st_gu[other, :, 0:FW] = r.in_gate[:, at : at + FW]
        r.st_gu[other, :, FW:GW] = r.in_up[:, at : at + FW]
        r.st_d[other] = r.in_down[:, at : at + FW]

    local_qkv.wait()
    sp_qkv.wait(lambda s: r.w_qkv.at[pl.ds(pl.multiple_of((z * PL + s) * shard, 16), shard)])
    zg_qkv.start(zg_qkv.block(z))
    sp_gu.start(mine_rows(r.w_gu, shard))
    local_gu = lcopy(r.st_gu.at[q], mine_rows(r.w_gu, shard))
    ag_cot.start(r.in_cot)
    sp_d.start(mine_rows(r.w_d, shard))
    local_d = lcopy(r.st_d.at[q], mine_rows(r.w_d, shard))
    zg_o.relay()
    ag_normed.relay()
    local_gu.wait()
    sp_gu.wait(lambda s: r.w_gu.at[pl.ds(pl.multiple_of((z * PL + s) * shard, 16), shard)])
    zg_gu.start(zg_gu.block(z))
    zg_qkv.relay()
    ag_cot.relay()
    local_d.wait()
    sp_d.wait(lambda s: r.w_d.at[pl.ds(pl.multiple_of((z * PL + s) * shard, 16), shard)])
    zg_d.start(zg_d.block(z))
    ag_normed.wait()
    zg_qkv.wait()

    TM = HS // 2
    table_specs = [pl.BlockSpec((TM, 128), lambda i: (lax.rem(i, 2), 0))] * 3
    tables = [r.tables.at[k] for k in range(3)]

    def qkv_body(x, w, cos, s_one, s_two, o):
        projected = nn(x[...], w[...]) + r.bias[0:1, :]
        for piece in range(2 * QW // 128):
            part = projected[:, piece * 128 : (piece + 1) * 128]
            turned = part * cos[...] + pltpu.roll(part, 128 - ROT // 2, 1) * s_one[...] + pltpu.roll(part, ROT // 2, 1) * s_two[...]
            o[:, piece * 128 : (piece + 1) * 128] = turned.astype(BF)
        o[:, 2 * QW :] = projected[:, 2 * QW :].astype(BF)

    pltpu.emit_pipeline(
        qkv_body,
        grid=(TOK // TM,),
        in_specs=[pl.BlockSpec((TM, D), lambda i: (i, 0)), pl.BlockSpec((D, 3 * QW), lambda i: (0, 0))] + table_specs,
        out_specs=[pl.BlockSpec((TM, 3 * QW), lambda i: (i, 0))],
    )(r.a_normed, r.w_qkv, *tables, r.qkv)

    heads = QW // HD

    def softmax_block(queries, keys, first):
        scores = nt(queries, keys) * 0.125
        at_query = lax.broadcasted_iota(jnp.int32, scores.shape, 0) + first
        at_key = lax.broadcasted_iota(jnp.int32, scores.shape, 1)
        allowed = at_key <= at_query
        scores = jnp.where(allowed, scores, -1e30)
        largest = jnp.max(scores, axis=1, keepdims=True)
        weights = jnp.where(allowed, jnp.exp(scores - largest), 0.0)
        return weights / jnp.sum(weights, axis=1, keepdims=True)

    QB = HS // 2

    def attention_body(x, o):
        for h in range(heads):
            at = h * HD
            for blk in range(HS // QB):
                here, seen = blk * QB, (blk + 1) * QB
                probs = softmax_block(x[here : here + QB, at : at + HD], x[0:seen, QW + at : QW + at + HD], here)
                out = nn(probs.astype(BF), x[0:seen, 2 * QW + at : 2 * QW + at + HD])
                o[here : here + QB, at : at + HD] = out.astype(BF)

    pltpu.emit_pipeline(
        attention_body,
        grid=(TOK // HS,),
        in_specs=[pl.BlockSpec((HS, 3 * QW), lambda i: (i, 0))],
        out_specs=[pl.BlockSpec((HS, QW), lambda i: (i, 0))],
    )(r.qkv, r.att)

    local_o.wait()
    zg_o.wait()
    zg_gu.relay()

    def halves(reduce, source, weight, width, compute):
        for half in range(2):
            seq = 1 - core if half == 0 else core
            part = source.at[pl.ds(pl.multiple_of(seq * HS, 16), HS)]

            def body(x, w, o):
                o[...] = compute(x[...], w[...]).astype(BF)

            pltpu.emit_pipeline(
                body,
                grid=(HS // TM,),
                in_specs=[pl.BlockSpec((TM, width), lambda i: (i, 0)), pl.BlockSpec(weight.shape, lambda i: (0, 0))],
                out_specs=[pl.BlockSpec((TM, D), lambda i: (i, 0))],
            )(part, weight, reduce.parts.at[half])
            if half == 0:
                reduce.send_sib()

    red_att = Reduce(0)
    halves(red_att, r.att, r.w_o, QW, nn)
    red_att.middle()
    zg_d.relay()
    ag_cot.wait()
    middle = r.in_tokens[...].astype(F32) + red_att.finish()
    r.middle[...] = middle
    unit, _ = norm_stats(middle)
    r.x_two[...] = (unit * r.vec[2:3, :] + r.vec[3:4, :]).astype(BF)
    ag_two.start(r.x_two)
    ag_two.relay()
    ag_two.wait()
    zg_gu.wait()

    def gu_body(x, w, hid, coef):
        both = nn(x[...], w[...])
        gate = both[:, :FW]
        up = both[:, FW:]
        sig = 1.0 / (1.0 + jnp.exp(-gate))
        swish = gate * sig
        hid[...] = (swish * up).astype(BF)
        coef[:, :FW] = (up * sig * (1.0 + gate * (1.0 - sig))).astype(BF)
        coef[:, FW:] = swish.astype(BF)

    pltpu.emit_pipeline(
        gu_body,
        grid=(TOK // TM,),
        in_specs=[pl.BlockSpec((TM, D), lambda i: (i, 0)), pl.BlockSpec((D, GW), lambda i: (0, 0))],
        out_specs=[pl.BlockSpec((TM, FW), lambda i: (i, 0)), pl.BlockSpec((TM, GW), lambda i: (i, 0))],
    )(r.a_two, r.w_gu, r.hid, r.coef)

    def weight_grad(acts, grads, out, width, tile):
        def body(x, g, o):
            o[...] = tn(x[...], g[...]).astype(BF)

        pltpu.emit_pipeline(
            body,
            grid=(acts.shape[1] // tile,),
            in_specs=[pl.BlockSpec((TOK, tile), lambda i: (0, i)), pl.BlockSpec((TOK, width), lambda i: (0, 0))],
            out_specs=[pl.BlockSpec((tile, width), lambda i: (i, 0))],
        )(acts, grads, out)

    zr_d = ZReduce(r.g_d, r.zin_d, r.zx_d, r.zs_d, KB)
    zr_gu = ZReduce(r.g_gu, r.zin_gu, r.zx_gu, r.zs_gu, KB)
    zr_o = ZReduce(r.g_o, r.zin_o, r.zx_o, r.zs_o, shard)
    zr_qkv = ZReduce(r.g_qkv, r.zin_qkv, r.zx_qkv, r.zs_qkv, KB)

    weight_grad(r.a_cot, r.hid, r.g_d, FW, 256)
    zr_d.start()
    zg_d.wait()

    def act_back_body(x, w, coef, o):
        hidden_grad = nn(x[...], w[...])
        o[:, :FW] = (hidden_grad * coef[:, :FW].astype(F32)).astype(BF)
        o[:, FW:] = (hidden_grad * coef[:, FW:].astype(F32)).astype(BF)

    pltpu.emit_pipeline(
        act_back_body,
        grid=(TOK // TM,),
        in_specs=[
            pl.BlockSpec((TM, D), lambda i: (i, 0)),
            pl.BlockSpec((D, FW), lambda i: (0, 0)),
            pl.BlockSpec((TM, GW), lambda i: (i, 0)),
        ],
        out_specs=[pl.BlockSpec((TM, GW), lambda i: (i, 0))],
    )(r.a_cot, r.w_d, r.coef, r.gug)

    red_two = Reduce(1)
    halves(red_two, r.gug, r.w_gu, GW, nt)
    red_two.middle()
    weight_grad(r.a_two, r.gug, r.g_gu, GW, 256)
    zr_gu.start()
    two_grad = red_two.finish()
    unit, scale = norm_stats(r.middle[...])
    middle_grad = r.in_cot[...].astype(F32) + norm_back(two_grad, unit, scale, r.vec[2:3, :])
    r.middle_grad[...] = middle_grad
    r.x_one[...] = middle_grad.astype(BF)
    ag_one.start(r.x_one)
    r.vec[6:7, :] = jnp.sum(two_grad * unit, axis=0, keepdims=True)
    r.vec[7:8, :] = jnp.sum(two_grad, axis=0, keepdims=True)
    red_mixed = Reduce(2)
    halves(red_mixed, r.hid, r.w_d, FW, nt)
    ag_one.relay()
    ag_one.wait()

    def att_grad_body(x, w, o):
        o[...] = nt(x[...], w[...]).astype(BF)

    pltpu.emit_pipeline(
        att_grad_body,
        grid=(TOK // TM,),
        in_specs=[pl.BlockSpec((TM, D), lambda i: (i, 0)), pl.BlockSpec((QW, D), lambda i: (0, 0))],
        out_specs=[pl.BlockSpec((TM, QW), lambda i: (i, 0))],
    )(r.a_one, r.w_o, r.attg)

    def o_grad_body(x, g, o):
        o[...] = tn(x[...], g[...]).astype(BF)

    pltpu.emit_pipeline(
        o_grad_body,
        grid=(D // 512,),
        in_specs=[pl.BlockSpec((TOK, QW), lambda i: (0, 0)), pl.BlockSpec((TOK, 512), lambda i: (0, i))],
        out_specs=[pl.BlockSpec((QW, 512), lambda i: (0, i))],
    )(r.att, r.a_one, r.g_o)
    zr_o.start()
    red_mixed.middle()
    zr_d.relay()

    def attention_back_body(x, g, cos, s_one, s_two, o):
        for h in range(heads):
            at = h * HD
            key_grad = [jnp.zeros((QB, HD), F32) for _ in range(HS // QB)]
            value_grad = [jnp.zeros((QB, HD), F32) for _ in range(HS // QB)]
            for blk in range(HS // QB):
                here, seen = blk * QB, (blk + 1) * QB
                queries = x[here : here + QB, at : at + HD]
                keys = x[0:seen, QW + at : QW + at + HD]
                values = x[0:seen, 2 * QW + at : 2 * QW + at + HD]
                grads = g[here : here + QB, at : at + HD]
                probs = softmax_block(queries, keys, here)
                prob_grad = nt(grads, values)
                delta = jnp.sum(probs * prob_grad, axis=1, keepdims=True)
                score_grad = (probs * (prob_grad - delta)).astype(BF)
                low_probs = probs.astype(BF)
                r.turn[here : here + QB, at : at + HD] = nn(score_grad, keys) * 0.125
                key_part = tn(score_grad, queries) * 0.125
                value_part = tn(low_probs, grads)
                for k in range(blk + 1):
                    key_grad[k] = key_grad[k] + key_part[k * QB : (k + 1) * QB]
                    value_grad[k] = value_grad[k] + value_part[k * QB : (k + 1) * QB]
            for k in range(HS // QB):
                r.turn[k * QB : (k + 1) * QB, QW + at : QW + at + HD] = key_grad[k]
                o[k * QB : (k + 1) * QB, 2 * QW + at : 2 * QW + at + HD] = value_grad[k].astype(BF)
        for piece in range(2 * QW // 128):
            part = r.turn[:, piece * 128 : (piece + 1) * 128]
            back = part * cos[...] + pltpu.roll(part * s_one[...], ROT // 2, 1) + pltpu.roll(part * s_two[...], 128 - ROT // 2, 1)
            o[:, piece * 128 : (piece + 1) * 128] = back.astype(BF)

    pltpu.emit_pipeline(
        attention_back_body,
        grid=(TOK // HS,),
        in_specs=[pl.BlockSpec((HS, 3 * QW), lambda i: (i, 0)), pl.BlockSpec((HS, QW), lambda i: (i, 0))]
        + [pl.BlockSpec((HS, 128), lambda i: (0, 0))] * 3,
        out_specs=[pl.BlockSpec((HS, 3 * QW), lambda i: (i, 0))],
    )(r.qkv, r.attg, *tables, r.pg)

    weight_grad(r.a_normed, r.pg, r.g_qkv, 3 * QW, 256)
    zr_qkv.start()
    red_one = Reduce(3)
    halves(red_one, r.pg, r.w_qkv, 3 * QW, nt)
    red_one.middle()
    zr_gu.relay()

    r.bias[0:1, :] = jnp.zeros((1, 3 * QW), F32)

    def bias_body(x):
        r.bias[0:1, :] += jnp.sum(x[...].astype(F32), axis=0, keepdims=True)

    pltpu.emit_pipeline(bias_body, grid=(TOK // TM,), in_specs=[pl.BlockSpec((TM, 3 * QW), lambda i: (i, 0))])(r.pg)

    back_d, back_gu, back_qkv = Spread(r.st_d), Spread(r.st_gu), Spread(r.st_qkv)

    def z_sum(reduce, sent, stage, spread, got, width, hbm):
        sent.wait_send()

        def put(o, total):
            o[...] = total.astype(BF)

        body, sources = reduce.finish(put)
        spec = pl.BlockSpec((shard, width), lambda i: (i, 0))
        pltpu.emit_pipeline(body, grid=(PL,), in_specs=[spec] * 4, out_specs=[spec])(*sources, hbm)
        load = [lcopy(hbm.at[pl.ds(k * shard, shard)], stage.at[k]) for k in range(PL)]
        for copy in load:
            copy.wait()
        spread.start(got.at[q])
        return lcopy(stage.at[q], got.at[q])

    local_d = z_sum(zr_d, sp_d, r.st_d, back_d, r.pin_d, FW, r.gp_d)
    zr_o.relay()

    mixed = r.middle[...] + red_mixed.finish()
    r.out_mixed[...] = mixed.astype(BF)

    one_grad = red_one.finish()
    unit, scale = norm_stats(r.in_tokens[...].astype(F32))
    r.out_tokens[...] = r.middle_grad[...] + norm_back(one_grad, unit, scale, r.vec[0:1, :])
    r.vec[4:5, :] = jnp.sum(one_grad * unit, axis=0, keepdims=True)
    r.vec[5:6, :] = jnp.sum(one_grad, axis=0, keepdims=True)
    r.sg[...] = jnp.zeros_like(r.sg)
    for d in range(R * PL):
        for k in range(4):
            r.sg[d, k : k + 1, 0:shard] = r.vec[4 + k : 5 + k, shard * d : shard * (d + 1)]
    for j in range(3):
        for zh in range(R):
            g = j * H + zh * PL + q
            r.sg[g // 3, pl.ds(4 + lax.rem(g, 3), 1), 0:HD] = r.bias[0:1, j * QW + zh * HD : j * QW + (zh + 1) * HD]
    base_sgz = slots(R)
    for i in range(1, R):
        t = lax.rem(z + i, R)
        copy = rcopy(r.sg.at[pl.ds(t * PL, PL)], r.sgz.at[i - 1], base_sgz + i, base_sgz + i, plane_dev(t))
        copy.start()
        drains.append(copy.wait_send)

    zr_qkv.relay()
    local_gu = z_sum(zr_gu, sp_gu, r.st_gu, back_gu, r.pin_gu, GW, r.gp_gu)

    def put_out(o, total):
        o[...] = total

    body, sources = zr_o.finish(put_out)
    spec = pl.BlockSpec((shard, 512), lambda i: (0, i))
    pltpu.emit_pipeline(body, grid=(D // 512,), in_specs=[spec] * 4, out_specs=[spec])(*sources, r.out_o)

    for i in range(1, R):
        rcopy(r.sgz.at[i - 1], r.sgz.at[i - 1], base_sgz, base_sgz + i, sibling).wait_recv()
    r.sgs[...] = r.sg[pl.ds(z * PL, PL)] + r.sgz[0] + r.sgz[1] + r.sgz[2]
    base_sgp = slots(PL)
    for i in range(1, PL):
        other = lax.rem(q + i, PL)
        copy = rcopy(r.sgs.at[other], r.sgp.at[i - 1], base_sgp + i, base_sgp + i, mate(i))
        copy.start()
        drains.append(copy.wait_send)

    def pin_block(got):
        return lambda s: got.at[s]

    local_d.wait()
    back_d.wait(pin_block(r.pin_d))
    for other in range(PL):
        r.out_down[:, other * FW : (other + 1) * FW] = r.pin_d[other].astype(F32)

    local_qkv = z_sum(zr_qkv, sp_qkv, r.st_qkv, back_qkv, r.pin_qkv, 3 * QW, r.gp_qkv)
    local_gu.wait()
    back_gu.wait(pin_block(r.pin_gu))
    for other in range(PL):
        r.out_gate[:, other * FW : (other + 1) * FW] = r.pin_gu[other, :, 0:FW].astype(F32)
        r.out_up[:, other * FW : (other + 1) * FW] = r.pin_gu[other, :, FW:GW].astype(F32)
    total = r.sgs[q]
    for i in range(1, PL):
        rcopy(r.sgp.at[i - 1], r.sgp.at[i - 1], base_sgp, base_sgp + i, sibling).wait_recv()
        total = total + r.sgp[i - 1]
    r.out_small[...] = total
    local_qkv.wait()
    back_qkv.wait(pin_block(r.pin_qkv))
    for other in range(PL):
        for j in range(3):
            for zh in range(R):
                at = j * D + zh * PL * HD + other * HD
                r.out_qkv[:, at : at + HD] = r.pin_qkv[other, :, j * QW + zh * HD : j * QW + (zh + 1) * HD].astype(F32)
    back_d.wait_send()
    back_gu.wait_send()
    back_qkv.wait_send()
    for drain in drains:
        drain()
    assert counter[0] <= REMOTE_SEMS and local_count[0] <= LOCAL_SEMS, (counter, local_count)


def fast_local(tokens, out_grad, ln1_gain, ln1_shift, qkv_weight, qkv_bias, out_weight, ln2_gain, ln2_shift, gate_weight, up_weight, down_weight):
    planes, columns = lax.axis_size("batch") // 2, lax.axis_size("ctx")
    members = 2 * columns
    rows = tokens.shape[1]
    seq = rows * columns
    total = members * rows
    shard = qkv_weight.shape[0]
    q_width = D // members
    f_width = FF // members
    plane_rows = members * shard
    dims = (planes, columns, members, rows, seq, shard, q_width, f_width)
    pieces = jnp.concatenate(
        [jnp.stack([ln1_gain, ln1_shift, ln2_gain, ln2_shift]), qkv_bias.reshape(3, HD)], axis=0
    ).astype(F32)
    small = jnp.pad(pieces, ((0, 1), (0, 128 - HD)))
    inputs = dict(
        in_tokens=(tokens.reshape(rows, D), VM),
        in_cot=(out_grad.reshape(rows, D), VM),
        in_small=(small, VM),
        in_qkv=(qkv_weight, VM),
        in_o=(out_weight, VM),
        in_gate=(gate_weight, VM),
        in_up=(up_weight, VM),
        in_down=(down_weight, VM),
        tables=(jnp.asarray(turn_tables(seq)), ANY),
    )
    outs = dict(
        out_mixed=((rows, D), BF, VM),
        out_tokens=((rows, D), F32, VM),
        out_small=((8, 128), F32, VM),
        out_qkv=((shard, 3 * D), F32, VM),
        out_o=((shard, D), F32, ANY),
        out_gate=((shard, FF), F32, VM),
        out_up=((shard, FF), F32, VM),
        out_down=((shard, FF), F32, VM),
    )
    final = list(outs)
    spaces = dict(
        w_qkv=(D, 3 * q_width), w_o=(q_width, D), w_gu=(D, 2 * f_width), w_d=(D, f_width),
        a_normed=(total, D), a_cot=(total, D), a_two=(total, D), a_one=(total, D),
        qkv=(total, 3 * q_width), att=(total, q_width), attg=(total, q_width), pg=(total, 3 * q_width),
        hid=(total, f_width), coef=(total, 2 * f_width), gug=(total, 2 * f_width),
        g_qkv=(D, 3 * q_width), g_o=(q_width, D), g_gu=(D, 2 * f_width), g_d=(D, f_width),
        zin_qkv=(3, plane_rows, 3 * q_width), zin_o=(3, shard, D), zin_gu=(3, plane_rows, 2 * f_width), zin_d=(3, plane_rows, f_width),
        zx_qkv=(plane_rows, 3 * q_width), zx_o=(shard, D), zx_gu=(plane_rows, 2 * f_width), zx_d=(plane_rows, f_width),
        zs_qkv=(plane_rows, 3 * q_width), zs_o=(shard, D), zs_gu=(plane_rows, 2 * f_width), zs_d=(plane_rows, f_width),
        gp_qkv=(plane_rows, 3 * q_width), gp_gu=(plane_rows, 2 * f_width), gp_d=(plane_rows, f_width),
    )
    for k in range(4):
        spaces[f"parts{k}"] = (2, seq, D)
        spaces[f"fromsib{k}"] = (seq, D)
    for name, shape in spaces.items():
        outs[name] = (shape, BF, ANY)
    scratch = dict(
        st_qkv=VM((members, shard, 3 * q_width), BF), st_gu=VM((members, shard, 2 * f_width), BF), st_d=VM((members, shard, f_width), BF),
        pin_qkv=VM((members, shard, 3 * q_width), BF), pin_gu=VM((members, shard, 2 * f_width), BF), pin_d=VM((members, shard, f_width), BF),
        small=VM((planes * members, 8, 128), F32), sg=VM((planes * members, 8, 128), F32),
        sgz=VM((3, members, 8, 128), F32), sgs=VM((members, 8, 128), F32), sgp=VM((members - 1, 8, 128), F32),
        vec=VM((8, D), F32), biases=VM((3 * H, 128), F32), bias=VM((8, 3 * q_width), F32),
        x_normed=VM((rows, D), BF), x_two=VM((rows, D), BF), x_one=VM((rows, D), BF),
        middle=VM((rows, D), F32), middle_grad=VM((rows, D), F32),
        mine=VM((seq, D), BF), theirs=VM((seq, D), BF),
        turn=VM((seq, 2 * q_width), F32),
    )
    for k in range(4):
        scratch[f"redout{k}"] = VM((columns - 1, rows, D), BF)
        scratch[f"redin{k}"] = VM((columns - 1, rows, D), BF)
        scratch[f"redown{k}"] = VM((rows, D), F32)
    scratch["ss"] = pltpu.SemaphoreType.DMA((REMOTE_SEMS,))
    scratch["rs"] = pltpu.SemaphoreType.DMA((REMOTE_SEMS,))
    scratch["ls"] = pltpu.SemaphoreType.DMA((LOCAL_SEMS,))
    results = pl.pallas_call(
        functools.partial(layer_kernel, dims, list(inputs), list(outs), list(scratch)),
        out_shape=[jax.ShapeDtypeStruct(shape, kind) for shape, kind, _ in outs.values()],
        in_specs=[pl.BlockSpec(memory_space=place) for _, place in inputs.values()],
        out_specs=[pl.BlockSpec(memory_space=place) for _, _, place in outs.values()],
        scratch_shapes=list(scratch.values()),
        compiler_params=pltpu.CompilerParams(collective_id=0, has_side_effects=True, vmem_limit_bytes=62 * 2**20),
        cost_estimate=pl.CostEstimate(flops=42 * 10**9, bytes_accessed=300 * 10**6, transcendentals=0),
        name="layer",
    )(*[array for array, _ in inputs.values()])
    got = dict(zip(final, results))
    vectors = got["out_small"][:, :HD]
    return (
        got["out_mixed"].reshape(1, rows, D),
        got["out_tokens"].reshape(1, rows, D),
        vectors[0],
        vectors[1],
        got["out_qkv"],
        vectors[4:7].reshape(3 * HD),
        got["out_o"],
        vectors[2],
        vectors[3],
        got["out_gate"],
        got["out_up"],
        got["out_down"],
    )


def fits(mesh):
    return mesh.shape["batch"] == 8 and mesh.shape["ctx"] == 4


def solution(mesh):
    in_specs = (
        P("batch", "ctx", None),
        P("batch", "ctx", None),
        P(("batch", "ctx")),
        P(("batch", "ctx")),
        P(("batch", "ctx"), None),
        P(("batch", "ctx")),
        P(("batch", "ctx"), None),
        P(("batch", "ctx")),
        P(("batch", "ctx")),
        P(("batch", "ctx"), None),
        P(("batch", "ctx"), None),
        P(("batch", "ctx"), None),
    )
    out_specs = (
        P("batch", "ctx", None),
        P("batch", "ctx", None),
        P(("batch", "ctx")),
        P(("batch", "ctx")),
        P(("batch", "ctx"), None),
        P(("batch", "ctx")),
        P(("batch", "ctx"), None),
        P(("batch", "ctx")),
        P(("batch", "ctx")),
        P(("batch", "ctx"), None),
        P(("batch", "ctx"), None),
        P(("batch", "ctx"), None),
    )
    body = fast_local if fits(mesh) else local
    return jax.shard_map(body, mesh=mesh, in_specs=in_specs, out_specs=out_specs, check_vma=False)
```

```python
import functools

import jax
import jax.numpy as jnp
import numpy as np
from jax import lax
from jax.experimental import pallas as pl
from jax.experimental.pallas import tpu as pltpu
from jax.sharding import PartitionSpec as P

D = 2048
FF = 5632
H = 32
HD = 64
ROT = 16


def layer_norm(values, gain, shift):
    centre = jnp.mean(values, axis=-1, keepdims=True)
    centred = values - centre
    spread = jnp.mean(centred * centred, axis=-1, keepdims=True)
    return centred * lax.rsqrt(spread + 1e-05) * gain + shift


def rotary(values, positions):
    half_dims = ROT // 2
    frequency = 10000.0 ** (-jnp.arange(half_dims, dtype=jnp.float32) * 2.0 / ROT)
    angles = positions.astype(jnp.float32)[:, None] * frequency[None, :]
    cosine_term = jnp.cos(angles)[:, None, :]
    sine_term = jnp.sin(angles)[:, None, :]
    first_half = values[..., :half_dims]
    second_half = values[..., half_dims:ROT]
    return jnp.concatenate(
        [
            first_half * cosine_term - second_half * sine_term,
            second_half * cosine_term + first_half * sine_term,
            values[..., ROT:],
        ],
        axis=-1,
    )


def swish_product(gate_value, up_value):
    return gate_value / (1.0 + jnp.exp(-gate_value)) * up_value


def project_back(left, right):
    return lax.dot_general(
        left, right, (((1,), (1,)), ((), ())), preferred_element_type=jnp.float32
    )


def outer_rows(left, right):
    return lax.dot_general(
        left, right, (((0,), (0,)), ((), ())), preferred_element_type=jnp.float32
    )


def local(
    tokens,
    out_grad,
    ln1_gain,
    ln1_shift,
    qkv_weight,
    qkv_bias,
    out_weight,
    ln2_gain,
    ln2_shift,
    gate_weight,
    up_weight,
    down_weight,
):
    local_rows = tokens.shape[1]
    seq_length = local_rows * lax.axis_size("ctx")
    inputs = tokens.reshape(local_rows, D).astype(jnp.float32)
    cotangent = out_grad.reshape(local_rows, D).astype(jnp.float32)
    places = lax.axis_index("ctx") * local_rows + jnp.arange(local_rows, dtype=jnp.int32)
    attn_set = (
        lax.all_gather(qkv_weight, ("batch", "ctx"), axis=0, tiled=True),
        lax.all_gather(out_weight, ("batch", "ctx"), axis=0, tiled=True),
        lax.all_gather(qkv_bias, ("batch", "ctx"), axis=0, tiled=True),
        lax.all_gather(ln1_gain, ("batch", "ctx"), axis=0, tiled=True),
        lax.all_gather(ln1_shift, ("batch", "ctx"), axis=0, tiled=True),
    )
    gain_one = attn_set[3].astype(jnp.float32)
    shift_one = attn_set[4].astype(jnp.float32)
    normed = layer_norm(inputs, gain_one, shift_one)
    normed_low = normed.astype(jnp.bfloat16)
    projected = jnp.dot(normed_low, attn_set[0], preferred_element_type=jnp.float32) + attn_set[
        2
    ].astype(jnp.float32)
    pair_heads = projected[:, : 2 * D].reshape(local_rows, 2 * H, HD)
    turned = rotary(pair_heads, places)
    queries = turned[:, :H].astype(jnp.bfloat16)
    key_rows = turned[:, H:].reshape(local_rows, D).astype(jnp.bfloat16)
    value_rows = projected[:, 2 * D :].astype(jnp.bfloat16)
    start_state = (
        jnp.full((H, local_rows), -1e30, jnp.float32),
        jnp.zeros((H, local_rows), jnp.float32),
        jnp.zeros((H, local_rows, HD), jnp.float32),
    )
    carry = start_state
    key_piece = lax.all_gather(key_rows, "ctx", axis=0, tiled=True)
    value_piece = lax.all_gather(value_rows, "ctx", axis=0, tiled=True)
    piece_rows = key_piece.shape[0]
    block_rows = 512
    block_count = piece_rows // block_rows

    def inner(state, block):
        largest, totals, accum = state
        key_block, value_block, offset = block
        raw_scores = (
            jnp.einsum("qhd,khd->hqk", queries, key_block, preferred_element_type=jnp.float32)
            * 0.125
        )
        key_places = offset + jnp.arange(block_rows, dtype=jnp.int32)
        allowed = (key_places[None, :] <= places[:, None])[None]
        raw_scores = jnp.where(allowed, raw_scores, -1e30)
        new_largest = jnp.maximum(largest, jnp.max(raw_scores, axis=-1))
        weights = jnp.where(allowed, jnp.exp(raw_scores - new_largest[..., None]), 0.0)
        factor = jnp.exp(largest - new_largest)
        totals = totals * factor + jnp.sum(weights, axis=-1)
        accum = accum * factor[..., None] + jnp.einsum(
            "hqk,khd->hqd",
            weights.astype(jnp.bfloat16),
            value_block,
            preferred_element_type=jnp.float32,
        )
        return ((new_largest, totals, accum), None)

    offsets = jnp.arange(block_count, dtype=jnp.int32) * block_rows
    blocks = (
        key_piece.reshape(block_count, block_rows, H, HD),
        value_piece.reshape(block_count, block_rows, H, HD),
        offsets,
    )
    carry, unused = lax.scan(inner, carry, blocks)
    largest, totals, accum = carry
    attended = jnp.transpose(accum / totals[..., None], (1, 0, 2)).reshape(local_rows, D)
    log_total = largest + jnp.log(totals)
    attended_low = attended.astype(jnp.bfloat16)
    middle = inputs + jnp.dot(attended_low, attn_set[1], preferred_element_type=jnp.float32)
    mlp_set = (
        lax.all_gather(gate_weight, ("batch", "ctx"), axis=0, tiled=True),
        lax.all_gather(up_weight, ("batch", "ctx"), axis=0, tiled=True),
        lax.all_gather(down_weight, ("batch", "ctx"), axis=0, tiled=True),
        lax.all_gather(ln2_gain, ("batch", "ctx"), axis=0, tiled=True),
        lax.all_gather(ln2_shift, ("batch", "ctx"), axis=0, tiled=True),
    )
    gain_two = mlp_set[3].astype(jnp.float32)
    shift_two = mlp_set[4].astype(jnp.float32)
    normed_two_low = layer_norm(middle, gain_two, shift_two).astype(jnp.bfloat16)
    gate_value = jnp.dot(normed_two_low, mlp_set[0], preferred_element_type=jnp.float32)
    up_value = jnp.dot(normed_two_low, mlp_set[1], preferred_element_type=jnp.float32)
    hidden_low = swish_product(gate_value, up_value).astype(jnp.bfloat16)
    mixed = (middle + project_back(hidden_low, mlp_set[2])).astype(jnp.bfloat16)
    mlp_back = (
        lax.all_gather(gate_weight, ("batch", "ctx"), axis=0, tiled=True),
        lax.all_gather(up_weight, ("batch", "ctx"), axis=0, tiled=True),
        lax.all_gather(down_weight, ("batch", "ctx"), axis=0, tiled=True),
        lax.all_gather(ln2_gain, ("batch", "ctx"), axis=0, tiled=True),
        lax.all_gather(ln2_shift, ("batch", "ctx"), axis=0, tiled=True),
    )
    attn_back = (
        lax.all_gather(qkv_weight, ("batch", "ctx"), axis=0, tiled=True),
        lax.all_gather(out_weight, ("batch", "ctx"), axis=0, tiled=True),
        lax.all_gather(qkv_bias, ("batch", "ctx"), axis=0, tiled=True),
        lax.all_gather(ln1_gain, ("batch", "ctx"), axis=0, tiled=True),
        lax.all_gather(ln1_shift, ("batch", "ctx"), axis=0, tiled=True),
    )
    branch_two = cotangent.astype(jnp.bfloat16)
    hidden_grad = jnp.dot(branch_two, mlp_back[2], preferred_element_type=jnp.float32)
    unused_value, act_pull = jax.vjp(swish_product, gate_value, up_value)
    gate_grad, up_grad = act_pull(hidden_grad)
    gate_low = gate_grad.astype(jnp.bfloat16)
    up_low = up_grad.astype(jnp.bfloat16)
    normed_two_grad = project_back(gate_low, mlp_back[0]) + project_back(up_low, mlp_back[1])
    unused_two, norm_pull_two = jax.vjp(layer_norm, middle, gain_two, shift_two)
    middle_part, gain_two_grad, shift_two_grad = norm_pull_two(normed_two_grad)
    middle_grad = cotangent + middle_part
    gate_weight_grad, up_weight_grad, down_weight_grad = (
        lax.psum_scatter(
            outer_rows(left, right).astype(jnp.bfloat16), ("batch", "ctx"), scatter_dimension=0, tiled=True
        ).astype(jnp.float32)
        for left, right in ((normed_two_low, gate_low), (normed_two_low, up_low), (branch_two, hidden_low))
    )
    branch_one = middle_grad.astype(jnp.bfloat16)
    out_term = outer_rows(attended_low, branch_one)
    attended_grad = project_back(branch_one, attn_back[1]).astype(jnp.bfloat16)
    grad_heads = attended_grad.reshape(local_rows, H, HD)
    delta = jnp.transpose(
        jnp.sum((attended_grad.astype(jnp.float32) * attended).reshape(local_rows, H, HD), axis=-1)
    )
    key_all, value_all = (
        lax.all_gather(key_rows, "ctx", axis=0, tiled=True),
        lax.all_gather(value_rows, "ctx", axis=0, tiled=True),
    )
    back_rows = 512
    back_count = seq_length // back_rows

    def back_block(query_grad, block):
        key_block, value_block, offset = block
        raw_scores = (
            jnp.einsum("qhd,khd->hqk", queries, key_block, preferred_element_type=jnp.float32)
            * 0.125
        )
        key_places = offset + jnp.arange(back_rows, dtype=jnp.int32)
        allowed = (key_places[None, :] <= places[:, None])[None]
        probs = jnp.where(allowed, jnp.exp(raw_scores - log_total[..., None]), 0.0)
        prob_grad = jnp.einsum(
            "qhd,khd->hqk", grad_heads, value_block, preferred_element_type=jnp.float32
        )
        score_grad = (probs * (prob_grad - delta[..., None])).astype(jnp.bfloat16)
        query_grad = (
            query_grad
            + jnp.einsum("hqk,khd->qhd", score_grad, key_block, preferred_element_type=jnp.float32)
            * 0.125
        )
        key_grad = (
            jnp.einsum("hqk,qhd->khd", score_grad, queries, preferred_element_type=jnp.float32)
            * 0.125
        )
        value_grad = jnp.einsum(
            "hqk,qhd->khd",
            probs.astype(jnp.bfloat16),
            grad_heads,
            preferred_element_type=jnp.float32,
        )
        return (
            query_grad,
            jnp.concatenate(
                [key_grad.reshape(back_rows, D), value_grad.reshape(back_rows, D)], axis=1
            ),
        )

    back_offsets = jnp.arange(back_count, dtype=jnp.int32) * back_rows
    back_blocks = (
        key_all.reshape(back_count, back_rows, H, HD),
        value_all.reshape(back_count, back_rows, H, HD),
        back_offsets,
    )
    query_grad, kv_terms = lax.scan(
        back_block, jnp.zeros((local_rows, H, HD), jnp.float32), back_blocks
    )
    kv_local = lax.psum_scatter(
        kv_terms.reshape(seq_length, 2 * D).astype(jnp.bfloat16),
        "ctx",
        scatter_dimension=0,
        tiled=True,
    ).astype(jnp.float32)

    def turn_heads(heads_in):
        return rotary(heads_in, places)

    unused_three, turn_pull = jax.vjp(turn_heads, pair_heads)
    pair_grad = turn_pull(
        jnp.concatenate([query_grad, kv_local[:, :D].reshape(local_rows, H, HD)], axis=1)
    )[0]
    projected_grad = jnp.concatenate(
        [pair_grad.reshape(local_rows, 2 * D), kv_local[:, D:]], axis=1
    ).astype(jnp.bfloat16)
    qkv_term = outer_rows(normed_low, projected_grad)
    bias_term = jnp.sum(projected_grad.astype(jnp.float32), axis=0)
    normed_grad = project_back(projected_grad, attn_back[0])
    unused_four, norm_pull = jax.vjp(layer_norm, inputs, gain_one, shift_one)
    input_part, gain_one_grad, shift_one_grad = norm_pull(normed_grad)
    tokens_grad = (middle_grad + input_part).reshape(1, local_rows, D)
    summed = (
        lax.psum_scatter(qkv_term, ("batch", "ctx"), scatter_dimension=0, tiled=True),
        lax.psum_scatter(out_term, ("batch", "ctx"), scatter_dimension=0, tiled=True),
        lax.psum_scatter(bias_term, ("batch", "ctx"), scatter_dimension=0, tiled=True),
        lax.psum_scatter(gain_one_grad, ("batch", "ctx"), scatter_dimension=0, tiled=True),
        lax.psum_scatter(shift_one_grad, ("batch", "ctx"), scatter_dimension=0, tiled=True),
        lax.psum_scatter(gain_two_grad, ("batch", "ctx"), scatter_dimension=0, tiled=True),
        lax.psum_scatter(shift_two_grad, ("batch", "ctx"), scatter_dimension=0, tiled=True),
    )
    return (
        mixed.reshape(1, local_rows, D),
        tokens_grad,
        summed[3],
        summed[4],
        summed[0],
        summed[2],
        summed[1],
        summed[5],
        summed[6],
        gate_weight_grad,
        up_weight_grad,
        down_weight_grad,
    )


BF = jnp.bfloat16
F32 = jnp.float32
MESH = pl.DeviceIdType.MESH
ANY = pl.ANY
VM = pltpu.VMEM
REMOTE_SEMS = 200
LOCAL_SEMS = 64


def nt(left, right):
    return lax.dot_general(left, right, (((1,), (1,)), ((), ())), preferred_element_type=F32)


def tn(left, right):
    return lax.dot_general(left, right, (((0,), (0,)), ((), ())), preferred_element_type=F32)


def nn(left, right):
    return jnp.dot(left, right, preferred_element_type=F32)


def norm_stats(values):
    centre = jnp.mean(values, axis=-1, keepdims=True)
    centred = values - centre
    spread = jnp.mean(centred * centred, axis=-1, keepdims=True)
    scale = lax.rsqrt(spread + 1e-05)
    return centred * scale, scale


def norm_back(grad, unit, scale, gain):
    weighted = grad * gain
    lead = jnp.mean(weighted, axis=-1, keepdims=True)
    tilt = jnp.mean(weighted * unit, axis=-1, keepdims=True)
    return scale * (weighted - lead - unit * tilt)


def turn_tables(length):
    half = ROT // 2
    freq = (np.float32(10000.0) ** (-np.arange(half, dtype=np.float32) * np.float32(2.0) / np.float32(ROT))).astype(np.float32)
    angles = np.arange(length, dtype=np.float32)[:, None] * freq[None, :]
    cosine, sine = np.cos(angles), np.sin(angles)
    tables = np.zeros((3, length, 128), np.float32)
    tables[0] = 1.0
    for start in (0, HD):
        tables[0, :, start : start + half] = cosine
        tables[0, :, start + half : start + ROT] = cosine
        tables[1, :, start : start + half] = -sine
        tables[2, :, start + half : start + ROT] = sine
    return tables


def aligned(value, to):
    return value if isinstance(value, int) else pl.multiple_of(value, to)


class Names:
    pass


def layer_kernel(dims, names_in, names_out, names_scratch, *refs):
    R, C, PL, rows, shard, QW, FW, PARTS = dims
    r = Names()
    for name, ref in zip(names_in + names_out + names_scratch, refs):
        setattr(r, name, ref)
    batch = lax.axis_index("batch")
    c = lax.axis_index("ctx")
    z = batch // 2
    core = lax.rem(batch, 2)
    q = core * C + c
    HS = PL // 2 * rows
    TOK = PL * rows
    KB = PL * shard
    STARTS = [sum(PARTS[:p]) for p in range(len(PARTS))]

    counter = [0]
    local_count = [0]

    def slots(count):
        first = counter[0]
        counter[0] += count
        return first

    def mate(i):
        other = lax.rem(q + i, PL)
        return (z * 2 + other // C, lax.rem(other, C))

    def row_mate(i):
        return (batch, lax.rem(c + i, C))

    sibling = (z * 2 + 1 - core, c)

    def plane_dev(t):
        return (t * 2 + core, c)

    def rcopy(src, dst, send, recv, dev):
        return pltpu.make_async_remote_copy(
            src_ref=src, dst_ref=dst, send_sem=r.ss.at[send], recv_sem=r.rs.at[recv], device_id=dev, device_id_type=MESH
        )

    drains = []

    def lcopy(src, dst):
        copy = pltpu.make_async_copy(src, dst, r.ls.at[local_count[0]])
        local_count[0] += 1
        copy.start()
        return copy

    barrier = pltpu.get_barrier_semaphore()
    for i in range(1, PL):
        pl.semaphore_signal(barrier, inc=1, device_id=mate(i), device_id_type=MESH)
    for i in range(1, R):
        pl.semaphore_signal(barrier, inc=1, device_id=plane_dev(lax.rem(z + i, R)), device_id_type=MESH)
    pl.semaphore_wait(barrier, PL - 1 + R - 1)

    OFFS = (2, -2, 1, -1)

    class ZGather:
        def __init__(self, whole, height, chunks=1):
            self.whole, self.height, self.chunks = whole, height, chunks
            self.base = [slots(6) for _ in range(chunks)]

        def block(self, s, chunk=None):
            if chunk is None:
                return self.whole.at[pl.ds(aligned(s * self.height, 16), self.height)]
            part = self.height // self.chunks
            return self.whole.at[pl.ds(aligned(s * self.height + chunk * part, 16), part)]

        def guarded(self, ok, make):
            @pl.when(ok)
            def _():
                make().start()

            def drain():
                @pl.when(ok)
                def _():
                    make().wait_send()

            drains.append(drain)

        def start(self, src=None):
            for chunk in range(self.chunks):
                for k, off in enumerate(OFFS):
                    t = z + off
                    ok = (t >= 0) & (t < R)
                    if off == 2:
                        ok = ok & (z == 0)
                    if off == -2:
                        ok = ok & (z == R - 1)

                    def make(chunk=chunk, k=k, t=t):
                        mine = self.block(z, chunk)
                        return rcopy(mine if src is None else src, mine, self.base[chunk] + k, self.base[chunk] + z, plane_dev(t))

                    self.guarded(ok, make)

        def got(self, s, chunk):
            block = self.block(s, chunk)
            rcopy(block, block, self.base[chunk], self.base[chunk] + s, sibling).wait_recv()

        def relay(self, chunk=0):
            for at, blocks, to in ((R - 2, (1, 0), R - 1), (1, (2, 3), 0)):
                for k, s in enumerate(blocks):

                    @pl.when(z == at)
                    def _():
                        self.got(s, chunk)

                    def make(s=s, to=to, k=k):
                        block = self.block(s, chunk)
                        return rcopy(block, block, self.base[chunk] + 4 + k, self.base[chunk] + s, plane_dev(to))

                    self.guarded(z == at, make)

        def wait(self):
            for chunk in range(self.chunks):
                for s in range(R):
                    skip = z == s
                    skip = skip | (z == (R - 2 if s < 2 else 1))

                    @pl.when(jnp.logical_not(skip))
                    def _():
                        self.got(s, chunk)

    class Spread:
        def __init__(self, stage):
            self.stage, self.base = stage, slots(PL)

        def start(self, target):
            self.target = target
            for i in range(1, PL):
                other = lax.rem(q + i, PL)
                copy = rcopy(self.stage.at[other], target, self.base + i, self.base + i, mate(i))
                copy.start()

        def wait_send(self):
            for i in range(1, PL):
                other = lax.rem(q + i, PL)
                rcopy(self.stage.at[other], self.target, self.base + i, self.base + i, mate(i)).wait_send()

        def wait(self, block):
            for i in range(1, PL):
                rcopy(self.stage.at[0], block(lax.rem(q - i + PL, PL)), self.base + i, self.base + i, mate(i)).wait_recv()

    class Gather:
        def __init__(self, whole):
            self.whole, self.base = whole, slots(2 * C)

        def block(self, s):
            return self.whole.at[pl.ds(aligned(s * rows, 16), rows)]

        def start(self, src):
            self.local = lcopy(src, self.block(q))
            sends = []
            for i in range(1, C):
                sends.append(rcopy(src, self.block(q), self.base + i, self.base + i, row_mate(i)))
            sends.append(rcopy(src, self.block(q), self.base, self.base, sibling))
            for copy in sends:
                copy.start()
                drains.append(copy.wait_send)

        def relay(self):
            for i in range(1, C):
                block = self.block(core * C + lax.rem(c - i + C, C))
                rcopy(block, block, self.base, self.base + i, sibling).wait_recv()
                copy = rcopy(block, block, self.base + C - 1 + i, self.base + C - 1 + i, sibling)
                copy.start()
                drains.append(copy.wait_send)

        def wait(self):
            for i in range(C):
                block = self.block((1 - core) * C + lax.rem(c - i + C, C))
                sem = self.base if i == 0 else self.base + C - 1 + i
                rcopy(block, block, self.base, sem, sibling).wait_recv()
            self.local.wait()

    class Reduce:
        def __init__(self, k, before=None):
            self.sibout, self.theirs = getattr(r, f"sibout{k}"), getattr(r, f"theirs{k}")
            self.out, self.got, self.own = getattr(r, f"redout{k}"), getattr(r, f"redin{k}"), getattr(r, f"redown{k}")
            self.base = slots(C)
            self.sent = []
            self.before = before

        def partial(self, pairs, compute):
            def to_sibling():
                return rcopy(self.sibout, self.theirs, self.base, self.base, sibling)

            def body(*bufs):
                loads = [lcopy(src, buf) for pair, two in zip(pairs, zip(bufs[::2], bufs[1::2])) for src, buf in zip(pair, two)]
                for load in loads:
                    load.wait()
                if self.before is not None:
                    self.before.drain()
                for half in range(2):
                    target = self.sibout if half == 0 else r.mine
                    first = (1 - core if half == 0 else core) * HS

                    @pl.loop(0, HS // TM)
                    def _(i):
                        total = None
                        for x, w in zip(bufs[::2], bufs[1::2]):
                            rows_in = x[pl.ds(aligned(first + i * TM, TM), TM), :]
                            term = compute(rows_in, w[...])
                            total = term if total is None else total + term
                        target[pl.ds(aligned(i * TM, TM), TM), :] = total.astype(BF)

                    if half == 0:
                        to_sibling().start()

            pl.run_scoped(body, *[VM(ref.shape, BF) for pair in pairs for ref in pair])
            self.sent.append(to_sibling())

        def middle(self):
            rcopy(self.sibout, self.theirs, self.base, self.base, sibling).wait_recv()
            for i in (1, 2, 3, 0):
                span = pl.ds(aligned(lax.rem(c + i, C) * rows, 16), rows)
                total = r.mine[span, :].astype(F32) + self.theirs[span, :].astype(F32)
                if i == 0:
                    self.own[...] = total
                else:
                    self.out[i - 1] = total.astype(BF)
                    copy = rcopy(self.out.at[i - 1], self.got.at[i - 1], self.base + i, self.base + i, row_mate(i))
                    copy.start()
                    self.sent.append(copy)

        def finish(self):
            for i in range(1, C):
                rcopy(self.out.at[i - 1], self.got.at[i - 1], self.base + i, self.base + i, row_mate(i)).wait_recv()
            total = self.own[...]
            for i in range(1, C):
                total = total + self.got[i - 1].astype(F32)
            return total

        def drain(self):
            for copy in self.sent:
                copy.wait_send()
            self.sent = []

    ORDER = ((3, 2, 1, 0), (0, 3, 2, 1), (3, 0, 1, 2), (0, 1, 2, 3))

    class ZReduce:
        def __init__(self, grads, got, extra, merged, height):
            self.grads, self.got, self.extra, self.merged, self.height = grads, got, extra, merged, height
            self.base = slots(12)

        def block(self, t):
            return self.grads.at[pl.ds(aligned(t * self.height, 16), self.height)]

        def guarded(self, ok, make):
            @pl.when(ok)
            def _():
                make().start()

            def drain():
                @pl.when(ok)
                def _():
                    make().wait_send()

            drains.append(drain)

        def send(self, at, owner):
            b = self.base
            via = {0: 1, R - 1: R - 2}.get(at)
            if owner == at or (via is None and abs(owner - at) == 2) or (via is None and owner == R - 1 - at):
                return
            if via is None:
                slot = 1 if owner < at else 0
                make = lambda: rcopy(self.block(owner), self.got.at[slot], b + 3, b + slot, plane_dev(owner))
            elif owner == via:
                slot = 0 if at == 0 else 1
                make = lambda: rcopy(self.block(owner), self.got.at[slot], b + 2, b + slot, plane_dev(via))
            else:
                k = 0 if owner == R - 1 - at else 1
                make = lambda: rcopy(self.block(owner), self.extra.at[k], b + k, b + 2 + k, plane_dev(via))
            self.guarded(z == at, make)

        def start(self):
            for step in range(R):
                self.start_step(step)

        def start_step(self, step):
            for at in range(R):
                self.send(at, ORDER[at][step])

        def merge(self, steps=(0, 1)):
            b = self.base
            for k in steps:
                for at, to, slots_at in ((1, (3, 2), (1, 0)), (2, (0, 1), (0, 1))):
                    owner = to[k]

                    @pl.when(z == at)
                    def _():
                        def body(own, other, sem):
                            first = pltpu.make_async_copy(self.block(owner), own, sem.at[0])
                            first.start()
                            rcopy(self.extra.at[k], self.extra.at[k], b, b + 2 + k, sibling).wait_recv()
                            second = pltpu.make_async_copy(self.extra.at[k], other, sem.at[1])
                            second.start()
                            first.wait()
                            second.wait()
                            own[...] = (own[...].astype(F32) + other[...].astype(F32)).astype(BF)
                            pltpu.sync_copy(own, self.merged.at[k])

                        shape = (self.height, self.grads.shape[1])
                        pl.run_scoped(body, VM(shape, BF), VM(shape, BF), pltpu.SemaphoreType.DMA((2,)))

                    self.guarded(
                        z == at,
                        lambda k=k, owner=owner, slot=slots_at[k]: rcopy(
                            self.merged.at[k], self.got.at[slot], b + 4 + k, b + slot, plane_dev(owner)
                        ),
                    )

        def finish(self, put):
            for slot in range(2):
                rcopy(self.got.at[slot], self.got.at[slot], self.base, self.base + slot, sibling).wait_recv()

            def body(own, one, two):
                loads = [lcopy(self.block(z), own), lcopy(self.got.at[0], one), lcopy(self.got.at[1], two)]
                for load in loads:
                    load.wait()
                for k in range(self.height // shard):
                    span = pl.ds(k * shard, shard)
                    put(k, own[span, :].astype(F32) + one[span, :].astype(F32) + two[span, :].astype(F32))

            shape = (self.height, self.grads.shape[1])
            pl.run_scoped(body, *[VM(shape, BF)] * 3)

    zg_o, zg_qkv = ZGather(r.w_o, shard), ZGather(r.w_qkv, KB, 2)
    sp_qkv = Spread(r.st_qkv)
    parts = range(len(PARTS))
    w_f, st_f = [r.w_f0, r.w_f1], [r.st_f0, r.st_f1]
    zg_f, sp_f = [ZGather(w, KB) for w in w_f], [Spread(st) for st in st_f]
    ag_normed, ag_cot, ag_two, ag_one = Gather(r.a_normed), Gather(r.a_cot), Gather(r.a_two), Gather(r.a_one)

    def mine_rows(whole, height):
        return whole.at[pl.ds(aligned((z * PL + q) * height, 16), height)]

    zg_o.start(r.in_o)
    local_o = lcopy(r.in_o, zg_o.block(z))
    base_small = slots(PL)
    for i in range(1, PL):
        copy = rcopy(r.in_small, r.small.at[z * PL + q], base_small + i, base_small + i, mate(i))
        copy.start()
        drains.append(copy.wait_send)
    local_small = lcopy(r.in_small, r.small.at[z * PL + q])
    for other in range(PL):
        for j in range(3):
            for zh in range(R):
                at = j * D + zh * PL * HD + other * HD
                r.st_qkv[other, :, j * QW + zh * HD : j * QW + (zh + 1) * HD] = r.in_qkv[:, at : at + HD]
    sp_qkv.start(mine_rows(r.w_qkv, shard))
    local_qkv = lcopy(r.st_qkv.at[q], mine_rows(r.w_qkv, shard))
    local_f = [None] * len(PARTS)

    def stage_f(p):
        width = PARTS[p]
        for other in range(PL):
            at = other * FW + STARTS[p]
            for k, source in enumerate((r.in_gate, r.in_up, r.in_down)):
                st_f[p][other, :, k * width : (k + 1) * width] = source[:, at : at + width]
        sp_f[p].start(mine_rows(w_f[p], shard))
        local_f[p] = lcopy(st_f[p].at[q], mine_rows(w_f[p], shard))

    def arrived(spread, whole):
        spread.wait(lambda s: whole.at[pl.ds(aligned((z * PL + s) * shard, 16), shard)])

    stage_f(0)

    local_small.wait()
    for i in range(1, PL):
        rcopy(r.in_small, r.small.at[z * PL + lax.rem(q - i + PL, PL)], base_small, base_small + i, mate(i)).wait_recv()
    base_smallz = slots(R)
    plane_small = r.small.at[pl.ds(z * PL, PL)]
    for i in range(1, R):
        copy = rcopy(plane_small, plane_small, base_smallz + i, base_smallz + i, plane_dev(lax.rem(z + i, R)))
        copy.start()
        drains.append(copy.wait_send)
    tokens = r.in_tokens[...].astype(F32)
    unit, _ = norm_stats(tokens)
    for i in range(1, R):
        block = r.small.at[pl.ds(lax.rem(z - i + R, R) * PL, PL)]
        rcopy(block, block, base_smallz, base_smallz + i, sibling).wait_recv()
    for d in range(R * PL):
        for k in range(4):
            r.vec[k : k + 1, shard * d : shard * (d + 1)] = r.small[d, k : k + 1, 0:shard]
        for k in range(3):
            r.biases[3 * d + k : 3 * d + k + 1, 0:HD] = r.small[d, 4 + k : 5 + k, 0:HD]
    for j in range(3):
        for zh in range(R):
            row = r.biases[pl.ds(j * H + zh * PL + q, 1), 0:HD]
            r.bias[0:1, j * QW + zh * HD : j * QW + (zh + 1) * HD] = row
    r.x_normed[...] = (unit * r.vec[0:1, :] + r.vec[1:2, :]).astype(BF)
    ag_normed.start(r.x_normed)

    stage_f(1)
    ag_cot.start(r.in_cot)
    zg_o.relay()
    local_qkv.wait()
    arrived(sp_qkv, r.w_qkv)
    zg_qkv.start()
    local_f[0].wait()
    arrived(sp_f[0], w_f[0])
    zg_qkv.relay(0)
    ag_normed.relay()
    zg_qkv.relay(1)
    zg_f[0].start()
    ag_normed.wait()
    zg_qkv.wait()

    TM = HS // 2
    table_specs = [pl.BlockSpec((HS, 128), lambda i: (0, 0))] * 3
    tables = [r.tables.at[k] for k in range(3)]

    def qkv_body(x, w, cos, s_one, s_two, o):
        projected = nn(x[...], w[...]) + r.bias[0:1, :]
        for piece in range(2 * QW // 128):
            part = projected[:, piece * 128 : (piece + 1) * 128]
            turned = part * cos[...] + pltpu.roll(part, 128 - ROT // 2, 1) * s_one[...] + pltpu.roll(part, ROT // 2, 1) * s_two[...]
            o[:, piece * 128 : (piece + 1) * 128] = turned.astype(BF)
        o[:, 2 * QW :] = projected[:, 2 * QW :].astype(BF)

    pltpu.emit_pipeline(
        qkv_body,
        grid=(TOK // HS,),
        in_specs=[pl.BlockSpec((HS, D), lambda i: (i, 0)), pl.BlockSpec((D, 3 * QW), lambda i: (0, 0))] + table_specs,
        out_specs=[pl.BlockSpec((HS, 3 * QW), lambda i: (i, 0))],
    )(r.a_normed, r.w_qkv, *tables, r.qkv)

    heads = QW // HD

    def softmax_block(queries, keys, first):
        scores = nt(keys, queries) * 0.125
        at_key = lax.broadcasted_iota(jnp.int32, scores.shape, 0)
        at_query = lax.broadcasted_iota(jnp.int32, scores.shape, 1) + first
        allowed = at_key <= at_query
        scores = jnp.where(allowed, scores, -1e30)
        largest = jnp.max(scores, axis=0, keepdims=True)
        weights = jnp.where(allowed, jnp.exp(scores - largest), 0.0)
        return weights / jnp.sum(weights, axis=0, keepdims=True)

    QB = HS // 2

    def attention_body(x, o):
        for h in range(heads):
            at = h * HD
            for blk in range(HS // QB):
                here, seen = blk * QB, (blk + 1) * QB
                probs = softmax_block(x[here : here + QB, at : at + HD], x[0:seen, QW + at : QW + at + HD], here)
                out = tn(probs.astype(BF), x[0:seen, 2 * QW + at : 2 * QW + at + HD])
                o[here : here + QB, at : at + HD] = out.astype(BF)

    pltpu.emit_pipeline(
        attention_body,
        grid=(TOK // HS,),
        in_specs=[pl.BlockSpec((HS, 3 * QW), lambda i: (i, 0))],
        out_specs=[pl.BlockSpec((HS, QW), lambda i: (i, 0))],
    )(r.qkv, r.att)

    local_f[1].wait()
    arrived(sp_f[1], w_f[1])
    ag_cot.relay()
    local_o.wait()
    zg_o.wait()

    red_att = Reduce(0)
    red_att.partial([(r.att, r.w_o)], nn)
    red_att.middle()
    zg_f[0].relay()
    zg_f[1].start()
    ag_cot.wait()
    middle = r.in_tokens[...].astype(F32) + red_att.finish()
    r.middle[...] = middle
    unit, _ = norm_stats(middle)
    r.x_two[...] = (unit * r.vec[2:3, :] + r.vec[3:4, :]).astype(BF)
    ag_two.start(r.x_two)
    ag_two.relay()
    ag_two.wait()
    zg_f[1].relay()

    hid, gug, g_f = [r.hid0, r.hid1], [r.gug0, r.gug1], [r.g_f0, r.g_f1]

    def feed_forward(p):
        width = PARTS[p]
        zg_f[p].wait()

        def feed_body(x, cot, w, hid_out, grad_out):
            both = nn(x[...], w[:, : 2 * width])
            gate = both[:, :width]
            up = both[:, width:]
            sig = 1.0 / (1.0 + jnp.exp(-gate))
            swish = gate * sig
            hid_out[...] = (swish * up).astype(BF)
            hidden_grad = nn(cot[...], w[:, 2 * width :])
            grad_out[:, :width] = (hidden_grad * up * sig * (1.0 + gate * (1.0 - sig))).astype(BF)
            grad_out[:, width:] = (hidden_grad * swish).astype(BF)

        pltpu.emit_pipeline(
            feed_body,
            grid=(TOK // TM,),
            in_specs=[pl.BlockSpec((TM, D), lambda i: (i, 0))] * 2
            + [pl.BlockSpec((D, 3 * width), lambda i: (0, 0), pipeline_mode=pl.Buffered(1))],
            out_specs=[pl.BlockSpec((TM, width), lambda i: (i, 0)), pl.BlockSpec((TM, 2 * width), lambda i: (i, 0))],
        )(r.a_two, r.a_cot, w_f[p], hid[p], gug[p])

    def feed_weight_grads(p):
        width = PARTS[p]

        def feed_grad_body(x, cot, grad, hidden, o):
            o[:, : 2 * width] = tn(x[...], grad[...]).astype(BF)
            o[:, 2 * width :] = tn(cot[...], hidden[...]).astype(BF)

        pltpu.emit_pipeline(
            feed_grad_body,
            grid=(D // 512,),
            in_specs=[pl.BlockSpec((TOK, 512), lambda i: (0, i))] * 2
            + [pl.BlockSpec((TOK, 2 * width), lambda i: (0, 0)), pl.BlockSpec((TOK, width), lambda i: (0, 0))],
            out_specs=[pl.BlockSpec((512, 3 * width), lambda i: (i, 0))],
        )(r.a_two, r.a_cot, gug[p], hid[p], g_f[p])

    def weight_grad(acts, grads, out, width, tile):
        def body(x, g, o):
            o[...] = tn(x[...], g[...]).astype(BF)

        pltpu.emit_pipeline(
            body,
            grid=(acts.shape[1] // tile,),
            in_specs=[pl.BlockSpec((TOK, tile), lambda i: (0, i)), pl.BlockSpec((TOK, width), lambda i: (0, 0))],
            out_specs=[pl.BlockSpec((tile, width), lambda i: (i, 0))],
        )(acts, grads, out)

    zr_f = [ZReduce(r.g_f0, r.zin_f0, r.zx_f0, r.zs_f0, KB), ZReduce(r.g_f1, r.zin_f1, r.zx_f1, r.zs_f1, KB)]
    zr_o = ZReduce(r.g_o, r.zin_o, r.zx_o, r.zs_o, shard)
    zr_qkv = ZReduce(r.g_qkv, r.zin_qkv, r.zx_qkv, r.zs_qkv, KB)

    feed_forward(0)
    feed_weight_grads(0)
    zr_f[0].start()
    feed_forward(1)
    red_two = Reduce(0, red_att)
    red_two.partial([(gug[p], w_f[p].at[:, pl.ds(0, 2 * PARTS[p])]) for p in parts], nt)
    red_two.middle()
    feed_weight_grads(1)
    zr_f[1].start()
    zr_f[0].merge()
    two_grad = red_two.finish()
    unit, scale = norm_stats(r.middle[...])
    middle_grad = r.in_cot[...].astype(F32) + norm_back(two_grad, unit, scale, r.vec[2:3, :])
    r.middle_grad[...] = middle_grad
    r.x_one[...] = middle_grad.astype(BF)
    ag_one.start(r.x_one)
    r.vec[6:7, :] = jnp.sum(two_grad * unit, axis=0, keepdims=True)
    r.vec[7:8, :] = jnp.sum(two_grad, axis=0, keepdims=True)

    def mixed_product(x, w):
        return nt(x, w[:, w.shape[1] - x.shape[1] :])

    red_mixed = Reduce(1)
    red_mixed.partial([(hid[p], w_f[p]) for p in parts], mixed_product)
    red_mixed.middle()
    ag_one.relay()
    ag_one.wait()

    def att_grad_body(x, w, o):
        o[...] = nt(x[...], w[...]).astype(BF)

    pltpu.emit_pipeline(
        att_grad_body,
        grid=(TOK // HS,),
        in_specs=[pl.BlockSpec((HS, D), lambda i: (i, 0)), pl.BlockSpec((QW, D), lambda i: (0, 0))],
        out_specs=[pl.BlockSpec((HS, QW), lambda i: (i, 0))],
    )(r.a_one, r.w_o, r.attg)

    zr_f[1].merge((0,))

    def attention_back_body(x, g, cos, s_one, s_two, o):
        for h in range(heads):
            at = h * HD
            key_grad = [jnp.zeros((QB, HD), F32) for _ in range(HS // QB)]
            value_grad = [jnp.zeros((QB, HD), F32) for _ in range(HS // QB)]
            for blk in range(HS // QB):
                here, seen = blk * QB, (blk + 1) * QB
                queries = x[here : here + QB, at : at + HD]
                keys = x[0:seen, QW + at : QW + at + HD]
                values = x[0:seen, 2 * QW + at : 2 * QW + at + HD]
                grads = g[here : here + QB, at : at + HD]
                probs = softmax_block(queries, keys, here)
                prob_grad = nt(values, grads)
                delta = jnp.sum(probs * prob_grad, axis=0, keepdims=True)
                score_grad = (probs * (prob_grad - delta)).astype(BF)
                low_probs = probs.astype(BF)
                r.turn[here : here + QB, at : at + HD] = tn(score_grad, keys) * 0.125
                key_part = nn(score_grad, queries) * 0.125
                value_part = nn(low_probs, grads)
                for k in range(blk + 1):
                    key_grad[k] = key_grad[k] + key_part[k * QB : (k + 1) * QB]
                    value_grad[k] = value_grad[k] + value_part[k * QB : (k + 1) * QB]
            for k in range(HS // QB):
                r.turn[k * QB : (k + 1) * QB, QW + at : QW + at + HD] = key_grad[k]
                o[k * QB : (k + 1) * QB, 2 * QW + at : 2 * QW + at + HD] = value_grad[k].astype(BF)
        for piece in range(2 * QW // 128):
            part = r.turn[:, piece * 128 : (piece + 1) * 128]
            back = part * cos[...] + pltpu.roll(part * s_one[...], ROT // 2, 1) + pltpu.roll(part * s_two[...], 128 - ROT // 2, 1)
            o[:, piece * 128 : (piece + 1) * 128] = back.astype(BF)

    pltpu.emit_pipeline(
        attention_back_body,
        grid=(TOK // HS,),
        in_specs=[pl.BlockSpec((HS, 3 * QW), lambda i: (i, 0)), pl.BlockSpec((HS, QW), lambda i: (i, 0))]
        + [pl.BlockSpec((HS, 128), lambda i: (0, 0))] * 3,
        out_specs=[pl.BlockSpec((HS, 3 * QW), lambda i: (i, 0))],
    )(r.qkv, r.attg, *tables, r.pg)

    weight_grad(r.a_normed, r.pg, r.g_qkv, 3 * QW, 512)
    zr_qkv.start()
    zr_f[1].merge((1,))
    red_one = Reduce(0, red_two)
    red_one.partial([(r.pg, r.w_qkv)], nt)
    red_one.middle()
    def o_grad_body(x, g, o):
        o[...] = tn(x[...], g[...]).astype(BF)

    pltpu.emit_pipeline(
        o_grad_body,
        grid=(D // 512,),
        in_specs=[pl.BlockSpec((TOK, QW), lambda i: (0, 0)), pl.BlockSpec((TOK, 512), lambda i: (0, i))],
        out_specs=[pl.BlockSpec((QW, 512), lambda i: (0, i))],
    )(r.att, r.a_one, r.g_o)
    zr_o.start()
    r.bias[0:1, :] = jnp.zeros((1, 3 * QW), F32)

    def bias_body(x):
        r.bias[0:1, :] += jnp.sum(x[...].astype(F32), axis=0, keepdims=True)

    pltpu.emit_pipeline(bias_body, grid=(TOK // TM,), in_specs=[pl.BlockSpec((TM, 3 * QW), lambda i: (i, 0))])(r.pg)

    back_f, back_qkv = [Spread(st) for st in st_f], Spread(r.st_qkv)
    pin_f = [r.pin_f0, r.pin_f1]

    def z_sum(reduce, sent, stage, spread, got):
        sent.wait_send()

        def put(k, total):
            stage[k] = total.astype(BF)

        reduce.finish(put)
        spread.start(got.at[q])
        return lcopy(stage.at[q], got.at[q])

    local_f[0] = z_sum(zr_f[0], sp_f[0], st_f[0], back_f[0], pin_f[0])
    zr_qkv.merge((0,))
    mixed = r.middle[...] + red_mixed.finish()
    r.out_mixed[0] = mixed.astype(BF)
    zr_qkv.merge((1,))
    local_f[1] = z_sum(zr_f[1], sp_f[1], st_f[1], back_f[1], pin_f[1])
    one_grad = red_one.finish()
    unit, scale = norm_stats(r.in_tokens[...].astype(F32))
    r.out_tokens[0] = r.middle_grad[...] + norm_back(one_grad, unit, scale, r.vec[0:1, :])
    r.vec[4:5, :] = jnp.sum(one_grad * unit, axis=0, keepdims=True)
    r.vec[5:6, :] = jnp.sum(one_grad, axis=0, keepdims=True)
    zr_o.merge()
    r.sg[...] = jnp.zeros_like(r.sg)
    for d in range(R * PL):
        for k in range(4):
            r.sg[d, k : k + 1, 0:shard] = r.vec[4 + k : 5 + k, shard * d : shard * (d + 1)]
    for j in range(3):
        for zh in range(R):
            g = j * H + zh * PL + q
            r.sg[g // 3, pl.ds(4 + lax.rem(g, 3), 1), 0:HD] = r.bias[0:1, j * QW + zh * HD : j * QW + (zh + 1) * HD]
    base_sgz = slots(R)
    for i in range(1, R):
        t = lax.rem(z + i, R)
        copy = rcopy(r.sg.at[pl.ds(t * PL, PL)], r.sgz.at[i - 1], base_sgz + i, base_sgz + i, plane_dev(t))
        copy.start()
        drains.append(copy.wait_send)

    def put_out(k, total):
        r.out_o[...] = total


    def pin_block(got):
        return lambda s: got.at[s]

    def feed_out(p):
        width = PARTS[p]
        local_f[p].wait()
        back_f[p].wait(pin_block(pin_f[p]))
        for other in range(PL):
            at = other * FW + STARTS[p]
            for k, target in enumerate((r.out_gate, r.out_up, r.out_down)):
                target[:, at : at + width] = pin_f[p][other, :, k * width : (k + 1) * width].astype(F32)

    feed_out(0)
    local_qkv = z_sum(zr_qkv, sp_qkv, r.st_qkv, back_qkv, r.pin_qkv)
    for i in range(1, R):
        rcopy(r.sgz.at[i - 1], r.sgz.at[i - 1], base_sgz, base_sgz + i, sibling).wait_recv()
    r.sgs[...] = r.sg[pl.ds(z * PL, PL)] + r.sgz[0] + r.sgz[1] + r.sgz[2]
    base_sgp = slots(PL)
    for i in range(1, PL):
        other = lax.rem(q + i, PL)
        copy = rcopy(r.sgs.at[other], r.sgp.at[i - 1], base_sgp + i, base_sgp + i, mate(i))
        copy.start()
        drains.append(copy.wait_send)

    feed_out(1)
    zr_o.finish(put_out)
    total = r.sgs[q]
    for i in range(1, PL):
        rcopy(r.sgp.at[i - 1], r.sgp.at[i - 1], base_sgp, base_sgp + i, sibling).wait_recv()
        total = total + r.sgp[i - 1]
    r.out_small[...] = total
    local_qkv.wait()
    back_qkv.wait(pin_block(r.pin_qkv))
    for other in range(PL):
        for j in range(3):
            for zh in range(R):
                at = j * D + zh * PL * HD + other * HD
                r.out_qkv[:, at : at + HD] = r.pin_qkv[other, :, j * QW + zh * HD : j * QW + (zh + 1) * HD].astype(F32)
    for spread in back_f:
        spread.wait_send()
    back_qkv.wait_send()
    red_mixed.drain()
    red_one.drain()
    for drain in drains:
        drain()
    assert counter[0] <= REMOTE_SEMS and local_count[0] <= LOCAL_SEMS, (counter, local_count)


def fast_local(tokens, out_grad, ln1_gain, ln1_shift, qkv_weight, qkv_bias, out_weight, ln2_gain, ln2_shift, gate_weight, up_weight, down_weight):
    planes, columns = lax.axis_size("batch") // 2, lax.axis_size("ctx")
    members = 2 * columns
    rows = tokens.shape[1]
    seq = rows * columns
    total = members * rows
    shard = qkv_weight.shape[0]
    q_width = D // members
    f_width = FF // members
    plane_rows = members * shard
    parts = (384, f_width - 384)
    dims = (planes, columns, members, rows, shard, q_width, f_width, parts)
    pieces = jnp.concatenate(
        [jnp.stack([ln1_gain, ln1_shift, ln2_gain, ln2_shift]), qkv_bias.reshape(3, HD)], axis=0
    ).astype(F32)
    small = jnp.pad(pieces, ((0, 1), (0, 128 - HD)))
    inputs = dict(
        in_tokens=(tokens.reshape(rows, D), VM),
        in_cot=(out_grad.reshape(rows, D), VM),
        in_small=(small, VM),
        in_qkv=(qkv_weight, VM),
        in_o=(out_weight, VM),
        in_gate=(gate_weight, VM),
        in_up=(up_weight, VM),
        in_down=(down_weight, VM),
        tables=(jnp.asarray(turn_tables(seq)), ANY),
    )
    outs = dict(
        out_mixed=((1, rows, D), BF, VM),
        out_tokens=((1, rows, D), F32, VM),
        out_small=((8, 128), F32, VM),
        out_qkv=((shard, 3 * D), F32, VM),
        out_o=((shard, D), F32, VM),
        out_gate=((shard, FF), F32, VM),
        out_up=((shard, FF), F32, VM),
        out_down=((shard, FF), F32, VM),
    )
    final = list(outs)
    spaces = dict(
        w_qkv=(D, 3 * q_width), w_o=(q_width, D),
        a_normed=(total, D), a_cot=(total, D), a_two=(total, D), a_one=(total, D),
        qkv=(total, 3 * q_width), att=(total, q_width), attg=(total, q_width), pg=(total, 3 * q_width),
        g_qkv=(D, 3 * q_width), g_o=(q_width, D),
        zin_qkv=(2, plane_rows, 3 * q_width), zin_o=(2, shard, D),
        zx_qkv=(2, plane_rows, 3 * q_width), zx_o=(2, shard, D),
        zs_qkv=(2, plane_rows, 3 * q_width), zs_o=(2, shard, D),
    )
    for p, width in enumerate(parts):
        spaces[f"w_f{p}"] = spaces[f"g_f{p}"] = (D, 3 * width)
        spaces[f"hid{p}"], spaces[f"gug{p}"] = (total, width), (total, 2 * width)
        for kind in ("zin", "zx", "zs"):
            spaces[f"{kind}_f{p}"] = (2, plane_rows, 3 * width)
    for name, shape in spaces.items():
        outs[name] = (shape, BF, ANY)
    scratch = dict(
        st_qkv=VM((members, shard, 3 * q_width), BF), pin_qkv=VM((members, shard, 3 * q_width), BF),
        small=VM((planes * members, 8, 128), F32), sg=VM((planes * members, 8, 128), F32),
        sgz=VM((3, members, 8, 128), F32), sgs=VM((members, 8, 128), F32), sgp=VM((members - 1, 8, 128), F32),
        vec=VM((8, D), F32), biases=VM((3 * H, 128), F32), bias=VM((8, 3 * q_width), F32),
        x_normed=VM((rows, D), BF), x_two=VM((rows, D), BF), x_one=VM((rows, D), BF),
        middle=VM((rows, D), F32), middle_grad=VM((rows, D), F32),
        mine=VM((seq, D), BF),
        turn=VM((seq, 2 * q_width), F32),
    )
    for p, width in enumerate(parts):
        scratch[f"st_f{p}"] = scratch[f"pin_f{p}"] = VM((members, shard, 3 * width), BF)
    for k in range(2):
        scratch[f"sibout{k}"] = VM((seq, D), BF)
        scratch[f"theirs{k}"] = VM((seq, D), BF)
        scratch[f"redout{k}"] = VM((columns - 1, rows, D), BF)
        scratch[f"redin{k}"] = VM((columns - 1, rows, D), BF)
        scratch[f"redown{k}"] = VM((rows, D), F32)
    scratch["ss"] = pltpu.SemaphoreType.DMA((REMOTE_SEMS,))
    scratch["rs"] = pltpu.SemaphoreType.DMA((REMOTE_SEMS,))
    scratch["ls"] = pltpu.SemaphoreType.DMA((LOCAL_SEMS,))
    results = pl.pallas_call(
        functools.partial(layer_kernel, dims, list(inputs), list(outs), list(scratch)),
        out_shape=[jax.ShapeDtypeStruct(shape, kind) for shape, kind, _ in outs.values()],
        in_specs=[pl.BlockSpec(memory_space=place) for _, place in inputs.values()],
        out_specs=[pl.BlockSpec(memory_space=place) for _, _, place in outs.values()],
        scratch_shapes=list(scratch.values()),
        compiler_params=pltpu.CompilerParams(collective_id=0, has_side_effects=True, vmem_limit_bytes=62 * 2**20),
        cost_estimate=pl.CostEstimate(flops=42 * 10**9, bytes_accessed=300 * 10**6, transcendentals=0),
        name="layer",
    )(*[array for array, _ in inputs.values()])
    got = dict(zip(final, results))
    vectors = got["out_small"][:, :HD]
    return (
        got["out_mixed"],
        got["out_tokens"],
        vectors[0],
        vectors[1],
        got["out_qkv"],
        vectors[4:7].reshape(3 * HD),
        got["out_o"],
        vectors[2],
        vectors[3],
        got["out_gate"],
        got["out_up"],
        got["out_down"],
    )


def fits(mesh):
    return mesh.shape["batch"] == 8 and mesh.shape["ctx"] == 4


def solution(mesh):
    in_specs = (
        P("batch", "ctx", None),
        P("batch", "ctx", None),
        P(("batch", "ctx")),
        P(("batch", "ctx")),
        P(("batch", "ctx"), None),
        P(("batch", "ctx")),
        P(("batch", "ctx"), None),
        P(("batch", "ctx")),
        P(("batch", "ctx")),
        P(("batch", "ctx"), None),
        P(("batch", "ctx"), None),
        P(("batch", "ctx"), None),
    )
    out_specs = (
        P("batch", "ctx", None),
        P("batch", "ctx", None),
        P(("batch", "ctx")),
        P(("batch", "ctx")),
        P(("batch", "ctx"), None),
        P(("batch", "ctx")),
        P(("batch", "ctx"), None),
        P(("batch", "ctx")),
        P(("batch", "ctx")),
        P(("batch", "ctx"), None),
        P(("batch", "ctx"), None),
        P(("batch", "ctx"), None),
    )
    body = fast_local if fits(mesh) else local
    return jax.shard_map(body, mesh=mesh, in_specs=in_specs, out_specs=out_specs, check_vma=False)
```

```python
import functools

import jax
import jax.numpy as jnp
import numpy as np
from jax import lax
from jax.experimental import pallas as pl
from jax.experimental.pallas import tpu as pltpu
from jax.sharding import PartitionSpec as P

D = 2048
FF = 5632
H = 32
HD = 64
ROT = 16


def layer_norm(values, gain, shift):
    centre = jnp.mean(values, axis=-1, keepdims=True)
    centred = values - centre
    spread = jnp.mean(centred * centred, axis=-1, keepdims=True)
    return centred * lax.rsqrt(spread + 1e-05) * gain + shift


def rotary(values, positions):
    half_dims = ROT // 2
    frequency = 10000.0 ** (-jnp.arange(half_dims, dtype=jnp.float32) * 2.0 / ROT)
    angles = positions.astype(jnp.float32)[:, None] * frequency[None, :]
    cosine_term = jnp.cos(angles)[:, None, :]
    sine_term = jnp.sin(angles)[:, None, :]
    first_half = values[..., :half_dims]
    second_half = values[..., half_dims:ROT]
    return jnp.concatenate(
        [
            first_half * cosine_term - second_half * sine_term,
            second_half * cosine_term + first_half * sine_term,
            values[..., ROT:],
        ],
        axis=-1,
    )


def swish_product(gate_value, up_value):
    return gate_value / (1.0 + jnp.exp(-gate_value)) * up_value


def project_back(left, right):
    return lax.dot_general(
        left, right, (((1,), (1,)), ((), ())), preferred_element_type=jnp.float32
    )


def outer_rows(left, right):
    return lax.dot_general(
        left, right, (((0,), (0,)), ((), ())), preferred_element_type=jnp.float32
    )


def local(
    tokens,
    out_grad,
    ln1_gain,
    ln1_shift,
    qkv_weight,
    qkv_bias,
    out_weight,
    ln2_gain,
    ln2_shift,
    gate_weight,
    up_weight,
    down_weight,
):
    local_rows = tokens.shape[1]
    seq_length = local_rows * lax.axis_size("ctx")
    inputs = tokens.reshape(local_rows, D).astype(jnp.float32)
    cotangent = out_grad.reshape(local_rows, D).astype(jnp.float32)
    places = lax.axis_index("ctx") * local_rows + jnp.arange(local_rows, dtype=jnp.int32)
    attn_set = (
        lax.all_gather(qkv_weight, ("batch", "ctx"), axis=0, tiled=True),
        lax.all_gather(out_weight, ("batch", "ctx"), axis=0, tiled=True),
        lax.all_gather(qkv_bias, ("batch", "ctx"), axis=0, tiled=True),
        lax.all_gather(ln1_gain, ("batch", "ctx"), axis=0, tiled=True),
        lax.all_gather(ln1_shift, ("batch", "ctx"), axis=0, tiled=True),
    )
    gain_one = attn_set[3].astype(jnp.float32)
    shift_one = attn_set[4].astype(jnp.float32)
    normed = layer_norm(inputs, gain_one, shift_one)
    normed_low = normed.astype(jnp.bfloat16)
    projected = jnp.dot(normed_low, attn_set[0], preferred_element_type=jnp.float32) + attn_set[
        2
    ].astype(jnp.float32)
    pair_heads = projected[:, : 2 * D].reshape(local_rows, 2 * H, HD)
    turned = rotary(pair_heads, places)
    queries = turned[:, :H].astype(jnp.bfloat16)
    key_rows = turned[:, H:].reshape(local_rows, D).astype(jnp.bfloat16)
    value_rows = projected[:, 2 * D :].astype(jnp.bfloat16)
    start_state = (
        jnp.full((H, local_rows), -1e30, jnp.float32),
        jnp.zeros((H, local_rows), jnp.float32),
        jnp.zeros((H, local_rows, HD), jnp.float32),
    )
    carry = start_state
    key_piece = lax.all_gather(key_rows, "ctx", axis=0, tiled=True)
    value_piece = lax.all_gather(value_rows, "ctx", axis=0, tiled=True)
    piece_rows = key_piece.shape[0]
    block_rows = 512
    block_count = piece_rows // block_rows

    def inner(state, block):
        largest, totals, accum = state
        key_block, value_block, offset = block
        raw_scores = (
            jnp.einsum("qhd,khd->hqk", queries, key_block, preferred_element_type=jnp.float32)
            * 0.125
        )
        key_places = offset + jnp.arange(block_rows, dtype=jnp.int32)
        allowed = (key_places[None, :] <= places[:, None])[None]
        raw_scores = jnp.where(allowed, raw_scores, -1e30)
        new_largest = jnp.maximum(largest, jnp.max(raw_scores, axis=-1))
        weights = jnp.where(allowed, jnp.exp(raw_scores - new_largest[..., None]), 0.0)
        factor = jnp.exp(largest - new_largest)
        totals = totals * factor + jnp.sum(weights, axis=-1)
        accum = accum * factor[..., None] + jnp.einsum(
            "hqk,khd->hqd",
            weights.astype(jnp.bfloat16),
            value_block,
            preferred_element_type=jnp.float32,
        )
        return ((new_largest, totals, accum), None)

    offsets = jnp.arange(block_count, dtype=jnp.int32) * block_rows
    blocks = (
        key_piece.reshape(block_count, block_rows, H, HD),
        value_piece.reshape(block_count, block_rows, H, HD),
        offsets,
    )
    carry, unused = lax.scan(inner, carry, blocks)
    largest, totals, accum = carry
    attended = jnp.transpose(accum / totals[..., None], (1, 0, 2)).reshape(local_rows, D)
    log_total = largest + jnp.log(totals)
    attended_low = attended.astype(jnp.bfloat16)
    middle = inputs + jnp.dot(attended_low, attn_set[1], preferred_element_type=jnp.float32)
    mlp_set = (
        lax.all_gather(gate_weight, ("batch", "ctx"), axis=0, tiled=True),
        lax.all_gather(up_weight, ("batch", "ctx"), axis=0, tiled=True),
        lax.all_gather(down_weight, ("batch", "ctx"), axis=0, tiled=True),
        lax.all_gather(ln2_gain, ("batch", "ctx"), axis=0, tiled=True),
        lax.all_gather(ln2_shift, ("batch", "ctx"), axis=0, tiled=True),
    )
    gain_two = mlp_set[3].astype(jnp.float32)
    shift_two = mlp_set[4].astype(jnp.float32)
    normed_two_low = layer_norm(middle, gain_two, shift_two).astype(jnp.bfloat16)
    gate_value = jnp.dot(normed_two_low, mlp_set[0], preferred_element_type=jnp.float32)
    up_value = jnp.dot(normed_two_low, mlp_set[1], preferred_element_type=jnp.float32)
    hidden_low = swish_product(gate_value, up_value).astype(jnp.bfloat16)
    mixed = (middle + project_back(hidden_low, mlp_set[2])).astype(jnp.bfloat16)
    mlp_back = (
        lax.all_gather(gate_weight, ("batch", "ctx"), axis=0, tiled=True),
        lax.all_gather(up_weight, ("batch", "ctx"), axis=0, tiled=True),
        lax.all_gather(down_weight, ("batch", "ctx"), axis=0, tiled=True),
        lax.all_gather(ln2_gain, ("batch", "ctx"), axis=0, tiled=True),
        lax.all_gather(ln2_shift, ("batch", "ctx"), axis=0, tiled=True),
    )
    attn_back = (
        lax.all_gather(qkv_weight, ("batch", "ctx"), axis=0, tiled=True),
        lax.all_gather(out_weight, ("batch", "ctx"), axis=0, tiled=True),
        lax.all_gather(qkv_bias, ("batch", "ctx"), axis=0, tiled=True),
        lax.all_gather(ln1_gain, ("batch", "ctx"), axis=0, tiled=True),
        lax.all_gather(ln1_shift, ("batch", "ctx"), axis=0, tiled=True),
    )
    branch_two = cotangent.astype(jnp.bfloat16)
    hidden_grad = jnp.dot(branch_two, mlp_back[2], preferred_element_type=jnp.float32)
    unused_value, act_pull = jax.vjp(swish_product, gate_value, up_value)
    gate_grad, up_grad = act_pull(hidden_grad)
    gate_low = gate_grad.astype(jnp.bfloat16)
    up_low = up_grad.astype(jnp.bfloat16)
    normed_two_grad = project_back(gate_low, mlp_back[0]) + project_back(up_low, mlp_back[1])
    unused_two, norm_pull_two = jax.vjp(layer_norm, middle, gain_two, shift_two)
    middle_part, gain_two_grad, shift_two_grad = norm_pull_two(normed_two_grad)
    middle_grad = cotangent + middle_part
    gate_weight_grad, up_weight_grad, down_weight_grad = (
        lax.psum_scatter(
            outer_rows(left, right).astype(jnp.bfloat16), ("batch", "ctx"), scatter_dimension=0, tiled=True
        ).astype(jnp.float32)
        for left, right in ((normed_two_low, gate_low), (normed_two_low, up_low), (branch_two, hidden_low))
    )
    branch_one = middle_grad.astype(jnp.bfloat16)
    out_term = outer_rows(attended_low, branch_one)
    attended_grad = project_back(branch_one, attn_back[1]).astype(jnp.bfloat16)
    grad_heads = attended_grad.reshape(local_rows, H, HD)
    delta = jnp.transpose(
        jnp.sum((attended_grad.astype(jnp.float32) * attended).reshape(local_rows, H, HD), axis=-1)
    )
    key_all, value_all = (
        lax.all_gather(key_rows, "ctx", axis=0, tiled=True),
        lax.all_gather(value_rows, "ctx", axis=0, tiled=True),
    )
    back_rows = 512
    back_count = seq_length // back_rows

    def back_block(query_grad, block):
        key_block, value_block, offset = block
        raw_scores = (
            jnp.einsum("qhd,khd->hqk", queries, key_block, preferred_element_type=jnp.float32)
            * 0.125
        )
        key_places = offset + jnp.arange(back_rows, dtype=jnp.int32)
        allowed = (key_places[None, :] <= places[:, None])[None]
        probs = jnp.where(allowed, jnp.exp(raw_scores - log_total[..., None]), 0.0)
        prob_grad = jnp.einsum(
            "qhd,khd->hqk", grad_heads, value_block, preferred_element_type=jnp.float32
        )
        score_grad = (probs * (prob_grad - delta[..., None])).astype(jnp.bfloat16)
        query_grad = (
            query_grad
            + jnp.einsum("hqk,khd->qhd", score_grad, key_block, preferred_element_type=jnp.float32)
            * 0.125
        )
        key_grad = (
            jnp.einsum("hqk,qhd->khd", score_grad, queries, preferred_element_type=jnp.float32)
            * 0.125
        )
        value_grad = jnp.einsum(
            "hqk,qhd->khd",
            probs.astype(jnp.bfloat16),
            grad_heads,
            preferred_element_type=jnp.float32,
        )
        return (
            query_grad,
            jnp.concatenate(
                [key_grad.reshape(back_rows, D), value_grad.reshape(back_rows, D)], axis=1
            ),
        )

    back_offsets = jnp.arange(back_count, dtype=jnp.int32) * back_rows
    back_blocks = (
        key_all.reshape(back_count, back_rows, H, HD),
        value_all.reshape(back_count, back_rows, H, HD),
        back_offsets,
    )
    query_grad, kv_terms = lax.scan(
        back_block, jnp.zeros((local_rows, H, HD), jnp.float32), back_blocks
    )
    kv_local = lax.psum_scatter(
        kv_terms.reshape(seq_length, 2 * D).astype(jnp.bfloat16),
        "ctx",
        scatter_dimension=0,
        tiled=True,
    ).astype(jnp.float32)

    def turn_heads(heads_in):
        return rotary(heads_in, places)

    unused_three, turn_pull = jax.vjp(turn_heads, pair_heads)
    pair_grad = turn_pull(
        jnp.concatenate([query_grad, kv_local[:, :D].reshape(local_rows, H, HD)], axis=1)
    )[0]
    projected_grad = jnp.concatenate(
        [pair_grad.reshape(local_rows, 2 * D), kv_local[:, D:]], axis=1
    ).astype(jnp.bfloat16)
    qkv_term = outer_rows(normed_low, projected_grad)
    bias_term = jnp.sum(projected_grad.astype(jnp.float32), axis=0)
    normed_grad = project_back(projected_grad, attn_back[0])
    unused_four, norm_pull = jax.vjp(layer_norm, inputs, gain_one, shift_one)
    input_part, gain_one_grad, shift_one_grad = norm_pull(normed_grad)
    tokens_grad = (middle_grad + input_part).reshape(1, local_rows, D)
    summed = (
        lax.psum_scatter(qkv_term, ("batch", "ctx"), scatter_dimension=0, tiled=True),
        lax.psum_scatter(out_term, ("batch", "ctx"), scatter_dimension=0, tiled=True),
        lax.psum_scatter(bias_term, ("batch", "ctx"), scatter_dimension=0, tiled=True),
        lax.psum_scatter(gain_one_grad, ("batch", "ctx"), scatter_dimension=0, tiled=True),
        lax.psum_scatter(shift_one_grad, ("batch", "ctx"), scatter_dimension=0, tiled=True),
        lax.psum_scatter(gain_two_grad, ("batch", "ctx"), scatter_dimension=0, tiled=True),
        lax.psum_scatter(shift_two_grad, ("batch", "ctx"), scatter_dimension=0, tiled=True),
    )
    return (
        mixed.reshape(1, local_rows, D),
        tokens_grad,
        summed[3],
        summed[4],
        summed[0],
        summed[2],
        summed[1],
        summed[5],
        summed[6],
        gate_weight_grad,
        up_weight_grad,
        down_weight_grad,
    )


BF = jnp.bfloat16
F32 = jnp.float32
MESH = pl.DeviceIdType.MESH
ANY = pl.ANY
VM = pltpu.VMEM
REMOTE_SEMS = 240
LOCAL_SEMS = 64


def nt(left, right):
    return lax.dot_general(left, right, (((1,), (1,)), ((), ())), preferred_element_type=F32)


def tn(left, right):
    return lax.dot_general(left, right, (((0,), (0,)), ((), ())), preferred_element_type=F32)


def nn(left, right):
    return jnp.dot(left, right, preferred_element_type=F32)


def norm_stats(values):
    centre = jnp.mean(values, axis=-1, keepdims=True)
    centred = values - centre
    spread = jnp.mean(centred * centred, axis=-1, keepdims=True)
    scale = lax.rsqrt(spread + 1e-05)
    return centred * scale, scale


def norm_back(grad, unit, scale, gain):
    weighted = grad * gain
    lead = jnp.mean(weighted, axis=-1, keepdims=True)
    tilt = jnp.mean(weighted * unit, axis=-1, keepdims=True)
    return scale * (weighted - lead - unit * tilt)


def turn_tables(length):
    half = ROT // 2
    freq = (np.float32(10000.0) ** (-np.arange(half, dtype=np.float32) * np.float32(2.0) / np.float32(ROT))).astype(np.float32)
    angles = np.arange(length, dtype=np.float32)[:, None] * freq[None, :]
    cosine, sine = np.cos(angles), np.sin(angles)
    tables = np.zeros((2, length, 128), np.float32)
    tables[0] = 1.0
    for start in (0, HD):
        tables[0, :, start : start + half] = cosine
        tables[0, :, start + half : start + ROT] = cosine
        tables[1, :, start : start + half] = -sine
        tables[1, :, start + half : start + ROT] = sine
    return tables


def aligned(value, to):
    return value if isinstance(value, int) else pl.multiple_of(value, to)


def feed_columns(width):
    return 2 * width + -(-width // 128) * 128


class Names:
    pass


def layer_kernel(dims, names_in, names_out, names_scratch, *refs):
    R, C, PL, rows, shard, QW, FW, PARTS = dims
    r = Names()
    for name, ref in zip(names_in + names_out + names_scratch, refs):
        setattr(r, name, ref)
    batch = lax.axis_index("batch")
    c = lax.axis_index("ctx")
    z = batch // 2
    core = lax.rem(batch, 2)
    q = core * C + c
    HS = PL // 2 * rows
    TOK = PL * rows
    KB = PL * shard
    STARTS = [sum(PARTS[:p]) for p in range(len(PARTS))]
    WC = [feed_columns(width) for width in PARTS]

    at_plane = [z == at for at in range(R)]
    counter = [0]
    local_count = [0]

    def slots(count):
        first = counter[0]
        counter[0] += count
        return first

    def mate(i):
        other = lax.rem(q + i, PL)
        return (z * 2 + other // C, lax.rem(other, C))

    def row_index(i):
        across, along = lax.rem(lax.rem(c, 2) + lax.rem(i, 2), 2), lax.rem(c // 2 + i // 2, 2)
        return 2 * along + across

    def row_mate(i):
        return (batch, row_index(i))

    sibling = (z * 2 + 1 - core, c)

    def plane_dev(t):
        return (t * 2 + core, c)

    def rcopy(src, dst, send, recv, dev):
        return pltpu.make_async_remote_copy(
            src_ref=src, dst_ref=dst, send_sem=r.ss.at[send], recv_sem=r.rs.at[recv], device_id=dev, device_id_type=MESH
        )

    drains = []

    def lcopy(src, dst):
        copy = pltpu.make_async_copy(src, dst, r.ls.at[local_count[0]])
        local_count[0] += 1
        copy.start()
        return copy

    loads = {name: lcopy(getattr(r, "in_" + name), getattr(r, "v_" + name)) for name in ("tokens", "cot")}

    local_tables = lcopy(r.tables, r.turns)
    barrier = pltpu.get_barrier_semaphore()
    for i in range(1, PL):
        pl.semaphore_signal(barrier, inc=1, device_id=mate(i), device_id_type=MESH)
    for i in range(1, R):
        pl.semaphore_signal(barrier, inc=1, device_id=plane_dev(lax.rem(z + i, R)), device_id_type=MESH)
    pl.semaphore_wait(barrier, PL - 1 + R - 1)

    OFFS = (2, -2, 1, -1)

    class ZGather:
        def __init__(self, whole, height, chunks=1):
            self.whole, self.height, self.chunks = whole, height, chunks
            self.base = [slots(6) for _ in range(chunks)]

        def block(self, s, chunk=None):
            if chunk is None:
                return self.whole.at[pl.ds(aligned(s * self.height, 16), self.height)]
            part = self.height // self.chunks
            return self.whole.at[pl.ds(aligned(s * self.height + chunk * part, 16), part)]

        def guarded(self, ok, make):
            @pl.when(ok)
            def _():
                make().start()

            def drain():
                @pl.when(ok)
                def _():
                    make().wait_send()

            drains.append(drain)

        def start(self, src=None):
            for chunk in range(self.chunks):
                for k, off in enumerate(OFFS):
                    t = z + off
                    ok = (t >= 0) & (t < R)
                    if off == 2:
                        ok = ok & (z == 0)
                    if off == -2:
                        ok = ok & (z == R - 1)

                    def make(chunk=chunk, k=k, t=t):
                        mine = self.block(z, chunk)
                        return rcopy(mine if src is None else src, mine, self.base[chunk] + k, self.base[chunk] + z, plane_dev(t))

                    self.guarded(ok, make)

        def got(self, s, chunk):
            block = self.block(s, chunk)
            rcopy(block, block, self.base[chunk], self.base[chunk] + s, sibling).wait_recv()

        def relay(self, chunk=0):
            for at, blocks, to in ((R - 2, (1, 0), R - 1), (1, (2, 3), 0)):
                for k, s in enumerate(blocks):

                    @pl.when(z == at)
                    def _():
                        self.got(s, chunk)

                    def make(s=s, to=to, k=k):
                        block = self.block(s, chunk)
                        return rcopy(block, block, self.base[chunk] + 4 + k, self.base[chunk] + s, plane_dev(to))

                    self.guarded(z == at, make)

        def wait_block(self, s):
            for chunk in range(self.chunks):
                skip = z == s
                skip = skip | (z == (R - 2 if s < 2 else 1))

                @pl.when(jnp.logical_not(skip))
                def _():
                    self.got(s, chunk)

        def wait(self):
            for s in range(R):
                self.wait_block(s)

    class Spread:
        def __init__(self, stage):
            self.stage, self.base = stage, slots(PL)

        def start(self, target):
            self.target = target
            for i in range(1, PL):
                other = lax.rem(q + i, PL)
                copy = rcopy(self.stage.at[other], target, self.base + i, self.base + i, mate(i))
                copy.start()

        def wait_send(self):
            for i in range(1, PL):
                other = lax.rem(q + i, PL)
                rcopy(self.stage.at[other], self.target, self.base + i, self.base + i, mate(i)).wait_send()

        def wait(self, block):
            for i in range(1, PL):
                rcopy(self.stage.at[0], block(lax.rem(q - i + PL, PL)), self.base + i, self.base + i, mate(i)).wait_recv()

    class Gather:
        def __init__(self, whole):
            self.whole, self.base = whole, slots(2 * C)

        def block(self, s):
            return self.whole.at[pl.ds(aligned(s * rows, 16), rows)]

        def start(self, src):
            self.local = lcopy(src, self.block(q))
            sends = []
            for i in range(1, C):
                sends.append(rcopy(src, self.block(q), self.base + i, self.base + i, row_mate(i)))
            sends.append(rcopy(src, self.block(q), self.base, self.base, sibling))
            for copy in sends:
                copy.start()
            self.sends = sends

        def drain(self):
            for copy in self.sends:
                copy.wait_send()
            for i in range(1, C):
                self.passed(i).wait_send()

        def relay(self):
            for i in range(1, C):
                self.relay_one(i)

        def passed(self, i):
            block = self.block(core * C + row_index(i))
            return rcopy(block, block, self.base + C - 1 + i, self.base + C - 1 + i, sibling)

        def relay_one(self, i):
            block = self.block(core * C + row_index(i))
            rcopy(block, block, self.base, self.base + i, sibling).wait_recv()
            self.passed(i).start()

        def wait_one(self, i):
            block = self.block((1 - core) * C + row_index(i))
            sem = self.base + jnp.where(i == 0, 0, C - 1 + i)
            rcopy(block, block, self.base, sem, sibling).wait_recv()

        def wait(self):
            for i in range(C):
                self.wait_one(i)
            self.local.wait()

        def each(self, use):
            self.local.wait()

            @pl.loop(0, C)
            def _(i):
                @pl.when(i > 0)
                def _():
                    self.relay_one(i)

                use(core * C + row_index(i))
                self.wait_one(i)
                use((1 - core) * C + row_index(i))

    class Reduce:
        def __init__(self, k, before=None):
            self.sibout, self.theirs = getattr(r, f"sibout{k}"), getattr(r, f"theirs{k}")
            self.out, self.got, self.own = getattr(r, f"redout{k}"), getattr(r, f"redin{k}"), getattr(r, f"redown{k}")
            self.base = slots(C + 2)
            self.before = before


        def run(self, pairs, compute, later=False):
            chunk_rows = HS // 2

            def to_sibling(chunk):
                span = pl.ds(chunk * chunk_rows, chunk_rows)
                return rcopy(self.sibout.at[span], self.theirs.at[span], self.base + C + chunk, self.base + C + chunk, sibling)

            def product(target, weights, seq, chunk):
                total = None
                for (x, _), w in zip(pairs, weights):
                    term = compute(x[pl.ds(aligned(seq * HS + chunk * chunk_rows, 16), chunk_rows), :], w)
                    total = term if total is None else total + term
                target[chunk * chunk_rows : (chunk + 1) * chunk_rows, :] = total.astype(BF)

            def pass_on(chunk):
                to_sibling(chunk).wait_recv()
                for blk in range(chunk * C // 2, (chunk + 1) * C // 2):
                    i = lax.rem(blk + c, 2) + 2 * lax.rem(blk // 2 + c // 2, 2)
                    span = pl.ds(blk * rows, rows)
                    total = r.mine[span, :].astype(F32) + self.theirs[span, :].astype(F32)

                    @pl.when(i == 0)
                    def _():
                        self.own[...] = total.astype(self.own.dtype)

                    @pl.when(i != 0)
                    def _():
                        self.out[i - 1] = total.astype(BF)
                        self.to_row(i, blk).start()

            def body(*bufs):
                bufs = list(bufs)
                weights, loads = [], []
                for _, w in pairs:
                    if isinstance(w, tuple):
                        weights.append(bufs.pop(0))
                        loads.append(lcopy(w[0], weights[-1]))
                    else:
                        weights.append(w)
                for load in loads:
                    load.wait()
                if self.before is not None:
                    self.before.drain()
                product(self.sibout, weights, 1 - core, 0)
                to_sibling(0).start()
                product(r.mine, weights, core, 0)
                product(self.sibout, weights, 1 - core, 1)
                to_sibling(1).start()
                if not later:
                    pass_on(0)
                product(r.mine, weights, core, 1)
                if not later:
                    pass_on(1)

            pl.run_scoped(body, *[VM(w[0].shape, BF) for _, w in pairs if isinstance(w, tuple)])
            self.drain = lambda: self.drain_all(to_sibling)
            self.pass_on = lambda: (pass_on(0), pass_on(1))

        def to_row(self, i, blk):
            return rcopy(self.out.at[i - 1], self.got.at[i - 1], self.base + i, self.base + i, (batch, blk))

        def drain_all(self, to_sibling):
            to_sibling(0).wait_send()
            to_sibling(1).wait_send()
            for i in range(1, C):
                self.to_row(i, row_index(i)).wait_send()

        def finish(self):
            for i in range(1, C):
                rcopy(self.out.at[i - 1], self.got.at[i - 1], self.base + i, self.base + i, row_mate(i)).wait_recv()
            total = self.own[...].astype(F32)
            for i in range(1, C):
                total = total + self.got[i - 1].astype(F32)
            return total

    ORDER = ((3, 2, 1, 0), (0, 3, 2, 1), (3, 0, 1, 2), (0, 1, 2, 3))

    class ZReduce:
        def __init__(self, grads, got, extra, merged, height):
            self.grads, self.got, self.extra, self.merged, self.height = grads, got, extra, merged, height
            self.base = slots(12)

        def block(self, t):
            return self.grads.at[pl.ds(aligned(t * self.height, 16), self.height)]

        def guarded(self, ok, make):
            @pl.when(ok)
            def _():
                make().start()

            def drain():
                @pl.when(ok)
                def _():
                    make().wait_send()

            drains.append(drain)

        def send(self, at, owner):
            b = self.base
            via = {0: 1, R - 1: R - 2}.get(at)
            if owner == at or (via is None and abs(owner - at) == 2) or (via is None and owner == R - 1 - at):
                return
            if via is None:
                slot = 1 if owner < at else 0
                make = lambda: rcopy(self.block(owner), self.got.at[slot], b + 3, b + slot, plane_dev(owner))
            elif owner == via:
                slot = 0 if at == 0 else 1
                make = lambda: rcopy(self.block(owner), self.got.at[slot], b + 2, b + slot, plane_dev(via))
            else:
                k = 0 if owner == R - 1 - at else 1
                make = lambda: rcopy(self.block(owner), self.extra.at[k], b + k, b + 2 + k, plane_dev(via))
            self.guarded(at_plane[at], make)

        def start(self):
            for step in range(R):
                self.start_step(step)

        def start_step(self, step):
            for at in range(R):
                self.send(at, ORDER[at][step])

        def merge(self, steps=(0, 1)):
            b = self.base
            for k in steps:
                for at, to, slots_at in ((1, (3, 2), (1, 0)), (2, (0, 1), (0, 1))):
                    owner = to[k]

                    @pl.when(z == at)
                    def _():
                        def body(own, other, sem):
                            first = pltpu.make_async_copy(self.block(owner), own, sem.at[0])
                            first.start()
                            rcopy(self.extra.at[k], self.extra.at[k], b, b + 2 + k, sibling).wait_recv()
                            second = pltpu.make_async_copy(self.extra.at[k], other, sem.at[1])
                            second.start()
                            first.wait()
                            second.wait()
                            own[...] = (own[...].astype(F32) + other[...].astype(F32)).astype(BF)
                            pltpu.sync_copy(own, self.merged.at[k])

                        shape = (self.height, self.grads.shape[1])
                        pl.run_scoped(body, VM(shape, BF), VM(shape, BF), pltpu.SemaphoreType.DMA((2,)))

                    self.guarded(
                        z == at,
                        lambda k=k, owner=owner, slot=slots_at[k]: rcopy(
                            self.merged.at[k], self.got.at[slot], b + 4 + k, b + slot, plane_dev(owner)
                        ),
                    )

        def wait(self):
            for slot in range(2):
                rcopy(self.got.at[slot], self.got.at[slot], self.base, self.base + slot, sibling).wait_recv()

        def finish(self, put):
            self.wait()

            def body(own, one, two):
                loads = [lcopy(self.block(z), own), lcopy(self.got.at[0], one), lcopy(self.got.at[1], two)]
                for load in loads:
                    load.wait()
                for k in range(self.height // shard):
                    span = pl.ds(k * shard, shard)
                    put(k, own[span, :].astype(F32) + one[span, :].astype(F32) + two[span, :].astype(F32))

            shape = (self.height, self.grads.shape[1])
            pl.run_scoped(body, *[VM(shape, BF)] * 3)

    zg_o, zg_qkv = ZGather(r.w_o, shard), ZGather(r.w_qkv, KB, 2)
    sp_qkv = Spread(r.st_qkv)
    parts = range(len(PARTS))
    w_f, st_f = [r.w_f0, r.w_f1], [r.st_f0, r.st_f1]
    zg_f, sp_f = [ZGather(w, KB) for w in w_f], [Spread(st) for st in st_f]
    ag_normed, ag_cot, ag_two, ag_one = Gather(r.a_normed), Gather(r.a_cot), Gather(r.a_two), Gather(r.a_one)

    def mine_rows(whole, height):
        return whole.at[pl.ds(aligned((z * PL + q) * height, 16), height)]

    zg_o.start(r.in_o)
    local_o = lcopy(r.in_o, zg_o.block(z))
    base_small = slots(PL)
    for i in range(1, PL):
        copy = rcopy(r.in_small, r.small.at[z * PL + q], base_small + i, base_small + i, mate(i))
        copy.start()
        drains.append(copy.wait_send)
    local_small = lcopy(r.in_small, r.small.at[z * PL + q])
    def stage_qkv(v):
        lcopy(r.in_qkv, v).wait()
        for other in range(PL):
            for j in range(3):
                for zh in range(R):
                    at = j * D + zh * PL * HD + other * HD
                    r.st_qkv[other, :, j * QW + zh * HD : j * QW + (zh + 1) * HD] = v[:, at : at + HD]

    pl.run_scoped(stage_qkv, VM(r.in_qkv.shape, BF))
    sp_qkv.start(mine_rows(r.w_qkv, shard))
    local_qkv = lcopy(r.st_qkv.at[q], mine_rows(r.w_qkv, shard))
    local_f = [None] * len(PARTS)

    def stage_f(*bufs):
        loads = [lcopy(source, buf) for source, buf in zip((r.in_gate, r.in_up, r.in_down), bufs)]
        for load in loads:
            load.wait()
        for p, width in enumerate(PARTS):
            for other in range(PL):
                at = other * FW + STARTS[p]
                for k, source in enumerate(bufs):
                    st_f[p][other, :, k * width : (k + 1) * width] = source[:, at : at + width]
                if WC[p] > 3 * width:
                    st_f[p][other, :, 3 * width :] = jnp.zeros((shard, WC[p] - 3 * width), BF)

    def spread_f(p):
        sp_f[p].start(mine_rows(w_f[p], shard))
        local_f[p] = lcopy(st_f[p].at[q], mine_rows(w_f[p], shard))

    def arrived(spread, whole):
        spread.wait(lambda s: whole.at[pl.ds(aligned((z * PL + s) * shard, 16), shard)])

    pl.run_scoped(stage_f, *[VM(r.in_gate.shape, BF)] * 3)
    spread_f(0)

    local_small.wait()
    for i in range(1, PL):
        rcopy(r.in_small, r.small.at[z * PL + lax.rem(q - i + PL, PL)], base_small, base_small + i, mate(i)).wait_recv()
    base_smallz = slots(R)
    plane_small = r.small.at[pl.ds(z * PL, PL)]
    for i in range(1, R):
        copy = rcopy(plane_small, plane_small, base_smallz + i, base_smallz + i, plane_dev(lax.rem(z + i, R)))
        copy.start()
        drains.append(copy.wait_send)
    loads["tokens"].wait()
    loads["cot"].wait()
    tokens = r.v_tokens[...].astype(F32)
    unit, _ = norm_stats(tokens)
    for i in range(1, R):
        block = r.small.at[pl.ds(lax.rem(z - i + R, R) * PL, PL)]
        rcopy(block, block, base_smallz, base_smallz + i, sibling).wait_recv()
    for d in range(R * PL):
        for k in range(4):
            r.vec[k : k + 1, shard * d : shard * (d + 1)] = r.small[d, k : k + 1, 0:shard]
        for k in range(3):
            r.biases[3 * d + k : 3 * d + k + 1, 0:HD] = r.small[d, 4 + k : 5 + k, 0:HD]
    for j in range(3):
        for zh in range(R):
            row = r.biases[pl.ds(j * H + zh * PL + q, 1), 0:HD]
            r.bias[0:1, j * QW + zh * HD : j * QW + (zh + 1) * HD] = row
    r.x_normed[...] = (unit * r.vec[0:1, :] + r.vec[1:2, :]).astype(BF)
    ag_normed.start(r.x_normed)

    spread_f(1)
    ag_cot.start(r.v_cot)
    local_qkv.wait()
    arrived(sp_qkv, r.w_qkv)
    zg_qkv.start()
    local_f[0].wait()
    arrived(sp_f[0], w_f[0])
    zg_qkv.relay(0)
    zg_qkv.relay(1)
    zg_o.relay()
    zg_f[0].start()
    ag_normed.relay()
    ag_normed.wait()
    zg_qkv.wait()

    def lower(shape):
        return lax.rem(lax.broadcasted_iota(jnp.int32, shape, 1), HD) < ROT // 2

    def in_turn(shape):
        return lax.rem(lax.broadcasted_iota(jnp.int32, shape, 1), HD) < ROT

    TM = HS // 2
    local_tables.wait()

    @pl.loop(0, TOK // HS)
    def _(i):
        span = pl.ds(aligned(i * HS, HS), HS)
        projected = nn(r.a_normed[span, :], r.w_qkv[...]) + r.bias[0:1, :]
        for piece in range(2 * QW // 128):
            part = projected[:, piece * 128 : (piece + 1) * 128]
            other = jnp.where(lower(part.shape), pltpu.roll(part, 128 - ROT // 2, 1), pltpu.roll(part, ROT // 2, 1))
            turned = part * r.turns[0] + other * r.turns[1]
            r.qkv[span, piece * 128 : (piece + 1) * 128] = turned.astype(BF)
        r.qkv[span, 2 * QW :] = projected[:, 2 * QW :].astype(BF)

    heads = QW // HD

    def softmax_block(queries, keys, first):
        scores = nt(keys, queries) * 0.125
        at_key = lax.broadcasted_iota(jnp.int32, scores.shape, 0)
        at_query = lax.broadcasted_iota(jnp.int32, scores.shape, 1) + first
        allowed = at_key <= at_query
        scores = jnp.where(allowed, scores, -1e30)
        largest = jnp.max(scores, axis=0, keepdims=True)
        weights = jnp.where(allowed, jnp.exp(scores - largest), 0.0)
        return weights / jnp.sum(weights, axis=0, keepdims=True)

    QB = HS // 2

    @pl.loop(0, TOK // HS)
    def _(i):
        first = i * HS
        for h in range(heads):
            at = h * HD
            for blk in range(HS // QB):
                here = pl.ds(aligned(first + blk * QB, 16), QB)
                seen = pl.ds(aligned(first, 16), (blk + 1) * QB)
                probs = softmax_block(r.qkv[here, at : at + HD], r.qkv[seen, QW + at : QW + at + HD], blk * QB)
                out = tn(probs.astype(BF), r.qkv[seen, 2 * QW + at : 2 * QW + at + HD])
                r.att[here, at : at + HD] = out.astype(BF)

    local_f[1].wait()
    arrived(sp_f[1], w_f[1])
    ag_cot.relay()
    local_o.wait()
    zg_o.wait()

    red_att = Reduce(0)
    red_att.run([(r.att, r.w_o)], lambda x, w: nn(x, w[...]))
    zg_f[0].relay()
    zg_f[1].start()
    ag_cot.wait()
    middle = r.v_tokens[...].astype(F32) + red_att.finish()
    r.middle[...] = middle
    unit, _ = norm_stats(middle)
    r.x_two[...] = (unit * r.vec[2:3, :] + r.vec[3:4, :]).astype(BF)
    ag_two.start(r.x_two)

    hid, gug, g_f = [r.hid0, r.hid1], [r.gug0, r.gug1], [r.g_f0, r.g_f1]

    def feed_forward(p, then=None):
        width = PARTS[p]
        def body(w, *others):
            loads = []
            for load_in, buf in zip(earlier, others):
                loads.append(lcopy(load_in, buf))
            for s in range(R):
                zg_f[p].wait_block(s)
                loads.append(lcopy(zg_f[p].block(s), w.at[pl.ds(s * KB, KB)]))
            for load in loads:
                load.wait()

            def use(span):
                both = nn(r.a_two[span, :], w[:, : 2 * width])
                gate = both[:, :width]
                up = both[:, width:]
                sig = 1.0 / (1.0 + jnp.exp(-gate))
                swish = gate * sig
                hid[p][span, :] = (swish * up).astype(BF)
                hidden_grad = nn(r.a_cot[span, :], w[:, 2 * width : 3 * width])
                gug[p][span, :width] = (hidden_grad * up * sig * (1.0 + gate * (1.0 - sig))).astype(BF)
                gug[p][span, width:] = (hidden_grad * swish).astype(BF)

            if p == 0:
                ag_two.each(lambda s: use(pl.ds(aligned(s * rows, 16), rows)))
            else:

                @pl.loop(0, TOK // TM)
                def _(i):
                    use(pl.ds(aligned(i * TM, TM), TM))

            if then is not None:
                then(w, *others)

        earlier = [w_f[k].at[:, pl.ds(0, 2 * PARTS[k])] for k in range(p)]
        pl.run_scoped(body, VM(w_f[p].shape, BF), *[VM(ref.shape, BF) for ref in earlier])

    def grads_by_owner(terms, out, reduce, padded=None, steps=range(R)):
        width = out.shape[1]

        def body(tile, sem):
            pending = []

            def hand_on():
                store, step = pending.pop(0)
                store.wait()
                reduce.start_step(step)

            for step in steps:
                owner = R - 1 - step
                for at in range(1, R):
                    owner = jnp.where(z == at, ORDER[at][step], owner)
                for left, right, first in terms:
                    part = tn(left[:, pl.ds(aligned(owner * KB, KB), KB)], right[...])
                    tile[step % depth, :, first : first + right.shape[1]] = part.astype(BF)
                if padded is not None:
                    tile[step % depth, :, padded:] = jnp.zeros((KB, width - padded), BF)
                store = pltpu.make_async_copy(tile.at[step % depth], reduce.block(owner), sem.at[step % depth])
                store.start()
                pending.append((store, step))
                while len(pending) > (0 if step in (0, steps[-1]) else 1):
                    hand_on()

        depth = min(2, len(steps))
        pl.run_scoped(body, VM((depth, KB, width), BF), pltpu.SemaphoreType.DMA((depth,)))

    def feed_weight_grads(p, steps=range(R)):
        width = PARTS[p]
        terms = [(r.a_two, gug[p], 0), (r.a_cot, hid[p], 2 * width)]
        grads_by_owner(terms, g_f[p], zr_f[p], 3 * width if WC[p] > 3 * width else None, steps)

    zr_f = [ZReduce(r.g_f0, r.zin_f0, r.zx_f0, r.zs_f0, KB), ZReduce(r.g_f1, r.zin_f1, r.zx_f1, r.zs_f1, KB)]
    zr_o = ZReduce(r.g_o, r.zin_o, r.zx_o, r.zs_o, shard)
    zr_qkv = ZReduce(r.g_qkv, r.zin_qkv, r.zx_qkv, r.zs_qkv, KB)

    feed_forward(0)
    zg_f[1].relay()
    feed_weight_grads(0)
    red_two = Reduce(0, red_att)

    def back_into_layer(w_last, w_first):
        feed_weight_grads(1, (0,))
        weights = (w_first, w_last.at[:, pl.ds(0, 2 * PARTS[1])])
        red_two.run(list(zip(gug, weights)), lambda x, w: nt(x, w[...]))

    feed_forward(1, back_into_layer)
    feed_weight_grads(1, (1, 2, 3))
    zr_f[0].merge()
    two_grad = red_two.finish()
    unit, scale = norm_stats(r.middle[...])
    middle_grad = r.v_cot[...].astype(F32) + norm_back(two_grad, unit, scale, r.vec[2:3, :])
    r.middle_grad[...] = middle_grad
    ag_normed.drain()
    r.x_normed[...] = middle_grad.astype(BF)
    ag_one.start(r.x_normed)
    r.vec[6:7, :] = jnp.sum(two_grad * unit, axis=0, keepdims=True)
    r.vec[7:8, :] = jnp.sum(two_grad, axis=0, keepdims=True)

    red_mixed = Reduce(1)
    mixed_pairs = [(hid[p], (w_f[p].at[:, pl.ds(2 * PARTS[p], WC[p] - 2 * PARTS[p])],)) for p in parts]
    red_mixed.run(mixed_pairs, lambda x, w: nt(x, w[:, : x.shape[1]]), later=True)

    def att_grad(s):
        span = pl.ds(aligned(s * rows, 16), rows)
        pltpu.sync_copy(ag_one.block(s), r.a_two.at[span])
        r.a_cot[span, 0:QW] = nt(r.a_two[span, :], r.w_o[...]).astype(BF)

    ag_two.drain()
    ag_cot.drain()
    ag_one.each(att_grad)
    red_mixed.pass_on()
    def o_grad(buf):
        for k in range(R):
            span = pl.ds(k * KB, KB)
            buf[:, span] = tn(r.att[...], r.a_two[:, span]).astype(BF)
        pltpu.sync_copy(buf, r.g_o)

    pl.run_scoped(o_grad, VM((QW, D), BF))
    zr_o.start()
    zr_f[1].merge((0,))

    def attention_back(turn):
        @pl.loop(0, TOK // HS)
        def _(i):
            first = i * HS
            for h in range(heads):
                at = h * HD
                key_grad = [jnp.zeros((QB, HD), F32) for _ in range(HS // QB)]
                value_grad = [jnp.zeros((QB, HD), F32) for _ in range(HS // QB)]
                for blk in range(HS // QB):
                    here = pl.ds(aligned(first + blk * QB, 16), QB)
                    seen = pl.ds(aligned(first, 16), (blk + 1) * QB)
                    queries = r.qkv[here, at : at + HD]
                    keys = r.qkv[seen, QW + at : QW + at + HD]
                    values = r.qkv[seen, 2 * QW + at : 2 * QW + at + HD]
                    grads = r.a_cot[here, at : at + HD]
                    probs = softmax_block(queries, keys, blk * QB)
                    prob_grad = nt(values, grads)
                    delta = jnp.sum(probs * prob_grad, axis=0, keepdims=True)
                    score_grad = (probs * (prob_grad - delta)).astype(BF)
                    low_probs = probs.astype(BF)
                    turn[blk * QB : (blk + 1) * QB, at : at + HD] = tn(score_grad, keys) * 0.125
                    key_part = nn(score_grad, queries) * 0.125
                    value_part = nn(low_probs, grads)
                    for k in range(blk + 1):
                        key_grad[k] = key_grad[k] + key_part[k * QB : (k + 1) * QB]
                        value_grad[k] = value_grad[k] + value_part[k * QB : (k + 1) * QB]
                for k in range(HS // QB):
                    turn[k * QB : (k + 1) * QB, QW + at : QW + at + HD] = key_grad[k]
                    r.qkv[pl.ds(aligned(first + k * QB, 16), QB), 2 * QW + at : 2 * QW + at + HD] = value_grad[k].astype(BF)
            for piece in range(2 * QW // 128):
                part = turn[:, piece * 128 : (piece + 1) * 128]
                cross = part * r.turns[1]
                other = jnp.where(lower(part.shape), pltpu.roll(cross, 128 - ROT // 2, 1), pltpu.roll(cross, ROT // 2, 1))
                back = part * r.turns[0] + jnp.where(in_turn(part.shape), other, 0.0)
                r.qkv[pl.ds(aligned(first, 16), HS), piece * 128 : (piece + 1) * 128] = back.astype(BF)

    pl.run_scoped(attention_back, VM((HS, 2 * QW), F32))
    grads_by_owner([(r.a_normed, r.qkv, 0)], r.g_qkv, zr_qkv)
    zr_f[1].merge((1,))
    red_one = Reduce(0, red_two)
    red_one.run([(r.qkv, r.w_qkv)], lambda x, w: nt(x, w[...]))
    r.bias[0:1, :] = jnp.sum(r.qkv[...].astype(F32), axis=0, keepdims=True)

    zr_o.merge()
    back_f, back_qkv = [Spread(st) for st in st_f], Spread(r.st_qkv)
    pin_f = [r.pin_f0, r.pin_f1]

    def z_sum(reduce, sent, stage, spread, got):
        sent.wait_send()

        def put(k, total):
            stage[k] = total.astype(BF)

        reduce.finish(put)
        spread.start(got.at[q])
        return lcopy(stage.at[q], got.at[q])

    def pin_block(got):
        return lambda s: got.at[s]

    local_f[0] = z_sum(zr_f[0], sp_f[0], st_f[0], back_f[0], pin_f[0])
    zr_qkv.merge((0,))
    mixed = r.middle[...] + red_mixed.finish()
    r.x_two[...] = mixed.astype(BF)
    outputs = [lcopy(r.x_two, r.out_mixed)]
    zr_qkv.merge((1,))
    local_f[1] = z_sum(zr_f[1], sp_f[1], st_f[1], back_f[1], pin_f[1])
    one_grad = red_one.finish()
    unit, scale = norm_stats(r.v_tokens[...].astype(F32))
    r.middle_grad[...] = r.middle_grad[...] + norm_back(one_grad, unit, scale, r.vec[0:1, :])
    outputs.append(lcopy(r.middle_grad, r.out_tokens))
    r.vec[4:5, :] = jnp.sum(one_grad * unit, axis=0, keepdims=True)
    r.vec[5:6, :] = jnp.sum(one_grad, axis=0, keepdims=True)
    r.sg[...] = jnp.zeros_like(r.sg)
    for d in range(R * PL):
        for k in range(4):
            r.sg[d % PL, d // PL, k : k + 1, 0:shard] = r.vec[4 + k : 5 + k, shard * d : shard * (d + 1)]
    for j in range(3):
        for zh in range(R):
            g = j * H + zh * PL + q
            piece = r.bias[0:1, j * QW + zh * HD : j * QW + (zh + 1) * HD]
            r.sg[lax.rem(g // 3, PL), g // (3 * PL), pl.ds(4 + lax.rem(g, 3), 1), 0:HD] = piece
    base_sgp = slots(PL)
    for i in range(1, PL):
        other = lax.rem(q + i, PL)
        copy = rcopy(r.sg.at[other], r.sgp.at[i - 1], base_sgp + i, base_sgp + i, mate(i))
        copy.start()
        drains.append(copy.wait_send)
    zr_o.wait()
    outputs.append(lcopy(zr_o.block(z), r.own_o))
    local_f[0].wait()
    back_f[0].wait(pin_block(pin_f[0]))
    total = r.sg[q]
    for i in range(1, PL):
        rcopy(r.sgp.at[i - 1], r.sgp.at[i - 1], base_sgp, base_sgp + i, sibling).wait_recv()
        total = total + r.sgp[i - 1]
    r.sgs[...] = total
    base_sgz = slots(R)
    for i in range(1, R):
        t = lax.rem(z + i, R)
        copy = rcopy(r.sgs.at[t], r.sgz.at[i - 1], base_sgz + i, base_sgz + i, plane_dev(t))
        copy.start()
        drains.append(copy.wait_send)
    local_qkv = z_sum(zr_qkv, sp_qkv, r.st_qkv, back_qkv, r.pin_qkv)
    for i in range(1, R):
        rcopy(r.sgz.at[i - 1], r.sgz.at[i - 1], base_sgz, base_sgz + i, sibling).wait_recv()
    r.sgt[...] = r.sgs[z] + r.sgz[0] + r.sgz[1] + r.sgz[2]
    outputs.append(lcopy(r.sgt, r.out_small))
    local_f[1].wait()
    back_f[1].wait(pin_block(pin_f[1]))
    local_qkv.wait()
    back_qkv.wait(pin_block(r.pin_qkv))
    for copy in outputs:
        copy.wait()
    for spread in back_f:
        spread.wait_send()
    back_qkv.wait_send()
    ag_one.drain()
    red_mixed.drain()
    red_one.drain()
    for drain in drains:
        drain()
    assert counter[0] <= REMOTE_SEMS and local_count[0] <= LOCAL_SEMS, (counter, local_count)


def finish_outputs(got, parts, starts, planes, members, rows, shard, q_width, f_width):
    steps = 4
    tall, low = rows // steps, shard // steps

    def body(mixed_in, tokens_in, small_in, pin_qkv, own_o, zin_o, pin_f0, pin_f1, mixed, tokens, gains, bias, qkv, o, gate, up, down):
        mixed[0] = mixed_in[...]
        tokens[0] = tokens_in[...]
        o[...] = own_o[...].astype(F32) + zin_o[0].astype(F32) + zin_o[1].astype(F32)
        for k in range(4):
            gains[0:1, k * shard : (k + 1) * shard] = small_in[k : k + 1, 0:shard]
        for k in range(3):
            bias[0:1, k * HD : (k + 1) * HD] = small_in[4 + k : 5 + k, 0:HD]
        for other in range(members):
            for j in range(3):
                for zh in range(planes):
                    at = j * D + zh * members * HD + other * HD
                    qkv[:, at : at + HD] = pin_qkv[other, :, j * q_width + zh * HD : j * q_width + (zh + 1) * HD].astype(F32)
            for pin, width, start in zip((pin_f0, pin_f1), parts, starts):
                at = other * f_width + start
                for k, target in enumerate((gate, up, down)):
                    target[:, at : at + width] = pin[other, :, k * width : (k + 1) * width].astype(F32)

    def tiles(shape, axis, size):
        block = tuple(size if k == axis else n for k, n in enumerate(shape))
        return pl.BlockSpec(block, lambda i: tuple(i if k == axis else 0 for k in range(len(shape))))

    ins = [
        (got["out_mixed"], 0, tall), (got["out_tokens"], 0, tall), (got["out_small"], None, 0), (got["pin_qkv"], 1, low),
        (got["own_o"], 0, low), (got["zin_o"], 1, low), (got["pin_f0"], 1, low), (got["pin_f1"], 1, low),
    ]
    outs = dict(
        mixed=((1, rows, D), BF, 1, tall), tokens=((1, rows, D), F32, 1, tall),
        gains=((1, 4 * shard), F32, None, 0), bias=((1, 3 * HD), F32, None, 0),
        qkv=((shard, 3 * D), F32, 0, low), o=((shard, D), F32, 0, low),
        gate=((shard, FF), F32, 0, low), up=((shard, FF), F32, 0, low), down=((shard, FF), F32, 0, low),
    )
    results = pl.pallas_call(
        body,
        grid=(steps,),
        out_shape=[jax.ShapeDtypeStruct(shape, kind) for shape, kind, _, _ in outs.values()],
        in_specs=[tiles(array.shape, axis, size) for array, axis, size in ins],
        out_specs=[tiles(shape, axis, size) for shape, _, axis, size in outs.values()],
        name="finish",
    )(*[array for array, _, _ in ins])
    return dict(zip(outs, results))


def fast_local(tokens, out_grad, ln1_gain, ln1_shift, qkv_weight, qkv_bias, out_weight, ln2_gain, ln2_shift, gate_weight, up_weight, down_weight):
    planes, columns = lax.axis_size("batch") // 2, lax.axis_size("ctx")
    members = 2 * columns
    rows = tokens.shape[1]
    seq = rows * columns
    total = members * rows
    shard = qkv_weight.shape[0]
    q_width = D // members
    f_width = FF // members
    plane_rows = members * shard
    parts = (384, f_width - 384)
    dims = (planes, columns, members, rows, shard, q_width, f_width, parts)
    pieces = jnp.concatenate(
        [jnp.stack([ln1_gain, ln1_shift, ln2_gain, ln2_shift]), qkv_bias.reshape(3, HD)], axis=0
    ).astype(F32)
    small = jnp.pad(pieces, ((0, 1), (0, 128 - HD)))
    inputs = dict(
        in_tokens=(tokens.reshape(rows, D), ANY),
        in_cot=(out_grad.reshape(rows, D), ANY),
        in_small=(small, VM),
        in_qkv=(qkv_weight, ANY),
        in_o=(out_weight, ANY),
        in_gate=(gate_weight, ANY),
        in_up=(up_weight, ANY),
        in_down=(down_weight, ANY),
        tables=(jnp.asarray(turn_tables(seq)), ANY),
    )
    columns_f = [feed_columns(width) for width in parts]
    outs = dict(
        out_mixed=((rows, D), BF, ANY),
        out_tokens=((rows, D), F32, ANY),
        out_small=((8, 128), F32, ANY),
        pin_qkv=((members, shard, 3 * q_width), BF, ANY),
        own_o=((shard, D), BF, ANY),
        zin_o=((2, shard, D), BF, ANY),
    )
    for p, width in enumerate(columns_f):
        outs[f"pin_f{p}"] = ((members, shard, width), BF, ANY)
    final = list(outs)
    spaces = dict(
        a_one=(total, D),
        g_qkv=(D, 3 * q_width), g_o=(q_width, D),
        zin_qkv=(2, plane_rows, 3 * q_width),
        zx_qkv=(2, plane_rows, 3 * q_width), zx_o=(2, shard, D),
        zs_qkv=(2, plane_rows, 3 * q_width), zs_o=(2, shard, D),
    )
    for p, width in enumerate(columns_f):
        spaces[f"w_f{p}"] = spaces[f"g_f{p}"] = (D, width)
        for kind in ("zin", "zx", "zs"):
            spaces[f"{kind}_f{p}"] = (2, plane_rows, width)
    for name, shape in spaces.items():
        outs[name] = (shape, BF, ANY)
    scratch = dict(
        v_tokens=VM((rows, D), BF), v_cot=VM((rows, D), BF),
        turns=VM((2, seq, 128), F32),
        a_normed=VM((total, D), BF), a_two=VM((total, D), BF), a_cot=VM((total, D), BF),
        w_qkv=VM((D, 3 * q_width), BF), w_o=VM((q_width, D), BF),
        qkv=VM((total, 3 * q_width), BF), att=VM((total, q_width), BF),
        st_qkv=VM((members, shard, 3 * q_width), BF),
        small=VM((planes * members, 8, 128), F32), sg=VM((members, planes, 8, 128), F32),
        sgz=VM((planes - 1, 8, 128), F32), sgs=VM((planes, 8, 128), F32), sgp=VM((members - 1, planes, 8, 128), F32), sgt=VM((8, 128), F32),
        vec=VM((8, D), F32), biases=VM((3 * H, 128), F32), bias=VM((8, 3 * q_width), F32),
        x_normed=VM((rows, D), BF), x_two=VM((rows, D), BF),
        middle=VM((rows, D), F32), middle_grad=VM((rows, D), F32),
        mine=VM((seq, D), BF),
    )
    for p, width in enumerate(parts):
        scratch[f"st_f{p}"] = VM((members, shard, columns_f[p]), BF)
        scratch[f"hid{p}"], scratch[f"gug{p}"] = VM((total, width), BF), VM((total, 2 * width), BF)
    for k in range(2):
        scratch[f"sibout{k}"] = VM((seq, D), BF)
        scratch[f"theirs{k}"] = VM((seq, D), BF)
        scratch[f"redout{k}"] = VM((columns - 1, rows, D), BF)
        scratch[f"redin{k}"] = VM((columns - 1, rows, D), BF)
        scratch[f"redown{k}"] = VM((rows, D), F32 if k == 0 else BF)
    scratch["ss"] = pltpu.SemaphoreType.DMA((REMOTE_SEMS,))
    scratch["rs"] = pltpu.SemaphoreType.DMA((REMOTE_SEMS,))
    scratch["ls"] = pltpu.SemaphoreType.DMA((LOCAL_SEMS,))
    results = pl.pallas_call(
        functools.partial(layer_kernel, dims, list(inputs), list(outs), list(scratch)),
        out_shape=[jax.ShapeDtypeStruct(shape, kind) for shape, kind, _ in outs.values()],
        in_specs=[pl.BlockSpec(memory_space=place) for _, place in inputs.values()],
        out_specs=[pl.BlockSpec(memory_space=place) for _, _, place in outs.values()],
        scratch_shapes=list(scratch.values()),
        compiler_params=pltpu.CompilerParams(collective_id=0, has_side_effects=True, vmem_limit_bytes=63 * 2**20),
        cost_estimate=pl.CostEstimate(flops=42 * 10**9, bytes_accessed=300 * 10**6, transcendentals=0),
        name="layer",
    )(*[array for array, _ in inputs.values()])
    got = dict(zip(final, results))
    f_starts = [sum(parts[:p]) for p in range(len(parts))]
    done = finish_outputs(got, parts, f_starts, planes, members, rows, shard, q_width, f_width)
    return (
        done["mixed"],
        done["tokens"],
        done["gains"].reshape(4, shard)[0],
        done["gains"].reshape(4, shard)[1],
        done["qkv"],
        done["bias"].reshape(3 * HD),
        done["o"],
        done["gains"].reshape(4, shard)[2],
        done["gains"].reshape(4, shard)[3],
        done["gate"],
        done["up"],
        done["down"],
    )


def fits(mesh):
    return mesh.shape["batch"] == 8 and mesh.shape["ctx"] == 4


def solution(mesh):
    in_specs = (
        P("batch", "ctx", None),
        P("batch", "ctx", None),
        P(("batch", "ctx")),
        P(("batch", "ctx")),
        P(("batch", "ctx"), None),
        P(("batch", "ctx")),
        P(("batch", "ctx"), None),
        P(("batch", "ctx")),
        P(("batch", "ctx")),
        P(("batch", "ctx"), None),
        P(("batch", "ctx"), None),
        P(("batch", "ctx"), None),
    )
    out_specs = (
        P("batch", "ctx", None),
        P("batch", "ctx", None),
        P(("batch", "ctx")),
        P(("batch", "ctx")),
        P(("batch", "ctx"), None),
        P(("batch", "ctx")),
        P(("batch", "ctx"), None),
        P(("batch", "ctx")),
        P(("batch", "ctx")),
        P(("batch", "ctx"), None),
        P(("batch", "ctx"), None),
        P(("batch", "ctx"), None),
    )
    body = fast_local if fits(mesh) else local
    return jax.shard_map(body, mesh=mesh, in_specs=in_specs, out_specs=out_specs, check_vma=False)
```

```python
import functools

import jax
import jax.numpy as jnp
import numpy as np
from jax import lax
from jax.experimental import pallas as pl
from jax.experimental.pallas import tpu as pltpu
from jax.sharding import PartitionSpec as P

D = 2048
FF = 5632
H = 32
HD = 64
ROT = 16


def layer_norm(values, gain, shift):
    centre = jnp.mean(values, axis=-1, keepdims=True)
    centred = values - centre
    spread = jnp.mean(centred * centred, axis=-1, keepdims=True)
    return centred * lax.rsqrt(spread + 1e-05) * gain + shift


def rotary(values, positions):
    half_dims = ROT // 2
    frequency = 10000.0 ** (-jnp.arange(half_dims, dtype=jnp.float32) * 2.0 / ROT)
    angles = positions.astype(jnp.float32)[:, None] * frequency[None, :]
    cosine_term = jnp.cos(angles)[:, None, :]
    sine_term = jnp.sin(angles)[:, None, :]
    first_half = values[..., :half_dims]
    second_half = values[..., half_dims:ROT]
    return jnp.concatenate(
        [
            first_half * cosine_term - second_half * sine_term,
            second_half * cosine_term + first_half * sine_term,
            values[..., ROT:],
        ],
        axis=-1,
    )


def swish_product(gate_value, up_value):
    return gate_value / (1.0 + jnp.exp(-gate_value)) * up_value


def project_back(left, right):
    return lax.dot_general(
        left, right, (((1,), (1,)), ((), ())), preferred_element_type=jnp.float32
    )


def outer_rows(left, right):
    return lax.dot_general(
        left, right, (((0,), (0,)), ((), ())), preferred_element_type=jnp.float32
    )


def local(
    tokens,
    out_grad,
    ln1_gain,
    ln1_shift,
    qkv_weight,
    qkv_bias,
    out_weight,
    ln2_gain,
    ln2_shift,
    gate_weight,
    up_weight,
    down_weight,
):
    local_rows = tokens.shape[1]
    seq_length = local_rows * lax.axis_size("ctx")
    inputs = tokens.reshape(local_rows, D).astype(jnp.float32)
    cotangent = out_grad.reshape(local_rows, D).astype(jnp.float32)
    places = lax.axis_index("ctx") * local_rows + jnp.arange(local_rows, dtype=jnp.int32)
    attn_set = (
        lax.all_gather(qkv_weight, ("batch", "ctx"), axis=0, tiled=True),
        lax.all_gather(out_weight, ("batch", "ctx"), axis=0, tiled=True),
        lax.all_gather(qkv_bias, ("batch", "ctx"), axis=0, tiled=True),
        lax.all_gather(ln1_gain, ("batch", "ctx"), axis=0, tiled=True),
        lax.all_gather(ln1_shift, ("batch", "ctx"), axis=0, tiled=True),
    )
    gain_one = attn_set[3].astype(jnp.float32)
    shift_one = attn_set[4].astype(jnp.float32)
    normed = layer_norm(inputs, gain_one, shift_one)
    normed_low = normed.astype(jnp.bfloat16)
    projected = jnp.dot(normed_low, attn_set[0], preferred_element_type=jnp.float32) + attn_set[
        2
    ].astype(jnp.float32)
    pair_heads = projected[:, : 2 * D].reshape(local_rows, 2 * H, HD)
    turned = rotary(pair_heads, places)
    queries = turned[:, :H].astype(jnp.bfloat16)
    key_rows = turned[:, H:].reshape(local_rows, D).astype(jnp.bfloat16)
    value_rows = projected[:, 2 * D :].astype(jnp.bfloat16)
    start_state = (
        jnp.full((H, local_rows), -1e30, jnp.float32),
        jnp.zeros((H, local_rows), jnp.float32),
        jnp.zeros((H, local_rows, HD), jnp.float32),
    )
    carry = start_state
    key_piece = lax.all_gather(key_rows, "ctx", axis=0, tiled=True)
    value_piece = lax.all_gather(value_rows, "ctx", axis=0, tiled=True)
    piece_rows = key_piece.shape[0]
    block_rows = 512
    block_count = piece_rows // block_rows

    def inner(state, block):
        largest, totals, accum = state
        key_block, value_block, offset = block
        raw_scores = (
            jnp.einsum("qhd,khd->hqk", queries, key_block, preferred_element_type=jnp.float32)
            * 0.125
        )
        key_places = offset + jnp.arange(block_rows, dtype=jnp.int32)
        allowed = (key_places[None, :] <= places[:, None])[None]
        raw_scores = jnp.where(allowed, raw_scores, -1e30)
        new_largest = jnp.maximum(largest, jnp.max(raw_scores, axis=-1))
        weights = jnp.where(allowed, jnp.exp(raw_scores - new_largest[..., None]), 0.0)
        factor = jnp.exp(largest - new_largest)
        totals = totals * factor + jnp.sum(weights, axis=-1)
        accum = accum * factor[..., None] + jnp.einsum(
            "hqk,khd->hqd",
            weights.astype(jnp.bfloat16),
            value_block,
            preferred_element_type=jnp.float32,
        )
        return ((new_largest, totals, accum), None)

    offsets = jnp.arange(block_count, dtype=jnp.int32) * block_rows
    blocks = (
        key_piece.reshape(block_count, block_rows, H, HD),
        value_piece.reshape(block_count, block_rows, H, HD),
        offsets,
    )
    carry, unused = lax.scan(inner, carry, blocks)
    largest, totals, accum = carry
    attended = jnp.transpose(accum / totals[..., None], (1, 0, 2)).reshape(local_rows, D)
    log_total = largest + jnp.log(totals)
    attended_low = attended.astype(jnp.bfloat16)
    middle = inputs + jnp.dot(attended_low, attn_set[1], preferred_element_type=jnp.float32)
    mlp_set = (
        lax.all_gather(gate_weight, ("batch", "ctx"), axis=0, tiled=True),
        lax.all_gather(up_weight, ("batch", "ctx"), axis=0, tiled=True),
        lax.all_gather(down_weight, ("batch", "ctx"), axis=0, tiled=True),
        lax.all_gather(ln2_gain, ("batch", "ctx"), axis=0, tiled=True),
        lax.all_gather(ln2_shift, ("batch", "ctx"), axis=0, tiled=True),
    )
    gain_two = mlp_set[3].astype(jnp.float32)
    shift_two = mlp_set[4].astype(jnp.float32)
    normed_two_low = layer_norm(middle, gain_two, shift_two).astype(jnp.bfloat16)
    gate_value = jnp.dot(normed_two_low, mlp_set[0], preferred_element_type=jnp.float32)
    up_value = jnp.dot(normed_two_low, mlp_set[1], preferred_element_type=jnp.float32)
    hidden_low = swish_product(gate_value, up_value).astype(jnp.bfloat16)
    mixed = (middle + project_back(hidden_low, mlp_set[2])).astype(jnp.bfloat16)
    mlp_back = (
        lax.all_gather(gate_weight, ("batch", "ctx"), axis=0, tiled=True),
        lax.all_gather(up_weight, ("batch", "ctx"), axis=0, tiled=True),
        lax.all_gather(down_weight, ("batch", "ctx"), axis=0, tiled=True),
        lax.all_gather(ln2_gain, ("batch", "ctx"), axis=0, tiled=True),
        lax.all_gather(ln2_shift, ("batch", "ctx"), axis=0, tiled=True),
    )
    attn_back = (
        lax.all_gather(qkv_weight, ("batch", "ctx"), axis=0, tiled=True),
        lax.all_gather(out_weight, ("batch", "ctx"), axis=0, tiled=True),
        lax.all_gather(qkv_bias, ("batch", "ctx"), axis=0, tiled=True),
        lax.all_gather(ln1_gain, ("batch", "ctx"), axis=0, tiled=True),
        lax.all_gather(ln1_shift, ("batch", "ctx"), axis=0, tiled=True),
    )
    branch_two = cotangent.astype(jnp.bfloat16)
    hidden_grad = jnp.dot(branch_two, mlp_back[2], preferred_element_type=jnp.float32)
    unused_value, act_pull = jax.vjp(swish_product, gate_value, up_value)
    gate_grad, up_grad = act_pull(hidden_grad)
    gate_low = gate_grad.astype(jnp.bfloat16)
    up_low = up_grad.astype(jnp.bfloat16)
    normed_two_grad = project_back(gate_low, mlp_back[0]) + project_back(up_low, mlp_back[1])
    unused_two, norm_pull_two = jax.vjp(layer_norm, middle, gain_two, shift_two)
    middle_part, gain_two_grad, shift_two_grad = norm_pull_two(normed_two_grad)
    middle_grad = cotangent + middle_part
    gate_weight_grad, up_weight_grad, down_weight_grad = (
        lax.psum_scatter(
            outer_rows(left, right).astype(jnp.bfloat16), ("batch", "ctx"), scatter_dimension=0, tiled=True
        ).astype(jnp.float32)
        for left, right in ((normed_two_low, gate_low), (normed_two_low, up_low), (branch_two, hidden_low))
    )
    branch_one = middle_grad.astype(jnp.bfloat16)
    out_term = outer_rows(attended_low, branch_one)
    attended_grad = project_back(branch_one, attn_back[1]).astype(jnp.bfloat16)
    grad_heads = attended_grad.reshape(local_rows, H, HD)
    delta = jnp.transpose(
        jnp.sum((attended_grad.astype(jnp.float32) * attended).reshape(local_rows, H, HD), axis=-1)
    )
    key_all, value_all = (
        lax.all_gather(key_rows, "ctx", axis=0, tiled=True),
        lax.all_gather(value_rows, "ctx", axis=0, tiled=True),
    )
    back_rows = 512
    back_count = seq_length // back_rows

    def back_block(query_grad, block):
        key_block, value_block, offset = block
        raw_scores = (
            jnp.einsum("qhd,khd->hqk", queries, key_block, preferred_element_type=jnp.float32)
            * 0.125
        )
        key_places = offset + jnp.arange(back_rows, dtype=jnp.int32)
        allowed = (key_places[None, :] <= places[:, None])[None]
        probs = jnp.where(allowed, jnp.exp(raw_scores - log_total[..., None]), 0.0)
        prob_grad = jnp.einsum(
            "qhd,khd->hqk", grad_heads, value_block, preferred_element_type=jnp.float32
        )
        score_grad = (probs * (prob_grad - delta[..., None])).astype(jnp.bfloat16)
        query_grad = (
            query_grad
            + jnp.einsum("hqk,khd->qhd", score_grad, key_block, preferred_element_type=jnp.float32)
            * 0.125
        )
        key_grad = (
            jnp.einsum("hqk,qhd->khd", score_grad, queries, preferred_element_type=jnp.float32)
            * 0.125
        )
        value_grad = jnp.einsum(
            "hqk,qhd->khd",
            probs.astype(jnp.bfloat16),
            grad_heads,
            preferred_element_type=jnp.float32,
        )
        return (
            query_grad,
            jnp.concatenate(
                [key_grad.reshape(back_rows, D), value_grad.reshape(back_rows, D)], axis=1
            ),
        )

    back_offsets = jnp.arange(back_count, dtype=jnp.int32) * back_rows
    back_blocks = (
        key_all.reshape(back_count, back_rows, H, HD),
        value_all.reshape(back_count, back_rows, H, HD),
        back_offsets,
    )
    query_grad, kv_terms = lax.scan(
        back_block, jnp.zeros((local_rows, H, HD), jnp.float32), back_blocks
    )
    kv_local = lax.psum_scatter(
        kv_terms.reshape(seq_length, 2 * D).astype(jnp.bfloat16),
        "ctx",
        scatter_dimension=0,
        tiled=True,
    ).astype(jnp.float32)

    def turn_heads(heads_in):
        return rotary(heads_in, places)

    unused_three, turn_pull = jax.vjp(turn_heads, pair_heads)
    pair_grad = turn_pull(
        jnp.concatenate([query_grad, kv_local[:, :D].reshape(local_rows, H, HD)], axis=1)
    )[0]
    projected_grad = jnp.concatenate(
        [pair_grad.reshape(local_rows, 2 * D), kv_local[:, D:]], axis=1
    ).astype(jnp.bfloat16)
    qkv_term = outer_rows(normed_low, projected_grad)
    bias_term = jnp.sum(projected_grad.astype(jnp.float32), axis=0)
    normed_grad = project_back(projected_grad, attn_back[0])
    unused_four, norm_pull = jax.vjp(layer_norm, inputs, gain_one, shift_one)
    input_part, gain_one_grad, shift_one_grad = norm_pull(normed_grad)
    tokens_grad = (middle_grad + input_part).reshape(1, local_rows, D)
    summed = (
        lax.psum_scatter(qkv_term, ("batch", "ctx"), scatter_dimension=0, tiled=True),
        lax.psum_scatter(out_term, ("batch", "ctx"), scatter_dimension=0, tiled=True),
        lax.psum_scatter(bias_term, ("batch", "ctx"), scatter_dimension=0, tiled=True),
        lax.psum_scatter(gain_one_grad, ("batch", "ctx"), scatter_dimension=0, tiled=True),
        lax.psum_scatter(shift_one_grad, ("batch", "ctx"), scatter_dimension=0, tiled=True),
        lax.psum_scatter(gain_two_grad, ("batch", "ctx"), scatter_dimension=0, tiled=True),
        lax.psum_scatter(shift_two_grad, ("batch", "ctx"), scatter_dimension=0, tiled=True),
    )
    return (
        mixed.reshape(1, local_rows, D),
        tokens_grad,
        summed[3],
        summed[4],
        summed[0],
        summed[2],
        summed[1],
        summed[5],
        summed[6],
        gate_weight_grad,
        up_weight_grad,
        down_weight_grad,
    )


BF = jnp.bfloat16
F32 = jnp.float32
MESH = pl.DeviceIdType.MESH
ANY = pl.ANY
VM = pltpu.VMEM
REMOTE_SEMS = 320
LOCAL_SEMS = 64


def nt(left, right):
    return lax.dot_general(left, right, (((1,), (1,)), ((), ())), preferred_element_type=F32)


def tn(left, right):
    return lax.dot_general(left, right, (((0,), (0,)), ((), ())), preferred_element_type=F32)


def nn(left, right):
    return jnp.dot(left, right, preferred_element_type=F32)


def norm_stats(values):
    centre = jnp.mean(values, axis=-1, keepdims=True)
    centred = values - centre
    spread = jnp.mean(centred * centred, axis=-1, keepdims=True)
    scale = lax.rsqrt(spread + 1e-05)
    return centred * scale, scale


def norm_back(grad, unit, scale, gain):
    weighted = grad * gain
    lead = jnp.mean(weighted, axis=-1, keepdims=True)
    tilt = jnp.mean(weighted * unit, axis=-1, keepdims=True)
    return scale * (weighted - lead - unit * tilt)


def turn_tables(length):
    half = ROT // 2
    freq = (np.float32(10000.0) ** (-np.arange(half, dtype=np.float32) * np.float32(2.0) / np.float32(ROT))).astype(np.float32)
    angles = np.arange(length, dtype=np.float32)[:, None] * freq[None, :]
    cosine, sine = np.cos(angles), np.sin(angles)
    tables = np.zeros((2, length, 128), np.float32)
    tables[0] = 1.0
    for start in (0, HD):
        tables[0, :, start : start + half] = cosine
        tables[0, :, start + half : start + ROT] = cosine
        tables[1, :, start : start + half] = -sine
        tables[1, :, start + half : start + ROT] = sine
    return tables


def aligned(value, to):
    return value if isinstance(value, int) else pl.multiple_of(value, to)


def feed_columns(width):
    return 2 * width + -(-width // 128) * 128


def qkv_lane(kind, head, heads):
    half = heads // 2
    return ((head // half * 3 + kind) * half + head % half) * HD


class Names:
    pass


def layer_kernel(dims, names_in, names_out, names_scratch, *refs):
    R, C, PL, rows, shard, QW, FW, PARTS = dims
    r = Names()
    for name, ref in zip(names_in + names_out + names_scratch, refs):
        setattr(r, name, ref)
    batch = lax.axis_index("batch")
    c = lax.axis_index("ctx")
    z = batch // 2
    core = lax.rem(batch, 2)
    q = core * C + c
    HS = PL // 2 * rows
    TOK = PL * rows
    KB = PL * shard
    STARTS = [sum(PARTS[:p]) for p in range(len(PARTS))]
    WC = [feed_columns(width) for width in PARTS]
    heads = QW // HD
    QH = QW // 2

    def lanes(kind, head):
        first = qkv_lane(kind, head, heads)
        return slice(first, first + HD)


    at_plane = [z == at for at in range(R)]
    counter = [0]
    local_count = [0]

    def slots(count):
        first = counter[0]
        counter[0] += count
        return first

    def mate(i):
        other = lax.rem(q + i, PL)
        return (z * 2 + other // C, lax.rem(other, C))

    def row_index(i):
        across, along = lax.rem(lax.rem(c, 2) + lax.rem(i, 2), 2), lax.rem(c // 2 + i // 2, 2)
        return 2 * along + across

    def row_mate(i):
        return (batch, row_index(i))

    sibling = (z * 2 + 1 - core, c)

    def plane_dev(t):
        return (t * 2 + core, c)

    def rcopy(src, dst, send, recv, dev):
        return pltpu.make_async_remote_copy(
            src_ref=src, dst_ref=dst, send_sem=r.ss.at[send], recv_sem=r.rs.at[recv], device_id=dev, device_id_type=MESH
        )

    drains = []

    def lcopy(src, dst):
        copy = pltpu.make_async_copy(src, dst, r.ls.at[local_count[0]])
        local_count[0] += 1
        copy.start()
        return copy

    loads = {name: lcopy(getattr(r, "in_" + name), getattr(r, "v_" + name)) for name in ("tokens", "cot")}

    local_tables = lcopy(r.tables, r.turns)
    r.sgt[...] = jnp.zeros_like(r.sgt)
    for k, vector in enumerate((r.in_g0, r.in_g1, r.in_g2, r.in_g3)):
        r.sgt[k : k + 1, 0:shard] = vector[...].astype(F32)
    for k in range(3):
        r.sgt[4 + k : 5 + k, 0:HD] = r.in_bias[0:1, k * HD : (k + 1) * HD].astype(F32)

    barrier = pltpu.get_barrier_semaphore()
    for i in range(1, PL):
        pl.semaphore_signal(barrier, inc=1, device_id=mate(i), device_id_type=MESH)
    for i in range(1, R):
        pl.semaphore_signal(barrier, inc=1, device_id=plane_dev(lax.rem(z + i, R)), device_id_type=MESH)
    pl.semaphore_wait(barrier, PL - 1 + R - 1)

    OFFS = (2, -2, 1, -1)

    class ZGather:
        def __init__(self, whole, height, chunks=1):
            self.whole, self.height, self.chunks = whole, height, chunks
            self.base = [slots(6) for _ in range(chunks)]

        def block(self, s, chunk=None):
            if chunk is None:
                return self.whole.at[pl.ds(aligned(s * self.height, 16), self.height)]
            part = self.height // self.chunks
            return self.whole.at[pl.ds(aligned(s * self.height + chunk * part, 16), part)]

        def guarded(self, ok, make):
            @pl.when(ok)
            def _():
                make().start()

            def drain():
                @pl.when(ok)
                def _():
                    make().wait_send()

            drains.append(drain)

        def start(self, src=None):
            for chunk in range(self.chunks):
                for k, off in enumerate(OFFS):
                    t = z + off
                    ok = (t >= 0) & (t < R)
                    if off == 2:
                        ok = ok & (z == 0)
                    if off == -2:
                        ok = ok & (z == R - 1)

                    def make(chunk=chunk, k=k, t=t):
                        mine = self.block(z, chunk)
                        return rcopy(mine if src is None else src, mine, self.base[chunk] + k, self.base[chunk] + z, plane_dev(t))

                    self.guarded(ok, make)

        def got(self, s, chunk):
            block = self.block(s, chunk)
            rcopy(block, block, self.base[chunk], self.base[chunk] + s, sibling).wait_recv()

        def relay(self, chunk=0):
            for at, blocks, to in ((R - 2, (1, 0), R - 1), (1, (2, 3), 0)):
                for k, s in enumerate(blocks):

                    @pl.when(z == at)
                    def _():
                        self.got(s, chunk)

                    def make(s=s, to=to, k=k):
                        block = self.block(s, chunk)
                        return rcopy(block, block, self.base[chunk] + 4 + k, self.base[chunk] + s, plane_dev(to))

                    self.guarded(z == at, make)

        def wait_block(self, s):
            for chunk in range(self.chunks):
                skip = z == s
                skip = skip | (z == (R - 2 if s < 2 else 1))

                @pl.when(jnp.logical_not(skip))
                def _():
                    self.got(s, chunk)

        def wait(self):
            for s in range(R):
                self.wait_block(s)

    class Spread:
        def __init__(self, stage):
            self.stage, self.base = stage, slots(PL)

        def start(self, target):
            self.target = target
            for i in range(1, PL):
                other = lax.rem(q + i, PL)
                copy = rcopy(self.stage.at[other], target, self.base + i, self.base + i, mate(i))
                copy.start()

        def wait_send(self):
            for i in range(1, PL):
                other = lax.rem(q + i, PL)
                rcopy(self.stage.at[other], self.target, self.base + i, self.base + i, mate(i)).wait_send()

        def wait(self, block):
            for i in range(1, PL):
                rcopy(self.stage.at[0], block(lax.rem(q - i + PL, PL)), self.base + i, self.base + i, mate(i)).wait_recv()

    class Gather:
        def __init__(self, whole):
            self.whole, self.base = whole, slots(2 * C)

        def block(self, s):
            return self.whole.at[pl.ds(aligned(s * rows, 16), rows)]

        def start(self, src):
            self.local = lcopy(src, self.block(q))
            sends = []
            for i in range(1, C):
                sends.append(rcopy(src, self.block(q), self.base + i, self.base + i, row_mate(i)))
            sends.append(rcopy(src, self.block(q), self.base, self.base, sibling))
            for copy in sends:
                copy.start()
            self.sends = sends

        def drain(self):
            for copy in self.sends:
                copy.wait_send()
            for i in range(1, C):
                self.passed(i).wait_send()

        def relay(self):
            for i in range(1, C):
                self.relay_one(i)

        def passed(self, i):
            block = self.block(core * C + row_index(i))
            return rcopy(block, block, self.base + C - 1 + i, self.base + C - 1 + i, sibling)

        def relay_one(self, i):
            block = self.block(core * C + row_index(i))
            rcopy(block, block, self.base, self.base + i, sibling).wait_recv()
            self.passed(i).start()

        def wait_one(self, i):
            block = self.block((1 - core) * C + row_index(i))
            sem = self.base + jnp.where(i == 0, 0, C - 1 + i)
            rcopy(block, block, self.base, sem, sibling).wait_recv()

        def wait(self):
            for i in range(C):
                self.wait_one(i)
            self.local.wait()

        def each(self, use, first=0, last=None):
            if first == 0:
                self.local.wait()

            @pl.loop(first, C if last is None else last)
            def _(i):
                @pl.when(i > 0)
                def _():
                    self.relay_one(i)

                use(core * C + row_index(i))
                self.wait_one(i)
                use((1 - core) * C + row_index(i))

    class Reduce:
        def __init__(self, k, before=None):
            self.sibout, self.theirs = getattr(r, f"sibout{k}"), getattr(r, f"theirs{k}")
            self.out, self.got, self.own = getattr(r, f"redout{k}"), getattr(r, f"redin{k}"), getattr(r, f"redown{k}")
            self.base = slots(C + 2)
            self.before = before


        def run(self, pairs, compute, later=False, more=False, only_prepare=False):
            chunk_rows = HS // 2

            def to_sibling(chunk):
                span = pl.ds(chunk * chunk_rows, chunk_rows)
                return rcopy(self.sibout.at[span], self.theirs.at[span], self.base + C + chunk, self.base + C + chunk, sibling)

            def product(target, weights, seq, chunk):
                total = None
                for (x, _), w in zip(pairs, weights):
                    term = compute(x[pl.ds(aligned(seq * HS + chunk * chunk_rows, 16), chunk_rows), :], w)
                    total = term if total is None else total + term
                span = pl.ds(chunk * chunk_rows, chunk_rows)
                if more:
                    total = total + target[span, :].astype(F32)
                target[span, :] = total.astype(BF)

            def pass_on(chunk):
                to_sibling(chunk).wait_recv()
                for blk in range(chunk * C // 2, (chunk + 1) * C // 2):
                    i = lax.rem(blk + c, 2) + 2 * lax.rem(blk // 2 + c // 2, 2)
                    span = pl.ds(blk * rows, rows)
                    total = r.mine[span, :].astype(F32) + self.theirs[span, :].astype(F32)

                    @pl.when(i == 0)
                    def _():
                        self.own[...] = total.astype(self.own.dtype)

                    @pl.when(i != 0)
                    def _():
                        self.out[i - 1] = total.astype(BF)
                        self.to_row(i, blk).start()

            def body(*bufs):
                bufs = list(bufs)
                weights, loads = [], []
                for _, w in pairs:
                    if isinstance(w, tuple):
                        weights.append(bufs.pop(0))
                        loads.append(lcopy(w[0], weights[-1]))
                    else:
                        weights.append(w)
                for load in loads:
                    load.wait()
                if self.before is not None and not more:
                    self.before.drain()
                if only_prepare:
                    for chunk in range(2):
                        product(self.sibout, weights, 1 - core, chunk)
                        product(r.mine, weights, core, chunk)
                    return
                product(self.sibout, weights, 1 - core, 0)
                to_sibling(0).start()
                product(r.mine, weights, core, 0)
                product(self.sibout, weights, 1 - core, 1)
                to_sibling(1).start()
                if not later:
                    pass_on(0)
                product(r.mine, weights, core, 1)
                if not later:
                    pass_on(1)

            pl.run_scoped(body, *[VM(w[0].shape, BF) for _, w in pairs if isinstance(w, tuple)])
            self.drain = lambda: self.drain_all(to_sibling)
            self.pass_on = lambda: (pass_on(0), pass_on(1))

        def prepare(self, pairs, compute):
            self.run(pairs, compute, only_prepare=True)

        def to_row(self, i, blk):
            return rcopy(self.out.at[i - 1], self.got.at[i - 1], self.base + i, self.base + i, (batch, blk))

        def drain_all(self, to_sibling):
            to_sibling(0).wait_send()
            to_sibling(1).wait_send()
            for i in range(1, C):
                self.to_row(i, row_index(i)).wait_send()

        def finish(self):
            for i in range(1, C):
                rcopy(self.out.at[i - 1], self.got.at[i - 1], self.base + i, self.base + i, row_mate(i)).wait_recv()
            total = self.own[...].astype(F32)
            for i in range(1, C):
                total = total + self.got[i - 1].astype(F32)
            return total

    ORDER = ((3, 2, 1, 0), (0, 3, 2, 1), (3, 0, 1, 2), (0, 1, 2, 3))

    class ZReduce:
        def __init__(self, grads, got, extra, merged, height):
            self.grads, self.got, self.extra, self.merged, self.height = grads, got, extra, merged, height
            self.base = slots(12)

        def block(self, t):
            return self.grads.at[pl.ds(aligned(t * self.height, 16), self.height)]

        def guarded(self, ok, make):
            @pl.when(ok)
            def _():
                make().start()

            def drain():
                @pl.when(ok)
                def _():
                    make().wait_send()

            drains.append(drain)

        def send(self, at, owner):
            b = self.base
            via = {0: 1, R - 1: R - 2}.get(at)
            if owner == at or (via is None and abs(owner - at) == 2) or (via is None and owner == R - 1 - at):
                return
            if via is None:
                slot = 1 if owner < at else 0
                return
            elif owner == via:
                slot = 0 if at == 0 else 1
                make = lambda: rcopy(self.block(owner), self.got.at[slot], b + 2, b + slot, plane_dev(via))
            else:
                k = 0 if owner == R - 1 - at else 1
                make = lambda: rcopy(self.block(owner), self.extra.at[k], b + k, b + 2 + k, plane_dev(via))
            self.guarded(at_plane[at], make)

        def start(self):
            for step in range(R):
                self.start_step(step)

        def start_step(self, step):
            for at in range(R):
                self.send(at, ORDER[at][step])

        def merge(self, steps=(0, 1)):
            b = self.base
            if 0 in steps:
                for at, owner, slot in ((1, 0, 1), (2, 3, 0)):
                    self.guarded(
                        at_plane[at],
                        lambda owner=owner, slot=slot: rcopy(self.block(owner), self.got.at[slot], b + 3, b + slot, plane_dev(owner)),
                    )
            for k in steps:
                for at, to, slots_at in ((1, (3, 2), (1, 0)), (2, (0, 1), (0, 1))):
                    owner = to[k]

                    @pl.when(z == at)
                    def _():
                        def body(own, other, sem):
                            first = pltpu.make_async_copy(self.block(owner), own, sem.at[0])
                            first.start()
                            rcopy(self.extra.at[k], self.extra.at[k], b, b + 2 + k, sibling).wait_recv()
                            second = pltpu.make_async_copy(self.extra.at[k], other, sem.at[1])
                            second.start()
                            first.wait()
                            second.wait()
                            own[...] = (own[...].astype(F32) + other[...].astype(F32)).astype(BF)
                            pltpu.sync_copy(own, self.merged.at[k])

                        shape = (self.height, self.grads.shape[1])
                        pl.run_scoped(body, VM(shape, BF), VM(shape, BF), pltpu.SemaphoreType.DMA((2,)))

                    self.guarded(
                        z == at,
                        lambda k=k, owner=owner, slot=slots_at[k]: rcopy(
                            self.merged.at[k], self.got.at[slot], b + 4 + k, b + slot, plane_dev(owner)
                        ),
                    )

        def wait(self):
            for slot in range(2):
                rcopy(self.got.at[slot], self.got.at[slot], self.base, self.base + slot, sibling).wait_recv()

        def finish(self, put):
            self.wait()

            def body(own, one, two):
                loads = [lcopy(self.block(z), own), lcopy(self.got.at[0], one), lcopy(self.got.at[1], two)]
                for load in loads:
                    load.wait()
                for k in range(self.height // shard):
                    span = pl.ds(k * shard, shard)
                    put(k, own[span, :].astype(F32) + one[span, :].astype(F32) + two[span, :].astype(F32))

            shape = (self.height, self.grads.shape[1])
            pl.run_scoped(body, *[VM(shape, BF)] * 3)

    zg_o, zg_qkv = ZGather(r.w_o, shard), ZGather(r.w_qkv, KB, 2)
    sp_qkv = Spread(r.st_qkv)
    parts = range(len(PARTS))
    def each_part(name):
        return [getattr(r, f"{name}{p}") for p in parts]

    w_f, st_f = each_part("w_f"), each_part("st_f")
    zg_f, sp_f = [ZGather(w, KB) for w in w_f], [Spread(st) for st in st_f]
    ag_normed, ag_cot, ag_two, ag_one = Gather(r.a_normed), Gather(r.a_cot), Gather(r.a_two), Gather(r.a_one)

    def mine_rows(whole, height):
        return whole.at[pl.ds(aligned((z * PL + q) * height, 16), height)]

    zg_o.start(r.in_o)
    local_o = lcopy(r.in_o, zg_o.block(z))
    base_small = slots(PL)
    small_sent = []
    for i in range(1, PL):
        copy = rcopy(r.sgt, r.small.at[z * PL + q], base_small + i, base_small + i, mate(i))
        copy.start()
        small_sent.append(copy)
    local_small = lcopy(r.sgt, r.small.at[z * PL + q])
    def stage_qkv(v):
        lcopy(r.in_qkv, v).wait()
        for other in range(PL):
            for j in range(3):
                for zh in range(R):
                    at = j * D + zh * PL * HD + other * HD
                    r.st_qkv[other, :, lanes(j, zh)] = v[:, at : at + HD]

    pl.run_scoped(stage_qkv, VM(r.in_qkv.shape, BF))
    sp_qkv.start(mine_rows(r.w_qkv, shard))
    local_qkv = lcopy(r.st_qkv.at[q], mine_rows(r.w_qkv, shard))
    local_f = [None] * len(PARTS)

    def stage_f(*bufs):
        loads = [lcopy(source, buf) for source, buf in zip((r.in_gate, r.in_up, r.in_down), bufs)]
        for load in loads:
            load.wait()
        for p, width in enumerate(PARTS):
            for other in range(PL):
                at = other * FW + STARTS[p]
                for k, source in enumerate(bufs):
                    st_f[p][other, :, k * width : (k + 1) * width] = source[:, at : at + width]
                if WC[p] > 3 * width:
                    st_f[p][other, :, 3 * width :] = jnp.zeros((shard, WC[p] - 3 * width), BF)

    def spread_f(p):
        sp_f[p].start(mine_rows(w_f[p], shard))
        local_f[p] = lcopy(st_f[p].at[q], mine_rows(w_f[p], shard))

    def arrived(spread, whole):
        spread.wait(lambda s: whole.at[pl.ds(aligned((z * PL + s) * shard, 16), shard)])

    pl.run_scoped(stage_f, *[VM(r.in_gate.shape, BF)] * 3)
    spread_f(0)

    local_small.wait()
    for i in range(1, PL):
        rcopy(r.sgt, r.small.at[z * PL + lax.rem(q - i + PL, PL)], base_small, base_small + i, mate(i)).wait_recv()
    base_smallz = slots(R)
    plane_small = r.small.at[pl.ds(z * PL, PL)]
    for i in range(1, R):
        copy = rcopy(plane_small, plane_small, base_smallz + i, base_smallz + i, plane_dev(lax.rem(z + i, R)))
        copy.start()
        drains.append(copy.wait_send)
    loads["tokens"].wait()
    loads["cot"].wait()
    tokens = r.v_tokens[...].astype(F32)
    unit, _ = norm_stats(tokens)
    for i in range(1, R):
        block = r.small.at[pl.ds(lax.rem(z - i + R, R) * PL, PL)]
        rcopy(block, block, base_smallz, base_smallz + i, sibling).wait_recv()
    for d in range(R * PL):
        for k in range(4):
            r.vec[k : k + 1, shard * d : shard * (d + 1)] = r.small[d, k : k + 1, 0:shard]
        for k in range(3):
            r.biases[3 * d + k : 3 * d + k + 1, 0:HD] = r.small[d, 4 + k : 5 + k, 0:HD]
    for j in range(3):
        for zh in range(R):
            row = r.biases[pl.ds(j * H + zh * PL + q, 1), 0:HD]
            r.bias[0:1, lanes(j, zh)] = row
    r.x_normed[...] = (unit * r.vec[0:1, :] + r.vec[1:2, :]).astype(BF)
    ag_normed.start(r.x_normed)

    spread_f(1)
    spread_f(2)
    ag_cot.start(r.v_cot)
    local_qkv.wait()
    arrived(sp_qkv, r.w_qkv)
    zg_qkv.start()
    local_f[0].wait()
    arrived(sp_f[0], w_f[0])
    zg_qkv.relay(0)
    zg_qkv.relay(1)
    zg_o.relay()
    zg_f[0].start()
    ag_normed.relay()
    ag_normed.wait()
    zg_qkv.wait()

    def lower(shape):
        return lax.rem(lax.broadcasted_iota(jnp.int32, shape, 1), HD) < ROT // 2

    def in_turn(shape):
        return lax.rem(lax.broadcasted_iota(jnp.int32, shape, 1), HD) < ROT

    TM = HS // 2
    local_tables.wait()

    @pl.loop(0, TOK // HS)
    def _(i):
        span = pl.ds(aligned(i * HS, HS), HS)
        projected = nn(r.a_normed[span, :], r.w_qkv[...]) + r.bias[0:1, :]
        for first in [half * 3 * QH + k * 128 for half in range(2) for k in range(2 * QH // 128)]:
            part = projected[:, first : first + 128]
            other = jnp.where(lower(part.shape), pltpu.roll(part, 128 - ROT // 2, 1), pltpu.roll(part, ROT // 2, 1))
            turned = part * r.turns[0] + other * r.turns[1]
            r.qkv[span, first : first + 128] = turned.astype(BF)
        for half in range(2):
            values = slice(half * 3 * QH + 2 * QH, (half + 1) * 3 * QH)
            r.qkv[span, values] = projected[:, values].astype(BF)

    def softmax_block(queries, keys, first):
        scores = nt(keys, queries) * 0.125
        at_key = lax.broadcasted_iota(jnp.int32, scores.shape, 0)
        at_query = lax.broadcasted_iota(jnp.int32, scores.shape, 1) + first
        allowed = at_key <= at_query
        scores = jnp.where(allowed, scores, -1e30)
        largest = jnp.max(scores, axis=0, keepdims=True)
        weights = jnp.where(allowed, jnp.exp(scores - largest), 0.0)
        return weights / jnp.sum(weights, axis=0, keepdims=True)

    QB = HS // 2

    kept = []
    for seq, keep in enumerate((r.sibout1, r.theirs1)):

        for h in range(heads):
            for blk in range(HS // QB):
                here = pl.ds(seq * HS + blk * QB, QB)
                seen = pl.ds(seq * HS, (blk + 1) * QB)
                probs = softmax_block(r.qkv[here, lanes(0, h)], r.qkv[seen, lanes(1, h)], blk * QB).astype(BF)
                keep[0 : (blk + 1) * QB, h * HS + blk * QB : h * HS + (blk + 1) * QB] = probs
                r.att[here, h * HD : (h + 1) * HD] = tn(probs, r.qkv[seen, lanes(2, h)]).astype(BF)
        kept.append(lcopy(keep, r.probs.at[pl.ds(seq * HS, HS)]))

    for p in (1, 2):
        local_f[p].wait()
        arrived(sp_f[p], w_f[p])
    ag_cot.relay()
    local_o.wait()
    zg_o.wait()

    red_att = Reduce(0)
    red_att.run([(r.att, r.w_o)], lambda x, w: nn(x, w[...]))
    zg_f[0].relay()
    zg_f[1].start()
    ag_cot.wait()
    middle = r.v_tokens[...].astype(F32) + red_att.finish()
    r.middle[...] = middle
    unit, _ = norm_stats(middle)
    r.x_two[...] = (unit * r.vec[2:3, :] + r.vec[3:4, :]).astype(BF)
    for copy in kept:
        copy.wait()
    ag_two.start(r.x_two)
    zg_f[1].relay()
    zg_f[2].start()

    hid, gug, g_f = each_part("hid"), each_part("gug"), each_part("g_f")

    def feed_forward(p, then=None):
        width = PARTS[p]
        def body(w):
            loads = []
            for s in range(R):
                zg_f[p].wait_block(s)
                loads.append(lcopy(zg_f[p].block(s), w.at[pl.ds(s * KB, KB)]))
            for load in loads:
                load.wait()

            def use(span):
                both = nn(r.a_two[span, :], w[:, : 2 * width])
                gate = both[:, :width]
                up = both[:, width:]
                sig = 1.0 / (1.0 + jnp.exp(-gate))
                swish = gate * sig
                hid[p][span, :] = (swish * up).astype(BF)
                hidden_grad = nn(r.a_cot[span, :], w[:, 2 * width : 3 * width])
                gug[p][span, :width] = (hidden_grad * up * sig * (1.0 + gate * (1.0 - sig))).astype(BF)
                gug[p][span, width:] = (hidden_grad * swish).astype(BF)

            if p == 0:
                ag_two.each(lambda s: use(pl.ds(aligned(s * rows, 16), rows)))
            else:

                @pl.loop(0, TOK // TM)
                def _(i):
                    use(pl.ds(aligned(i * TM, TM), TM))

            if then is not None:
                then(w)

        pl.run_scoped(body, VM(w_f[p].shape, BF))

    def grads_by_owner(terms, out, reduce, padded=None, steps=range(R)):
        width = out.shape[1]

        def body(tile, sem):
            pending = []

            def hand_on():
                store, step = pending.pop(0)
                store.wait()
                reduce.start_step(step)

            for step in steps:
                owner = R - 1 - step
                for at in range(1, R):
                    owner = jnp.where(z == at, ORDER[at][step], owner)
                for left, right, first in terms:
                    part = tn(left[:, pl.ds(aligned(owner * KB, KB), KB)], right[...])
                    tile[step % depth, :, first : first + right.shape[1]] = part.astype(BF)
                if padded is not None:
                    tile[step % depth, :, padded:] = jnp.zeros((KB, width - padded), BF)
                store = pltpu.make_async_copy(tile.at[step % depth], reduce.block(owner), sem.at[step % depth])
                store.start()
                pending.append((store, step))
                while len(pending) > (0 if step in (0, steps[-1]) else 1):
                    hand_on()

        depth = min(2, len(steps))
        pl.run_scoped(body, VM((depth, KB, width), BF), pltpu.SemaphoreType.DMA((depth,)))

    def feed_weight_grads(p, steps=range(R)):
        width = PARTS[p]
        terms = [(r.a_two, gug[p], 0), (r.a_cot, hid[p], 2 * width)]
        grads_by_owner(terms, g_f[p], zr_f[p], 3 * width if WC[p] > 3 * width else None, steps)

    zr_f = [ZReduce(*bufs, KB) for bufs in zip(g_f, each_part("zin_f"), each_part("zx_f"), each_part("zs_f"))]
    zr_o = ZReduce(r.g_o, r.zin_o, r.zx_o, r.zs_o, shard)
    g_q = [r.g_q0, r.g_q1]
    zr_q = [ZReduce(g_q[0], r.zin_q0, r.zx_q0, r.zs_q0, KB), ZReduce(g_q[1], r.zin_q1, r.zx_q1, r.zs_q1, KB)]

    feed_forward(0)
    zg_f[2].relay()
    feed_weight_grads(0)
    feed_forward(1)
    feed_weight_grads(1)
    red_two = Reduce(0, red_att)
    first_pairs = [(gug[p], (w_f[p].at[:, pl.ds(0, 2 * PARTS[p])],)) for p in (0, 1)]
    red_two.prepare(first_pairs, lambda x, w: nt(x, w[...]))

    def back_into_layer(w):
        feed_weight_grads(2, (0,))
        red_two.run([(gug[2], w.at[:, pl.ds(0, 2 * PARTS[2])])], lambda x, w: nt(x, w[...]), more=True)

    feed_forward(2, back_into_layer)
    feed_weight_grads(2, (1, 2, 3))
    two_grad = red_two.finish()
    unit, scale = norm_stats(r.middle[...])
    middle_grad = r.v_cot[...].astype(F32) + norm_back(two_grad, unit, scale, r.vec[2:3, :])
    r.middle_grad[...] = middle_grad
    ag_normed.drain()
    r.x_normed[...] = middle_grad.astype(BF)
    ag_one.start(r.x_normed)
    r.vec[6:7, :] = jnp.sum(two_grad * unit, axis=0, keepdims=True)
    r.vec[7:8, :] = jnp.sum(two_grad, axis=0, keepdims=True)

    zr_f[0].merge()
    red_mixed = Reduce(1)
    mixed_pairs = [(hid[p], (w_f[p].at[:, pl.ds(2 * PARTS[p], WC[p] - 2 * PARTS[p])],)) for p in parts]
    red_mixed.run(mixed_pairs, lambda x, w: nt(x, w[:, : x.shape[1]]), later=True)

    attg = gug[1]

    def att_grad(s):
        span = pl.ds(aligned(s * rows, 16), rows)
        pltpu.sync_copy(ag_one.block(s), r.a_two.at[span])
        attg[span, 0:QW] = nt(r.a_two[span, :], r.w_o[...]).astype(BF)

    ag_two.drain()
    ag_cot.drain()
    zr_f[1].merge()

    weights_back = lcopy(r.probs, r.a_cot)

    back_f, back_q = [Spread(st) for st in st_f], [Spread(r.st_q0), Spread(r.st_q1)]
    pin_f = each_part("pin_f")
    pin_q, st_q = [r.pin_q0, r.pin_q1], [r.st_q0, r.st_q1]

    def pin_block(got):
        return lambda s: got.at[s]

    def z_sum(reduce, sent, stage, spread, got):
        if sent is not None:
            sent.wait_send()

        def put(k, total):
            stage[k] = total.astype(BF)

        reduce.finish(put)
        spread.start(got.at[q])
        return lcopy(stage.at[q], got.at[q])

    ag_one.each(att_grad, 0, C - 1)
    local_f[0] = z_sum(zr_f[0], sp_f[0], st_f[0], back_f[0], pin_f[0])
    red_mixed.pass_on()
    ag_one.each(att_grad, C - 1, C)
    def o_grad(buf):
        for k in range(R):
            span = pl.ds(k * KB, KB)
            buf[:, span] = tn(r.att[...], r.a_two[:, span]).astype(BF)
        pltpu.sync_copy(buf, r.g_o)

    pl.run_scoped(o_grad, VM((QW, D), BF))
    zr_o.start()
    zr_f[2].merge((0,))

    def attention_back(half):
        def body(turn):
            @pl.loop(0, TOK // HS)
            def _(i):
                first = i * HS
                for hh in range(heads // 2):
                    h = half * heads // 2 + hh
                    key_grad = [jnp.zeros((QB, HD), F32) for _ in range(HS // QB)]
                    value_grad = [jnp.zeros((QB, HD), F32) for _ in range(HS // QB)]
                    for blk in range(HS // QB):
                        here = pl.ds(aligned(first + blk * QB, 16), QB)
                        seen = pl.ds(aligned(first, 16), (blk + 1) * QB)
                        queries, keys, values = r.qkv[here, lanes(0, h)], r.qkv[seen, lanes(1, h)], r.qkv[seen, lanes(2, h)]
                        grads = attg[here, h * HD : (h + 1) * HD]
                        low_probs = r.a_cot[seen, h * HS + blk * QB : h * HS + (blk + 1) * QB]
                        probs = low_probs.astype(F32)
                        prob_grad = nt(values, grads)
                        delta = jnp.sum(probs * prob_grad, axis=0, keepdims=True)
                        score_grad = (probs * (prob_grad - delta)).astype(BF)
                        turn[blk * QB : (blk + 1) * QB, hh * HD : (hh + 1) * HD] = tn(score_grad, keys) * 0.125
                        key_part = nn(score_grad, queries) * 0.125
                        value_part = nn(low_probs, grads)
                        for k in range(blk + 1):
                            key_grad[k] = key_grad[k] + key_part[k * QB : (k + 1) * QB]
                            value_grad[k] = value_grad[k] + value_part[k * QB : (k + 1) * QB]
                    for k in range(HS // QB):
                        turn[k * QB : (k + 1) * QB, QH + hh * HD : QH + (hh + 1) * HD] = key_grad[k]
                        r.qkv[pl.ds(aligned(first + k * QB, 16), QB), lanes(2, h)] = value_grad[k].astype(BF)
                for k in range(2 * QH // 128):
                    part = turn[:, k * 128 : (k + 1) * 128]
                    cross = part * r.turns[1]
                    other = jnp.where(lower(part.shape), pltpu.roll(cross, 128 - ROT // 2, 1), pltpu.roll(cross, ROT // 2, 1))
                    back = part * r.turns[0] + jnp.where(in_turn(part.shape), other, 0.0)
                    at = half * 3 * QH + k * 128
                    r.qkv[pl.ds(aligned(first, 16), HS), at : at + 128] = back.astype(BF)

        pl.run_scoped(body, VM((HS, 2 * QH), F32))
        grads_by_owner([(r.a_normed, r.qkv.at[:, pl.ds(half * 3 * QH, 3 * QH)], 0)], g_q[half], zr_q[half])

    weights_back.wait()
    attention_back(0)
    attention_back(1)
    zr_f[2].merge((1,))
    red_one = Reduce(0, red_two)
    red_one.run([(r.qkv, r.w_qkv)], lambda x, w: nt(x, w[...]))
    r.bias[0:1, :] = jnp.sum(r.qkv[...].astype(F32), axis=0, keepdims=True)

    zr_o.merge()
    local_f[1] = z_sum(zr_f[1], sp_f[1], st_f[1], back_f[1], pin_f[1])
    zr_q[0].merge()
    mixed = r.middle[...] + red_mixed.finish()
    r.x_two[...] = mixed.astype(BF)
    outputs = [lcopy(r.x_two, r.out_mixed)]
    local_f[2] = z_sum(zr_f[2], sp_f[2], st_f[2], back_f[2], pin_f[2])
    zr_q[1].merge()
    one_grad = red_one.finish()
    unit, scale = norm_stats(r.v_tokens[...].astype(F32))
    r.middle_grad[...] = r.middle_grad[...] + norm_back(one_grad, unit, scale, r.vec[0:1, :])
    outputs.append(lcopy(r.middle_grad, r.out_tokens))
    r.vec[4:5, :] = jnp.sum(one_grad * unit, axis=0, keepdims=True)
    r.vec[5:6, :] = jnp.sum(one_grad, axis=0, keepdims=True)
    r.sg[...] = jnp.zeros_like(r.sg)
    for d in range(R * PL):
        for k in range(4):
            r.sg[d % PL, d // PL, k : k + 1, 0:shard] = r.vec[4 + k : 5 + k, shard * d : shard * (d + 1)]
    for j in range(3):
        for zh in range(R):
            g = j * H + zh * PL + q
            piece = r.bias[0:1, lanes(j, zh)]
            r.sg[lax.rem(g // 3, PL), g // (3 * PL), pl.ds(4 + lax.rem(g, 3), 1), 0:HD] = piece
    base_sgp = slots(PL)
    for i in range(1, PL):
        other = lax.rem(q + i, PL)
        copy = rcopy(r.sg.at[other], r.sgp.at[i - 1], base_sgp + i, base_sgp + i, mate(i))
        copy.start()
        drains.append(copy.wait_send)
    zr_o.wait()
    outputs.append(lcopy(zr_o.block(z), r.own_o))
    local_f[0].wait()
    back_f[0].wait(pin_block(pin_f[0]))
    total = r.sg[q]
    for i in range(1, PL):
        rcopy(r.sgp.at[i - 1], r.sgp.at[i - 1], base_sgp, base_sgp + i, sibling).wait_recv()
        total = total + r.sgp[i - 1]
    r.sgs[...] = total
    base_sgz = slots(R)
    for i in range(1, R):
        t = lax.rem(z + i, R)
        copy = rcopy(r.sgs.at[t], r.sgz.at[i - 1], base_sgz + i, base_sgz + i, plane_dev(t))
        copy.start()
        drains.append(copy.wait_send)
    local_q = [z_sum(zr_q[half], None, st_q[half], back_q[half], pin_q[half]) for half in range(2)]
    for i in range(1, R):
        rcopy(r.sgz.at[i - 1], r.sgz.at[i - 1], base_sgz, base_sgz + i, sibling).wait_recv()
    for copy in small_sent:
        copy.wait_send()
    r.sgt[...] = r.sgs[z] + r.sgz[0] + r.sgz[1] + r.sgz[2]
    outputs.append(lcopy(r.sgt, r.out_small))
    for p in (1, 2):
        local_f[p].wait()
        back_f[p].wait(pin_block(pin_f[p]))
    for half in range(2):
        local_q[half].wait()
        back_q[half].wait(pin_block(pin_q[half]))
    for copy in outputs:
        copy.wait()
    for spread in back_f:
        spread.wait_send()
    sp_qkv.wait_send()
    for spread in back_q:
        spread.wait_send()
    ag_one.drain()
    red_mixed.drain()
    red_one.drain()
    for drain in drains:
        drain()
    assert counter[0] <= REMOTE_SEMS and local_count[0] <= LOCAL_SEMS, (counter, local_count)


def finish_outputs(got, parts, starts, planes, members, rows, shard, q_width, f_width):
    steps = 4
    tall, low = rows // steps, shard // steps

    heads = q_width // HD

    def body(mixed_in, tokens_in, small_in, pin_q0, pin_q1, own_o, zin_o, *rest):
        pins, (mixed, tokens, g0, g1, g2, g3, bias, qkv, o, gate, up, down) = rest[: len(parts)], rest[len(parts) :]
        mixed[0] = mixed_in[...]
        tokens[0] = tokens_in[...]
        o[...] = own_o[...].astype(F32) + zin_o[0].astype(F32) + zin_o[1].astype(F32)
        for k, gain in enumerate((g0, g1, g2, g3)):
            gain[...] = small_in[k : k + 1, 0:shard]
        for k in range(3):
            bias[0:1, k * HD : (k + 1) * HD] = small_in[4 + k : 5 + k, 0:HD]
        for other in range(members):
            for j in range(3):
                for zh in range(planes):
                    at = j * D + zh * members * HD + other * HD
                    pin = (pin_q0, pin_q1)[zh // (heads // 2)]
                    first = qkv_lane(j, zh % (heads // 2), heads)
                    qkv[:, at : at + HD] = pin[other, :, first : first + HD].astype(F32)
            for pin, width, start in zip(pins, parts, starts):
                at = other * f_width + start
                for k, target in enumerate((gate, up, down)):
                    target[:, at : at + width] = pin[other, :, k * width : (k + 1) * width].astype(F32)

    def tiles(shape, axis, size):
        block = tuple(size if k == axis else n for k, n in enumerate(shape))
        return pl.BlockSpec(block, lambda i: tuple(i if k == axis else 0 for k in range(len(shape))))

    ins = [
        (got["out_mixed"], 0, tall), (got["out_tokens"], 0, tall), (got["out_small"], None, 0), (got["pin_q0"], 1, low), (got["pin_q1"], 1, low),
        (got["own_o"], 0, low), (got["zin_o"], 1, low),
    ] + [(got[f"pin_f{p}"], 1, low) for p in range(len(parts))]
    outs = dict(
        mixed=((1, rows, D), BF, 1, tall), tokens=((1, rows, D), F32, 1, tall),
        g0=((1, shard), F32, None, 0), g1=((1, shard), F32, None, 0), g2=((1, shard), F32, None, 0), g3=((1, shard), F32, None, 0),
        bias=((1, 3 * HD), F32, None, 0),
        qkv=((shard, 3 * D), F32, 0, low), o=((shard, D), F32, 0, low),
        gate=((shard, FF), F32, 0, low), up=((shard, FF), F32, 0, low), down=((shard, FF), F32, 0, low),
    )
    results = pl.pallas_call(
        body,
        grid=(steps,),
        out_shape=[jax.ShapeDtypeStruct(shape, kind) for shape, kind, _, _ in outs.values()],
        in_specs=[tiles(array.shape, axis, size) for array, axis, size in ins],
        out_specs=[tiles(shape, axis, size) for shape, _, axis, size in outs.values()],
        name="finish",
    )(*[array for array, _, _ in ins])
    return dict(zip(outs, results))


def fast_local(tokens, out_grad, ln1_gain, ln1_shift, qkv_weight, qkv_bias, out_weight, ln2_gain, ln2_shift, gate_weight, up_weight, down_weight):
    planes, columns = lax.axis_size("batch") // 2, lax.axis_size("ctx")
    members = 2 * columns
    rows = tokens.shape[1]
    seq = rows * columns
    total = members * rows
    shard = qkv_weight.shape[0]
    q_width = D // members
    f_width = FF // members
    plane_rows = members * shard
    parts = (256, 256, f_width - 512)
    dims = (planes, columns, members, rows, shard, q_width, f_width, parts)
    inputs = dict(
        in_tokens=(tokens.reshape(rows, D), ANY),
        in_cot=(out_grad.reshape(rows, D), ANY),
        in_g0=(ln1_gain.reshape(1, shard), VM), in_g1=(ln1_shift.reshape(1, shard), VM),
        in_g2=(ln2_gain.reshape(1, shard), VM), in_g3=(ln2_shift.reshape(1, shard), VM), in_bias=(qkv_bias.reshape(1, 3 * HD), VM),
        in_qkv=(qkv_weight, ANY),
        in_o=(out_weight, ANY),
        in_gate=(gate_weight, ANY),
        in_up=(up_weight, ANY),
        in_down=(down_weight, ANY),
        tables=(jnp.asarray(turn_tables(seq)), ANY),
    )
    columns_f = [feed_columns(width) for width in parts]
    outs = dict(
        out_mixed=((rows, D), BF, ANY),
        out_tokens=((rows, D), F32, ANY),
        out_small=((8, 128), F32, ANY),
        pin_q0=((members, shard, 3 * q_width // 2), BF, ANY), pin_q1=((members, shard, 3 * q_width // 2), BF, ANY),
        own_o=((shard, D), BF, ANY),
        zin_o=((2, shard, D), BF, ANY),
    )
    for p, width in enumerate(columns_f):
        outs[f"pin_f{p}"] = ((members, shard, width), BF, ANY)
    final = list(outs)
    spaces = dict(
        a_one=(total, D), probs=(total, D),
        g_o=(q_width, D), zx_o=(2, shard, D), zs_o=(2, shard, D),
    )
    for half in range(2):
        spaces[f"g_q{half}"] = (D, 3 * q_width // 2)
        for kind in ("zin", "zx", "zs"):
            spaces[f"{kind}_q{half}"] = (2, plane_rows, 3 * q_width // 2)
    for p, width in enumerate(columns_f):
        spaces[f"w_f{p}"] = spaces[f"g_f{p}"] = (D, width)
        for kind in ("zin", "zx", "zs"):
            spaces[f"{kind}_f{p}"] = (2, plane_rows, width)
    for name, shape in spaces.items():
        outs[name] = (shape, BF, ANY)
    scratch = dict(
        v_tokens=VM((rows, D), BF), v_cot=VM((rows, D), BF),
        turns=VM((2, seq, 128), F32),
        a_normed=VM((total, D), BF), a_two=VM((total, D), BF), a_cot=VM((total, D), BF),
        w_qkv=VM((D, 3 * q_width), BF), w_o=VM((q_width, D), BF),
        qkv=VM((total, 3 * q_width), BF), att=VM((total, q_width), BF),
        st_qkv=VM((members, shard, 3 * q_width), BF),
        st_q0=VM((members, shard, 3 * q_width // 2), BF), st_q1=VM((members, shard, 3 * q_width // 2), BF),
        small=VM((planes * members, 8, 128), F32), sg=VM((members, planes, 8, 128), F32),
        sgz=VM((planes - 1, 8, 128), F32), sgs=VM((planes, 8, 128), F32), sgp=VM((members - 1, planes, 8, 128), F32), sgt=VM((8, 128), F32),
        vec=VM((8, D), F32), biases=VM((3 * H, 128), F32), bias=VM((8, 3 * q_width), F32),
        x_normed=VM((rows, D), BF), x_two=VM((rows, D), BF),
        middle=VM((rows, D), F32), middle_grad=VM((rows, D), F32),
        mine=VM((seq, D), BF),
    )
    for p, width in enumerate(parts):
        scratch[f"st_f{p}"] = VM((members, shard, columns_f[p]), BF)
        scratch[f"hid{p}"], scratch[f"gug{p}"] = VM((total, width), BF), VM((total, 2 * width), BF)
    for k in range(2):
        scratch[f"sibout{k}"] = VM((seq, D), BF)
        scratch[f"theirs{k}"] = VM((seq, D), BF)
        scratch[f"redout{k}"] = VM((columns - 1, rows, D), BF)
        scratch[f"redin{k}"] = VM((columns - 1, rows, D), BF)
        scratch[f"redown{k}"] = VM((rows, D), F32 if k == 0 else BF)
    scratch["ss"] = pltpu.SemaphoreType.DMA((REMOTE_SEMS,))
    scratch["rs"] = pltpu.SemaphoreType.DMA((REMOTE_SEMS,))
    scratch["ls"] = pltpu.SemaphoreType.DMA((LOCAL_SEMS,))
    results = pl.pallas_call(
        functools.partial(layer_kernel, dims, list(inputs), list(outs), list(scratch)),
        out_shape=[jax.ShapeDtypeStruct(shape, kind) for shape, kind, _ in outs.values()],
        in_specs=[pl.BlockSpec(memory_space=place) for _, place in inputs.values()],
        out_specs=[pl.BlockSpec(memory_space=place) for _, _, place in outs.values()],
        scratch_shapes=list(scratch.values()),
        compiler_params=pltpu.CompilerParams(collective_id=0, has_side_effects=True, vmem_limit_bytes=63 * 2**20),
        cost_estimate=pl.CostEstimate(flops=42 * 10**9, bytes_accessed=300 * 10**6, transcendentals=0),
        name="layer",
    )(*[array for array, _ in inputs.values()])
    got = dict(zip(final, results))
    f_starts = [sum(parts[:p]) for p in range(len(parts))]
    done = finish_outputs(got, parts, f_starts, planes, members, rows, shard, q_width, f_width)
    return (
        done["mixed"],
        done["tokens"],
        done["g0"].reshape(shard),
        done["g1"].reshape(shard),
        done["qkv"],
        done["bias"].reshape(3 * HD),
        done["o"],
        done["g2"].reshape(shard),
        done["g3"].reshape(shard),
        done["gate"],
        done["up"],
        done["down"],
    )


def fits(mesh):
    return mesh.shape["batch"] == 8 and mesh.shape["ctx"] == 4


def solution(mesh):
    in_specs = (
        P("batch", "ctx", None),
        P("batch", "ctx", None),
        P(("batch", "ctx")),
        P(("batch", "ctx")),
        P(("batch", "ctx"), None),
        P(("batch", "ctx")),
        P(("batch", "ctx"), None),
        P(("batch", "ctx")),
        P(("batch", "ctx")),
        P(("batch", "ctx"), None),
        P(("batch", "ctx"), None),
        P(("batch", "ctx"), None),
    )
    out_specs = (
        P("batch", "ctx", None),
        P("batch", "ctx", None),
        P(("batch", "ctx")),
        P(("batch", "ctx")),
        P(("batch", "ctx"), None),
        P(("batch", "ctx")),
        P(("batch", "ctx"), None),
        P(("batch", "ctx")),
        P(("batch", "ctx")),
        P(("batch", "ctx"), None),
        P(("batch", "ctx"), None),
        P(("batch", "ctx"), None),
    )
    body = fast_local if fits(mesh) else local
    return jax.shard_map(body, mesh=mesh, in_specs=in_specs, out_specs=out_specs, check_vma=False)
```

```python
import functools

import jax
import jax.numpy as jnp
import numpy as np
from jax import lax
from jax.experimental import pallas as pl
from jax.experimental.pallas import tpu as pltpu
from jax.sharding import PartitionSpec as P

D = 2048
FF = 5632
H = 32
HD = 64
ROT = 16


def layer_norm(values, gain, shift):
    centre = jnp.mean(values, axis=-1, keepdims=True)
    centred = values - centre
    spread = jnp.mean(centred * centred, axis=-1, keepdims=True)
    return centred * lax.rsqrt(spread + 1e-05) * gain + shift


def rotary(values, positions):
    half_dims = ROT // 2
    frequency = 10000.0 ** (-jnp.arange(half_dims, dtype=jnp.float32) * 2.0 / ROT)
    angles = positions.astype(jnp.float32)[:, None] * frequency[None, :]
    cosine_term = jnp.cos(angles)[:, None, :]
    sine_term = jnp.sin(angles)[:, None, :]
    first_half = values[..., :half_dims]
    second_half = values[..., half_dims:ROT]
    return jnp.concatenate(
        [
            first_half * cosine_term - second_half * sine_term,
            second_half * cosine_term + first_half * sine_term,
            values[..., ROT:],
        ],
        axis=-1,
    )


def swish_product(gate_value, up_value):
    return gate_value / (1.0 + jnp.exp(-gate_value)) * up_value


def project_back(left, right):
    return lax.dot_general(
        left, right, (((1,), (1,)), ((), ())), preferred_element_type=jnp.float32
    )


def outer_rows(left, right):
    return lax.dot_general(
        left, right, (((0,), (0,)), ((), ())), preferred_element_type=jnp.float32
    )


def local(
    tokens,
    out_grad,
    ln1_gain,
    ln1_shift,
    qkv_weight,
    qkv_bias,
    out_weight,
    ln2_gain,
    ln2_shift,
    gate_weight,
    up_weight,
    down_weight,
):
    local_rows = tokens.shape[1]
    seq_length = local_rows * lax.axis_size("ctx")
    inputs = tokens.reshape(local_rows, D).astype(jnp.float32)
    cotangent = out_grad.reshape(local_rows, D).astype(jnp.float32)
    places = lax.axis_index("ctx") * local_rows + jnp.arange(local_rows, dtype=jnp.int32)
    attn_set = (
        lax.all_gather(qkv_weight, ("batch", "ctx"), axis=0, tiled=True),
        lax.all_gather(out_weight, ("batch", "ctx"), axis=0, tiled=True),
        lax.all_gather(qkv_bias, ("batch", "ctx"), axis=0, tiled=True),
        lax.all_gather(ln1_gain, ("batch", "ctx"), axis=0, tiled=True),
        lax.all_gather(ln1_shift, ("batch", "ctx"), axis=0, tiled=True),
    )
    gain_one = attn_set[3].astype(jnp.float32)
    shift_one = attn_set[4].astype(jnp.float32)
    normed = layer_norm(inputs, gain_one, shift_one)
    normed_low = normed.astype(jnp.bfloat16)
    projected = jnp.dot(normed_low, attn_set[0], preferred_element_type=jnp.float32) + attn_set[
        2
    ].astype(jnp.float32)
    pair_heads = projected[:, : 2 * D].reshape(local_rows, 2 * H, HD)
    turned = rotary(pair_heads, places)
    queries = turned[:, :H].astype(jnp.bfloat16)
    key_rows = turned[:, H:].reshape(local_rows, D).astype(jnp.bfloat16)
    value_rows = projected[:, 2 * D :].astype(jnp.bfloat16)
    start_state = (
        jnp.full((H, local_rows), -1e30, jnp.float32),
        jnp.zeros((H, local_rows), jnp.float32),
        jnp.zeros((H, local_rows, HD), jnp.float32),
    )
    carry = start_state
    key_piece = lax.all_gather(key_rows, "ctx", axis=0, tiled=True)
    value_piece = lax.all_gather(value_rows, "ctx", axis=0, tiled=True)
    piece_rows = key_piece.shape[0]
    block_rows = 512
    block_count = piece_rows // block_rows

    def inner(state, block):
        largest, totals, accum = state
        key_block, value_block, offset = block
        raw_scores = (
            jnp.einsum("qhd,khd->hqk", queries, key_block, preferred_element_type=jnp.float32)
            * 0.125
        )
        key_places = offset + jnp.arange(block_rows, dtype=jnp.int32)
        allowed = (key_places[None, :] <= places[:, None])[None]
        raw_scores = jnp.where(allowed, raw_scores, -1e30)
        new_largest = jnp.maximum(largest, jnp.max(raw_scores, axis=-1))
        weights = jnp.where(allowed, jnp.exp(raw_scores - new_largest[..., None]), 0.0)
        factor = jnp.exp(largest - new_largest)
        totals = totals * factor + jnp.sum(weights, axis=-1)
        accum = accum * factor[..., None] + jnp.einsum(
            "hqk,khd->hqd",
            weights.astype(jnp.bfloat16),
            value_block,
            preferred_element_type=jnp.float32,
        )
        return ((new_largest, totals, accum), None)

    offsets = jnp.arange(block_count, dtype=jnp.int32) * block_rows
    blocks = (
        key_piece.reshape(block_count, block_rows, H, HD),
        value_piece.reshape(block_count, block_rows, H, HD),
        offsets,
    )
    carry, unused = lax.scan(inner, carry, blocks)
    largest, totals, accum = carry
    attended = jnp.transpose(accum / totals[..., None], (1, 0, 2)).reshape(local_rows, D)
    log_total = largest + jnp.log(totals)
    attended_low = attended.astype(jnp.bfloat16)
    middle = inputs + jnp.dot(attended_low, attn_set[1], preferred_element_type=jnp.float32)
    mlp_set = (
        lax.all_gather(gate_weight, ("batch", "ctx"), axis=0, tiled=True),
        lax.all_gather(up_weight, ("batch", "ctx"), axis=0, tiled=True),
        lax.all_gather(down_weight, ("batch", "ctx"), axis=0, tiled=True),
        lax.all_gather(ln2_gain, ("batch", "ctx"), axis=0, tiled=True),
        lax.all_gather(ln2_shift, ("batch", "ctx"), axis=0, tiled=True),
    )
    gain_two = mlp_set[3].astype(jnp.float32)
    shift_two = mlp_set[4].astype(jnp.float32)
    normed_two_low = layer_norm(middle, gain_two, shift_two).astype(jnp.bfloat16)
    gate_value = jnp.dot(normed_two_low, mlp_set[0], preferred_element_type=jnp.float32)
    up_value = jnp.dot(normed_two_low, mlp_set[1], preferred_element_type=jnp.float32)
    hidden_low = swish_product(gate_value, up_value).astype(jnp.bfloat16)
    mixed = (middle + project_back(hidden_low, mlp_set[2])).astype(jnp.bfloat16)
    mlp_back = (
        lax.all_gather(gate_weight, ("batch", "ctx"), axis=0, tiled=True),
        lax.all_gather(up_weight, ("batch", "ctx"), axis=0, tiled=True),
        lax.all_gather(down_weight, ("batch", "ctx"), axis=0, tiled=True),
        lax.all_gather(ln2_gain, ("batch", "ctx"), axis=0, tiled=True),
        lax.all_gather(ln2_shift, ("batch", "ctx"), axis=0, tiled=True),
    )
    attn_back = (
        lax.all_gather(qkv_weight, ("batch", "ctx"), axis=0, tiled=True),
        lax.all_gather(out_weight, ("batch", "ctx"), axis=0, tiled=True),
        lax.all_gather(qkv_bias, ("batch", "ctx"), axis=0, tiled=True),
        lax.all_gather(ln1_gain, ("batch", "ctx"), axis=0, tiled=True),
        lax.all_gather(ln1_shift, ("batch", "ctx"), axis=0, tiled=True),
    )
    branch_two = cotangent.astype(jnp.bfloat16)
    hidden_grad = jnp.dot(branch_two, mlp_back[2], preferred_element_type=jnp.float32)
    unused_value, act_pull = jax.vjp(swish_product, gate_value, up_value)
    gate_grad, up_grad = act_pull(hidden_grad)
    gate_low = gate_grad.astype(jnp.bfloat16)
    up_low = up_grad.astype(jnp.bfloat16)
    normed_two_grad = project_back(gate_low, mlp_back[0]) + project_back(up_low, mlp_back[1])
    unused_two, norm_pull_two = jax.vjp(layer_norm, middle, gain_two, shift_two)
    middle_part, gain_two_grad, shift_two_grad = norm_pull_two(normed_two_grad)
    middle_grad = cotangent + middle_part
    gate_weight_grad, up_weight_grad, down_weight_grad = (
        lax.psum_scatter(
            outer_rows(left, right).astype(jnp.bfloat16), ("batch", "ctx"), scatter_dimension=0, tiled=True
        ).astype(jnp.float32)
        for left, right in ((normed_two_low, gate_low), (normed_two_low, up_low), (branch_two, hidden_low))
    )
    branch_one = middle_grad.astype(jnp.bfloat16)
    out_term = outer_rows(attended_low, branch_one)
    attended_grad = project_back(branch_one, attn_back[1]).astype(jnp.bfloat16)
    grad_heads = attended_grad.reshape(local_rows, H, HD)
    delta = jnp.transpose(
        jnp.sum((attended_grad.astype(jnp.float32) * attended).reshape(local_rows, H, HD), axis=-1)
    )
    key_all, value_all = (
        lax.all_gather(key_rows, "ctx", axis=0, tiled=True),
        lax.all_gather(value_rows, "ctx", axis=0, tiled=True),
    )
    back_rows = 512
    back_count = seq_length // back_rows

    def back_block(query_grad, block):
        key_block, value_block, offset = block
        raw_scores = (
            jnp.einsum("qhd,khd->hqk", queries, key_block, preferred_element_type=jnp.float32)
            * 0.125
        )
        key_places = offset + jnp.arange(back_rows, dtype=jnp.int32)
        allowed = (key_places[None, :] <= places[:, None])[None]
        probs = jnp.where(allowed, jnp.exp(raw_scores - log_total[..., None]), 0.0)
        prob_grad = jnp.einsum(
            "qhd,khd->hqk", grad_heads, value_block, preferred_element_type=jnp.float32
        )
        score_grad = (probs * (prob_grad - delta[..., None])).astype(jnp.bfloat16)
        query_grad = (
            query_grad
            + jnp.einsum("hqk,khd->qhd", score_grad, key_block, preferred_element_type=jnp.float32)
            * 0.125
        )
        key_grad = (
            jnp.einsum("hqk,qhd->khd", score_grad, queries, preferred_element_type=jnp.float32)
            * 0.125
        )
        value_grad = jnp.einsum(
            "hqk,qhd->khd",
            probs.astype(jnp.bfloat16),
            grad_heads,
            preferred_element_type=jnp.float32,
        )
        return (
            query_grad,
            jnp.concatenate(
                [key_grad.reshape(back_rows, D), value_grad.reshape(back_rows, D)], axis=1
            ),
        )

    back_offsets = jnp.arange(back_count, dtype=jnp.int32) * back_rows
    back_blocks = (
        key_all.reshape(back_count, back_rows, H, HD),
        value_all.reshape(back_count, back_rows, H, HD),
        back_offsets,
    )
    query_grad, kv_terms = lax.scan(
        back_block, jnp.zeros((local_rows, H, HD), jnp.float32), back_blocks
    )
    kv_local = lax.psum_scatter(
        kv_terms.reshape(seq_length, 2 * D).astype(jnp.bfloat16),
        "ctx",
        scatter_dimension=0,
        tiled=True,
    ).astype(jnp.float32)

    def turn_heads(heads_in):
        return rotary(heads_in, places)

    unused_three, turn_pull = jax.vjp(turn_heads, pair_heads)
    pair_grad = turn_pull(
        jnp.concatenate([query_grad, kv_local[:, :D].reshape(local_rows, H, HD)], axis=1)
    )[0]
    projected_grad = jnp.concatenate(
        [pair_grad.reshape(local_rows, 2 * D), kv_local[:, D:]], axis=1
    ).astype(jnp.bfloat16)
    qkv_term = outer_rows(normed_low, projected_grad)
    bias_term = jnp.sum(projected_grad.astype(jnp.float32), axis=0)
    normed_grad = project_back(projected_grad, attn_back[0])
    unused_four, norm_pull = jax.vjp(layer_norm, inputs, gain_one, shift_one)
    input_part, gain_one_grad, shift_one_grad = norm_pull(normed_grad)
    tokens_grad = (middle_grad + input_part).reshape(1, local_rows, D)
    summed = (
        lax.psum_scatter(qkv_term, ("batch", "ctx"), scatter_dimension=0, tiled=True),
        lax.psum_scatter(out_term, ("batch", "ctx"), scatter_dimension=0, tiled=True),
        lax.psum_scatter(bias_term, ("batch", "ctx"), scatter_dimension=0, tiled=True),
        lax.psum_scatter(gain_one_grad, ("batch", "ctx"), scatter_dimension=0, tiled=True),
        lax.psum_scatter(shift_one_grad, ("batch", "ctx"), scatter_dimension=0, tiled=True),
        lax.psum_scatter(gain_two_grad, ("batch", "ctx"), scatter_dimension=0, tiled=True),
        lax.psum_scatter(shift_two_grad, ("batch", "ctx"), scatter_dimension=0, tiled=True),
    )
    return (
        mixed.reshape(1, local_rows, D),
        tokens_grad,
        summed[3],
        summed[4],
        summed[0],
        summed[2],
        summed[1],
        summed[5],
        summed[6],
        gate_weight_grad,
        up_weight_grad,
        down_weight_grad,
    )


BF = jnp.bfloat16
F32 = jnp.float32
MESH = pl.DeviceIdType.MESH
ANY = pl.ANY
VM = pltpu.VMEM
REMOTE_SEMS = 320
LOCAL_SEMS = 64


def nt(left, right):
    return lax.dot_general(left, right, (((1,), (1,)), ((), ())), preferred_element_type=F32)


def tn(left, right):
    return lax.dot_general(left, right, (((0,), (0,)), ((), ())), preferred_element_type=F32)


def nn(left, right):
    return jnp.dot(left, right, preferred_element_type=F32)


def norm_stats(values):
    centre = jnp.mean(values, axis=-1, keepdims=True)
    centred = values - centre
    spread = jnp.mean(centred * centred, axis=-1, keepdims=True)
    scale = lax.rsqrt(spread + 1e-05)
    return centred * scale, scale


def norm_back(grad, unit, scale, gain):
    weighted = grad * gain
    lead = jnp.mean(weighted, axis=-1, keepdims=True)
    tilt = jnp.mean(weighted * unit, axis=-1, keepdims=True)
    return scale * (weighted - lead - unit * tilt)


def turn_tables(length):
    half = ROT // 2
    freq = (np.float32(10000.0) ** (-np.arange(half, dtype=np.float32) * np.float32(2.0) / np.float32(ROT))).astype(np.float32)
    angles = np.arange(length, dtype=np.float32)[:, None] * freq[None, :]
    cosine, sine = np.cos(angles), np.sin(angles)
    tables = np.zeros((2, length, 128), np.float32)
    tables[0] = 1.0
    for start in (0, HD):
        tables[0, :, start : start + half] = cosine
        tables[0, :, start + half : start + ROT] = cosine
        tables[1, :, start : start + half] = -sine
        tables[1, :, start + half : start + ROT] = sine
    return tables


def aligned(value, to):
    return value if isinstance(value, int) else pl.multiple_of(value, to)


def feed_columns(width):
    return 2 * width + -(-width // 128) * 128


def qkv_lane(kind, head, heads):
    half = heads // 2
    return ((head // half * 3 + kind) * half + head % half) * HD


class Names:
    pass


def layer_kernel(dims, names_in, names_out, names_scratch, *refs):
    R, C, PL, rows, shard, QW, FW, PARTS = dims
    r = Names()
    for name, ref in zip(names_in + names_out + names_scratch, refs):
        setattr(r, name, ref)
    batch = lax.axis_index("batch")
    c = lax.axis_index("ctx")
    z = batch // 2
    core = lax.rem(batch, 2)
    q = core * C + c
    HS = PL // 2 * rows
    TOK = PL * rows
    KB = PL * shard
    STARTS = [sum(PARTS[:p]) for p in range(len(PARTS))]
    WC = [feed_columns(width) for width in PARTS]
    heads = QW // HD
    QH = QW // 2

    def lanes(kind, head):
        first = qkv_lane(kind, head, heads)
        return slice(first, first + HD)


    at_plane = [z == at for at in range(R)]
    counter = [0]
    local_count = [0]

    def slots(count):
        first = counter[0]
        counter[0] += count
        return first

    def mate(i):
        other = lax.rem(q + i, PL)
        return (z * 2 + other // C, lax.rem(other, C))

    def row_index(i):
        across, along = lax.rem(lax.rem(c, 2) + lax.rem(i, 2), 2), lax.rem(c // 2 + i // 2, 2)
        return 2 * along + across

    def row_mate(i):
        return (batch, row_index(i))

    sibling = (z * 2 + 1 - core, c)

    def plane_dev(t):
        return (t * 2 + core, c)

    def rcopy(src, dst, send, recv, dev):
        return pltpu.make_async_remote_copy(
            src_ref=src, dst_ref=dst, send_sem=r.ss.at[send], recv_sem=r.rs.at[recv], device_id=dev, device_id_type=MESH
        )

    drains = []

    def lcopy(src, dst):
        copy = pltpu.make_async_copy(src, dst, r.ls.at[local_count[0]])
        local_count[0] += 1
        copy.start()
        return copy

    loads = {name: lcopy(getattr(r, "in_" + name), getattr(r, "v_" + name)) for name in ("tokens", "cot")}

    local_tables = lcopy(r.tables, r.turns)
    r.sgt[...] = jnp.zeros_like(r.sgt)
    for k, vector in enumerate((r.in_g0, r.in_g1, r.in_g2, r.in_g3)):
        r.sgt[k : k + 1, 0:shard] = vector[...].astype(F32)
    for k in range(3):
        r.sgt[4 + k : 5 + k, 0:HD] = r.in_bias[0:1, k * HD : (k + 1) * HD].astype(F32)

    barrier = pltpu.get_barrier_semaphore()
    for i in range(1, PL):
        pl.semaphore_signal(barrier, inc=1, device_id=mate(i), device_id_type=MESH)
    for i in range(1, R):
        pl.semaphore_signal(barrier, inc=1, device_id=plane_dev(lax.rem(z + i, R)), device_id_type=MESH)
    pl.semaphore_wait(barrier, PL - 1 + R - 1)

    OFFS = (1, -1)

    class ZGather:
        def __init__(self, whole, height, chunks=1):
            self.whole, self.height, self.chunks = whole, height, chunks
            self.base = [slots(6) for _ in range(chunks)]

        def block(self, s, chunk=None):
            if chunk is None:
                return self.whole.at[pl.ds(aligned(s * self.height, 16), self.height)]
            part = self.height // self.chunks
            return self.whole.at[pl.ds(aligned(s * self.height + chunk * part, 16), part)]

        def guarded(self, ok, make):
            @pl.when(ok)
            def _():
                make().start()

            def drain():
                @pl.when(ok)
                def _():
                    make().wait_send()

            drains.append(drain)

        def start(self, src=None):
            for chunk in range(self.chunks):
                for k, off in enumerate(OFFS):
                    t = z + off
                    ok = (t >= 0) & (t < R)

                    def make(chunk=chunk, k=k, t=t):
                        mine = self.block(z, chunk)
                        return rcopy(mine if src is None else src, mine, self.base[chunk] + k, self.base[chunk] + z, plane_dev(t))

                    self.guarded(ok, make)

        def got(self, s, chunk):
            block = self.block(s, chunk)
            rcopy(block, block, self.base[chunk], self.base[chunk] + s, sibling).wait_recv()

        def relay(self, chunk=0):
            for at, passes in ((R - 2, ((3, 1), (1, 3), (0, 3))), (1, ((0, 2), (2, 0), (3, 0)))):
                for k, (s, to) in enumerate(passes):

                    @pl.when(z == at)
                    def _():
                        self.got(s, chunk)

                    def make(s=s, to=to, k=k):
                        block = self.block(s, chunk)
                        return rcopy(block, block, self.base[chunk] + 2 + k, self.base[chunk] + s, plane_dev(to))

                    self.guarded(z == at, make)

        def wait_block(self, s):
            for chunk in range(self.chunks):
                skip = z == s
                skip = skip | ((z > 0) & (z < R - 1))

                @pl.when(jnp.logical_not(skip))
                def _():
                    self.got(s, chunk)

        def wait(self):
            for s in range(R):
                self.wait_block(s)

    class Spread:
        def __init__(self, stage):
            self.stage, self.base = stage, slots(PL)

        def start(self, target):
            self.target = target
            for i in range(1, PL):
                other = lax.rem(q + i, PL)
                copy = rcopy(self.stage.at[other], target, self.base + i, self.base + i, mate(i))
                copy.start()

        def wait_send(self):
            for i in range(1, PL):
                other = lax.rem(q + i, PL)
                rcopy(self.stage.at[other], self.target, self.base + i, self.base + i, mate(i)).wait_send()

        def wait(self, block):
            for i in range(1, PL):
                rcopy(self.stage.at[0], block(lax.rem(q - i + PL, PL)), self.base + i, self.base + i, mate(i)).wait_recv()

    class Gather:
        def __init__(self, whole):
            self.whole, self.base = whole, slots(2 * C)

        def block(self, s):
            return self.whole.at[pl.ds(aligned(s * rows, 16), rows)]

        def start(self, src):
            self.local = lcopy(src, self.block(q))
            sends = []
            for i in range(1, C):
                sends.append(rcopy(src, self.block(q), self.base + i, self.base + i, row_mate(i)))
            sends.append(rcopy(src, self.block(q), self.base, self.base, sibling))
            for copy in sends:
                copy.start()
            self.sends = sends

        def drain(self):
            for copy in self.sends:
                copy.wait_send()
            for i in range(1, C):
                self.passed(i).wait_send()

        def relay(self):
            for i in range(1, C):
                self.relay_one(i)

        def passed(self, i):
            block = self.block(core * C + row_index(i))
            return rcopy(block, block, self.base + C - 1 + i, self.base + C - 1 + i, sibling)

        def relay_one(self, i):
            block = self.block(core * C + row_index(i))
            rcopy(block, block, self.base, self.base + i, sibling).wait_recv()
            self.passed(i).start()

        def wait_one(self, i):
            block = self.block((1 - core) * C + row_index(i))
            sem = self.base + jnp.where(i == 0, 0, C - 1 + i)
            rcopy(block, block, self.base, sem, sibling).wait_recv()

        def wait(self):
            for i in range(C):
                self.wait_one(i)
            self.local.wait()

        def each(self, use, first=0, last=None):
            if first == 0:
                self.local.wait()

            @pl.loop(first, C if last is None else last)
            def _(i):
                @pl.when(i > 0)
                def _():
                    self.relay_one(i)

                use(core * C + row_index(i))
                self.wait_one(i)
                use((1 - core) * C + row_index(i))

    class Reduce:
        def __init__(self, k, before=None):
            self.sibout, self.theirs = getattr(r, f"sibout{k}"), getattr(r, f"theirs{k}")
            self.out, self.got, self.own = getattr(r, f"redout{k}"), getattr(r, f"redin{k}"), getattr(r, f"redown{k}")
            self.base = slots(C + 2)
            self.before = before


        def run(self, pairs, compute, later=False, more=False, only_prepare=False):
            chunk_rows = HS // 2

            def to_sibling(chunk):
                span = pl.ds(chunk * chunk_rows, chunk_rows)
                return rcopy(self.sibout.at[span], self.theirs.at[span], self.base + C + chunk, self.base + C + chunk, sibling)

            def product(target, weights, seq, chunk):
                total = None
                for (x, _), w in zip(pairs, weights):
                    term = compute(x[pl.ds(aligned(seq * HS + chunk * chunk_rows, 16), chunk_rows), :], w)
                    total = term if total is None else total + term
                span = pl.ds(chunk * chunk_rows, chunk_rows)
                if more:
                    total = total + target[span, :].astype(F32)
                target[span, :] = total.astype(BF)

            def pass_on(chunk):
                to_sibling(chunk).wait_recv()
                for blk in range(chunk * C // 2, (chunk + 1) * C // 2):
                    i = lax.rem(blk + c, 2) + 2 * lax.rem(blk // 2 + c // 2, 2)
                    span = pl.ds(blk * rows, rows)
                    total = r.mine[span, :].astype(F32) + self.theirs[span, :].astype(F32)

                    @pl.when(i == 0)
                    def _():
                        self.own[...] = total.astype(self.own.dtype)

                    @pl.when(i != 0)
                    def _():
                        self.out[i - 1] = total.astype(BF)
                        self.to_row(i, blk).start()

            def body(*bufs):
                bufs = list(bufs)
                weights, loads = [], []
                for _, w in pairs:
                    if isinstance(w, tuple):
                        weights.append(bufs.pop(0))
                        loads.append(lcopy(w[0], weights[-1]))
                    else:
                        weights.append(w)
                for load in loads:
                    load.wait()
                if self.before is not None and not more:
                    self.before.drain()
                if only_prepare:
                    for chunk in range(2):
                        product(self.sibout, weights, 1 - core, chunk)
                        product(r.mine, weights, core, chunk)
                    return
                product(self.sibout, weights, 1 - core, 0)
                to_sibling(0).start()
                product(r.mine, weights, core, 0)
                product(self.sibout, weights, 1 - core, 1)
                to_sibling(1).start()
                if not later:
                    pass_on(0)
                product(r.mine, weights, core, 1)
                if not later:
                    pass_on(1)

            pl.run_scoped(body, *[VM(w[0].shape, BF) for _, w in pairs if isinstance(w, tuple)])
            self.drain = lambda: self.drain_all(to_sibling)
            self.pass_on = lambda: (pass_on(0), pass_on(1))

        def prepare(self, pairs, compute):
            self.run(pairs, compute, only_prepare=True)

        def to_row(self, i, blk):
            return rcopy(self.out.at[i - 1], self.got.at[i - 1], self.base + i, self.base + i, (batch, blk))

        def drain_all(self, to_sibling):
            to_sibling(0).wait_send()
            to_sibling(1).wait_send()
            for i in range(1, C):
                self.to_row(i, row_index(i)).wait_send()

        def finish(self):
            for i in range(1, C):
                rcopy(self.out.at[i - 1], self.got.at[i - 1], self.base + i, self.base + i, row_mate(i)).wait_recv()
            total = self.own[...].astype(F32)
            for i in range(1, C):
                total = total + self.got[i - 1].astype(F32)
            return total

    middle_plane = (z > 0) & (z < R - 1)
    ORDER = ((3, 2, 1, 0), (0, 3, 2, 1), (3, 0, 1, 2), (0, 1, 2, 3))

    class ZReduce:
        def __init__(self, grads, got, extra, merged, height, direct=False, chain=False):
            self.direct, self.chain = direct, chain
            self.grads, self.got, self.extra, self.merged, self.height = grads, got, extra, merged, height
            self.base = slots(12)

        def block(self, t):
            return self.grads.at[pl.ds(aligned(t * self.height, 16), self.height)]

        def guarded(self, ok, make):
            @pl.when(ok)
            def _():
                make().start()

            def drain():
                @pl.when(ok)
                def _():
                    make().wait_send()

            drains.append(drain)

        def send(self, at, owner):
            b = self.base
            via = {0: 1, R - 1: R - 2}.get(at)
            if owner == at or (via is None and abs(owner - at) == 2) or (via is None and owner == R - 1 - at):
                return
            if via is None:
                slot = 1 if owner < at else 0
                return
            elif owner == via:
                slot = 0 if at == 0 else 1
                make = lambda: rcopy(self.block(owner), self.got.at[slot], b + 2, b + slot, plane_dev(via))
            elif self.direct and abs(owner - at) == 2:
                make = lambda: rcopy(self.block(owner), self.got.at[2], b + 1, b + 6, plane_dev(owner))
            else:
                k = 0 if owner == R - 1 - at else 1
                make = lambda: rcopy(self.block(owner), self.extra.at[k], b + k, b + 2 + k, plane_dev(via))
            self.guarded(at_plane[at], make)

        def start(self):
            for step in range(R):
                self.start_step(step)

        def start_step(self, step):
            for at in range(R):
                self.send(at, ORDER[at][step])

        def add_block(self, owner, other, waited, out):
            def body(own, more, sem):
                first = pltpu.make_async_copy(self.block(owner), own, sem.at[0])
                first.start()
                waited.wait_recv()
                second = pltpu.make_async_copy(other, more, sem.at[1])
                second.start()
                first.wait()
                second.wait()
                own[...] = (own[...].astype(F32) + more[...].astype(F32)).astype(BF)
                pltpu.sync_copy(own, out)

            shape = (self.height, self.grads.shape[1])
            pl.run_scoped(body, VM(shape, BF), VM(shape, BF), pltpu.SemaphoreType.DMA((2,)))

        def merge(self, steps=(0, 1)):
            b = self.base
            if 0 in steps and not self.chain:
                for at, owner, slot in ((1, 0, 1), (2, 3, 0)):
                    self.guarded(
                        at_plane[at],
                        lambda owner=owner, slot=slot: rcopy(self.block(owner), self.got.at[slot], b + 3, b + slot, plane_dev(owner)),
                    )
            if self.direct:
                steps = (0,)
                for at, owner, slot in ((1, 2, 0), (2, 1, 1)):
                    self.guarded(
                        at_plane[at],
                        lambda owner=owner, slot=slot: rcopy(self.block(owner), self.got.at[slot], b + 5, b + slot, plane_dev(owner)),
                    )
            for k in steps:
                for at, to, slots_at in ((1, (3, 2, 0), (1, 0, 1)), (2, (0, 1, 3), (0, 1, 0))):
                    owner = to[k]

                    @pl.when(z == at)
                    def _():
                        source = self.merged.at[3] if k == 2 else self.extra.at[k]
                        self.add_block(owner, source, rcopy(source, source, b, b + (7 if k == 2 else 2 + k), sibling), self.merged.at[k])

                    def make(k=k, at=at, owner=owner, slot=slots_at[k]):
                        if k == 0 and self.chain:
                            return rcopy(self.merged.at[0], self.merged.at[3], b + 4, b + 7, plane_dev(3 - at))
                        return rcopy(self.merged.at[k], self.got.at[slot], b + 4 + k, b + slot, plane_dev(owner))

                    self.guarded(z == at, make)

        def wait(self):
            for slot, lone in ((0, 0), (1, R - 1)):

                @pl.when(z != lone if self.chain else z >= 0)
                def _():
                    rcopy(self.got.at[slot], self.got.at[slot], self.base, self.base + slot, sibling).wait_recv()

            if self.direct:

                @pl.when(middle_plane)
                def _():
                    rcopy(self.got.at[2], self.got.at[2], self.base, self.base + 6, sibling).wait_recv()

        def finish(self, put):
            self.wait()

            def body(own, one, two, *three):
                at_one, at_two = 0, 1
                if self.chain:
                    at_one, at_two = jnp.where(z == 0, 1, 0), jnp.where(z == R - 1, 0, 1)
                loads = [lcopy(self.block(z), own), lcopy(self.got.at[at_one], one), lcopy(self.got.at[at_two], two)]
                if three:
                    loads.append(lcopy(self.got.at[jnp.where(middle_plane, 2, 0)], three[0]))
                for load in loads:
                    load.wait()
                for k in range(self.height // shard):
                    span = pl.ds(k * shard, shard)
                    total = own[span, :].astype(F32) + one[span, :].astype(F32)
                    last = two[span, :].astype(F32)
                    total = total + (jnp.where(middle_plane, last, 0.0) if self.chain else last)
                    if three:
                        total = total + jnp.where(middle_plane, three[0][span, :].astype(F32), 0.0)
                    put(k, total)

            shape = (self.height, self.grads.shape[1])
            pl.run_scoped(body, *[VM(shape, BF)] * (4 if self.direct else 3))

    zg_o, zg_qkv = ZGather(r.w_o, shard), ZGather(r.w_qkv, KB, 2)
    sp_qkv = Spread(r.st_qkv)
    parts = range(len(PARTS))
    def each_part(name):
        return [getattr(r, f"{name}{p}") for p in parts]

    w_f, st_f = each_part("w_f"), each_part("st_f")
    zg_f, sp_f = [ZGather(w, KB) for w in w_f], [Spread(st) for st in st_f]
    ag_normed, ag_cot, ag_two, ag_one = Gather(r.a_normed), Gather(r.a_cot), Gather(r.a_two), Gather(r.a_one)

    def mine_rows(whole, height):
        return whole.at[pl.ds(aligned((z * PL + q) * height, 16), height)]

    zg_o.start(r.in_o)
    local_o = lcopy(r.in_o, zg_o.block(z))
    base_small = slots(PL)
    small_sent = []
    for i in range(1, PL):
        copy = rcopy(r.sgt, r.small.at[z * PL + q], base_small + i, base_small + i, mate(i))
        copy.start()
        small_sent.append(copy)
    local_small = lcopy(r.sgt, r.small.at[z * PL + q])
    def stage_qkv(v):
        lcopy(r.in_qkv, v).wait()
        for other in range(PL):
            for j in range(3):
                for zh in range(R):
                    at = j * D + zh * PL * HD + other * HD
                    r.st_qkv[other, :, lanes(j, zh)] = v[:, at : at + HD]

    pl.run_scoped(stage_qkv, VM(r.in_qkv.shape, BF))
    sp_qkv.start(mine_rows(r.w_qkv, shard))
    local_qkv = lcopy(r.st_qkv.at[q], mine_rows(r.w_qkv, shard))
    local_f = [None] * len(PARTS)

    def stage_f(*bufs):
        loads = [lcopy(source, buf) for source, buf in zip((r.in_gate, r.in_up, r.in_down), bufs)]
        for load in loads:
            load.wait()
        for p, width in enumerate(PARTS):
            for other in range(PL):
                at = other * FW + STARTS[p]
                for k, source in enumerate(bufs):
                    st_f[p][other, :, k * width : (k + 1) * width] = source[:, at : at + width]
                if WC[p] > 3 * width:
                    st_f[p][other, :, 3 * width :] = jnp.zeros((shard, WC[p] - 3 * width), BF)

    def spread_f(p):
        sp_f[p].start(mine_rows(w_f[p], shard))
        local_f[p] = lcopy(st_f[p].at[q], mine_rows(w_f[p], shard))

    def arrived(spread, whole):
        spread.wait(lambda s: whole.at[pl.ds(aligned((z * PL + s) * shard, 16), shard)])

    pl.run_scoped(stage_f, *[VM(r.in_gate.shape, BF)] * 3)
    spread_f(0)

    local_small.wait()
    for i in range(1, PL):
        rcopy(r.sgt, r.small.at[z * PL + lax.rem(q - i + PL, PL)], base_small, base_small + i, mate(i)).wait_recv()
    base_smallz = slots(R)
    plane_small = r.small.at[pl.ds(z * PL, PL)]
    for i in range(1, R):
        copy = rcopy(plane_small, plane_small, base_smallz + i, base_smallz + i, plane_dev(lax.rem(z + i, R)))
        copy.start()
        drains.append(copy.wait_send)
    local_qkv.wait()
    arrived(sp_qkv, r.w_qkv)
    zg_qkv.start()
    loads["tokens"].wait()
    loads["cot"].wait()
    tokens = r.v_tokens[...].astype(F32)
    unit, _ = norm_stats(tokens)
    for i in range(1, R):
        block = r.small.at[pl.ds(lax.rem(z - i + R, R) * PL, PL)]
        rcopy(block, block, base_smallz, base_smallz + i, sibling).wait_recv()
    for d in range(R * PL):
        for k in range(4):
            r.vec[k : k + 1, shard * d : shard * (d + 1)] = r.small[d, k : k + 1, 0:shard]
        for k in range(3):
            r.biases[3 * d + k : 3 * d + k + 1, 0:HD] = r.small[d, 4 + k : 5 + k, 0:HD]
    for j in range(3):
        for zh in range(R):
            row = r.biases[pl.ds(j * H + zh * PL + q, 1), 0:HD]
            r.bias[0:1, lanes(j, zh)] = row
    r.x_normed[...] = (unit * r.vec[0:1, :] + r.vec[1:2, :]).astype(BF)
    ag_normed.start(r.x_normed)

    spread_f(1)
    spread_f(2)
    ag_cot.start(r.v_cot)
    local_f[0].wait()
    arrived(sp_f[0], w_f[0])
    zg_qkv.relay(0)
    zg_qkv.relay(1)
    zg_o.relay()
    zg_f[0].start()
    ag_normed.relay()
    ag_normed.wait()
    zg_qkv.wait()

    def lower(shape):
        return lax.rem(lax.broadcasted_iota(jnp.int32, shape, 1), HD) < ROT // 2

    def in_turn(shape):
        return lax.rem(lax.broadcasted_iota(jnp.int32, shape, 1), HD) < ROT

    TM = HS // 2
    local_tables.wait()

    @pl.loop(0, TOK // HS)
    def _(i):
        span = pl.ds(aligned(i * HS, HS), HS)
        projected = nn(r.a_normed[span, :], r.w_qkv[...]) + r.bias[0:1, :]
        for first in [half * 3 * QH + k * 128 for half in range(2) for k in range(2 * QH // 128)]:
            part = projected[:, first : first + 128]
            other = jnp.where(lower(part.shape), pltpu.roll(part, 128 - ROT // 2, 1), pltpu.roll(part, ROT // 2, 1))
            turned = part * r.turns[0] + other * r.turns[1]
            r.qkv[span, first : first + 128] = turned.astype(BF)
        for half in range(2):
            values = slice(half * 3 * QH + 2 * QH, (half + 1) * 3 * QH)
            r.qkv[span, values] = projected[:, values].astype(BF)

    def softmax_block(queries, keys, first):
        scores = nt(keys, queries) * 0.125
        at_key = lax.broadcasted_iota(jnp.int32, scores.shape, 0)
        at_query = lax.broadcasted_iota(jnp.int32, scores.shape, 1) + first
        allowed = at_key <= at_query
        scores = jnp.where(allowed, scores, -1e30)
        largest = jnp.max(scores, axis=0, keepdims=True)
        weights = jnp.where(allowed, jnp.exp(scores - largest), 0.0)
        return weights / jnp.sum(weights, axis=0, keepdims=True)

    QB = HS // 2

    kept = []
    for seq, keep in enumerate((r.sibout1, r.theirs1)):

        for h in range(heads):
            for blk in range(HS // QB):
                here = pl.ds(seq * HS + blk * QB, QB)
                seen = pl.ds(seq * HS, (blk + 1) * QB)
                probs = softmax_block(r.qkv[here, lanes(0, h)], r.qkv[seen, lanes(1, h)], blk * QB).astype(BF)
                keep[0 : (blk + 1) * QB, h * HS + blk * QB : h * HS + (blk + 1) * QB] = probs
                r.att[here, h * HD : (h + 1) * HD] = tn(probs, r.qkv[seen, lanes(2, h)]).astype(BF)
        kept.append(lcopy(keep, r.probs.at[pl.ds(seq * HS, HS)]))

    for p in (1, 2):
        local_f[p].wait()
        arrived(sp_f[p], w_f[p])
    ag_cot.relay()
    local_o.wait()
    zg_o.wait()

    red_att = Reduce(0)
    red_att.run([(r.att, r.w_o)], lambda x, w: nn(x, w[...]))
    zg_f[0].relay()
    zg_f[1].start()
    ag_cot.wait()
    middle = r.v_tokens[...].astype(F32) + red_att.finish()
    r.middle[...] = middle
    unit, _ = norm_stats(middle)
    r.x_two[...] = (unit * r.vec[2:3, :] + r.vec[3:4, :]).astype(BF)
    for copy in kept:
        copy.wait()
    ag_two.start(r.x_two)
    zg_f[1].relay()
    zg_f[2].start()

    hid, gug, g_f = each_part("hid"), each_part("gug"), each_part("g_f")

    def feed_forward(p, then=None):
        width = PARTS[p]
        def body(w):
            loads = []
            for s in range(R):
                zg_f[p].wait_block(s)
                loads.append(lcopy(zg_f[p].block(s), w.at[pl.ds(s * KB, KB)]))
            for load in loads:
                load.wait()

            def use(span):
                both = nn(r.a_two[span, :], w[:, : 2 * width])
                gate = both[:, :width]
                up = both[:, width:]
                sig = 1.0 / (1.0 + jnp.exp(-gate))
                swish = gate * sig
                hid[p][span, :] = (swish * up).astype(BF)
                hidden_grad = nn(r.a_cot[span, :], w[:, 2 * width : 3 * width])
                gug[p][span, :width] = (hidden_grad * up * sig * (1.0 + gate * (1.0 - sig))).astype(BF)
                gug[p][span, width:] = (hidden_grad * swish).astype(BF)

            if p == 0:
                ag_two.each(lambda s: use(pl.ds(aligned(s * rows, 16), rows)))
            else:

                @pl.loop(0, TOK // TM)
                def _(i):
                    use(pl.ds(aligned(i * TM, TM), TM))

            if then is not None:
                then(w)

        pl.run_scoped(body, VM(w_f[p].shape, BF))

    def grads_by_owner(terms, out, reduce, padded=None, steps=range(R)):
        width = out.shape[1]

        def body(tile, sem):
            pending = []

            def hand_on():
                store, step = pending.pop(0)
                store.wait()
                reduce.start_step(step)

            for step in steps:
                owner = R - 1 - step
                for at in range(1, R):
                    owner = jnp.where(z == at, ORDER[at][step], owner)
                for left, right, first in terms:
                    part = tn(left[:, pl.ds(aligned(owner * KB, KB), KB)], right[...])
                    tile[step % depth, :, first : first + right.shape[1]] = part.astype(BF)
                if padded is not None:
                    tile[step % depth, :, padded:] = jnp.zeros((KB, width - padded), BF)
                store = pltpu.make_async_copy(tile.at[step % depth], reduce.block(owner), sem.at[step % depth])
                store.start()
                pending.append((store, step))
                while len(pending) > (0 if step in (0, steps[-1]) else 1):
                    hand_on()

        depth = min(2, len(steps))
        pl.run_scoped(body, VM((depth, KB, width), BF), pltpu.SemaphoreType.DMA((depth,)))

    def feed_weight_grads(p, steps=range(R)):
        width = PARTS[p]
        terms = [(r.a_two, gug[p], 0), (r.a_cot, hid[p], 2 * width)]
        grads_by_owner(terms, g_f[p], zr_f[p], 3 * width if WC[p] > 3 * width else None, steps)

    zr_f = [ZReduce(*bufs, KB, chain=True) for bufs in zip(g_f, each_part("zin_f"), each_part("zx_f"), each_part("zs_f"))]
    zr_o = ZReduce(r.g_o, r.zin_o, r.zx_o, r.zs_o, shard)
    g_q = [r.g_q0, r.g_q1]
    zr_q = [ZReduce(g_q[0], r.zin_q0, r.zx_q0, r.zs_q0, KB), ZReduce(g_q[1], r.zin_q1, r.zx_q1, r.zs_q1, KB)]

    feed_forward(0)
    zg_f[2].relay()
    feed_weight_grads(0)
    feed_forward(1)
    feed_weight_grads(1)
    red_two = Reduce(0, red_att)
    first_pairs = [(gug[p], (w_f[p].at[:, pl.ds(0, 2 * PARTS[p])],)) for p in (0, 1)]
    red_two.prepare(first_pairs, lambda x, w: nt(x, w[...]))

    def back_into_layer(w):
        feed_weight_grads(2, (0,))
        red_two.run([(gug[2], w.at[:, pl.ds(0, 2 * PARTS[2])])], lambda x, w: nt(x, w[...]), more=True)

    zr_f[0].merge((0, 1))
    feed_forward(2, back_into_layer)
    feed_weight_grads(2, (1, 2, 3))
    zr_f[0].merge((2,))
    two_grad = red_two.finish()
    unit, scale = norm_stats(r.middle[...])
    middle_grad = r.v_cot[...].astype(F32) + norm_back(two_grad, unit, scale, r.vec[2:3, :])
    r.middle_grad[...] = middle_grad
    ag_normed.drain()
    r.x_normed[...] = middle_grad.astype(BF)
    ag_one.start(r.x_normed)
    r.vec[6:7, :] = jnp.sum(two_grad * unit, axis=0, keepdims=True)
    r.vec[7:8, :] = jnp.sum(two_grad, axis=0, keepdims=True)

    zr_f[1].merge((0,))
    red_mixed = Reduce(1)
    mixed_pairs = [(hid[p], (w_f[p].at[:, pl.ds(2 * PARTS[p], WC[p] - 2 * PARTS[p])],)) for p in parts]
    red_mixed.run(mixed_pairs, lambda x, w: nt(x, w[:, : x.shape[1]]), later=True)

    attg = gug[1]

    def att_grad(s):
        span = pl.ds(aligned(s * rows, 16), rows)
        pltpu.sync_copy(ag_one.block(s), r.a_two.at[span])
        attg[span, 0:QW] = nt(r.a_two[span, :], r.w_o[...]).astype(BF)

    ag_two.drain()
    ag_cot.drain()
    zr_f[1].merge((1,))

    weights_back = lcopy(r.probs, r.a_cot)

    back_f, back_q = [Spread(st) for st in st_f], [Spread(r.st_q0), Spread(r.st_q1)]
    pin_f = each_part("pin_f")
    pin_q, st_q = [r.pin_q0, r.pin_q1], [r.st_q0, r.st_q1]

    def pin_block(got):
        return lambda s: got.at[s]

    def z_sum(reduce, sent, stage, spread, got):
        if sent is not None:
            sent.wait_send()

        def put(k, total):
            stage[k] = total.astype(BF)

        reduce.finish(put)
        spread.start(got.at[q])
        return lcopy(stage.at[q], got.at[q])

    ag_one.each(att_grad, 0, C - 1)
    local_f[0] = z_sum(zr_f[0], sp_f[0], st_f[0], back_f[0], pin_f[0])
    red_mixed.pass_on()
    ag_one.each(att_grad, C - 1, C)
    zr_f[1].merge((2,))
    def o_grad(buf):
        for k in range(R):
            span = pl.ds(k * KB, KB)
            buf[:, span] = tn(r.att[...], r.a_two[:, span]).astype(BF)
        pltpu.sync_copy(buf, r.g_o)

    pl.run_scoped(o_grad, VM((QW, D), BF))
    zr_o.start()
    zr_f[2].merge((0,))

    def attention_back(half):
        def body(turn):
            @pl.loop(0, TOK // HS)
            def _(i):
                first = i * HS
                for hh in range(heads // 2):
                    h = half * heads // 2 + hh
                    key_grad = [jnp.zeros((QB, HD), F32) for _ in range(HS // QB)]
                    value_grad = [jnp.zeros((QB, HD), F32) for _ in range(HS // QB)]
                    for blk in range(HS // QB):
                        here = pl.ds(aligned(first + blk * QB, 16), QB)
                        seen = pl.ds(aligned(first, 16), (blk + 1) * QB)
                        queries, keys, values = r.qkv[here, lanes(0, h)], r.qkv[seen, lanes(1, h)], r.qkv[seen, lanes(2, h)]
                        grads = attg[here, h * HD : (h + 1) * HD]
                        low_probs = r.a_cot[seen, h * HS + blk * QB : h * HS + (blk + 1) * QB]
                        probs = low_probs.astype(F32)
                        prob_grad = nt(values, grads)
                        delta = jnp.sum(probs * prob_grad, axis=0, keepdims=True)
                        score_grad = (probs * (prob_grad - delta)).astype(BF)
                        turn[blk * QB : (blk + 1) * QB, hh * HD : (hh + 1) * HD] = tn(score_grad, keys) * 0.125
                        key_part = nn(score_grad, queries) * 0.125
                        value_part = nn(low_probs, grads)
                        for k in range(blk + 1):
                            key_grad[k] = key_grad[k] + key_part[k * QB : (k + 1) * QB]
                            value_grad[k] = value_grad[k] + value_part[k * QB : (k + 1) * QB]
                    for k in range(HS // QB):
                        turn[k * QB : (k + 1) * QB, QH + hh * HD : QH + (hh + 1) * HD] = key_grad[k]
                        r.qkv[pl.ds(aligned(first + k * QB, 16), QB), lanes(2, h)] = value_grad[k].astype(BF)
                for k in range(2 * QH // 128):
                    part = turn[:, k * 128 : (k + 1) * 128]
                    cross = part * r.turns[1]
                    other = jnp.where(lower(part.shape), pltpu.roll(cross, 128 - ROT // 2, 1), pltpu.roll(cross, ROT // 2, 1))
                    back = part * r.turns[0] + jnp.where(in_turn(part.shape), other, 0.0)
                    at = half * 3 * QH + k * 128
                    r.qkv[pl.ds(aligned(first, 16), HS), at : at + 128] = back.astype(BF)

        pl.run_scoped(body, VM((HS, 2 * QH), F32))
        grads_by_owner([(r.a_normed, r.qkv.at[:, pl.ds(half * 3 * QH, 3 * QH)], 0)], g_q[half], zr_q[half])

    weights_back.wait()
    attention_back(0)
    attention_back(1)
    zr_f[2].merge((1,))
    zr_f[2].merge((2,))
    red_one = Reduce(0, red_two)
    red_one.run([(r.qkv, r.w_qkv)], lambda x, w: nt(x, w[...]))
    r.bias[0:1, :] = jnp.sum(r.qkv[...].astype(F32), axis=0, keepdims=True)

    zr_o.merge()
    local_f[1] = z_sum(zr_f[1], sp_f[1], st_f[1], back_f[1], pin_f[1])
    zr_q[0].merge()
    mixed = r.middle[...] + red_mixed.finish()
    r.x_two[...] = mixed.astype(BF)
    outputs = [lcopy(r.x_two, r.out_mixed)]
    local_f[2] = z_sum(zr_f[2], sp_f[2], st_f[2], back_f[2], pin_f[2])
    zr_q[1].merge()
    one_grad = red_one.finish()
    unit, scale = norm_stats(r.v_tokens[...].astype(F32))
    r.middle_grad[...] = r.middle_grad[...] + norm_back(one_grad, unit, scale, r.vec[0:1, :])
    outputs.append(lcopy(r.middle_grad, r.out_tokens))
    r.vec[4:5, :] = jnp.sum(one_grad * unit, axis=0, keepdims=True)
    r.vec[5:6, :] = jnp.sum(one_grad, axis=0, keepdims=True)
    r.sg[...] = jnp.zeros_like(r.sg)
    for d in range(R * PL):
        for k in range(4):
            r.sg[d % PL, d // PL, k : k + 1, 0:shard] = r.vec[4 + k : 5 + k, shard * d : shard * (d + 1)]
    for j in range(3):
        for zh in range(R):
            g = j * H + zh * PL + q
            piece = r.bias[0:1, lanes(j, zh)]
            r.sg[lax.rem(g // 3, PL), g // (3 * PL), pl.ds(4 + lax.rem(g, 3), 1), 0:HD] = piece
    base_sgp = slots(PL)
    for i in range(1, PL):
        other = lax.rem(q + i, PL)
        copy = rcopy(r.sg.at[other], r.sgp.at[i - 1], base_sgp + i, base_sgp + i, mate(i))
        copy.start()
        drains.append(copy.wait_send)
    zr_o.wait()
    outputs.append(lcopy(zr_o.block(z), r.own_o))
    local_f[0].wait()
    back_f[0].wait(pin_block(pin_f[0]))
    total = r.sg[q]
    for i in range(1, PL):
        rcopy(r.sgp.at[i - 1], r.sgp.at[i - 1], base_sgp, base_sgp + i, sibling).wait_recv()
        total = total + r.sgp[i - 1]
    r.sgs[...] = total
    base_sgz = slots(R)
    for i in range(1, R):
        t = lax.rem(z + i, R)
        copy = rcopy(r.sgs.at[t], r.sgz.at[i - 1], base_sgz + i, base_sgz + i, plane_dev(t))
        copy.start()
        drains.append(copy.wait_send)
    local_q = [z_sum(zr_q[half], None, st_q[half], back_q[half], pin_q[half]) for half in range(2)]
    for i in range(1, R):
        rcopy(r.sgz.at[i - 1], r.sgz.at[i - 1], base_sgz, base_sgz + i, sibling).wait_recv()
    for copy in small_sent:
        copy.wait_send()
    r.sgt[...] = r.sgs[z] + r.sgz[0] + r.sgz[1] + r.sgz[2]
    outputs.append(lcopy(r.sgt, r.out_small))
    for p in (1, 2):
        local_f[p].wait()
        back_f[p].wait(pin_block(pin_f[p]))
    for half in range(2):
        local_q[half].wait()
        back_q[half].wait(pin_block(pin_q[half]))
    for copy in outputs:
        copy.wait()
    for spread in back_f:
        spread.wait_send()
    sp_qkv.wait_send()
    for spread in back_q:
        spread.wait_send()
    ag_one.drain()
    red_mixed.drain()
    red_one.drain()
    for drain in drains:
        drain()
    assert counter[0] <= REMOTE_SEMS and local_count[0] <= LOCAL_SEMS, (counter, local_count)


def finish_outputs(got, parts, starts, planes, members, rows, shard, q_width, f_width):
    steps = 4
    tall, low = rows // steps, shard // steps

    heads = q_width // HD

    def body(mixed_in, tokens_in, small_in, pin_q0, pin_q1, own_o, zin_o, *rest):
        pins, (mixed, tokens, g0, g1, g2, g3, bias, qkv, o, gate, up, down) = rest[: len(parts)], rest[len(parts) :]
        mixed[0] = mixed_in[...]
        tokens[0] = tokens_in[...]
        o[...] = own_o[...].astype(F32) + zin_o[0].astype(F32) + zin_o[1].astype(F32)
        for k, gain in enumerate((g0, g1, g2, g3)):
            gain[...] = small_in[k : k + 1, 0:shard]
        for k in range(3):
            bias[0:1, k * HD : (k + 1) * HD] = small_in[4 + k : 5 + k, 0:HD]
        for other in range(members):
            for j in range(3):
                for zh in range(planes):
                    at = j * D + zh * members * HD + other * HD
                    pin = (pin_q0, pin_q1)[zh // (heads // 2)]
                    first = qkv_lane(j, zh % (heads // 2), heads)
                    qkv[:, at : at + HD] = pin[other, :, first : first + HD].astype(F32)
            for pin, width, start in zip(pins, parts, starts):
                at = other * f_width + start
                for k, target in enumerate((gate, up, down)):
                    target[:, at : at + width] = pin[other, :, k * width : (k + 1) * width].astype(F32)

    def tiles(shape, axis, size):
        block = tuple(size if k == axis else n for k, n in enumerate(shape))
        return pl.BlockSpec(block, lambda i: tuple(i if k == axis else 0 for k in range(len(shape))))

    ins = [
        (got["out_mixed"], 0, tall), (got["out_tokens"], 0, tall), (got["out_small"], None, 0), (got["pin_q0"], 1, low), (got["pin_q1"], 1, low),
        (got["own_o"], 0, low), (got["zin_o"], 1, low),
    ] + [(got[f"pin_f{p}"], 1, low) for p in range(len(parts))]
    outs = dict(
        mixed=((1, rows, D), BF, 1, tall), tokens=((1, rows, D), F32, 1, tall),
        g0=((1, shard), F32, None, 0), g1=((1, shard), F32, None, 0), g2=((1, shard), F32, None, 0), g3=((1, shard), F32, None, 0),
        bias=((1, 3 * HD), F32, None, 0),
        qkv=((shard, 3 * D), F32, 0, low), o=((shard, D), F32, 0, low),
        gate=((shard, FF), F32, 0, low), up=((shard, FF), F32, 0, low), down=((shard, FF), F32, 0, low),
    )
    results = pl.pallas_call(
        body,
        grid=(steps,),
        out_shape=[jax.ShapeDtypeStruct(shape, kind) for shape, kind, _, _ in outs.values()],
        in_specs=[tiles(array.shape, axis, size) for array, axis, size in ins],
        out_specs=[tiles(shape, axis, size) for shape, _, axis, size in outs.values()],
        name="finish",
    )(*[array for array, _, _ in ins])
    return dict(zip(outs, results))


def fast_local(tokens, out_grad, ln1_gain, ln1_shift, qkv_weight, qkv_bias, out_weight, ln2_gain, ln2_shift, gate_weight, up_weight, down_weight):
    planes, columns = lax.axis_size("batch") // 2, lax.axis_size("ctx")
    members = 2 * columns
    rows = tokens.shape[1]
    seq = rows * columns
    total = members * rows
    shard = qkv_weight.shape[0]
    q_width = D // members
    f_width = FF // members
    plane_rows = members * shard
    parts = (256, 256, f_width - 512)
    dims = (planes, columns, members, rows, shard, q_width, f_width, parts)
    inputs = dict(
        in_tokens=(tokens.reshape(rows, D), ANY),
        in_cot=(out_grad.reshape(rows, D), ANY),
        in_g0=(ln1_gain.reshape(1, shard), VM), in_g1=(ln1_shift.reshape(1, shard), VM),
        in_g2=(ln2_gain.reshape(1, shard), VM), in_g3=(ln2_shift.reshape(1, shard), VM), in_bias=(qkv_bias.reshape(1, 3 * HD), VM),
        in_qkv=(qkv_weight, ANY),
        in_o=(out_weight, ANY),
        in_gate=(gate_weight, ANY),
        in_up=(up_weight, ANY),
        in_down=(down_weight, ANY),
        tables=(jnp.asarray(turn_tables(seq)), ANY),
    )
    columns_f = [feed_columns(width) for width in parts]
    outs = dict(
        out_mixed=((rows, D), BF, ANY),
        out_tokens=((rows, D), F32, ANY),
        out_small=((8, 128), F32, ANY),
        pin_q0=((members, shard, 3 * q_width // 2), BF, ANY), pin_q1=((members, shard, 3 * q_width // 2), BF, ANY),
        own_o=((shard, D), BF, ANY),
        zin_o=((2, shard, D), BF, ANY),
    )
    for p, width in enumerate(columns_f):
        outs[f"pin_f{p}"] = ((members, shard, width), BF, ANY)
    final = list(outs)
    spaces = dict(
        a_one=(total, D), probs=(total, D),
        g_o=(q_width, D), zx_o=(2, shard, D), zs_o=(2, shard, D),
    )
    for half in range(2):
        spaces[f"g_q{half}"] = (D, 3 * q_width // 2)
        for kind, count in (("zin", 3), ("zx", 2), ("zs", 2)):
            spaces[f"{kind}_q{half}"] = (count, plane_rows, 3 * q_width // 2)
    for p, width in enumerate(columns_f):
        spaces[f"w_f{p}"] = spaces[f"g_f{p}"] = (D, width)
        for kind, count in (("zin", 2), ("zx", 2), ("zs", 4)):
            spaces[f"{kind}_f{p}"] = (count, plane_rows, width)
    for name, shape in spaces.items():
        outs[name] = (shape, BF, ANY)
    scratch = dict(
        v_tokens=VM((rows, D), BF), v_cot=VM((rows, D), BF),
        turns=VM((2, seq, 128), F32),
        a_normed=VM((total, D), BF), a_two=VM((total, D), BF), a_cot=VM((total, D), BF),
        w_qkv=VM((D, 3 * q_width), BF), w_o=VM((q_width, D), BF),
        qkv=VM((total, 3 * q_width), BF), att=VM((total, q_width), BF),
        st_qkv=VM((members, shard, 3 * q_width), BF),
        st_q0=VM((members, shard, 3 * q_width // 2), BF), st_q1=VM((members, shard, 3 * q_width // 2), BF),
        small=VM((planes * members, 8, 128), F32), sg=VM((members, planes, 8, 128), F32),
        sgz=VM((planes - 1, 8, 128), F32), sgs=VM((planes, 8, 128), F32), sgp=VM((members - 1, planes, 8, 128), F32), sgt=VM((8, 128), F32),
        vec=VM((8, D), F32), biases=VM((3 * H, 128), F32), bias=VM((8, 3 * q_width), F32),
        x_normed=VM((rows, D), BF), x_two=VM((rows, D), BF),
        middle=VM((rows, D), F32), middle_grad=VM((rows, D), F32),
        mine=VM((seq, D), BF),
    )
    for p, width in enumerate(parts):
        scratch[f"st_f{p}"] = VM((members, shard, columns_f[p]), BF)
        scratch[f"hid{p}"], scratch[f"gug{p}"] = VM((total, width), BF), VM((total, 2 * width), BF)
    for k in range(2):
        scratch[f"sibout{k}"] = VM((seq, D), BF)
        scratch[f"theirs{k}"] = VM((seq, D), BF)
        scratch[f"redout{k}"] = VM((columns - 1, rows, D), BF)
        scratch[f"redin{k}"] = VM((columns - 1, rows, D), BF)
        scratch[f"redown{k}"] = VM((rows, D), F32 if k == 0 else BF)
    scratch["ss"] = pltpu.SemaphoreType.DMA((REMOTE_SEMS,))
    scratch["rs"] = pltpu.SemaphoreType.DMA((REMOTE_SEMS,))
    scratch["ls"] = pltpu.SemaphoreType.DMA((LOCAL_SEMS,))
    results = pl.pallas_call(
        functools.partial(layer_kernel, dims, list(inputs), list(outs), list(scratch)),
        out_shape=[jax.ShapeDtypeStruct(shape, kind) for shape, kind, _ in outs.values()],
        in_specs=[pl.BlockSpec(memory_space=place) for _, place in inputs.values()],
        out_specs=[pl.BlockSpec(memory_space=place) for _, _, place in outs.values()],
        scratch_shapes=list(scratch.values()),
        compiler_params=pltpu.CompilerParams(collective_id=0, has_side_effects=True, vmem_limit_bytes=63 * 2**20),
        cost_estimate=pl.CostEstimate(flops=42 * 10**9, bytes_accessed=300 * 10**6, transcendentals=0),
        name="layer",
    )(*[array for array, _ in inputs.values()])
    got = dict(zip(final, results))
    f_starts = [sum(parts[:p]) for p in range(len(parts))]
    done = finish_outputs(got, parts, f_starts, planes, members, rows, shard, q_width, f_width)
    return (
        done["mixed"],
        done["tokens"],
        done["g0"].reshape(shard),
        done["g1"].reshape(shard),
        done["qkv"],
        done["bias"].reshape(3 * HD),
        done["o"],
        done["g2"].reshape(shard),
        done["g3"].reshape(shard),
        done["gate"],
        done["up"],
        done["down"],
    )


def fits(mesh):
    return mesh.shape["batch"] == 8 and mesh.shape["ctx"] == 4


def solution(mesh):
    in_specs = (
        P("batch", "ctx", None),
        P("batch", "ctx", None),
        P(("batch", "ctx")),
        P(("batch", "ctx")),
        P(("batch", "ctx"), None),
        P(("batch", "ctx")),
        P(("batch", "ctx"), None),
        P(("batch", "ctx")),
        P(("batch", "ctx")),
        P(("batch", "ctx"), None),
        P(("batch", "ctx"), None),
        P(("batch", "ctx"), None),
    )
    out_specs = (
        P("batch", "ctx", None),
        P("batch", "ctx", None),
        P(("batch", "ctx")),
        P(("batch", "ctx")),
        P(("batch", "ctx"), None),
        P(("batch", "ctx")),
        P(("batch", "ctx"), None),
        P(("batch", "ctx")),
        P(("batch", "ctx")),
        P(("batch", "ctx"), None),
        P(("batch", "ctx"), None),
        P(("batch", "ctx"), None),
    )
    body = fast_local if fits(mesh) else local
    return jax.shard_map(body, mesh=mesh, in_specs=in_specs, out_specs=out_specs, check_vma=False)
```

```python
import functools

import jax
import jax.numpy as jnp
import numpy as np
from jax import lax
from jax.experimental import pallas as pl
from jax.experimental.pallas import tpu as pltpu
from jax.sharding import PartitionSpec as P

D = 2048
FF = 5632
H = 32
HD = 64
ROT = 16


def layer_norm(values, gain, shift):
    centre = jnp.mean(values, axis=-1, keepdims=True)
    centred = values - centre
    spread = jnp.mean(centred * centred, axis=-1, keepdims=True)
    return centred * lax.rsqrt(spread + 1e-05) * gain + shift


def rotary(values, positions):
    half_dims = ROT // 2
    frequency = 10000.0 ** (-jnp.arange(half_dims, dtype=jnp.float32) * 2.0 / ROT)
    angles = positions.astype(jnp.float32)[:, None] * frequency[None, :]
    cosine_term = jnp.cos(angles)[:, None, :]
    sine_term = jnp.sin(angles)[:, None, :]
    first_half = values[..., :half_dims]
    second_half = values[..., half_dims:ROT]
    return jnp.concatenate(
        [
            first_half * cosine_term - second_half * sine_term,
            second_half * cosine_term + first_half * sine_term,
            values[..., ROT:],
        ],
        axis=-1,
    )


def swish_product(gate_value, up_value):
    return gate_value / (1.0 + jnp.exp(-gate_value)) * up_value


def project_back(left, right):
    return lax.dot_general(
        left, right, (((1,), (1,)), ((), ())), preferred_element_type=jnp.float32
    )


def outer_rows(left, right):
    return lax.dot_general(
        left, right, (((0,), (0,)), ((), ())), preferred_element_type=jnp.float32
    )


def local(
    tokens,
    out_grad,
    ln1_gain,
    ln1_shift,
    qkv_weight,
    qkv_bias,
    out_weight,
    ln2_gain,
    ln2_shift,
    gate_weight,
    up_weight,
    down_weight,
):
    local_rows = tokens.shape[1]
    seq_length = local_rows * lax.axis_size("ctx")
    inputs = tokens.reshape(local_rows, D).astype(jnp.float32)
    cotangent = out_grad.reshape(local_rows, D).astype(jnp.float32)
    places = lax.axis_index("ctx") * local_rows + jnp.arange(local_rows, dtype=jnp.int32)
    attn_set = (
        lax.all_gather(qkv_weight, ("batch", "ctx"), axis=0, tiled=True),
        lax.all_gather(out_weight, ("batch", "ctx"), axis=0, tiled=True),
        lax.all_gather(qkv_bias, ("batch", "ctx"), axis=0, tiled=True),
        lax.all_gather(ln1_gain, ("batch", "ctx"), axis=0, tiled=True),
        lax.all_gather(ln1_shift, ("batch", "ctx"), axis=0, tiled=True),
    )
    gain_one = attn_set[3].astype(jnp.float32)
    shift_one = attn_set[4].astype(jnp.float32)
    normed = layer_norm(inputs, gain_one, shift_one)
    normed_low = normed.astype(jnp.bfloat16)
    projected = jnp.dot(normed_low, attn_set[0], preferred_element_type=jnp.float32) + attn_set[
        2
    ].astype(jnp.float32)
    pair_heads = projected[:, : 2 * D].reshape(local_rows, 2 * H, HD)
    turned = rotary(pair_heads, places)
    queries = turned[:, :H].astype(jnp.bfloat16)
    key_rows = turned[:, H:].reshape(local_rows, D).astype(jnp.bfloat16)
    value_rows = projected[:, 2 * D :].astype(jnp.bfloat16)
    start_state = (
        jnp.full((H, local_rows), -1e30, jnp.float32),
        jnp.zeros((H, local_rows), jnp.float32),
        jnp.zeros((H, local_rows, HD), jnp.float32),
    )
    carry = start_state
    key_piece = lax.all_gather(key_rows, "ctx", axis=0, tiled=True)
    value_piece = lax.all_gather(value_rows, "ctx", axis=0, tiled=True)
    piece_rows = key_piece.shape[0]
    block_rows = 512
    block_count = piece_rows // block_rows

    def inner(state, block):
        largest, totals, accum = state
        key_block, value_block, offset = block
        raw_scores = (
            jnp.einsum("qhd,khd->hqk", queries, key_block, preferred_element_type=jnp.float32)
            * 0.125
        )
        key_places = offset + jnp.arange(block_rows, dtype=jnp.int32)
        allowed = (key_places[None, :] <= places[:, None])[None]
        raw_scores = jnp.where(allowed, raw_scores, -1e30)
        new_largest = jnp.maximum(largest, jnp.max(raw_scores, axis=-1))
        weights = jnp.where(allowed, jnp.exp(raw_scores - new_largest[..., None]), 0.0)
        factor = jnp.exp(largest - new_largest)
        totals = totals * factor + jnp.sum(weights, axis=-1)
        accum = accum * factor[..., None] + jnp.einsum(
            "hqk,khd->hqd",
            weights.astype(jnp.bfloat16),
            value_block,
            preferred_element_type=jnp.float32,
        )
        return ((new_largest, totals, accum), None)

    offsets = jnp.arange(block_count, dtype=jnp.int32) * block_rows
    blocks = (
        key_piece.reshape(block_count, block_rows, H, HD),
        value_piece.reshape(block_count, block_rows, H, HD),
        offsets,
    )
    carry, unused = lax.scan(inner, carry, blocks)
    largest, totals, accum = carry
    attended = jnp.transpose(accum / totals[..., None], (1, 0, 2)).reshape(local_rows, D)
    log_total = largest + jnp.log(totals)
    attended_low = attended.astype(jnp.bfloat16)
    middle = inputs + jnp.dot(attended_low, attn_set[1], preferred_element_type=jnp.float32)
    mlp_set = (
        lax.all_gather(gate_weight, ("batch", "ctx"), axis=0, tiled=True),
        lax.all_gather(up_weight, ("batch", "ctx"), axis=0, tiled=True),
        lax.all_gather(down_weight, ("batch", "ctx"), axis=0, tiled=True),
        lax.all_gather(ln2_gain, ("batch", "ctx"), axis=0, tiled=True),
        lax.all_gather(ln2_shift, ("batch", "ctx"), axis=0, tiled=True),
    )
    gain_two = mlp_set[3].astype(jnp.float32)
    shift_two = mlp_set[4].astype(jnp.float32)
    normed_two_low = layer_norm(middle, gain_two, shift_two).astype(jnp.bfloat16)
    gate_value = jnp.dot(normed_two_low, mlp_set[0], preferred_element_type=jnp.float32)
    up_value = jnp.dot(normed_two_low, mlp_set[1], preferred_element_type=jnp.float32)
    hidden_low = swish_product(gate_value, up_value).astype(jnp.bfloat16)
    mixed = (middle + project_back(hidden_low, mlp_set[2])).astype(jnp.bfloat16)
    mlp_back = (
        lax.all_gather(gate_weight, ("batch", "ctx"), axis=0, tiled=True),
        lax.all_gather(up_weight, ("batch", "ctx"), axis=0, tiled=True),
        lax.all_gather(down_weight, ("batch", "ctx"), axis=0, tiled=True),
        lax.all_gather(ln2_gain, ("batch", "ctx"), axis=0, tiled=True),
        lax.all_gather(ln2_shift, ("batch", "ctx"), axis=0, tiled=True),
    )
    attn_back = (
        lax.all_gather(qkv_weight, ("batch", "ctx"), axis=0, tiled=True),
        lax.all_gather(out_weight, ("batch", "ctx"), axis=0, tiled=True),
        lax.all_gather(qkv_bias, ("batch", "ctx"), axis=0, tiled=True),
        lax.all_gather(ln1_gain, ("batch", "ctx"), axis=0, tiled=True),
        lax.all_gather(ln1_shift, ("batch", "ctx"), axis=0, tiled=True),
    )
    branch_two = cotangent.astype(jnp.bfloat16)
    hidden_grad = jnp.dot(branch_two, mlp_back[2], preferred_element_type=jnp.float32)
    unused_value, act_pull = jax.vjp(swish_product, gate_value, up_value)
    gate_grad, up_grad = act_pull(hidden_grad)
    gate_low = gate_grad.astype(jnp.bfloat16)
    up_low = up_grad.astype(jnp.bfloat16)
    normed_two_grad = project_back(gate_low, mlp_back[0]) + project_back(up_low, mlp_back[1])
    unused_two, norm_pull_two = jax.vjp(layer_norm, middle, gain_two, shift_two)
    middle_part, gain_two_grad, shift_two_grad = norm_pull_two(normed_two_grad)
    middle_grad = cotangent + middle_part
    gate_weight_grad, up_weight_grad, down_weight_grad = (
        lax.psum_scatter(
            outer_rows(left, right).astype(jnp.bfloat16), ("batch", "ctx"), scatter_dimension=0, tiled=True
        ).astype(jnp.float32)
        for left, right in ((normed_two_low, gate_low), (normed_two_low, up_low), (branch_two, hidden_low))
    )
    branch_one = middle_grad.astype(jnp.bfloat16)
    out_term = outer_rows(attended_low, branch_one)
    attended_grad = project_back(branch_one, attn_back[1]).astype(jnp.bfloat16)
    grad_heads = attended_grad.reshape(local_rows, H, HD)
    delta = jnp.transpose(
        jnp.sum((attended_grad.astype(jnp.float32) * attended).reshape(local_rows, H, HD), axis=-1)
    )
    key_all, value_all = (
        lax.all_gather(key_rows, "ctx", axis=0, tiled=True),
        lax.all_gather(value_rows, "ctx", axis=0, tiled=True),
    )
    back_rows = 512
    back_count = seq_length // back_rows

    def back_block(query_grad, block):
        key_block, value_block, offset = block
        raw_scores = (
            jnp.einsum("qhd,khd->hqk", queries, key_block, preferred_element_type=jnp.float32)
            * 0.125
        )
        key_places = offset + jnp.arange(back_rows, dtype=jnp.int32)
        allowed = (key_places[None, :] <= places[:, None])[None]
        probs = jnp.where(allowed, jnp.exp(raw_scores - log_total[..., None]), 0.0)
        prob_grad = jnp.einsum(
            "qhd,khd->hqk", grad_heads, value_block, preferred_element_type=jnp.float32
        )
        score_grad = (probs * (prob_grad - delta[..., None])).astype(jnp.bfloat16)
        query_grad = (
            query_grad
            + jnp.einsum("hqk,khd->qhd", score_grad, key_block, preferred_element_type=jnp.float32)
            * 0.125
        )
        key_grad = (
            jnp.einsum("hqk,qhd->khd", score_grad, queries, preferred_element_type=jnp.float32)
            * 0.125
        )
        value_grad = jnp.einsum(
            "hqk,qhd->khd",
            probs.astype(jnp.bfloat16),
            grad_heads,
            preferred_element_type=jnp.float32,
        )
        return (
            query_grad,
            jnp.concatenate(
                [key_grad.reshape(back_rows, D), value_grad.reshape(back_rows, D)], axis=1
            ),
        )

    back_offsets = jnp.arange(back_count, dtype=jnp.int32) * back_rows
    back_blocks = (
        key_all.reshape(back_count, back_rows, H, HD),
        value_all.reshape(back_count, back_rows, H, HD),
        back_offsets,
    )
    query_grad, kv_terms = lax.scan(
        back_block, jnp.zeros((local_rows, H, HD), jnp.float32), back_blocks
    )
    kv_local = lax.psum_scatter(
        kv_terms.reshape(seq_length, 2 * D).astype(jnp.bfloat16),
        "ctx",
        scatter_dimension=0,
        tiled=True,
    ).astype(jnp.float32)

    def turn_heads(heads_in):
        return rotary(heads_in, places)

    unused_three, turn_pull = jax.vjp(turn_heads, pair_heads)
    pair_grad = turn_pull(
        jnp.concatenate([query_grad, kv_local[:, :D].reshape(local_rows, H, HD)], axis=1)
    )[0]
    projected_grad = jnp.concatenate(
        [pair_grad.reshape(local_rows, 2 * D), kv_local[:, D:]], axis=1
    ).astype(jnp.bfloat16)
    qkv_term = outer_rows(normed_low, projected_grad)
    bias_term = jnp.sum(projected_grad.astype(jnp.float32), axis=0)
    normed_grad = project_back(projected_grad, attn_back[0])
    unused_four, norm_pull = jax.vjp(layer_norm, inputs, gain_one, shift_one)
    input_part, gain_one_grad, shift_one_grad = norm_pull(normed_grad)
    tokens_grad = (middle_grad + input_part).reshape(1, local_rows, D)
    summed = (
        lax.psum_scatter(qkv_term, ("batch", "ctx"), scatter_dimension=0, tiled=True),
        lax.psum_scatter(out_term, ("batch", "ctx"), scatter_dimension=0, tiled=True),
        lax.psum_scatter(bias_term, ("batch", "ctx"), scatter_dimension=0, tiled=True),
        lax.psum_scatter(gain_one_grad, ("batch", "ctx"), scatter_dimension=0, tiled=True),
        lax.psum_scatter(shift_one_grad, ("batch", "ctx"), scatter_dimension=0, tiled=True),
        lax.psum_scatter(gain_two_grad, ("batch", "ctx"), scatter_dimension=0, tiled=True),
        lax.psum_scatter(shift_two_grad, ("batch", "ctx"), scatter_dimension=0, tiled=True),
    )
    return (
        mixed.reshape(1, local_rows, D),
        tokens_grad,
        summed[3],
        summed[4],
        summed[0],
        summed[2],
        summed[1],
        summed[5],
        summed[6],
        gate_weight_grad,
        up_weight_grad,
        down_weight_grad,
    )


BF = jnp.bfloat16
F32 = jnp.float32
MESH = pl.DeviceIdType.MESH
ANY = pl.ANY
VM = pltpu.VMEM
REMOTE_SEMS = 320
LOCAL_SEMS = 64


def nt(left, right):
    return lax.dot_general(left, right, (((1,), (1,)), ((), ())), preferred_element_type=F32)


def tn(left, right):
    return lax.dot_general(left, right, (((0,), (0,)), ((), ())), preferred_element_type=F32)


def nn(left, right):
    return jnp.dot(left, right, preferred_element_type=F32)


def norm_stats(values):
    centre = jnp.mean(values, axis=-1, keepdims=True)
    centred = values - centre
    spread = jnp.mean(centred * centred, axis=-1, keepdims=True)
    scale = lax.rsqrt(spread + 1e-05)
    return centred * scale, scale


def norm_back(grad, unit, scale, gain):
    weighted = grad * gain
    lead = jnp.mean(weighted, axis=-1, keepdims=True)
    tilt = jnp.mean(weighted * unit, axis=-1, keepdims=True)
    return scale * (weighted - lead - unit * tilt)


def turn_tables(length):
    half = ROT // 2
    freq = (np.float32(10000.0) ** (-np.arange(half, dtype=np.float32) * np.float32(2.0) / np.float32(ROT))).astype(np.float32)
    angles = np.arange(length, dtype=np.float32)[:, None] * freq[None, :]
    cosine, sine = np.cos(angles), np.sin(angles)
    tables = np.zeros((2, length, 128), np.float32)
    tables[0] = 1.0
    for start in (0, HD):
        tables[0, :, start : start + half] = cosine
        tables[0, :, start + half : start + ROT] = cosine
        tables[1, :, start : start + half] = -sine
        tables[1, :, start + half : start + ROT] = sine
    return tables


def aligned(value, to):
    return value if isinstance(value, int) else pl.multiple_of(value, to)


def feed_columns(width):
    return 2 * width + -(-width // 128) * 128


def qkv_lane(kind, head, heads):
    half = heads // 2
    return ((head // half * 3 + kind) * half + head % half) * HD


class Names:
    pass


def layer_kernel(dims, names_in, names_out, names_scratch, *refs):
    R, C, PL, rows, shard, QW, FW, PARTS = dims
    r = Names()
    for name, ref in zip(names_in + names_out + names_scratch, refs):
        setattr(r, name, ref)
    batch = lax.axis_index("batch")
    c = lax.axis_index("ctx")
    z = batch // 2
    core = lax.rem(batch, 2)
    q = core * C + c
    HS = PL // 2 * rows
    TOK = PL * rows
    KB = PL * shard
    STARTS = [sum(PARTS[:p]) for p in range(len(PARTS))]
    WC = [feed_columns(width) for width in PARTS]
    heads = QW // HD
    QH = QW // 2

    def lanes(kind, head):
        first = qkv_lane(kind, head, heads)
        return slice(first, first + HD)


    at_plane = [z == at for at in range(R)]
    counter = [0]
    local_count = [0]

    def slots(count):
        first = counter[0]
        counter[0] += count
        return first

    def mate(i):
        other = lax.rem(q + i, PL)
        return (z * 2 + other // C, lax.rem(other, C))

    def row_index(i):
        across, along = lax.rem(lax.rem(c, 2) + lax.rem(i, 2), 2), lax.rem(c // 2 + i // 2, 2)
        return 2 * along + across

    def row_mate(i):
        return (batch, row_index(i))

    sibling = (z * 2 + 1 - core, c)

    def plane_dev(t):
        return (t * 2 + core, c)

    def rcopy(src, dst, send, recv, dev):
        return pltpu.make_async_remote_copy(
            src_ref=src, dst_ref=dst, send_sem=r.ss.at[send], recv_sem=r.rs.at[recv], device_id=dev, device_id_type=MESH
        )

    drains = []

    def lcopy(src, dst):
        copy = pltpu.make_async_copy(src, dst, r.ls.at[local_count[0]])
        local_count[0] += 1
        copy.start()
        return copy

    barrier = pltpu.get_barrier_semaphore()
    for i in range(1, PL):
        pl.semaphore_signal(barrier, inc=1, device_id=mate(i), device_id_type=MESH)
    for i in range(1, R):
        pl.semaphore_signal(barrier, inc=1, device_id=plane_dev(lax.rem(z + i, R)), device_id_type=MESH)
    loads = {name: lcopy(getattr(r, "in_" + name), getattr(r, "v_" + name)) for name in ("tokens", "cot")}

    local_tables = lcopy(r.tables, r.turns)
    r.sgt[...] = jnp.zeros_like(r.sgt)
    for k, vector in enumerate((r.in_g0, r.in_g1, r.in_g2, r.in_g3)):
        r.sgt[k : k + 1, 0:shard] = vector[...].astype(F32)
    for k in range(3):
        r.sgt[4 + k : 5 + k, 0:HD] = r.in_bias[0:1, k * HD : (k + 1) * HD].astype(F32)

    pl.semaphore_wait(barrier, PL - 1 + R - 1)

    OFFS = (1, -1)

    class ZGather:
        def __init__(self, whole, height, chunks=1):
            self.whole, self.height, self.chunks = whole, height, chunks
            self.base = [slots(6) for _ in range(chunks)]

        def block(self, s, chunk=None):
            if chunk is None:
                return self.whole.at[pl.ds(aligned(s * self.height, 16), self.height)]
            part = self.height // self.chunks
            return self.whole.at[pl.ds(aligned(s * self.height + chunk * part, 16), part)]

        def guarded(self, ok, make):
            @pl.when(ok)
            def _():
                make().start()

            def drain():
                @pl.when(ok)
                def _():
                    make().wait_send()

            drains.append(drain)

        def start(self, src=None):
            for chunk in range(self.chunks):
                for k, off in enumerate(OFFS):
                    t = z + off
                    ok = (t >= 0) & (t < R)

                    def make(chunk=chunk, k=k, t=t):
                        mine = self.block(z, chunk)
                        return rcopy(mine if src is None else src, mine, self.base[chunk] + k, self.base[chunk] + z, plane_dev(t))

                    self.guarded(ok, make)

        def got(self, s, chunk):
            block = self.block(s, chunk)
            rcopy(block, block, self.base[chunk], self.base[chunk] + s, sibling).wait_recv()

        def relay(self, chunk=0):
            for at, passes in ((R - 2, ((3, 1), (1, 3), (0, 3))), (1, ((0, 2), (2, 0), (3, 0)))):
                for k, (s, to) in enumerate(passes):

                    @pl.when(z == at)
                    def _():
                        self.got(s, chunk)

                    def make(s=s, to=to, k=k):
                        block = self.block(s, chunk)
                        return rcopy(block, block, self.base[chunk] + 2 + k, self.base[chunk] + s, plane_dev(to))

                    self.guarded(z == at, make)

        def wait_block(self, s):
            for chunk in range(self.chunks):
                skip = z == s
                skip = skip | ((z > 0) & (z < R - 1))

                @pl.when(jnp.logical_not(skip))
                def _():
                    self.got(s, chunk)

        def wait(self):
            for s in range(R):
                self.wait_block(s)

    class Spread:
        def __init__(self, stage):
            self.stage, self.base = stage, slots(PL)

        def start(self, target):
            self.target = target
            for i in range(1, PL):
                other = lax.rem(q + i, PL)
                copy = rcopy(self.stage.at[other], target, self.base + i, self.base + i, mate(i))
                copy.start()

        def wait_send(self):
            for i in range(1, PL):
                other = lax.rem(q + i, PL)
                rcopy(self.stage.at[other], self.target, self.base + i, self.base + i, mate(i)).wait_send()

        def wait(self, block):
            for i in range(1, PL):
                rcopy(self.stage.at[0], block(lax.rem(q - i + PL, PL)), self.base + i, self.base + i, mate(i)).wait_recv()

    class Gather:
        def __init__(self, whole):
            self.whole, self.base = whole, slots(2 * C)

        def block(self, s):
            return self.whole.at[pl.ds(aligned(s * rows, 16), rows)]

        def start(self, src):
            self.local = lcopy(src, self.block(q))
            sends = []
            for i in (1, 2):
                sends.append(rcopy(src, self.block(q), self.base + i, self.base + i, row_mate(i)))
            sends.append(rcopy(src, self.block(q), self.base, self.base, sibling))
            for copy in sends:
                copy.start()
            self.sends = sends

        def half(self, s, part):
            return self.whole.at[pl.ds(aligned(s * rows + part * (rows // 2), 16), rows // 2)]

        def forward(self, i):
            part, sem = (0, self.base + 3) if i == 1 else (1, self.base + 2 * C - 1)
            half = self.half(core * C + row_index(i), part)
            return rcopy(half, half, sem, sem, row_mate(3 - i))

        def drain(self):
            for copy in self.sends:
                copy.wait_send()
            for i in (1, 2):
                self.forward(i).wait_send()
            for i in range(1, C):
                self.passed(i).wait_send()

        def relay(self):
            for i in range(1, C):
                self.relay_one(i)

        def passed(self, i):
            block = self.block(core * C + row_index(i))
            return rcopy(block, block, self.base + C - 1 + i, self.base + C - 1 + i, sibling)

        def relay_one(self, i):
            block = self.block(core * C + row_index(i))
            if i < 3:
                rcopy(block, block, self.base, self.base + i, sibling).wait_recv()
                self.forward(i).start()
            else:
                for part, sem in ((0, self.base + 3), (1, self.base + 2 * C - 1)):
                    half = self.half(core * C + row_index(i), part)
                    rcopy(half, half, self.base, sem, sibling).wait_recv()
            self.passed(i).start()

        def wait_one(self, i):
            block = self.block((1 - core) * C + row_index(i))
            sem = self.base + jnp.where(i == 0, 0, C - 1 + i)
            rcopy(block, block, self.base, sem, sibling).wait_recv()

        def wait(self):
            for i in range(C):
                self.wait_one(i)
            self.local.wait()

        def each(self, use, first=0, last=None):
            if first == 0:
                self.local.wait()

            @pl.loop(first, C if last is None else last)
            def _(i):
                @pl.when(i == 1)
                def _():
                    self.relay_one(1)
                    self.relay_one(2)

                @pl.when(i == 3)
                def _():
                    self.relay_one(3)

                use(core * C + row_index(i))
                self.wait_one(i)
                use((1 - core) * C + row_index(i))

    class Reduce:
        def __init__(self, k, before=None):
            self.sibout, self.theirs = getattr(r, f"sibout{k}"), getattr(r, f"theirs{k}")
            self.out, self.got, self.own = getattr(r, f"redout{k}"), getattr(r, f"redin{k}"), getattr(r, f"redown{k}")
            self.base = slots(C + 2)
            self.before = before


        def run(self, pairs, compute, later=False, more=False, only_prepare=False):
            chunk_rows = HS // 2

            def to_sibling(chunk):
                span = pl.ds(chunk * chunk_rows, chunk_rows)
                return rcopy(self.sibout.at[span], self.theirs.at[span], self.base + C + chunk, self.base + C + chunk, sibling)

            def product(target, weights, seq, chunk):
                total = None
                for (x, _), w in zip(pairs, weights):
                    term = compute(x[pl.ds(aligned(seq * HS + chunk * chunk_rows, 16), chunk_rows), :], w)
                    total = term if total is None else total + term
                span = pl.ds(chunk * chunk_rows, chunk_rows)
                if more:
                    total = total + target[span, :].astype(F32)
                target[span, :] = total.astype(BF)

            def pass_on(chunk):
                to_sibling(chunk).wait_recv()
                for blk in range(chunk * C // 2, (chunk + 1) * C // 2):
                    i = lax.rem(blk + c, 2) + 2 * lax.rem(blk // 2 + c // 2, 2)
                    span = pl.ds(blk * rows, rows)
                    total = r.mine[span, :].astype(F32) + self.theirs[span, :].astype(F32)

                    @pl.when(i == 0)
                    def _():
                        self.own[...] = total.astype(self.own.dtype)

                    @pl.when(i != 0)
                    def _():
                        self.out[i - 1] = total.astype(BF)
                        self.to_row(i, blk).start()

            def body(*bufs):
                bufs = list(bufs)
                weights, loads = [], []
                for _, w in pairs:
                    if isinstance(w, tuple):
                        weights.append(bufs.pop(0))
                        loads.append(lcopy(w[0], weights[-1]))
                    else:
                        weights.append(w)
                for load in loads:
                    load.wait()
                if self.before is not None and not more:
                    self.before.drain()
                if only_prepare:
                    for chunk in range(2):
                        product(self.sibout, weights, 1 - core, chunk)
                        product(r.mine, weights, core, chunk)
                    return
                product(self.sibout, weights, 1 - core, 0)
                to_sibling(0).start()
                product(r.mine, weights, core, 0)
                product(self.sibout, weights, 1 - core, 1)
                to_sibling(1).start()
                if not later:
                    pass_on(0)
                product(r.mine, weights, core, 1)
                if not later:
                    pass_on(1)

            pl.run_scoped(body, *[VM(w[0].shape, BF) for _, w in pairs if isinstance(w, tuple)])
            self.drain = lambda: self.drain_all(to_sibling)
            self.pass_on = lambda: (pass_on(0), pass_on(1))

        def prepare(self, pairs, compute):
            self.run(pairs, compute, only_prepare=True)

        def to_row(self, i, blk):
            return rcopy(self.out.at[i - 1], self.got.at[i - 1], self.base + i, self.base + i, (batch, blk))

        def drain_all(self, to_sibling):
            to_sibling(0).wait_send()
            to_sibling(1).wait_send()
            for i in range(1, C):
                self.to_row(i, row_index(i)).wait_send()

        def finish(self):
            for i in range(1, C):
                rcopy(self.out.at[i - 1], self.got.at[i - 1], self.base + i, self.base + i, row_mate(i)).wait_recv()
            total = self.own[...].astype(F32)
            for i in range(1, C):
                total = total + self.got[i - 1].astype(F32)
            return total

    middle_plane = (z > 0) & (z < R - 1)
    ORDER = ((3, 2, 1, 0), (0, 3, 2, 1), (3, 0, 1, 2), (0, 1, 2, 3))

    class ZReduce:
        def __init__(self, grads, got, extra, merged, height, direct=False, chain=False):
            self.direct, self.chain = direct, chain
            self.grads, self.got, self.extra, self.merged, self.height = grads, got, extra, merged, height
            self.base = slots(12)

        def block(self, t):
            return self.grads.at[pl.ds(aligned(t * self.height, 16), self.height)]

        def guarded(self, ok, make):
            @pl.when(ok)
            def _():
                make().start()

            def drain():
                @pl.when(ok)
                def _():
                    make().wait_send()

            drains.append(drain)

        def send(self, at, owner):
            b = self.base
            via = {0: 1, R - 1: R - 2}.get(at)
            if owner == at or (via is None and abs(owner - at) == 2) or (via is None and owner == R - 1 - at):
                return
            if via is None:
                slot = 1 if owner < at else 0
                return
            elif owner == via:
                slot = 0 if at == 0 else 1
                make = lambda: rcopy(self.block(owner), self.got.at[slot], b + 2, b + slot, plane_dev(via))
            elif self.direct and abs(owner - at) == 2:
                make = lambda: rcopy(self.block(owner), self.got.at[2], b + 1, b + 6, plane_dev(owner))
            else:
                k = 0 if owner == R - 1 - at else 1
                make = lambda: rcopy(self.block(owner), self.extra.at[k], b + k, b + 2 + k, plane_dev(via))
            self.guarded(at_plane[at], make)

        def start(self):
            for step in range(R):
                self.start_step(step)

        def start_step(self, step):
            for at in range(R):
                self.send(at, ORDER[at][step])

        def add_block(self, owner, other, waited, out):
            def body(own, more, sem):
                first = pltpu.make_async_copy(self.block(owner), own, sem.at[0])
                first.start()
                waited.wait_recv()
                second = pltpu.make_async_copy(other, more, sem.at[1])
                second.start()
                first.wait()
                second.wait()
                own[...] = (own[...].astype(F32) + more[...].astype(F32)).astype(BF)
                pltpu.sync_copy(own, out)

            shape = (self.height, self.grads.shape[1])
            pl.run_scoped(body, VM(shape, BF), VM(shape, BF), pltpu.SemaphoreType.DMA((2,)))

        def merge(self, steps=(0, 1)):
            b = self.base
            if 0 in steps and not self.chain:
                for at, owner, slot in ((1, 0, 1), (2, 3, 0)):
                    self.guarded(
                        at_plane[at],
                        lambda owner=owner, slot=slot: rcopy(self.block(owner), self.got.at[slot], b + 3, b + slot, plane_dev(owner)),
                    )
            if self.direct:
                steps = (0,)
                for at, owner, slot in ((1, 2, 0), (2, 1, 1)):
                    self.guarded(
                        at_plane[at],
                        lambda owner=owner, slot=slot: rcopy(self.block(owner), self.got.at[slot], b + 5, b + slot, plane_dev(owner)),
                    )
            for k in steps:
                for at, to, slots_at in ((1, (3, 2, 0), (1, 0, 1)), (2, (0, 1, 3), (0, 1, 0))):
                    owner = to[k]

                    @pl.when(z == at)
                    def _():
                        source = self.merged.at[3] if k == 2 else self.extra.at[k]
                        self.add_block(owner, source, rcopy(source, source, b, b + (7 if k == 2 else 2 + k), sibling), self.merged.at[k])

                    def make(k=k, at=at, owner=owner, slot=slots_at[k]):
                        if k == 0 and self.chain:
                            return rcopy(self.merged.at[0], self.merged.at[3], b + 4, b + 7, plane_dev(3 - at))
                        return rcopy(self.merged.at[k], self.got.at[slot], b + 4 + k, b + slot, plane_dev(owner))

                    self.guarded(z == at, make)

        def wait(self):
            for slot, lone in ((0, 0), (1, R - 1)):

                @pl.when(z != lone if self.chain else z >= 0)
                def _():
                    rcopy(self.got.at[slot], self.got.at[slot], self.base, self.base + slot, sibling).wait_recv()

            if self.direct:

                @pl.when(middle_plane)
                def _():
                    rcopy(self.got.at[2], self.got.at[2], self.base, self.base + 6, sibling).wait_recv()

        def finish(self, put):
            self.wait()

            def body(own, one, two, *three):
                at_one, at_two = 0, 1
                if self.chain:
                    at_one, at_two = jnp.where(z == 0, 1, 0), jnp.where(z == R - 1, 0, 1)
                loads = [lcopy(self.block(z), own), lcopy(self.got.at[at_one], one), lcopy(self.got.at[at_two], two)]
                if three:
                    loads.append(lcopy(self.got.at[jnp.where(middle_plane, 2, 0)], three[0]))
                for load in loads:
                    load.wait()
                for k in range(self.height // shard):
                    span = pl.ds(k * shard, shard)
                    total = own[span, :].astype(F32) + one[span, :].astype(F32)
                    last = two[span, :].astype(F32)
                    total = total + (jnp.where(middle_plane, last, 0.0) if self.chain else last)
                    if three:
                        total = total + jnp.where(middle_plane, three[0][span, :].astype(F32), 0.0)
                    put(k, total)

            shape = (self.height, self.grads.shape[1])
            pl.run_scoped(body, *[VM(shape, BF)] * (4 if self.direct else 3))

    zg_o, zg_qkv = ZGather(r.w_o, shard), ZGather(r.w_qkv, KB, 2)
    sp_qkv = Spread(r.st_qkv)
    parts = range(len(PARTS))
    def each_part(name):
        return [getattr(r, f"{name}{p}") for p in parts]

    w_f, st_f = each_part("w_f"), each_part("st_f")
    zg_f, sp_f = [ZGather(w, KB) for w in w_f], [Spread(st) for st in st_f]
    ag_normed, ag_cot, ag_two, ag_one = Gather(r.a_normed), Gather(r.a_cot), Gather(r.a_two), Gather(r.a_one)

    def mine_rows(whole, height):
        return whole.at[pl.ds(aligned((z * PL + q) * height, 16), height)]

    zg_o.start(r.in_o)
    local_o = lcopy(r.in_o, zg_o.block(z))
    base_small = slots(PL)
    small_sent = []
    for i in range(1, PL):
        copy = rcopy(r.sgt, r.small.at[z * PL + q], base_small + i, base_small + i, mate(i))
        copy.start()
        small_sent.append(copy)
    local_small = lcopy(r.sgt, r.small.at[z * PL + q])
    def stage_qkv(v):
        lcopy(r.in_qkv, v).wait()
        for other in range(PL):
            for j in range(3):
                for zh in range(R):
                    at = j * D + zh * PL * HD + other * HD
                    r.st_qkv[other, :, lanes(j, zh)] = v[:, at : at + HD]

    pl.run_scoped(stage_qkv, VM(r.in_qkv.shape, BF))
    sp_qkv.start(mine_rows(r.w_qkv, shard))
    local_qkv = lcopy(r.st_qkv.at[q], mine_rows(r.w_qkv, shard))
    local_f = [None] * len(PARTS)

    def stage_f(*bufs):
        loads = [lcopy(source, buf) for source, buf in zip((r.in_gate, r.in_up, r.in_down), bufs)]
        for load in loads:
            load.wait()
        for p, width in enumerate(PARTS):
            for other in range(PL):
                at = other * FW + STARTS[p]
                for k, source in enumerate(bufs):
                    st_f[p][other, :, k * width : (k + 1) * width] = source[:, at : at + width]
                if WC[p] > 3 * width:
                    st_f[p][other, :, 3 * width :] = jnp.zeros((shard, WC[p] - 3 * width), BF)

    def spread_f(p):
        sp_f[p].start(mine_rows(w_f[p], shard))
        local_f[p] = lcopy(st_f[p].at[q], mine_rows(w_f[p], shard))

    def arrived(spread, whole):
        spread.wait(lambda s: whole.at[pl.ds(aligned((z * PL + s) * shard, 16), shard)])

    pl.run_scoped(stage_f, *[VM(r.in_gate.shape, BF)] * 3)
    spread_f(0)

    local_small.wait()
    for i in range(1, PL):
        rcopy(r.sgt, r.small.at[z * PL + lax.rem(q - i + PL, PL)], base_small, base_small + i, mate(i)).wait_recv()
    base_smallz = slots(R)
    plane_small = r.small.at[pl.ds(z * PL, PL)]
    for i in range(1, R):
        copy = rcopy(plane_small, plane_small, base_smallz + i, base_smallz + i, plane_dev(lax.rem(z + i, R)))
        copy.start()
        drains.append(copy.wait_send)
    local_qkv.wait()
    arrived(sp_qkv, r.w_qkv)
    zg_qkv.start()
    loads["tokens"].wait()
    loads["cot"].wait()
    tokens = r.v_tokens[...].astype(F32)
    unit, _ = norm_stats(tokens)
    for i in range(1, R):
        block = r.small.at[pl.ds(lax.rem(z - i + R, R) * PL, PL)]
        rcopy(block, block, base_smallz, base_smallz + i, sibling).wait_recv()
    for d in range(R * PL):
        for k in range(4):
            r.vec[k : k + 1, shard * d : shard * (d + 1)] = r.small[d, k : k + 1, 0:shard]
        for k in range(3):
            r.biases[3 * d + k : 3 * d + k + 1, 0:HD] = r.small[d, 4 + k : 5 + k, 0:HD]
    for j in range(3):
        for zh in range(R):
            row = r.biases[pl.ds(j * H + zh * PL + q, 1), 0:HD]
            r.bias[0:1, lanes(j, zh)] = row
    r.x_normed[...] = (unit * r.vec[0:1, :] + r.vec[1:2, :]).astype(BF)
    ag_normed.start(r.x_normed)

    spread_f(1)
    spread_f(2)
    ag_cot.start(r.v_cot)
    local_f[0].wait()
    arrived(sp_f[0], w_f[0])
    zg_qkv.relay(0)
    zg_qkv.relay(1)
    zg_o.relay()
    zg_f[0].start()
    ag_normed.relay()
    ag_normed.wait()
    zg_qkv.wait()

    def lower(shape):
        return lax.rem(lax.broadcasted_iota(jnp.int32, shape, 1), HD) < ROT // 2

    def in_turn(shape):
        return lax.rem(lax.broadcasted_iota(jnp.int32, shape, 1), HD) < ROT

    TM = HS // 2
    local_tables.wait()

    @pl.loop(0, TOK // HS)
    def _(i):
        span = pl.ds(aligned(i * HS, HS), HS)
        projected = nn(r.a_normed[span, :], r.w_qkv[...]) + r.bias[0:1, :]
        for first in [half * 3 * QH + k * 128 for half in range(2) for k in range(2 * QH // 128)]:
            part = projected[:, first : first + 128]
            other = jnp.where(lower(part.shape), pltpu.roll(part, 128 - ROT // 2, 1), pltpu.roll(part, ROT // 2, 1))
            turned = part * r.turns[0] + other * r.turns[1]
            r.qkv[span, first : first + 128] = turned.astype(BF)
        for half in range(2):
            values = slice(half * 3 * QH + 2 * QH, (half + 1) * 3 * QH)
            r.qkv[span, values] = projected[:, values].astype(BF)

    def softmax_block(queries, keys, first):
        scores = nt(keys, queries) * 0.125
        at_key = lax.broadcasted_iota(jnp.int32, scores.shape, 0)
        at_query = lax.broadcasted_iota(jnp.int32, scores.shape, 1) + first
        allowed = at_key <= at_query
        scores = jnp.where(allowed, scores, -1e30)
        largest = jnp.max(scores, axis=0, keepdims=True)
        weights = jnp.where(allowed, jnp.exp(scores - largest), 0.0)
        return weights / jnp.sum(weights, axis=0, keepdims=True)

    QB = HS // 2

    kept = []
    for seq, keep in enumerate((r.sibout1, r.theirs1)):

        for h in range(heads):
            for blk in range(HS // QB):
                here = pl.ds(seq * HS + blk * QB, QB)
                seen = pl.ds(seq * HS, (blk + 1) * QB)
                probs = softmax_block(r.qkv[here, lanes(0, h)], r.qkv[seen, lanes(1, h)], blk * QB).astype(BF)
                keep[0 : (blk + 1) * QB, h * HS + blk * QB : h * HS + (blk + 1) * QB] = probs
                r.att[here, h * HD : (h + 1) * HD] = tn(probs, r.qkv[seen, lanes(2, h)]).astype(BF)
        kept.append(lcopy(keep, r.probs.at[pl.ds(seq * HS, HS)]))

    for p in (1, 2):
        local_f[p].wait()
        arrived(sp_f[p], w_f[p])
    ag_cot.relay()
    local_o.wait()
    zg_o.wait()

    red_att = Reduce(0)
    red_att.run([(r.att, r.w_o)], lambda x, w: nn(x, w[...]))
    zg_f[0].relay()
    zg_f[1].start()
    ag_cot.wait()
    middle = r.v_tokens[...].astype(F32) + red_att.finish()
    r.middle[...] = middle
    unit, _ = norm_stats(middle)
    r.x_two[...] = (unit * r.vec[2:3, :] + r.vec[3:4, :]).astype(BF)
    for copy in kept:
        copy.wait()
    ag_two.start(r.x_two)
    zg_f[1].relay()
    zg_f[2].start()

    hid, gug, g_f = each_part("hid"), each_part("gug"), each_part("g_f")

    def feed_forward(p, then=None):
        width = PARTS[p]
        def body(w):
            loads = []
            for s in range(R):
                zg_f[p].wait_block(s)
                loads.append(lcopy(zg_f[p].block(s), w.at[pl.ds(s * KB, KB)]))
            for load in loads:
                load.wait()

            def use(span):
                both = nn(r.a_two[span, :], w[:, : 2 * width])
                gate = both[:, :width]
                up = both[:, width:]
                sig = 1.0 / (1.0 + jnp.exp(-gate))
                swish = gate * sig
                hid[p][span, :] = (swish * up).astype(BF)
                hidden_grad = nn(r.a_cot[span, :], w[:, 2 * width : 3 * width])
                gug[p][span, :width] = (hidden_grad * up * sig * (1.0 + gate * (1.0 - sig))).astype(BF)
                gug[p][span, width:] = (hidden_grad * swish).astype(BF)

            if p == 0:
                ag_two.each(lambda s: use(pl.ds(aligned(s * rows, 16), rows)))
            else:

                @pl.loop(0, TOK // TM)
                def _(i):
                    use(pl.ds(aligned(i * TM, TM), TM))

            if then is not None:
                then(w)

        pl.run_scoped(body, VM(w_f[p].shape, BF))

    def grads_by_owner(terms, out, reduce, padded=None, steps=range(R)):
        width = out.shape[1]

        def body(tile, sem):
            pending = []

            def hand_on():
                store, step = pending.pop(0)
                store.wait()
                reduce.start_step(step)

            for step in steps:
                owner = R - 1 - step
                for at in range(1, R):
                    owner = jnp.where(z == at, ORDER[at][step], owner)
                for left, right, first in terms:
                    part = tn(left[:, pl.ds(aligned(owner * KB, KB), KB)], right[...])
                    tile[step % depth, :, first : first + right.shape[1]] = part.astype(BF)
                if padded is not None:
                    tile[step % depth, :, padded:] = jnp.zeros((KB, width - padded), BF)
                store = pltpu.make_async_copy(tile.at[step % depth], reduce.block(owner), sem.at[step % depth])
                store.start()
                pending.append((store, step))
                while len(pending) > (0 if step in (0, steps[-1]) else 1):
                    hand_on()

        depth = min(2, len(steps))
        pl.run_scoped(body, VM((depth, KB, width), BF), pltpu.SemaphoreType.DMA((depth,)))

    def feed_weight_grads(p, steps=range(R)):
        width = PARTS[p]
        terms = [(r.a_two, gug[p], 0), (r.a_cot, hid[p], 2 * width)]
        grads_by_owner(terms, g_f[p], zr_f[p], 3 * width if WC[p] > 3 * width else None, steps)

    zr_f = [ZReduce(*bufs, KB, chain=True) for bufs in zip(g_f, each_part("zin_f"), each_part("zx_f"), each_part("zs_f"))]
    zr_o = ZReduce(r.g_o, r.zin_o, r.zx_o, r.zs_o, shard)
    g_q = [r.g_q0, r.g_q1]
    zr_q = [ZReduce(g_q[0], r.zin_q0, r.zx_q0, r.zs_q0, KB, chain=True), ZReduce(g_q[1], r.zin_q1, r.zx_q1, r.zs_q1, KB)]

    feed_forward(0)
    zg_f[2].relay()
    feed_weight_grads(0)
    feed_forward(1)
    feed_weight_grads(1)
    red_two = Reduce(0, red_att)
    first_pairs = [(gug[p], (w_f[p].at[:, pl.ds(0, 2 * PARTS[p])],)) for p in (0, 1)]
    red_two.prepare(first_pairs, lambda x, w: nt(x, w[...]))

    def back_into_layer(w):
        feed_weight_grads(2, (0,))
        red_two.run([(gug[2], w.at[:, pl.ds(0, 2 * PARTS[2])])], lambda x, w: nt(x, w[...]), more=True)

    zr_f[0].merge((0, 1))
    feed_forward(2, back_into_layer)
    feed_weight_grads(2, (1, 2, 3))
    zr_f[0].merge((2,))
    two_grad = red_two.finish()
    unit, scale = norm_stats(r.middle[...])
    middle_grad = r.v_cot[...].astype(F32) + norm_back(two_grad, unit, scale, r.vec[2:3, :])
    r.middle_grad[...] = middle_grad
    ag_normed.drain()
    r.x_normed[...] = middle_grad.astype(BF)
    ag_one.start(r.x_normed)
    r.vec[6:7, :] = jnp.sum(two_grad * unit, axis=0, keepdims=True)
    r.vec[7:8, :] = jnp.sum(two_grad, axis=0, keepdims=True)

    zr_f[1].merge((0,))
    red_mixed = Reduce(1)
    mixed_pairs = [(hid[p], (w_f[p].at[:, pl.ds(2 * PARTS[p], WC[p] - 2 * PARTS[p])],)) for p in parts]
    red_mixed.run(mixed_pairs, lambda x, w: nt(x, w[:, : x.shape[1]]), later=True)

    attg = gug[1]

    def att_grad(s):
        span = pl.ds(aligned(s * rows, 16), rows)
        pltpu.sync_copy(ag_one.block(s), r.a_two.at[span])
        attg[span, 0:QW] = nt(r.a_two[span, :], r.w_o[...]).astype(BF)

    ag_two.drain()
    ag_cot.drain()
    zr_f[1].merge((1,))

    weights_back = lcopy(r.probs, r.a_cot)

    back_f, back_q = [Spread(st) for st in st_f], [Spread(r.st_q0), Spread(r.st_q1)]
    pin_f = each_part("pin_f")
    pin_q, st_q = [r.pin_q0, r.pin_q1], [r.st_q0, r.st_q1]

    def pin_block(got):
        return lambda s: got.at[s]

    def z_sum(reduce, sent, stage, spread, got):
        if sent is not None:
            sent.wait_send()

        def put(k, total):
            stage[k] = total.astype(BF)

        reduce.finish(put)
        spread.start(got.at[q])
        return lcopy(stage.at[q], got.at[q])

    ag_one.each(att_grad, 0, C - 1)
    local_f[0] = z_sum(zr_f[0], sp_f[0], st_f[0], back_f[0], pin_f[0])
    red_mixed.pass_on()
    ag_one.each(att_grad, C - 1, C)
    zr_f[1].merge((2,))
    def o_grad(buf):
        for k in range(R):
            span = pl.ds(k * KB, KB)
            buf[:, span] = tn(r.att[...], r.a_two[:, span]).astype(BF)
        pltpu.sync_copy(buf, r.g_o)

    pl.run_scoped(o_grad, VM((QW, D), BF))
    zr_o.start()
    zr_f[2].merge((0,))

    def attention_back(half):
        def body(turn):
            @pl.loop(0, TOK // HS)
            def _(i):
                first = i * HS
                for hh in range(heads // 2):
                    h = half * heads // 2 + hh
                    key_grad = [jnp.zeros((QB, HD), F32) for _ in range(HS // QB)]
                    value_grad = [jnp.zeros((QB, HD), F32) for _ in range(HS // QB)]
                    for blk in range(HS // QB):
                        here = pl.ds(aligned(first + blk * QB, 16), QB)
                        seen = pl.ds(aligned(first, 16), (blk + 1) * QB)
                        queries, keys, values = r.qkv[here, lanes(0, h)], r.qkv[seen, lanes(1, h)], r.qkv[seen, lanes(2, h)]
                        grads = attg[here, h * HD : (h + 1) * HD]
                        low_probs = r.a_cot[seen, h * HS + blk * QB : h * HS + (blk + 1) * QB]
                        probs = low_probs.astype(F32)
                        prob_grad = nt(values, grads)
                        delta = jnp.sum(probs * prob_grad, axis=0, keepdims=True)
                        score_grad = (probs * (prob_grad - delta)).astype(BF)
                        turn[blk * QB : (blk + 1) * QB, hh * HD : (hh + 1) * HD] = tn(score_grad, keys) * 0.125
                        key_part = nn(score_grad, queries) * 0.125
                        value_part = nn(low_probs, grads)
                        for k in range(blk + 1):
                            key_grad[k] = key_grad[k] + key_part[k * QB : (k + 1) * QB]
                            value_grad[k] = value_grad[k] + value_part[k * QB : (k + 1) * QB]
                    for k in range(HS // QB):
                        turn[k * QB : (k + 1) * QB, QH + hh * HD : QH + (hh + 1) * HD] = key_grad[k]
                        r.qkv[pl.ds(aligned(first + k * QB, 16), QB), lanes(2, h)] = value_grad[k].astype(BF)
                for k in range(2 * QH // 128):
                    part = turn[:, k * 128 : (k + 1) * 128]
                    cross = part * r.turns[1]
                    other = jnp.where(lower(part.shape), pltpu.roll(cross, 128 - ROT // 2, 1), pltpu.roll(cross, ROT // 2, 1))
                    back = part * r.turns[0] + jnp.where(in_turn(part.shape), other, 0.0)
                    at = half * 3 * QH + k * 128
                    r.qkv[pl.ds(aligned(first, 16), HS), at : at + 128] = back.astype(BF)

        pl.run_scoped(body, VM((HS, 2 * QH), F32))
        grads_by_owner([(r.a_normed, r.qkv.at[:, pl.ds(half * 3 * QH, 3 * QH)], 0)], g_q[half], zr_q[half])

    early = list(drains)
    drains.clear()
    weights_back.wait()
    attention_back(0)
    attention_back(1)
    zr_f[2].merge((1,))
    zr_f[2].merge((2,))
    red_one = Reduce(0, red_two)
    red_one.run([(r.qkv, r.w_qkv)], lambda x, w: nt(x, w[...]))
    r.bias[0:1, :] = jnp.sum(r.qkv[...].astype(F32), axis=0, keepdims=True)

    zr_o.merge()
    local_f[1] = z_sum(zr_f[1], sp_f[1], st_f[1], back_f[1], pin_f[1])
    zr_q[0].merge((0, 1))
    mixed = r.middle[...] + red_mixed.finish()
    r.x_two[...] = mixed.astype(BF)
    outputs = [lcopy(r.x_two, r.out_mixed)]
    local_f[2] = z_sum(zr_f[2], sp_f[2], st_f[2], back_f[2], pin_f[2])
    zr_q[0].merge((2,))
    zr_q[1].merge()
    for drain in early:
        drain()
    one_grad = red_one.finish()
    unit, scale = norm_stats(r.v_tokens[...].astype(F32))
    r.middle_grad[...] = r.middle_grad[...] + norm_back(one_grad, unit, scale, r.vec[0:1, :])
    outputs.append(lcopy(r.middle_grad, r.out_tokens))
    r.vec[4:5, :] = jnp.sum(one_grad * unit, axis=0, keepdims=True)
    r.vec[5:6, :] = jnp.sum(one_grad, axis=0, keepdims=True)
    r.sg[...] = jnp.zeros_like(r.sg)
    for d in range(R * PL):
        for k in range(4):
            r.sg[d % PL, d // PL, k : k + 1, 0:shard] = r.vec[4 + k : 5 + k, shard * d : shard * (d + 1)]
    for j in range(3):
        for zh in range(R):
            g = j * H + zh * PL + q
            piece = r.bias[0:1, lanes(j, zh)]
            r.sg[lax.rem(g // 3, PL), g // (3 * PL), pl.ds(4 + lax.rem(g, 3), 1), 0:HD] = piece
    base_sgp = slots(PL)
    for i in range(1, PL):
        other = lax.rem(q + i, PL)
        copy = rcopy(r.sg.at[other], r.sgp.at[i - 1], base_sgp + i, base_sgp + i, mate(i))
        copy.start()
        drains.append(copy.wait_send)
    zr_o.wait()
    outputs.append(lcopy(zr_o.block(z), r.own_o))
    local_f[0].wait()
    back_f[0].wait(pin_block(pin_f[0]))
    total = r.sg[q]
    for i in range(1, PL):
        rcopy(r.sgp.at[i - 1], r.sgp.at[i - 1], base_sgp, base_sgp + i, sibling).wait_recv()
        total = total + r.sgp[i - 1]
    r.sgs[...] = total
    base_sgz = slots(R)
    for i in range(1, R):
        t = lax.rem(z + i, R)
        copy = rcopy(r.sgs.at[t], r.sgz.at[i - 1], base_sgz + i, base_sgz + i, plane_dev(t))
        copy.start()
        drains.append(copy.wait_send)
    local_q = [z_sum(zr_q[half], None, st_q[half], back_q[half], pin_q[half]) for half in range(2)]
    for i in range(1, R):
        rcopy(r.sgz.at[i - 1], r.sgz.at[i - 1], base_sgz, base_sgz + i, sibling).wait_recv()
    for copy in small_sent:
        copy.wait_send()
    r.sgt[...] = r.sgs[z] + r.sgz[0] + r.sgz[1] + r.sgz[2]
    outputs.append(lcopy(r.sgt, r.out_small))
    for p in (1, 2):
        local_f[p].wait()
        back_f[p].wait(pin_block(pin_f[p]))
    for half in range(2):
        local_q[half].wait()
        back_q[half].wait(pin_block(pin_q[half]))
    for copy in outputs:
        copy.wait()
    for spread in back_f:
        spread.wait_send()
    sp_qkv.wait_send()
    for spread in back_q:
        spread.wait_send()
    ag_one.drain()
    red_mixed.drain()
    red_one.drain()
    for drain in drains:
        drain()
    assert counter[0] <= REMOTE_SEMS and local_count[0] <= LOCAL_SEMS, (counter, local_count)


def finish_outputs(got, parts, starts, planes, members, rows, shard, q_width, f_width):
    steps = 4
    tall, low = rows // steps, shard // steps

    heads = q_width // HD

    def body(mixed_in, tokens_in, small_in, pin_q0, pin_q1, own_o, zin_o, *rest):
        pins, (mixed, tokens, g0, g1, g2, g3, bias, qkv, o, gate, up, down) = rest[: len(parts)], rest[len(parts) :]
        mixed[0] = mixed_in[...]
        tokens[0] = tokens_in[...]
        o[...] = own_o[...].astype(F32) + zin_o[0].astype(F32) + zin_o[1].astype(F32)
        for k, gain in enumerate((g0, g1, g2, g3)):
            gain[...] = small_in[k : k + 1, 0:shard]
        for k in range(3):
            bias[0:1, k * HD : (k + 1) * HD] = small_in[4 + k : 5 + k, 0:HD]
        for other in range(members):
            for j in range(3):
                for zh in range(planes):
                    at = j * D + zh * members * HD + other * HD
                    pin = (pin_q0, pin_q1)[zh // (heads // 2)]
                    first = qkv_lane(j, zh % (heads // 2), heads)
                    qkv[:, at : at + HD] = pin[other, :, first : first + HD].astype(F32)
            for pin, width, start in zip(pins, parts, starts):
                at = other * f_width + start
                for k, target in enumerate((gate, up, down)):
                    target[:, at : at + width] = pin[other, :, k * width : (k + 1) * width].astype(F32)

    def tiles(shape, axis, size):
        block = tuple(size if k == axis else n for k, n in enumerate(shape))
        return pl.BlockSpec(block, lambda i: tuple(i if k == axis else 0 for k in range(len(shape))))

    ins = [
        (got["out_mixed"], 0, tall), (got["out_tokens"], 0, tall), (got["out_small"], None, 0), (got["pin_q0"], 1, low), (got["pin_q1"], 1, low),
        (got["own_o"], 0, low), (got["zin_o"], 1, low),
    ] + [(got[f"pin_f{p}"], 1, low) for p in range(len(parts))]
    outs = dict(
        mixed=((1, rows, D), BF, 1, tall), tokens=((1, rows, D), F32, 1, tall),
        g0=((1, shard), F32, None, 0), g1=((1, shard), F32, None, 0), g2=((1, shard), F32, None, 0), g3=((1, shard), F32, None, 0),
        bias=((1, 3 * HD), F32, None, 0),
        qkv=((shard, 3 * D), F32, 0, low), o=((shard, D), F32, 0, low),
        gate=((shard, FF), F32, 0, low), up=((shard, FF), F32, 0, low), down=((shard, FF), F32, 0, low),
    )
    results = pl.pallas_call(
        body,
        grid=(steps,),
        out_shape=[jax.ShapeDtypeStruct(shape, kind) for shape, kind, _, _ in outs.values()],
        in_specs=[tiles(array.shape, axis, size) for array, axis, size in ins],
        out_specs=[tiles(shape, axis, size) for shape, _, axis, size in outs.values()],
        name="finish",
    )(*[array for array, _, _ in ins])
    return dict(zip(outs, results))


def fast_local(tokens, out_grad, ln1_gain, ln1_shift, qkv_weight, qkv_bias, out_weight, ln2_gain, ln2_shift, gate_weight, up_weight, down_weight):
    planes, columns = lax.axis_size("batch") // 2, lax.axis_size("ctx")
    members = 2 * columns
    rows = tokens.shape[1]
    seq = rows * columns
    total = members * rows
    shard = qkv_weight.shape[0]
    q_width = D // members
    f_width = FF // members
    plane_rows = members * shard
    parts = (256, 256, f_width - 512)
    dims = (planes, columns, members, rows, shard, q_width, f_width, parts)
    inputs = dict(
        in_tokens=(tokens.reshape(rows, D), ANY),
        in_cot=(out_grad.reshape(rows, D), ANY),
        in_g0=(ln1_gain.reshape(1, shard), VM), in_g1=(ln1_shift.reshape(1, shard), VM),
        in_g2=(ln2_gain.reshape(1, shard), VM), in_g3=(ln2_shift.reshape(1, shard), VM), in_bias=(qkv_bias.reshape(1, 3 * HD), VM),
        in_qkv=(qkv_weight, ANY),
        in_o=(out_weight, ANY),
        in_gate=(gate_weight, ANY),
        in_up=(up_weight, ANY),
        in_down=(down_weight, ANY),
        tables=(jnp.asarray(turn_tables(seq)), ANY),
    )
    columns_f = [feed_columns(width) for width in parts]
    outs = dict(
        out_mixed=((rows, D), BF, ANY),
        out_tokens=((rows, D), F32, ANY),
        out_small=((8, 128), F32, ANY),
        pin_q0=((members, shard, 3 * q_width // 2), BF, ANY), pin_q1=((members, shard, 3 * q_width // 2), BF, ANY),
        own_o=((shard, D), BF, ANY),
        zin_o=((2, shard, D), BF, ANY),
    )
    for p, width in enumerate(columns_f):
        outs[f"pin_f{p}"] = ((members, shard, width), BF, ANY)
    final = list(outs)
    spaces = dict(
        a_one=(total, D), probs=(total, D),
        g_o=(q_width, D), zx_o=(2, shard, D), zs_o=(2, shard, D),
    )
    for half in range(2):
        spaces[f"g_q{half}"] = (D, 3 * q_width // 2)
        for kind, count in (("zin", 3), ("zx", 2), ("zs", 4)):
            spaces[f"{kind}_q{half}"] = (count, plane_rows, 3 * q_width // 2)
    for p, width in enumerate(columns_f):
        spaces[f"w_f{p}"] = spaces[f"g_f{p}"] = (D, width)
        for kind, count in (("zin", 2), ("zx", 2), ("zs", 4)):
            spaces[f"{kind}_f{p}"] = (count, plane_rows, width)
    for name, shape in spaces.items():
        outs[name] = (shape, BF, ANY)
    scratch = dict(
        v_tokens=VM((rows, D), BF), v_cot=VM((rows, D), BF),
        turns=VM((2, seq, 128), F32),
        a_normed=VM((total, D), BF), a_two=VM((total, D), BF), a_cot=VM((total, D), BF),
        w_qkv=VM((D, 3 * q_width), BF), w_o=VM((q_width, D), BF),
        qkv=VM((total, 3 * q_width), BF), att=VM((total, q_width), BF),
        st_qkv=VM((members, shard, 3 * q_width), BF),
        st_q0=VM((members, shard, 3 * q_width // 2), BF), st_q1=VM((members, shard, 3 * q_width // 2), BF),
        small=VM((planes * members, 8, 128), F32), sg=VM((members, planes, 8, 128), F32),
        sgz=VM((planes - 1, 8, 128), F32), sgs=VM((planes, 8, 128), F32), sgp=VM((members - 1, planes, 8, 128), F32), sgt=VM((8, 128), F32),
        vec=VM((8, D), F32), biases=VM((3 * H, 128), F32), bias=VM((8, 3 * q_width), F32),
        x_normed=VM((rows, D), BF), x_two=VM((rows, D), BF),
        middle=VM((rows, D), F32), middle_grad=VM((rows, D), F32),
        mine=VM((seq, D), BF),
    )
    for p, width in enumerate(parts):
        scratch[f"st_f{p}"] = VM((members, shard, columns_f[p]), BF)
        scratch[f"hid{p}"], scratch[f"gug{p}"] = VM((total, width), BF), VM((total, 2 * width), BF)
    for k in range(2):
        scratch[f"sibout{k}"] = VM((seq, D), BF)
        scratch[f"theirs{k}"] = VM((seq, D), BF)
        scratch[f"redout{k}"] = VM((columns - 1, rows, D), BF)
        scratch[f"redin{k}"] = VM((columns - 1, rows, D), BF)
        scratch[f"redown{k}"] = VM((rows, D), F32 if k == 0 else BF)
    scratch["ss"] = pltpu.SemaphoreType.DMA((REMOTE_SEMS,))
    scratch["rs"] = pltpu.SemaphoreType.DMA((REMOTE_SEMS,))
    scratch["ls"] = pltpu.SemaphoreType.DMA((LOCAL_SEMS,))
    results = pl.pallas_call(
        functools.partial(layer_kernel, dims, list(inputs), list(outs), list(scratch)),
        out_shape=[jax.ShapeDtypeStruct(shape, kind) for shape, kind, _ in outs.values()],
        in_specs=[pl.BlockSpec(memory_space=place) for _, place in inputs.values()],
        out_specs=[pl.BlockSpec(memory_space=place) for _, _, place in outs.values()],
        scratch_shapes=list(scratch.values()),
        compiler_params=pltpu.CompilerParams(collective_id=0, has_side_effects=True, vmem_limit_bytes=63 * 2**20),
        cost_estimate=pl.CostEstimate(flops=42 * 10**9, bytes_accessed=300 * 10**6, transcendentals=0),
        name="layer",
    )(*[array for array, _ in inputs.values()])
    got = dict(zip(final, results))
    f_starts = [sum(parts[:p]) for p in range(len(parts))]
    done = finish_outputs(got, parts, f_starts, planes, members, rows, shard, q_width, f_width)
    return (
        done["mixed"],
        done["tokens"],
        done["g0"].reshape(shard),
        done["g1"].reshape(shard),
        done["qkv"],
        done["bias"].reshape(3 * HD),
        done["o"],
        done["g2"].reshape(shard),
        done["g3"].reshape(shard),
        done["gate"],
        done["up"],
        done["down"],
    )


def fits(mesh):
    return mesh.shape["batch"] == 8 and mesh.shape["ctx"] == 4


def solution(mesh):
    in_specs = (
        P("batch", "ctx", None),
        P("batch", "ctx", None),
        P(("batch", "ctx")),
        P(("batch", "ctx")),
        P(("batch", "ctx"), None),
        P(("batch", "ctx")),
        P(("batch", "ctx"), None),
        P(("batch", "ctx")),
        P(("batch", "ctx")),
        P(("batch", "ctx"), None),
        P(("batch", "ctx"), None),
        P(("batch", "ctx"), None),
    )
    out_specs = (
        P("batch", "ctx", None),
        P("batch", "ctx", None),
        P(("batch", "ctx")),
        P(("batch", "ctx")),
        P(("batch", "ctx"), None),
        P(("batch", "ctx")),
        P(("batch", "ctx"), None),
        P(("batch", "ctx")),
        P(("batch", "ctx")),
        P(("batch", "ctx"), None),
        P(("batch", "ctx"), None),
        P(("batch", "ctx"), None),
    )
    body = fast_local if fits(mesh) else local
    return jax.shard_map(body, mesh=mesh, in_specs=in_specs, out_specs=out_specs, check_vma=False)
```

```python
import functools

import jax
import jax.numpy as jnp
import numpy as np
from jax import lax
from jax.experimental import pallas as pl
from jax.experimental.pallas import tpu as pltpu
from jax.sharding import PartitionSpec as P

D = 2048
FF = 5632
H = 32
HD = 64
ROT = 16


def layer_norm(values, gain, shift):
    centre = jnp.mean(values, axis=-1, keepdims=True)
    centred = values - centre
    spread = jnp.mean(centred * centred, axis=-1, keepdims=True)
    return centred * lax.rsqrt(spread + 1e-05) * gain + shift


def rotary(values, positions):
    half_dims = ROT // 2
    frequency = 10000.0 ** (-jnp.arange(half_dims, dtype=jnp.float32) * 2.0 / ROT)
    angles = positions.astype(jnp.float32)[:, None] * frequency[None, :]
    cosine_term = jnp.cos(angles)[:, None, :]
    sine_term = jnp.sin(angles)[:, None, :]
    first_half = values[..., :half_dims]
    second_half = values[..., half_dims:ROT]
    return jnp.concatenate(
        [
            first_half * cosine_term - second_half * sine_term,
            second_half * cosine_term + first_half * sine_term,
            values[..., ROT:],
        ],
        axis=-1,
    )


def swish_product(gate_value, up_value):
    return gate_value / (1.0 + jnp.exp(-gate_value)) * up_value


def project_back(left, right):
    return lax.dot_general(
        left, right, (((1,), (1,)), ((), ())), preferred_element_type=jnp.float32
    )


def outer_rows(left, right):
    return lax.dot_general(
        left, right, (((0,), (0,)), ((), ())), preferred_element_type=jnp.float32
    )


def local(
    tokens,
    out_grad,
    ln1_gain,
    ln1_shift,
    qkv_weight,
    qkv_bias,
    out_weight,
    ln2_gain,
    ln2_shift,
    gate_weight,
    up_weight,
    down_weight,
):
    local_rows = tokens.shape[1]
    seq_length = local_rows * lax.axis_size("ctx")
    inputs = tokens.reshape(local_rows, D).astype(jnp.float32)
    cotangent = out_grad.reshape(local_rows, D).astype(jnp.float32)
    places = lax.axis_index("ctx") * local_rows + jnp.arange(local_rows, dtype=jnp.int32)
    attn_set = (
        lax.all_gather(qkv_weight, ("batch", "ctx"), axis=0, tiled=True),
        lax.all_gather(out_weight, ("batch", "ctx"), axis=0, tiled=True),
        lax.all_gather(qkv_bias, ("batch", "ctx"), axis=0, tiled=True),
        lax.all_gather(ln1_gain, ("batch", "ctx"), axis=0, tiled=True),
        lax.all_gather(ln1_shift, ("batch", "ctx"), axis=0, tiled=True),
    )
    gain_one = attn_set[3].astype(jnp.float32)
    shift_one = attn_set[4].astype(jnp.float32)
    normed = layer_norm(inputs, gain_one, shift_one)
    normed_low = normed.astype(jnp.bfloat16)
    projected = jnp.dot(normed_low, attn_set[0], preferred_element_type=jnp.float32) + attn_set[
        2
    ].astype(jnp.float32)
    pair_heads = projected[:, : 2 * D].reshape(local_rows, 2 * H, HD)
    turned = rotary(pair_heads, places)
    queries = turned[:, :H].astype(jnp.bfloat16)
    key_rows = turned[:, H:].reshape(local_rows, D).astype(jnp.bfloat16)
    value_rows = projected[:, 2 * D :].astype(jnp.bfloat16)
    start_state = (
        jnp.full((H, local_rows), -1e30, jnp.float32),
        jnp.zeros((H, local_rows), jnp.float32),
        jnp.zeros((H, local_rows, HD), jnp.float32),
    )
    carry = start_state
    key_piece = lax.all_gather(key_rows, "ctx", axis=0, tiled=True)
    value_piece = lax.all_gather(value_rows, "ctx", axis=0, tiled=True)
    piece_rows = key_piece.shape[0]
    block_rows = 512
    block_count = piece_rows // block_rows

    def inner(state, block):
        largest, totals, accum = state
        key_block, value_block, offset = block
        raw_scores = (
            jnp.einsum("qhd,khd->hqk", queries, key_block, preferred_element_type=jnp.float32)
            * 0.125
        )
        key_places = offset + jnp.arange(block_rows, dtype=jnp.int32)
        allowed = (key_places[None, :] <= places[:, None])[None]
        raw_scores = jnp.where(allowed, raw_scores, -1e30)
        new_largest = jnp.maximum(largest, jnp.max(raw_scores, axis=-1))
        weights = jnp.where(allowed, jnp.exp(raw_scores - new_largest[..., None]), 0.0)
        factor = jnp.exp(largest - new_largest)
        totals = totals * factor + jnp.sum(weights, axis=-1)
        accum = accum * factor[..., None] + jnp.einsum(
            "hqk,khd->hqd",
            weights.astype(jnp.bfloat16),
            value_block,
            preferred_element_type=jnp.float32,
        )
        return ((new_largest, totals, accum), None)

    offsets = jnp.arange(block_count, dtype=jnp.int32) * block_rows
    blocks = (
        key_piece.reshape(block_count, block_rows, H, HD),
        value_piece.reshape(block_count, block_rows, H, HD),
        offsets,
    )
    carry, unused = lax.scan(inner, carry, blocks)
    largest, totals, accum = carry
    attended = jnp.transpose(accum / totals[..., None], (1, 0, 2)).reshape(local_rows, D)
    log_total = largest + jnp.log(totals)
    attended_low = attended.astype(jnp.bfloat16)
    middle = inputs + jnp.dot(attended_low, attn_set[1], preferred_element_type=jnp.float32)
    mlp_set = (
        lax.all_gather(gate_weight, ("batch", "ctx"), axis=0, tiled=True),
        lax.all_gather(up_weight, ("batch", "ctx"), axis=0, tiled=True),
        lax.all_gather(down_weight, ("batch", "ctx"), axis=0, tiled=True),
        lax.all_gather(ln2_gain, ("batch", "ctx"), axis=0, tiled=True),
        lax.all_gather(ln2_shift, ("batch", "ctx"), axis=0, tiled=True),
    )
    gain_two = mlp_set[3].astype(jnp.float32)
    shift_two = mlp_set[4].astype(jnp.float32)
    normed_two_low = layer_norm(middle, gain_two, shift_two).astype(jnp.bfloat16)
    gate_value = jnp.dot(normed_two_low, mlp_set[0], preferred_element_type=jnp.float32)
    up_value = jnp.dot(normed_two_low, mlp_set[1], preferred_element_type=jnp.float32)
    hidden_low = swish_product(gate_value, up_value).astype(jnp.bfloat16)
    mixed = (middle + project_back(hidden_low, mlp_set[2])).astype(jnp.bfloat16)
    mlp_back = (
        lax.all_gather(gate_weight, ("batch", "ctx"), axis=0, tiled=True),
        lax.all_gather(up_weight, ("batch", "ctx"), axis=0, tiled=True),
        lax.all_gather(down_weight, ("batch", "ctx"), axis=0, tiled=True),
        lax.all_gather(ln2_gain, ("batch", "ctx"), axis=0, tiled=True),
        lax.all_gather(ln2_shift, ("batch", "ctx"), axis=0, tiled=True),
    )
    attn_back = (
        lax.all_gather(qkv_weight, ("batch", "ctx"), axis=0, tiled=True),
        lax.all_gather(out_weight, ("batch", "ctx"), axis=0, tiled=True),
        lax.all_gather(qkv_bias, ("batch", "ctx"), axis=0, tiled=True),
        lax.all_gather(ln1_gain, ("batch", "ctx"), axis=0, tiled=True),
        lax.all_gather(ln1_shift, ("batch", "ctx"), axis=0, tiled=True),
    )
    branch_two = cotangent.astype(jnp.bfloat16)
    hidden_grad = jnp.dot(branch_two, mlp_back[2], preferred_element_type=jnp.float32)
    unused_value, act_pull = jax.vjp(swish_product, gate_value, up_value)
    gate_grad, up_grad = act_pull(hidden_grad)
    gate_low = gate_grad.astype(jnp.bfloat16)
    up_low = up_grad.astype(jnp.bfloat16)
    normed_two_grad = project_back(gate_low, mlp_back[0]) + project_back(up_low, mlp_back[1])
    unused_two, norm_pull_two = jax.vjp(layer_norm, middle, gain_two, shift_two)
    middle_part, gain_two_grad, shift_two_grad = norm_pull_two(normed_two_grad)
    middle_grad = cotangent + middle_part
    gate_weight_grad, up_weight_grad, down_weight_grad = (
        lax.psum_scatter(
            outer_rows(left, right).astype(jnp.bfloat16), ("batch", "ctx"), scatter_dimension=0, tiled=True
        ).astype(jnp.float32)
        for left, right in ((normed_two_low, gate_low), (normed_two_low, up_low), (branch_two, hidden_low))
    )
    branch_one = middle_grad.astype(jnp.bfloat16)
    out_term = outer_rows(attended_low, branch_one)
    attended_grad = project_back(branch_one, attn_back[1]).astype(jnp.bfloat16)
    grad_heads = attended_grad.reshape(local_rows, H, HD)
    delta = jnp.transpose(
        jnp.sum((attended_grad.astype(jnp.float32) * attended).reshape(local_rows, H, HD), axis=-1)
    )
    key_all, value_all = (
        lax.all_gather(key_rows, "ctx", axis=0, tiled=True),
        lax.all_gather(value_rows, "ctx", axis=0, tiled=True),
    )
    back_rows = 512
    back_count = seq_length // back_rows

    def back_block(query_grad, block):
        key_block, value_block, offset = block
        raw_scores = (
            jnp.einsum("qhd,khd->hqk", queries, key_block, preferred_element_type=jnp.float32)
            * 0.125
        )
        key_places = offset + jnp.arange(back_rows, dtype=jnp.int32)
        allowed = (key_places[None, :] <= places[:, None])[None]
        probs = jnp.where(allowed, jnp.exp(raw_scores - log_total[..., None]), 0.0)
        prob_grad = jnp.einsum(
            "qhd,khd->hqk", grad_heads, value_block, preferred_element_type=jnp.float32
        )
        score_grad = (probs * (prob_grad - delta[..., None])).astype(jnp.bfloat16)
        query_grad = (
            query_grad
            + jnp.einsum("hqk,khd->qhd", score_grad, key_block, preferred_element_type=jnp.float32)
            * 0.125
        )
        key_grad = (
            jnp.einsum("hqk,qhd->khd", score_grad, queries, preferred_element_type=jnp.float32)
            * 0.125
        )
        value_grad = jnp.einsum(
            "hqk,qhd->khd",
            probs.astype(jnp.bfloat16),
            grad_heads,
            preferred_element_type=jnp.float32,
        )
        return (
            query_grad,
            jnp.concatenate(
                [key_grad.reshape(back_rows, D), value_grad.reshape(back_rows, D)], axis=1
            ),
        )

    back_offsets = jnp.arange(back_count, dtype=jnp.int32) * back_rows
    back_blocks = (
        key_all.reshape(back_count, back_rows, H, HD),
        value_all.reshape(back_count, back_rows, H, HD),
        back_offsets,
    )
    query_grad, kv_terms = lax.scan(
        back_block, jnp.zeros((local_rows, H, HD), jnp.float32), back_blocks
    )
    kv_local = lax.psum_scatter(
        kv_terms.reshape(seq_length, 2 * D).astype(jnp.bfloat16),
        "ctx",
        scatter_dimension=0,
        tiled=True,
    ).astype(jnp.float32)

    def turn_heads(heads_in):
        return rotary(heads_in, places)

    unused_three, turn_pull = jax.vjp(turn_heads, pair_heads)
    pair_grad = turn_pull(
        jnp.concatenate([query_grad, kv_local[:, :D].reshape(local_rows, H, HD)], axis=1)
    )[0]
    projected_grad = jnp.concatenate(
        [pair_grad.reshape(local_rows, 2 * D), kv_local[:, D:]], axis=1
    ).astype(jnp.bfloat16)
    qkv_term = outer_rows(normed_low, projected_grad)
    bias_term = jnp.sum(projected_grad.astype(jnp.float32), axis=0)
    normed_grad = project_back(projected_grad, attn_back[0])
    unused_four, norm_pull = jax.vjp(layer_norm, inputs, gain_one, shift_one)
    input_part, gain_one_grad, shift_one_grad = norm_pull(normed_grad)
    tokens_grad = (middle_grad + input_part).reshape(1, local_rows, D)
    summed = (
        lax.psum_scatter(qkv_term, ("batch", "ctx"), scatter_dimension=0, tiled=True),
        lax.psum_scatter(out_term, ("batch", "ctx"), scatter_dimension=0, tiled=True),
        lax.psum_scatter(bias_term, ("batch", "ctx"), scatter_dimension=0, tiled=True),
        lax.psum_scatter(gain_one_grad, ("batch", "ctx"), scatter_dimension=0, tiled=True),
        lax.psum_scatter(shift_one_grad, ("batch", "ctx"), scatter_dimension=0, tiled=True),
        lax.psum_scatter(gain_two_grad, ("batch", "ctx"), scatter_dimension=0, tiled=True),
        lax.psum_scatter(shift_two_grad, ("batch", "ctx"), scatter_dimension=0, tiled=True),
    )
    return (
        mixed.reshape(1, local_rows, D),
        tokens_grad,
        summed[3],
        summed[4],
        summed[0],
        summed[2],
        summed[1],
        summed[5],
        summed[6],
        gate_weight_grad,
        up_weight_grad,
        down_weight_grad,
    )


BF = jnp.bfloat16
F32 = jnp.float32
MESH = pl.DeviceIdType.MESH
ANY = pl.ANY
VM = pltpu.VMEM
REMOTE_SEMS = 320
LOCAL_SEMS = 64


def nt(left, right):
    return lax.dot_general(left, right, (((1,), (1,)), ((), ())), preferred_element_type=F32)


def tn(left, right):
    return lax.dot_general(left, right, (((0,), (0,)), ((), ())), preferred_element_type=F32)


def nn(left, right):
    return jnp.dot(left, right, preferred_element_type=F32)


def norm_stats(values):
    centre = jnp.mean(values, axis=-1, keepdims=True)
    centred = values - centre
    spread = jnp.mean(centred * centred, axis=-1, keepdims=True)
    scale = lax.rsqrt(spread + 1e-05)
    return centred * scale, scale


def norm_moments(values):
    centre = jnp.mean(values, axis=-1, keepdims=True)
    centred = values - centre
    return centre, lax.rsqrt(jnp.mean(centred * centred, axis=-1, keepdims=True) + 1e-05)


def norm_back(grad, unit, scale, gain):
    weighted = grad * gain
    lead = jnp.mean(weighted, axis=-1, keepdims=True)
    tilt = jnp.mean(weighted * unit, axis=-1, keepdims=True)
    return scale * (weighted - lead - unit * tilt)


def turn_tables(length):
    half = ROT // 2
    freq = (np.float32(10000.0) ** (-np.arange(half, dtype=np.float32) * np.float32(2.0) / np.float32(ROT))).astype(np.float32)
    angles = np.arange(length, dtype=np.float32)[:, None] * freq[None, :]
    cosine, sine = np.cos(angles), np.sin(angles)
    tables = np.zeros((2, length, 128), np.float32)
    tables[0] = 1.0
    for start in (0, HD):
        tables[0, :, start : start + half] = cosine
        tables[0, :, start + half : start + ROT] = cosine
        tables[1, :, start : start + half] = -sine
        tables[1, :, start + half : start + ROT] = sine
    return tables


def aligned(value, to):
    return value if isinstance(value, int) else pl.multiple_of(value, to)


def feed_columns(width):
    return 2 * width + -(-width // 128) * 128


def qkv_lane(kind, head, heads):
    half = heads // 2
    return ((head // half * 3 + kind) * half + head % half) * HD


class Names:
    pass


def layer_kernel(dims, names_in, names_out, names_scratch, *refs):
    R, C, PL, rows, shard, QW, FW, PARTS = dims
    r = Names()
    for name, ref in zip(names_in + names_out + names_scratch, refs):
        setattr(r, name, ref)
    batch = lax.axis_index("batch")
    c = lax.axis_index("ctx")
    z = batch // 2
    core = lax.rem(batch, 2)
    q = core * C + c
    HS = PL // 2 * rows
    TOK = PL * rows
    KB = PL * shard
    STARTS = [sum(PARTS[:p]) for p in range(len(PARTS))]
    WC = [feed_columns(width) for width in PARTS]
    heads = QW // HD
    QH = QW // 2

    def lanes(kind, head):
        first = qkv_lane(kind, head, heads)
        return slice(first, first + HD)


    at_plane = [z == at for at in range(R)]
    counter = [0]
    local_count = [0]

    def slots(count):
        first = counter[0]
        counter[0] += count
        return first

    def mate(i):
        other = lax.rem(q + i, PL)
        return (z * 2 + other // C, lax.rem(other, C))

    def row_index(i):
        across, along = lax.rem(lax.rem(c, 2) + lax.rem(i, 2), 2), lax.rem(c // 2 + i // 2, 2)
        return 2 * along + across

    def row_mate(i):
        return (batch, row_index(i))

    sibling = (z * 2 + 1 - core, c)

    def plane_dev(t):
        return (t * 2 + core, c)

    def rcopy(src, dst, send, recv, dev):
        return pltpu.make_async_remote_copy(
            src_ref=src, dst_ref=dst, send_sem=r.ss.at[send], recv_sem=r.rs.at[recv], device_id=dev, device_id_type=MESH
        )

    drains = []

    def lcopy(src, dst):
        copy = pltpu.make_async_copy(src, dst, r.ls.at[local_count[0]])
        local_count[0] += 1
        copy.start()
        return copy

    barrier = pltpu.get_barrier_semaphore()
    for i in range(1, PL):
        pl.semaphore_signal(barrier, inc=1, device_id=mate(i), device_id_type=MESH)
    for i in range(1, R):
        pl.semaphore_signal(barrier, inc=1, device_id=plane_dev(lax.rem(z + i, R)), device_id_type=MESH)
    loads = {name: lcopy(getattr(r, "in_" + name), getattr(r, "v_" + name)) for name in ("tokens", "cot")}

    local_tables = lcopy(r.tables, r.turns)
    r.sgt[...] = jnp.zeros_like(r.sgt)
    for k, vector in enumerate((r.in_g0, r.in_g1, r.in_g2, r.in_g3)):
        r.sgt[k : k + 1, 0:shard] = vector[...].astype(F32)
    for k in range(3):
        r.sgt[4 + k : 5 + k, 0:HD] = r.in_bias[0:1, k * HD : (k + 1) * HD].astype(F32)

    pl.semaphore_wait(barrier, PL - 1 + R - 1)

    OFFS = (1, -1)

    class ZGather:
        def __init__(self, whole, height, chunks=1):
            self.whole, self.height, self.chunks = whole, height, chunks
            self.base = [slots(6) for _ in range(chunks)]

        def block(self, s, chunk=None):
            if chunk is None:
                return self.whole.at[pl.ds(aligned(s * self.height, 16), self.height)]
            part = self.height // self.chunks
            return self.whole.at[pl.ds(aligned(s * self.height + chunk * part, 16), part)]

        def guarded(self, ok, make):
            @pl.when(ok)
            def _():
                make().start()

            def drain():
                @pl.when(ok)
                def _():
                    make().wait_send()

            drains.append(drain)

        def start(self, src=None):
            for chunk in range(self.chunks):
                for k, off in enumerate(OFFS):
                    t = z + off
                    ok = (t >= 0) & (t < R)

                    def make(chunk=chunk, k=k, t=t):
                        mine = self.block(z, chunk)
                        return rcopy(mine if src is None else src, mine, self.base[chunk] + k, self.base[chunk] + z, plane_dev(t))

                    self.guarded(ok, make)

        def got(self, s, chunk):
            block = self.block(s, chunk)
            rcopy(block, block, self.base[chunk], self.base[chunk] + s, sibling).wait_recv()

        def relay(self, chunk=0):
            for at, passes in ((R - 2, ((3, 1), (1, 3), (0, 3))), (1, ((0, 2), (2, 0), (3, 0)))):
                for k, (s, to) in enumerate(passes):

                    @pl.when(z == at)
                    def _():
                        self.got(s, chunk)

                    def make(s=s, to=to, k=k):
                        block = self.block(s, chunk)
                        return rcopy(block, block, self.base[chunk] + 2 + k, self.base[chunk] + s, plane_dev(to))

                    self.guarded(z == at, make)

        def wait_block(self, s):
            for chunk in range(self.chunks):
                skip = z == s
                skip = skip | ((z > 0) & (z < R - 1))

                @pl.when(jnp.logical_not(skip))
                def _():
                    self.got(s, chunk)

        def wait(self):
            for s in range(R):
                self.wait_block(s)

    class Spread:
        def __init__(self, stage):
            self.stage, self.base = stage, slots(PL)

        def start(self, target):
            self.target = target
            for i in range(1, PL):
                other = lax.rem(q + i, PL)
                copy = rcopy(self.stage.at[other], target, self.base + i, self.base + i, mate(i))
                copy.start()

        def wait_send(self):
            for i in range(1, PL):
                other = lax.rem(q + i, PL)
                rcopy(self.stage.at[other], self.target, self.base + i, self.base + i, mate(i)).wait_send()

        def wait(self, block):
            for i in range(1, PL):
                rcopy(self.stage.at[0], block(lax.rem(q - i + PL, PL)), self.base + i, self.base + i, mate(i)).wait_recv()

    class Gather:
        def __init__(self, whole):
            self.whole, self.base = whole, slots(2 * C)

        def block(self, s):
            return self.whole.at[pl.ds(aligned(s * rows, 16), rows)]

        def start(self, src):
            self.local = lcopy(src, self.block(q))
            sends = []
            for i in (1, 2):
                sends.append(rcopy(src, self.block(q), self.base + i, self.base + i, row_mate(i)))
            sends.append(rcopy(src, self.block(q), self.base, self.base, sibling))
            for copy in sends:
                copy.start()
            self.sends = sends

        def half(self, s, part):
            return self.whole.at[pl.ds(aligned(s * rows + part * (rows // 2), 16), rows // 2)]

        def forward(self, i):
            part, sem = (0, self.base + 3) if i == 1 else (1, self.base + 2 * C - 1)
            half = self.half(core * C + row_index(i), part)
            return rcopy(half, half, sem, sem, row_mate(3 - i))

        def drain(self):
            for copy in self.sends:
                copy.wait_send()
            for i in (1, 2):
                self.forward(i).wait_send()
            for i in range(1, C):
                self.passed(i).wait_send()

        def relay(self):
            for i in range(1, C):
                self.relay_one(i)

        def passed(self, i):
            block = self.block(core * C + row_index(i))
            return rcopy(block, block, self.base + C - 1 + i, self.base + C - 1 + i, sibling)

        def relay_one(self, i):
            block = self.block(core * C + row_index(i))
            if i < 3:
                rcopy(block, block, self.base, self.base + i, sibling).wait_recv()
                self.forward(i).start()
            else:
                for part, sem in ((0, self.base + 3), (1, self.base + 2 * C - 1)):
                    half = self.half(core * C + row_index(i), part)
                    rcopy(half, half, self.base, sem, sibling).wait_recv()
            self.passed(i).start()

        def wait_one(self, i):
            block = self.block((1 - core) * C + row_index(i))
            sem = self.base + jnp.where(i == 0, 0, C - 1 + i)
            rcopy(block, block, self.base, sem, sibling).wait_recv()

        def wait(self):
            for i in range(C):
                self.wait_one(i)
            self.local.wait()

        def each(self, use, first=0, last=None):
            if first == 0:
                self.local.wait()

            @pl.loop(first, C if last is None else last)
            def _(i):
                @pl.when(i == 1)
                def _():
                    self.relay_one(1)
                    self.relay_one(2)

                @pl.when(i == 3)
                def _():
                    self.relay_one(3)

                use(core * C + row_index(i))
                self.wait_one(i)
                use((1 - core) * C + row_index(i))

    class Reduce:
        def __init__(self, k, before=None):
            self.sibout, self.theirs = getattr(r, f"sibout{k}"), getattr(r, f"theirs{k}")
            self.out, self.got, self.own = getattr(r, f"redout{k}"), getattr(r, f"redin{k}"), getattr(r, f"redown{k}")
            self.base = slots(C + 2)
            self.before = before


        def run(self, pairs, compute, later=False, more=False, only_prepare=False):
            chunk_rows = HS // 2

            def to_sibling(chunk):
                span = pl.ds(chunk * chunk_rows, chunk_rows)
                return rcopy(self.sibout.at[span], self.theirs.at[span], self.base + C + chunk, self.base + C + chunk, sibling)

            def product(target, weights, seq, chunk):
                total = None
                for (x, _), w in zip(pairs, weights):
                    term = compute(x[pl.ds(aligned(seq * HS + chunk * chunk_rows, 16), chunk_rows), :], w)
                    total = term if total is None else total + term
                span = pl.ds(chunk * chunk_rows, chunk_rows)
                if more:
                    total = total + target[span, :].astype(F32)
                target[span, :] = total.astype(BF)

            def pass_on(chunk):
                to_sibling(chunk).wait_recv()
                for blk in range(chunk * C // 2, (chunk + 1) * C // 2):
                    i = lax.rem(blk + c, 2) + 2 * lax.rem(blk // 2 + c // 2, 2)
                    span = pl.ds(blk * rows, rows)
                    total = r.mine[span, :].astype(F32) + self.theirs[span, :].astype(F32)

                    @pl.when(i == 0)
                    def _():
                        self.own[...] = total.astype(self.own.dtype)

                    @pl.when(i != 0)
                    def _():
                        self.out[i - 1] = total.astype(BF)
                        self.to_row(i, blk).start()

            def body(*bufs):
                bufs = list(bufs)
                weights, loads = [], []
                for _, w in pairs:
                    if isinstance(w, tuple):
                        weights.append(bufs.pop(0))
                        loads.append(lcopy(w[0], weights[-1]))
                    else:
                        weights.append(w)
                for load in loads:
                    load.wait()
                if self.before is not None and not more:
                    self.before.drain()
                if only_prepare:
                    for chunk in range(2):
                        product(self.sibout, weights, 1 - core, chunk)
                        product(r.mine, weights, core, chunk)
                    return
                product(self.sibout, weights, 1 - core, 0)
                to_sibling(0).start()
                product(r.mine, weights, core, 0)
                product(self.sibout, weights, 1 - core, 1)
                to_sibling(1).start()
                if not later:
                    pass_on(0)
                product(r.mine, weights, core, 1)
                if not later:
                    pass_on(1)

            pl.run_scoped(body, *[VM(w[0].shape, BF) for _, w in pairs if isinstance(w, tuple)])
            self.drain = lambda: self.drain_all(to_sibling)
            self.pass_on = lambda: (pass_on(0), pass_on(1))

        def prepare(self, pairs, compute):
            self.run(pairs, compute, only_prepare=True)

        def to_row(self, i, blk):
            return rcopy(self.out.at[i - 1], self.got.at[i - 1], self.base + i, self.base + i, (batch, blk))

        def drain_all(self, to_sibling):
            to_sibling(0).wait_send()
            to_sibling(1).wait_send()
            for i in range(1, C):
                self.to_row(i, row_index(i)).wait_send()

        def finish(self):
            for i in range(1, C):
                rcopy(self.out.at[i - 1], self.got.at[i - 1], self.base + i, self.base + i, row_mate(i)).wait_recv()
            total = self.own[...].astype(F32)
            for i in range(1, C):
                total = total + self.got[i - 1].astype(F32)
            return total

    middle_plane = (z > 0) & (z < R - 1)
    ORDER = ((3, 2, 1, 0), (0, 3, 2, 1), (3, 0, 1, 2), (0, 1, 2, 3))

    class ZReduce:
        def __init__(self, grads, got, extra, merged, height, direct=False, chain=False):
            self.direct, self.chain = direct, chain
            self.grads, self.got, self.extra, self.merged, self.height = grads, got, extra, merged, height
            self.base = slots(12)

        def block(self, t):
            return self.grads.at[pl.ds(aligned(t * self.height, 16), self.height)]

        def guarded(self, ok, make):
            @pl.when(ok)
            def _():
                make().start()

            def drain():
                @pl.when(ok)
                def _():
                    make().wait_send()

            drains.append(drain)

        def send(self, at, owner):
            b = self.base
            via = {0: 1, R - 1: R - 2}.get(at)
            if owner == at or (via is None and abs(owner - at) == 2) or (via is None and owner == R - 1 - at):
                return
            if via is None:
                slot = 1 if owner < at else 0
                return
            elif owner == via:
                slot = 0 if at == 0 else 1
                make = lambda: rcopy(self.block(owner), self.got.at[slot], b + 2, b + slot, plane_dev(via))
            elif self.direct and abs(owner - at) == 2:
                make = lambda: rcopy(self.block(owner), self.got.at[2], b + 1, b + 6, plane_dev(owner))
            else:
                k = 0 if owner == R - 1 - at else 1
                make = lambda: rcopy(self.block(owner), self.extra.at[k], b + k, b + 2 + k, plane_dev(via))
            self.guarded(at_plane[at], make)

        def start(self):
            for step in range(R):
                self.start_step(step)

        def start_step(self, step):
            for at in range(R):
                self.send(at, ORDER[at][step])

        def add_block(self, owner, other, waited, out):
            def body(own, more, sem):
                first = pltpu.make_async_copy(self.block(owner), own, sem.at[0])
                first.start()
                waited.wait_recv()
                second = pltpu.make_async_copy(other, more, sem.at[1])
                second.start()
                first.wait()
                second.wait()
                own[...] = (own[...].astype(F32) + more[...].astype(F32)).astype(BF)
                pltpu.sync_copy(own, out)

            shape = (self.height, self.grads.shape[1])
            pl.run_scoped(body, VM(shape, BF), VM(shape, BF), pltpu.SemaphoreType.DMA((2,)))

        def merge(self, steps=(0, 1)):
            b = self.base
            if 0 in steps and not self.chain:
                for at, owner, slot in ((1, 0, 1), (2, 3, 0)):
                    self.guarded(
                        at_plane[at],
                        lambda owner=owner, slot=slot: rcopy(self.block(owner), self.got.at[slot], b + 3, b + slot, plane_dev(owner)),
                    )
            if self.direct:
                steps = (0,)
                for at, owner, slot in ((1, 2, 0), (2, 1, 1)):
                    self.guarded(
                        at_plane[at],
                        lambda owner=owner, slot=slot: rcopy(self.block(owner), self.got.at[slot], b + 5, b + slot, plane_dev(owner)),
                    )
            for k in steps:
                for at, to, slots_at in ((1, (3, 2, 0), (1, 0, 1)), (2, (0, 1, 3), (0, 1, 0))):
                    owner = to[k]

                    @pl.when(z == at)
                    def _():
                        source = self.merged.at[3] if k == 2 else self.extra.at[k]
                        self.add_block(owner, source, rcopy(source, source, b, b + (7 if k == 2 else 2 + k), sibling), self.merged.at[k])

                    def make(k=k, at=at, owner=owner, slot=slots_at[k]):
                        if k == 0 and self.chain:
                            return rcopy(self.merged.at[0], self.merged.at[3], b + 4, b + 7, plane_dev(3 - at))
                        return rcopy(self.merged.at[k], self.got.at[slot], b + 4 + k, b + slot, plane_dev(owner))

                    self.guarded(z == at, make)

        def wait(self):
            for slot, lone in ((0, 0), (1, R - 1)):

                @pl.when(z != lone if self.chain else z >= 0)
                def _():
                    rcopy(self.got.at[slot], self.got.at[slot], self.base, self.base + slot, sibling).wait_recv()

            if self.direct:

                @pl.when(middle_plane)
                def _():
                    rcopy(self.got.at[2], self.got.at[2], self.base, self.base + 6, sibling).wait_recv()

        def finish(self, put):
            self.wait()

            def body(own, one, two, *three):
                at_one, at_two = 0, 1
                if self.chain:
                    at_one, at_two = jnp.where(z == 0, 1, 0), jnp.where(z == R - 1, 0, 1)
                loads = [lcopy(self.block(z), own), lcopy(self.got.at[at_one], one), lcopy(self.got.at[at_two], two)]
                if three:
                    loads.append(lcopy(self.got.at[jnp.where(middle_plane, 2, 0)], three[0]))
                for load in loads:
                    load.wait()
                for k in range(self.height // shard):
                    span = pl.ds(k * shard, shard)
                    total = own[span, :].astype(F32) + one[span, :].astype(F32)
                    last = two[span, :].astype(F32)
                    total = total + (jnp.where(middle_plane, last, 0.0) if self.chain else last)
                    if three:
                        total = total + jnp.where(middle_plane, three[0][span, :].astype(F32), 0.0)
                    put(k, total)

            shape = (self.height, self.grads.shape[1])
            pl.run_scoped(body, *[VM(shape, BF)] * (4 if self.direct else 3))

    zg_o, zg_qkv = ZGather(r.w_o, shard), ZGather(r.w_qkv, KB, 2)
    sp_qkv = Spread(r.st_qkv)
    parts = range(len(PARTS))
    def each_part(name):
        return [getattr(r, f"{name}{p}") for p in parts]

    w_f, st_f = each_part("w_f"), each_part("st_f")
    zg_f, sp_f = [ZGather(w, KB) for w in w_f], [Spread(st) for st in st_f]
    ag_normed, ag_cot, ag_two, ag_one = Gather(r.a_normed), Gather(r.a_cot), Gather(r.a_two), Gather(r.a_one)

    def mine_rows(whole, height):
        return whole.at[pl.ds(aligned((z * PL + q) * height, 16), height)]

    zg_o.start(r.in_o)
    local_o = lcopy(r.in_o, zg_o.block(z))
    base_small = slots(PL)
    small_sent = []
    for i in range(1, PL):
        copy = rcopy(r.sgt, r.small.at[z * PL + q], base_small + i, base_small + i, mate(i))
        copy.start()
        small_sent.append(copy)
    local_small = lcopy(r.sgt, r.small.at[z * PL + q])
    def stage_qkv(v):
        lcopy(r.in_qkv, v).wait()
        for other in range(PL):
            for j in range(3):
                for zh in range(R):
                    at = j * D + zh * PL * HD + other * HD
                    r.st_qkv[other, :, lanes(j, zh)] = v[:, at : at + HD]

    pl.run_scoped(stage_qkv, VM(r.in_qkv.shape, BF))
    sp_qkv.start(mine_rows(r.w_qkv, shard))
    local_qkv = lcopy(r.st_qkv.at[q], mine_rows(r.w_qkv, shard))
    local_f = [None] * len(PARTS)

    def stage_f(*bufs):
        loads = [lcopy(source, buf) for source, buf in zip((r.in_gate, r.in_up, r.in_down), bufs)]
        for load in loads:
            load.wait()
        for p, width in enumerate(PARTS):
            for other in range(PL):
                at = other * FW + STARTS[p]
                for k, source in enumerate(bufs):
                    st_f[p][other, :, k * width : (k + 1) * width] = source[:, at : at + width]
                if WC[p] > 3 * width:
                    st_f[p][other, :, 3 * width :] = jnp.zeros((shard, WC[p] - 3 * width), BF)

    def spread_f(p):
        sp_f[p].start(mine_rows(w_f[p], shard))
        local_f[p] = lcopy(st_f[p].at[q], mine_rows(w_f[p], shard))

    def arrived(spread, whole):
        spread.wait(lambda s: whole.at[pl.ds(aligned((z * PL + s) * shard, 16), shard)])

    pl.run_scoped(stage_f, *[VM(r.in_gate.shape, BF)] * 3)
    spread_f(0)

    local_small.wait()
    for i in range(1, PL):
        rcopy(r.sgt, r.small.at[z * PL + lax.rem(q - i + PL, PL)], base_small, base_small + i, mate(i)).wait_recv()
    base_smallz = slots(R)
    plane_small = r.small.at[pl.ds(z * PL, PL)]
    for i in range(1, R):
        copy = rcopy(plane_small, plane_small, base_smallz + i, base_smallz + i, plane_dev(lax.rem(z + i, R)))
        copy.start()
        drains.append(copy.wait_send)
    local_qkv.wait()
    arrived(sp_qkv, r.w_qkv)
    zg_qkv.start()
    loads["tokens"].wait()
    loads["cot"].wait()
    tokens = r.v_tokens[...].astype(F32)
    unit, _ = norm_stats(tokens)
    for i in range(1, R):
        block = r.small.at[pl.ds(lax.rem(z - i + R, R) * PL, PL)]
        rcopy(block, block, base_smallz, base_smallz + i, sibling).wait_recv()
    for d in range(R * PL):
        for k in range(4):
            r.vec[k : k + 1, shard * d : shard * (d + 1)] = r.small[d, k : k + 1, 0:shard]
        for k in range(3):
            r.biases[3 * d + k : 3 * d + k + 1, 0:HD] = r.small[d, 4 + k : 5 + k, 0:HD]
    for j in range(3):
        for zh in range(R):
            row = r.biases[pl.ds(j * H + zh * PL + q, 1), 0:HD]
            r.bias[0:1, lanes(j, zh)] = row
    r.x_normed[...] = (unit * r.vec[0:1, :] + r.vec[1:2, :]).astype(BF)
    ag_normed.start(r.x_normed)

    spread_f(1)
    spread_f(2)
    ag_cot.start(r.v_cot)
    local_f[0].wait()
    arrived(sp_f[0], w_f[0])
    zg_qkv.relay(0)
    zg_qkv.relay(1)
    zg_o.relay()
    zg_f[0].start()
    ag_normed.relay()
    ag_normed.wait()
    zg_qkv.wait()

    def lower(shape):
        return lax.rem(lax.broadcasted_iota(jnp.int32, shape, 1), HD) < ROT // 2

    def in_turn(shape):
        return lax.rem(lax.broadcasted_iota(jnp.int32, shape, 1), HD) < ROT

    TM = HS // 2
    local_tables.wait()

    @pl.loop(0, TOK // HS)
    def _(i):
        span = pl.ds(aligned(i * HS, HS), HS)
        projected = nn(r.a_normed[span, :], r.w_qkv[...]) + r.bias[0:1, :]
        for first in [half * 3 * QH + k * 128 for half in range(2) for k in range(2 * QH // 128)]:
            part = projected[:, first : first + 128]
            other = jnp.where(lower(part.shape), pltpu.roll(part, 128 - ROT // 2, 1), pltpu.roll(part, ROT // 2, 1))
            turned = part * r.turns[0] + other * r.turns[1]
            r.qkv[span, first : first + 128] = turned.astype(BF)
        for half in range(2):
            values = slice(half * 3 * QH + 2 * QH, (half + 1) * 3 * QH)
            r.qkv[span, values] = projected[:, values].astype(BF)

    def softmax_block(queries, keys, first):
        scores = nt(keys, queries) * 0.125
        at_key = lax.broadcasted_iota(jnp.int32, scores.shape, 0)
        at_query = lax.broadcasted_iota(jnp.int32, scores.shape, 1) + first
        allowed = at_key <= at_query
        scores = jnp.where(allowed, scores, -1e30)
        largest = jnp.max(scores, axis=0, keepdims=True)
        weights = jnp.where(allowed, jnp.exp(scores - largest), 0.0)
        return weights / jnp.sum(weights, axis=0, keepdims=True)

    QB = HS // 2

    kept = []
    for seq, keep in enumerate((r.sibout1, r.theirs1)):

        for h in range(heads):
            for blk in range(HS // QB):
                here = pl.ds(seq * HS + blk * QB, QB)
                seen = pl.ds(seq * HS, (blk + 1) * QB)
                probs = softmax_block(r.qkv[here, lanes(0, h)], r.qkv[seen, lanes(1, h)], blk * QB).astype(BF)
                keep[0 : (blk + 1) * QB, h * HS + blk * QB : h * HS + (blk + 1) * QB] = probs
                r.att[here, h * HD : (h + 1) * HD] = tn(probs, r.qkv[seen, lanes(2, h)]).astype(BF)
        kept.append(lcopy(keep, r.probs.at[pl.ds(seq * HS, HS)]))

    for p in (1, 2):
        local_f[p].wait()
        arrived(sp_f[p], w_f[p])
    ag_cot.relay()
    local_o.wait()
    zg_o.wait()

    red_att = Reduce(0)
    red_att.run([(r.att, r.w_o)], lambda x, w: nn(x, w[...]))
    zg_f[0].relay()
    zg_f[1].start()
    ag_cot.wait()
    for copy in kept:
        copy.wait()
    middle = r.v_tokens[...].astype(F32) + red_att.finish()
    r.middle[...] = middle
    unit, _ = norm_stats(middle)
    r.x_two[...] = (unit * r.vec[2:3, :] + r.vec[3:4, :]).astype(BF)
    ag_two.start(r.x_two)
    zg_f[1].relay()
    zg_f[2].start()

    hid, gug, g_f = each_part("hid"), each_part("gug"), each_part("g_f")

    def feed_forward(p, then=None):
        width = PARTS[p]
        def body(w):
            loads = []
            for s in range(R):
                zg_f[p].wait_block(s)
                loads.append(lcopy(zg_f[p].block(s), w.at[pl.ds(s * KB, KB)]))
            for load in loads:
                load.wait()

            def use(span):
                both = nn(r.a_two[span, :], w[:, : 2 * width])
                gate = both[:, :width]
                up = both[:, width:]
                sig = 1.0 / (1.0 + jnp.exp(-gate))
                swish = gate * sig
                hid[p][span, :] = (swish * up).astype(BF)
                hidden_grad = nn(r.a_cot[span, :], w[:, 2 * width : 3 * width])
                gug[p][span, :width] = (hidden_grad * up * sig * (1.0 + gate * (1.0 - sig))).astype(BF)
                gug[p][span, width:] = (hidden_grad * swish).astype(BF)

            if p == 0:
                ag_two.each(lambda s: use(pl.ds(aligned(s * rows, 16), rows)))
            else:

                @pl.loop(0, TOK // TM)
                def _(i):
                    use(pl.ds(aligned(i * TM, TM), TM))

            if then is not None:
                then(w)

        pl.run_scoped(body, VM(w_f[p].shape, BF))

    def grads_by_owner(terms, out, reduce, padded=None, steps=range(R)):
        width = out.shape[1]

        def body(tile, sem):
            pending = []

            def hand_on():
                store, step = pending.pop(0)
                store.wait()
                reduce.start_step(step)

            for step in steps:
                owner = R - 1 - step
                for at in range(1, R):
                    owner = jnp.where(z == at, ORDER[at][step], owner)
                for left, right, first in terms:
                    part = tn(left[:, pl.ds(aligned(owner * KB, KB), KB)], right[...])
                    tile[step % depth, :, first : first + right.shape[1]] = part.astype(BF)
                if padded is not None:
                    tile[step % depth, :, padded:] = jnp.zeros((KB, width - padded), BF)
                store = pltpu.make_async_copy(tile.at[step % depth], reduce.block(owner), sem.at[step % depth])
                store.start()
                pending.append((store, step))
                while len(pending) > (0 if step in (0, steps[-1]) else 1):
                    hand_on()

        depth = min(2, len(steps))
        pl.run_scoped(body, VM((depth, KB, width), BF), pltpu.SemaphoreType.DMA((depth,)))

    def feed_weight_grads(p, steps=range(R)):
        width = PARTS[p]
        terms = [(r.a_two, gug[p], 0), (r.a_cot, hid[p], 2 * width)]
        grads_by_owner(terms, g_f[p], zr_f[p], 3 * width if WC[p] > 3 * width else None, steps)

    zr_f = [ZReduce(*bufs, KB, chain=True) for bufs in zip(g_f, each_part("zin_f"), each_part("zx_f"), each_part("zs_f"))]
    zr_o = ZReduce(r.g_o, r.zin_o, r.zx_o, r.zs_o, shard)
    g_q = [r.g_q0, r.g_q1]
    zr_q = [ZReduce(g_q[0], r.zin_q0, r.zx_q0, r.zs_q0, KB, chain=True), ZReduce(g_q[1], r.zin_q1, r.zx_q1, r.zs_q1, KB)]

    feed_forward(0)
    zg_f[2].relay()
    feed_weight_grads(0)
    feed_forward(1)
    feed_weight_grads(1)
    red_two = Reduce(0, red_att)
    first_pairs = [(gug[p], (w_f[p].at[:, pl.ds(0, 2 * PARTS[p])],)) for p in (0, 1)]
    red_two.prepare(first_pairs, lambda x, w: nt(x, w[...]))

    def back_into_layer(w):
        feed_weight_grads(2, (0,))
        red_two.run([(gug[2], w.at[:, pl.ds(0, 2 * PARTS[2])])], lambda x, w: nt(x, w[...]), more=True)

    zr_f[0].merge((0, 1))
    feed_forward(2, back_into_layer)
    feed_weight_grads(2, (1, 2, 3))
    zr_f[0].merge((2,))
    ag_normed.drain()
    centre, scale = norm_moments(r.middle[...])
    two_grad = red_two.finish()
    unit = (r.middle[...] - centre) * scale
    middle_grad = r.v_cot[...].astype(F32) + norm_back(two_grad, unit, scale, r.vec[2:3, :])
    r.x_normed[...] = middle_grad.astype(BF)
    ag_one.start(r.x_normed)
    r.middle_grad[...] = middle_grad
    r.vec[6:7, :] = jnp.sum(two_grad * unit, axis=0, keepdims=True)
    r.vec[7:8, :] = jnp.sum(two_grad, axis=0, keepdims=True)

    zr_f[1].merge((0,))
    red_mixed = Reduce(1)
    mixed_pairs = [(hid[p], (w_f[p].at[:, pl.ds(2 * PARTS[p], WC[p] - 2 * PARTS[p])],)) for p in parts]
    red_mixed.run(mixed_pairs, lambda x, w: nt(x, w[:, : x.shape[1]]), later=True)

    attg = gug[1]

    def att_grad(s):
        span = pl.ds(aligned(s * rows, 16), rows)
        pltpu.sync_copy(ag_one.block(s), r.a_two.at[span])
        attg[span, 0:QW] = nt(r.a_two[span, :], r.w_o[...]).astype(BF)

    ag_two.drain()
    ag_cot.drain()
    zr_f[1].merge((1,))

    weights_back = lcopy(r.probs, r.a_cot)

    back_f, back_q = [Spread(st) for st in st_f], [Spread(r.st_q0), Spread(r.st_q1)]
    pin_f = each_part("pin_f")
    pin_q, st_q = [r.pin_q0, r.pin_q1], [r.st_q0, r.st_q1]

    def pin_block(got):
        return lambda s: got.at[s]

    def z_sum(reduce, sent, stage, spread, got):
        if sent is not None:
            sent.wait_send()

        def put(k, total):
            stage[k] = total.astype(BF)

        reduce.finish(put)
        spread.start(got.at[q])
        return lcopy(stage.at[q], got.at[q])

    ag_one.each(att_grad, 0, C - 1)
    local_f[0] = z_sum(zr_f[0], sp_f[0], st_f[0], back_f[0], pin_f[0])
    red_mixed.pass_on()
    ag_one.each(att_grad, C - 1, C)
    zr_f[1].merge((2,))
    def o_grad(buf):
        for k in range(R):
            span = pl.ds(k * KB, KB)
            buf[:, span] = tn(r.att[...], r.a_two[:, span]).astype(BF)
        pltpu.sync_copy(buf, r.g_o)

    pl.run_scoped(o_grad, VM((QW, D), BF))
    zr_o.start()
    zr_f[2].merge((0,))

    def attention_back(half):
        def body(turn):
            @pl.loop(0, TOK // HS)
            def _(i):
                first = i * HS
                for hh in range(heads // 2):
                    h = half * heads // 2 + hh
                    key_grad = [jnp.zeros((QB, HD), F32) for _ in range(HS // QB)]
                    value_grad = [jnp.zeros((QB, HD), F32) for _ in range(HS // QB)]
                    for blk in range(HS // QB):
                        here = pl.ds(aligned(first + blk * QB, 16), QB)
                        seen = pl.ds(aligned(first, 16), (blk + 1) * QB)
                        queries, keys, values = r.qkv[here, lanes(0, h)], r.qkv[seen, lanes(1, h)], r.qkv[seen, lanes(2, h)]
                        grads = attg[here, h * HD : (h + 1) * HD]
                        low_probs = r.a_cot[seen, h * HS + blk * QB : h * HS + (blk + 1) * QB]
                        probs = low_probs.astype(F32)
                        prob_grad = nt(values, grads)
                        delta = jnp.sum(probs * prob_grad, axis=0, keepdims=True)
                        score_grad = (probs * (prob_grad - delta)).astype(BF)
                        turn[blk * QB : (blk + 1) * QB, hh * HD : (hh + 1) * HD] = tn(score_grad, keys) * 0.125
                        key_part = nn(score_grad, queries) * 0.125
                        value_part = nn(low_probs, grads)
                        for k in range(blk + 1):
                            key_grad[k] = key_grad[k] + key_part[k * QB : (k + 1) * QB]
                            value_grad[k] = value_grad[k] + value_part[k * QB : (k + 1) * QB]
                    for k in range(HS // QB):
                        turn[k * QB : (k + 1) * QB, QH + hh * HD : QH + (hh + 1) * HD] = key_grad[k]
                        r.qkv[pl.ds(aligned(first + k * QB, 16), QB), lanes(2, h)] = value_grad[k].astype(BF)
                for k in range(2 * QH // 128):
                    part = turn[:, k * 128 : (k + 1) * 128]
                    cross = part * r.turns[1]
                    other = jnp.where(lower(part.shape), pltpu.roll(cross, 128 - ROT // 2, 1), pltpu.roll(cross, ROT // 2, 1))
                    back = part * r.turns[0] + jnp.where(in_turn(part.shape), other, 0.0)
                    at = half * 3 * QH + k * 128
                    r.qkv[pl.ds(aligned(first, 16), HS), at : at + 128] = back.astype(BF)

        pl.run_scoped(body, VM((HS, 2 * QH), F32))
        grads_by_owner([(r.a_normed, r.qkv.at[:, pl.ds(half * 3 * QH, 3 * QH)], 0)], g_q[half], zr_q[half])

    early = list(drains)
    drains.clear()
    weights_back.wait()
    attention_back(0)
    attention_back(1)
    zr_f[2].merge((1,))
    zr_f[2].merge((2,))
    red_one = Reduce(0, red_two)
    red_one.run([(r.qkv, r.w_qkv)], lambda x, w: nt(x, w[...]))
    r.bias[0:1, :] = jnp.sum(r.qkv[...].astype(F32), axis=0, keepdims=True)

    zr_o.merge()
    local_f[1] = z_sum(zr_f[1], sp_f[1], st_f[1], back_f[1], pin_f[1])
    zr_q[0].merge((0, 1))
    mixed = r.middle[...] + red_mixed.finish()
    r.x_two[...] = mixed.astype(BF)
    outputs = [lcopy(r.x_two, r.out_mixed)]
    local_f[2] = z_sum(zr_f[2], sp_f[2], st_f[2], back_f[2], pin_f[2])
    zr_q[0].merge((2,))
    zr_q[1].merge()
    for drain in early:
        drain()
    centre, scale = norm_moments(r.v_tokens[...].astype(F32))
    one_grad = red_one.finish()
    unit = (r.v_tokens[...].astype(F32) - centre) * scale
    r.middle_grad[...] = r.middle_grad[...] + norm_back(one_grad, unit, scale, r.vec[0:1, :])
    outputs.append(lcopy(r.middle_grad, r.out_tokens))
    r.vec[4:5, :] = jnp.sum(one_grad * unit, axis=0, keepdims=True)
    r.vec[5:6, :] = jnp.sum(one_grad, axis=0, keepdims=True)
    r.sg[...] = jnp.zeros_like(r.sg)
    for d in range(R * PL):
        for k in range(4):
            r.sg[d % PL, d // PL, k : k + 1, 0:shard] = r.vec[4 + k : 5 + k, shard * d : shard * (d + 1)]
    for j in range(3):
        for zh in range(R):
            g = j * H + zh * PL + q
            piece = r.bias[0:1, lanes(j, zh)]
            r.sg[lax.rem(g // 3, PL), g // (3 * PL), pl.ds(4 + lax.rem(g, 3), 1), 0:HD] = piece
    base_sgp = slots(PL)
    for i in range(1, PL):
        other = lax.rem(q + i, PL)
        copy = rcopy(r.sg.at[other], r.sgp.at[i - 1], base_sgp + i, base_sgp + i, mate(i))
        copy.start()
        drains.append(copy.wait_send)
    zr_o.wait()
    outputs.append(lcopy(zr_o.block(z), r.own_o))
    local_f[0].wait()
    back_f[0].wait(pin_block(pin_f[0]))
    total = r.sg[q]
    for i in range(1, PL):
        rcopy(r.sgp.at[i - 1], r.sgp.at[i - 1], base_sgp, base_sgp + i, sibling).wait_recv()
        total = total + r.sgp[i - 1]
    r.sgs[...] = total
    base_sgz = slots(R)
    for i in range(1, R):
        t = lax.rem(z + i, R)
        copy = rcopy(r.sgs.at[t], r.sgz.at[i - 1], base_sgz + i, base_sgz + i, plane_dev(t))
        copy.start()
        drains.append(copy.wait_send)
    local_q = [z_sum(zr_q[half], None, st_q[half], back_q[half], pin_q[half]) for half in range(2)]
    for i in range(1, R):
        rcopy(r.sgz.at[i - 1], r.sgz.at[i - 1], base_sgz, base_sgz + i, sibling).wait_recv()
    for copy in small_sent:
        copy.wait_send()
    r.sgt[...] = r.sgs[z] + r.sgz[0] + r.sgz[1] + r.sgz[2]
    outputs.append(lcopy(r.sgt, r.out_small))
    for p in (1, 2):
        local_f[p].wait()
        back_f[p].wait(pin_block(pin_f[p]))
    for half in range(2):
        local_q[half].wait()
        back_q[half].wait(pin_block(pin_q[half]))
    for copy in outputs:
        copy.wait()
    for spread in back_f:
        spread.wait_send()
    sp_qkv.wait_send()
    for spread in back_q:
        spread.wait_send()
    ag_one.drain()
    red_mixed.drain()
    red_one.drain()
    for drain in drains:
        drain()
    assert counter[0] <= REMOTE_SEMS and local_count[0] <= LOCAL_SEMS, (counter, local_count)


def finish_outputs(got, parts, starts, planes, members, rows, shard, q_width, f_width):
    steps = 4
    tall, low = rows // steps, shard // steps

    heads = q_width // HD

    def body(mixed_in, tokens_in, small_in, pin_q0, pin_q1, own_o, zin_o, *rest):
        pins, (mixed, tokens, g0, g1, g2, g3, bias, qkv, o, gate, up, down) = rest[: len(parts)], rest[len(parts) :]
        mixed[0] = mixed_in[...]
        tokens[0] = tokens_in[...]
        o[...] = own_o[...].astype(F32) + zin_o[0].astype(F32) + zin_o[1].astype(F32)
        for k, gain in enumerate((g0, g1, g2, g3)):
            gain[...] = small_in[k : k + 1, 0:shard]
        for k in range(3):
            bias[0:1, k * HD : (k + 1) * HD] = small_in[4 + k : 5 + k, 0:HD]
        for other in range(members):
            for j in range(3):
                for zh in range(planes):
                    at = j * D + zh * members * HD + other * HD
                    pin = (pin_q0, pin_q1)[zh // (heads // 2)]
                    first = qkv_lane(j, zh % (heads // 2), heads)
                    qkv[:, at : at + HD] = pin[other, :, first : first + HD].astype(F32)
            for pin, width, start in zip(pins, parts, starts):
                at = other * f_width + start
                for k, target in enumerate((gate, up, down)):
                    target[:, at : at + width] = pin[other, :, k * width : (k + 1) * width].astype(F32)

    def tiles(shape, axis, size):
        block = tuple(size if k == axis else n for k, n in enumerate(shape))
        return pl.BlockSpec(block, lambda i: tuple(i if k == axis else 0 for k in range(len(shape))))

    ins = [
        (got["out_mixed"], 0, tall), (got["out_tokens"], 0, tall), (got["out_small"], None, 0), (got["pin_q0"], 1, low), (got["pin_q1"], 1, low),
        (got["own_o"], 0, low), (got["zin_o"], 1, low),
    ] + [(got[f"pin_f{p}"], 1, low) for p in range(len(parts))]
    outs = dict(
        mixed=((1, rows, D), BF, 1, tall), tokens=((1, rows, D), F32, 1, tall),
        g0=((1, shard), F32, None, 0), g1=((1, shard), F32, None, 0), g2=((1, shard), F32, None, 0), g3=((1, shard), F32, None, 0),
        bias=((1, 3 * HD), F32, None, 0),
        qkv=((shard, 3 * D), F32, 0, low), o=((shard, D), F32, 0, low),
        gate=((shard, FF), F32, 0, low), up=((shard, FF), F32, 0, low), down=((shard, FF), F32, 0, low),
    )
    results = pl.pallas_call(
        body,
        grid=(steps,),
        out_shape=[jax.ShapeDtypeStruct(shape, kind) for shape, kind, _, _ in outs.values()],
        in_specs=[tiles(array.shape, axis, size) for array, axis, size in ins],
        out_specs=[tiles(shape, axis, size) for shape, _, axis, size in outs.values()],
        name="finish",
    )(*[array for array, _, _ in ins])
    return dict(zip(outs, results))


def fast_local(tokens, out_grad, ln1_gain, ln1_shift, qkv_weight, qkv_bias, out_weight, ln2_gain, ln2_shift, gate_weight, up_weight, down_weight):
    planes, columns = lax.axis_size("batch") // 2, lax.axis_size("ctx")
    members = 2 * columns
    rows = tokens.shape[1]
    seq = rows * columns
    total = members * rows
    shard = qkv_weight.shape[0]
    q_width = D // members
    f_width = FF // members
    plane_rows = members * shard
    parts = (256, 256, f_width - 512)
    dims = (planes, columns, members, rows, shard, q_width, f_width, parts)
    inputs = dict(
        in_tokens=(tokens.reshape(rows, D), ANY),
        in_cot=(out_grad.reshape(rows, D), ANY),
        in_g0=(ln1_gain.reshape(1, shard), VM), in_g1=(ln1_shift.reshape(1, shard), VM),
        in_g2=(ln2_gain.reshape(1, shard), VM), in_g3=(ln2_shift.reshape(1, shard), VM), in_bias=(qkv_bias.reshape(1, 3 * HD), VM),
        in_qkv=(qkv_weight, ANY),
        in_o=(out_weight, ANY),
        in_gate=(gate_weight, ANY),
        in_up=(up_weight, ANY),
        in_down=(down_weight, ANY),
        tables=(jnp.asarray(turn_tables(seq)), ANY),
    )
    columns_f = [feed_columns(width) for width in parts]
    outs = dict(
        out_mixed=((rows, D), BF, ANY),
        out_tokens=((rows, D), F32, ANY),
        out_small=((8, 128), F32, ANY),
        pin_q0=((members, shard, 3 * q_width // 2), BF, ANY), pin_q1=((members, shard, 3 * q_width // 2), BF, ANY),
        own_o=((shard, D), BF, ANY),
        zin_o=((2, shard, D), BF, ANY),
    )
    for p, width in enumerate(columns_f):
        outs[f"pin_f{p}"] = ((members, shard, width), BF, ANY)
    final = list(outs)
    spaces = dict(
        a_one=(total, D), probs=(total, D),
        g_o=(q_width, D), zx_o=(2, shard, D), zs_o=(2, shard, D),
    )
    for half in range(2):
        spaces[f"g_q{half}"] = (D, 3 * q_width // 2)
        for kind, count in (("zin", 3), ("zx", 2), ("zs", 4)):
            spaces[f"{kind}_q{half}"] = (count, plane_rows, 3 * q_width // 2)
    for p, width in enumerate(columns_f):
        spaces[f"w_f{p}"] = spaces[f"g_f{p}"] = (D, width)
        for kind, count in (("zin", 2), ("zx", 2), ("zs", 4)):
            spaces[f"{kind}_f{p}"] = (count, plane_rows, width)
    for name, shape in spaces.items():
        outs[name] = (shape, BF, ANY)
    scratch = dict(
        v_tokens=VM((rows, D), BF), v_cot=VM((rows, D), BF),
        turns=VM((2, seq, 128), F32),
        a_normed=VM((total, D), BF), a_two=VM((total, D), BF), a_cot=VM((total, D), BF),
        w_qkv=VM((D, 3 * q_width), BF), w_o=VM((q_width, D), BF),
        qkv=VM((total, 3 * q_width), BF), att=VM((total, q_width), BF),
        st_qkv=VM((members, shard, 3 * q_width), BF),
        st_q0=VM((members, shard, 3 * q_width // 2), BF), st_q1=VM((members, shard, 3 * q_width // 2), BF),
        small=VM((planes * members, 8, 128), F32), sg=VM((members, planes, 8, 128), F32),
        sgz=VM((planes - 1, 8, 128), F32), sgs=VM((planes, 8, 128), F32), sgp=VM((members - 1, planes, 8, 128), F32), sgt=VM((8, 128), F32),
        vec=VM((8, D), F32), biases=VM((3 * H, 128), F32), bias=VM((8, 3 * q_width), F32),
        x_normed=VM((rows, D), BF), x_two=VM((rows, D), BF),
        middle=VM((rows, D), F32), middle_grad=VM((rows, D), F32),
        mine=VM((seq, D), BF),
    )
    for p, width in enumerate(parts):
        scratch[f"st_f{p}"] = VM((members, shard, columns_f[p]), BF)
        scratch[f"hid{p}"], scratch[f"gug{p}"] = VM((total, width), BF), VM((total, 2 * width), BF)
    for k in range(2):
        scratch[f"sibout{k}"] = VM((seq, D), BF)
        scratch[f"theirs{k}"] = VM((seq, D), BF)
        scratch[f"redout{k}"] = VM((columns - 1, rows, D), BF)
        scratch[f"redin{k}"] = VM((columns - 1, rows, D), BF)
        scratch[f"redown{k}"] = VM((rows, D), F32 if k == 0 else BF)
    scratch["ss"] = pltpu.SemaphoreType.DMA((REMOTE_SEMS,))
    scratch["rs"] = pltpu.SemaphoreType.DMA((REMOTE_SEMS,))
    scratch["ls"] = pltpu.SemaphoreType.DMA((LOCAL_SEMS,))
    results = pl.pallas_call(
        functools.partial(layer_kernel, dims, list(inputs), list(outs), list(scratch)),
        out_shape=[jax.ShapeDtypeStruct(shape, kind) for shape, kind, _ in outs.values()],
        in_specs=[pl.BlockSpec(memory_space=place) for _, place in inputs.values()],
        out_specs=[pl.BlockSpec(memory_space=place) for _, _, place in outs.values()],
        scratch_shapes=list(scratch.values()),
        compiler_params=pltpu.CompilerParams(collective_id=0, has_side_effects=True, vmem_limit_bytes=63 * 2**20),
        cost_estimate=pl.CostEstimate(flops=42 * 10**9, bytes_accessed=300 * 10**6, transcendentals=0),
        name="layer",
    )(*[array for array, _ in inputs.values()])
    got = dict(zip(final, results))
    f_starts = [sum(parts[:p]) for p in range(len(parts))]
    done = finish_outputs(got, parts, f_starts, planes, members, rows, shard, q_width, f_width)
    return (
        done["mixed"],
        done["tokens"],
        done["g0"].reshape(shard),
        done["g1"].reshape(shard),
        done["qkv"],
        done["bias"].reshape(3 * HD),
        done["o"],
        done["g2"].reshape(shard),
        done["g3"].reshape(shard),
        done["gate"],
        done["up"],
        done["down"],
    )


def fits(mesh):
    return mesh.shape["batch"] == 8 and mesh.shape["ctx"] == 4


def solution(mesh):
    in_specs = (
        P("batch", "ctx", None),
        P("batch", "ctx", None),
        P(("batch", "ctx")),
        P(("batch", "ctx")),
        P(("batch", "ctx"), None),
        P(("batch", "ctx")),
        P(("batch", "ctx"), None),
        P(("batch", "ctx")),
        P(("batch", "ctx")),
        P(("batch", "ctx"), None),
        P(("batch", "ctx"), None),
        P(("batch", "ctx"), None),
    )
    out_specs = (
        P("batch", "ctx", None),
        P("batch", "ctx", None),
        P(("batch", "ctx")),
        P(("batch", "ctx")),
        P(("batch", "ctx"), None),
        P(("batch", "ctx")),
        P(("batch", "ctx"), None),
        P(("batch", "ctx")),
        P(("batch", "ctx")),
        P(("batch", "ctx"), None),
        P(("batch", "ctx"), None),
        P(("batch", "ctx"), None),
    )
    body = fast_local if fits(mesh) else local
    return jax.shard_map(body, mesh=mesh, in_specs=in_specs, out_specs=out_specs, check_vma=False)
```
